32 devices in a mesh: dp: 16 (over z, x, core), tensor: 2 (over y).
Axes of the slice: x: 2, y: 2, z: 4, core: 2. Of those that a mesh axis runs over, the one named last changes fastest.
Arguments:
- residual: float32 [2048, 2048], P(('dp', 'tensor')), may hold values from -60 to 60
- norm_gain: bfloat16 [2048], P('dp'), may hold values from 0.5 to 1.5
- in_proj_x: bfloat16 [2048, 4096], P('dp', 'tensor'), may hold values from -0.125 to 0.125
- in_proj_z: bfloat16 [2048, 4096], P('dp', 'tensor'), may hold values from -0.125 to 0.125
- x_proj: bfloat16 [160, 4096], P(None, 'tensor'), may hold values from -0.09375 to 0.09375
- dt_proj: bfloat16 [128, 4096], P('dp', 'tensor'), may hold values from -0.5 to 0.5
- dt_bias: float32 [4096], P('tensor'), may hold values from -6 to -2
- conv_weight: float32 [4, 4096], P(None, 'tensor'), may hold values from -3 to 3
- conv_bias: float32 [4096], P('tensor'), may hold values from -0.5 to 0.5
- a_log: float32 [16, 4096], P(None, 'tensor'), may hold values from 0 to 2.77
- d_skip: float32 [4096], P('tensor'), may hold values from 0.5 to 1.5
- out_proj: bfloat16 [2048, 4096], P('dp', 'tensor'), may hold values from -0.1875 to 0.1875
- doc_ids: int32 [2048], P('dp'), may hold values from 0 to 127, never falling along the last dimension, each value on 1 to 128 neighbouring positions
- cotangent: float32 [2048, 2048], P(('dp', 'tensor')), may hold values from -6 to 6
Outputs:
- block_out: float32 [2048, 2048], P(('dp', 'tensor'))
- grad_residual: float32 [2048, 2048], P(('dp', 'tensor'))
- grad_norm_gain: float32 [2048], P('dp')
- grad_in_proj_x: float32 [2048, 4096], P('dp', 'tensor')
- grad_in_proj_z: float32 [2048, 4096], P('dp', 'tensor')
- grad_x_proj: float32 [160, 4096], P(None, 'tensor')
- grad_dt_proj: float32 [128, 4096], P('dp', 'tensor')
- grad_dt_bias: float32 [4096], P('tensor')
- grad_conv_weight: float32 [4, 4096], P(None, 'tensor')
- grad_conv_bias: float32 [4096], P('tensor')
- grad_a_log: float32 [16, 4096], P(None, 'tensor')
- grad_d_skip: float32 [4096], P('tensor')
- grad_out_proj: float32 [2048, 4096], P('dp', 'tensor')
- rms_resid: float32 [16], P('dp')
- rms_mixed: float32 [16], P('dp')
The draws below stay inside these ranges and needn't reach their ends.
Inputs may be any that keep to these rules, and one draw needn't show every extreme that they name: doc_ids never falls along the tokens; each document number covers 1 to 128 consecutive tokens.
All inputs are finite; a program needn't handle non-finite values.
Results may differ from the reference program's by a relative error of at most 0.011.
Values may be sent and summed in bfloat16 or wider, within the bound.
A program may use at most 256 MiB of HBM per device.

```python
import math
import jax
import jax.numpy as jnp
import numpy as np
from jax import lax

D = 2048
E = 4096
R = 128
N = 16
CONV = 4
TOK_DEV = 128
XW = 160
SEQS = 16
TOKENS = 2048
DOCS = 128
N_DP = 16


def draw_residual(key, part):
    key = jax.random.fold_in(key, 11)
    key_values, key_scales, key_pairs = jax.random.split(key, 3)
    values = jax.random.normal(key_values, (TOKENS, D), jnp.float32)
    scales = jnp.exp(jax.random.uniform(key_scales, (TOKENS, 1), jnp.float32, math.log(0.3), math.log(3.0)))
    pairing = jax.random.permutation(key_pairs, N_DP)
    token_block = jnp.arange(TOKENS) // TOK_DEV
    feature_block = jnp.arange(D) // (D // N_DP)
    boost = 1.0 + 2.0 * (pairing[token_block][:, None] == feature_block[None, :]).astype(jnp.float32)
    return jnp.clip(values * scales * boost, -60.0, 60.0)


def spiked(array, own_key, source, target, shards_of, factor):
    owner, partner = [(jnp.arange(array.shape[axis_at]) // (array.shape[axis_at] // shards_of)).reshape([-1 if axis == axis_at else 1 for axis in range(array.ndim)]) for axis_at in (source, target)]
    chosen = jax.random.permutation(own_key, shards_of)[partner]
    strong = (owner == chosen) | (owner == (partner + shards_of // 2) % shards_of)
    return jnp.where(strong, factor * array, array)


def block_levels(key, extent, cuts, low, largest):
    loudness = 1.0
    for axis_at, blocks in cuts:
        draws = jax.random.uniform(jax.random.fold_in(jax.random.fold_in(key, 6), axis_at), (blocks,), jnp.float32, low / len(cuts), largest / len(cuts))
        loudness = loudness * jnp.repeat(jnp.exp(draws), extent[axis_at] // blocks).reshape((-1,) + (1,) * (len(extent) - 1 - axis_at))
    return loudness


def length_profile(number_of, total, limit, skew):
    loads = [(1 << 20) // math.isqrt(rank ** skew) + 1 for rank in range(2, number_of + 1)]
    rest, holding = total - limit - (number_of - 1), [1] * (number_of - 1)
    while rest > 0:
        movable = [i for i in range(number_of - 1) if holding[i] < limit]
        pool, left = sum([loads[i] for i in movable]), rest
        for i in movable:
            addition = min(limit - holding[i], max(1, left * loads[i] // pool), rest)
            holding[i] = holding[i] + addition
            rest = rest - addition
    return np.array([limit] + holding)


def uneven_parts(stream_key, number_of, total, bound, lean):
    if number_of == 2:
        one = jax.random.randint(stream_key, (), max(1, total - bound), min(bound, total - 1) + 1)
        return jnp.stack([one, total - one])
    sizes = jnp.asarray(length_profile(number_of, total, bound, lean), jnp.int32)
    twos = (number_of - 1) // 2
    giver, taker = sizes[1:1 + 2 * twos:2], sizes[2:2 + 2 * twos:2]
    room = jnp.minimum(giver - 1, bound - taker)
    passed = jax.random.randint(jax.random.fold_in(stream_key, 1), (twos,), 0, 1 << 20) % (room + 1)
    sizes = sizes.at[1:1 + 2 * twos:2].set(giver - passed).at[2:2 + 2 * twos:2].set(taker + passed)
    return sizes[jax.random.permutation(jax.random.fold_in(stream_key, 2), number_of)]


def scatter_about(rng, dims, scale, most, cuts=(), held_as=jnp.bfloat16):
    values = jax.random.normal(rng, dims, jnp.float32) * scale
    if len(cuts) > 0:
        values = block_levels(rng, dims, cuts, -0.22, 0.18) * values
    return jnp.clip(values, min=-most, max=most).astype(held_as)


def heavy_noise(rng, shape, scale, limit, cuts, heavy, kind=jnp.bfloat16):
    array = scale * jax.random.normal(rng, shape, jnp.float32)
    if cuts:
        array = array * block_levels(rng, shape, cuts, -0.22, 0.18)
    return jnp.clip(spiked(array, jax.random.fold_in(rng, 3), *heavy), -limit, limit).astype(kind)


def setup_inputs(seed: int = 0) -> dict:
    arg_keys = jax.random.split(jax.random.key(seed), 15)
    residual = draw_residual(jax.random.fold_in(arg_keys[14], 71), 0)
    norm_gain = jnp.clip(1.0 + 0.1 * jax.random.normal(arg_keys[1], (D,), jnp.float32), 0.5, 1.5).astype(jnp.bfloat16)
    in_proj_x = scatter_about(arg_keys[2], (D, E), D ** -0.5, 0.125, ((0, 16), (1, 2)))
    in_proj_z = scatter_about(arg_keys[3], (D, E), D ** -0.5, 0.125, ((0, 16), (1, 2)))
    x_proj = scatter_about(arg_keys[4], (XW, E), E ** -0.5, 0.09375, ((1, 2),))
    dt_proj = scatter_about(arg_keys[5], (R, E), R ** -0.5, 0.5, ((0, 16), (1, 2)))
    dt_bias = jnp.clip(-6.0 + 4.0 * jax.random.uniform(arg_keys[6], (E,), jnp.float32) ** block_levels(arg_keys[6], (E,), ((0, 2),), -0.2, 0.2), -6.0, -2.0)
    conv_weight = scatter_about(arg_keys[7], (CONV, E), CONV ** -0.5, 3.0, ((1, 2),), jnp.float32)
    conv_bias = jnp.clip(jax.random.uniform(arg_keys[8], (E,), jnp.float32, -0.5, 0.5) * block_levels(arg_keys[8], (E,), ((0, 2),), -0.4, 0.0), -0.5, 0.5)
    a_log = jnp.clip(2.77 * jax.random.uniform(arg_keys[9], (N, E), jnp.float32) ** block_levels(arg_keys[9], (N, E), ((1, 2),), -0.2, 0.2), 0.0, 2.77)
    d_skip = jnp.clip(0.5 + 1.0 * jax.random.uniform(arg_keys[10], (E,), jnp.float32) ** block_levels(arg_keys[10], (E,), ((0, 2),), -0.2, 0.2), 0.5, 1.5)
    out_proj = scatter_about(arg_keys[11], (D, E), (E // 4) ** -0.5, 0.1875, ((0, 16), (1, 2)))
    doc_ids = jnp.searchsorted(jnp.cumsum(uneven_parts(arg_keys[12], DOCS, TOKENS, TOK_DEV, 2)), jnp.arange(TOKENS), side="right").astype(jnp.int32)
    cotangent = heavy_noise(arg_keys[13], (TOKENS, D), 1.0, 6.0, ((0, 32),), (0, 1, 32, 2.75), jnp.float32)
    return {"residual": residual, "norm_gain": norm_gain, "in_proj_x": in_proj_x, "in_proj_z": in_proj_z, "x_proj": x_proj, "dt_proj": dt_proj, "dt_bias": dt_bias, "conv_weight": conv_weight, "conv_bias": conv_bias, "a_log": a_log, "d_skip": d_skip, "out_proj": out_proj, "doc_ids": doc_ids, "cotangent": cotangent}


@jax.custom_vjp
def low(v):
    return lax.optimization_barrier(v.astype(jnp.bfloat16)).astype(jnp.float32)

@jax.custom_vjp
def low_back(v):
    return v

def low_keep(v):
    return (low(v), None)

def low_pass(kept, grad):
    return (grad,)

def back_keep(v):
    return (v, None)

def back_low(kept, grad):
    return (low(grad),)
low.defvjp(low_keep, low_pass)
low_back.defvjp(back_keep, back_low)
eps_norm = 1e-05
highest = lax.Precision.HIGHEST

def times_high(left, right):
    return jnp.matmul(left, right, precision=highest)

def conv_mix(x_in, segs, conv_weight, conv_bias):
    kernel_len = conv_weight.shape[0]
    length = x_in.shape[1]
    padded = jnp.pad(x_in, ((0, 0), (kernel_len - 1, 0), (0, 0)))
    id_pad = jnp.pad(segs, ((0, 0), (kernel_len - 1, 0)), constant_values=-1)
    summed = conv_bias + jnp.zeros_like(x_in)
    for offset in range(kernel_len):
        same_doc = (id_pad[:, offset:offset + length] == segs).astype(jnp.float32)
        summed = summed + conv_weight[offset] * padded[:, offset:offset + length, :] * same_doc[:, :, None]
    return summed

def selective_scan(step_size, conv_val, input_map, output_map, carry_keep, a_rates):
    groups, length, chans = step_size.shape
    block_len = math.gcd(length, 32)
    block_count = length // block_len

    def time_major(value):
        moved = jnp.moveaxis(value, 1, 0)
        return moved.reshape((block_count, block_len) + moved.shape[1:])

    def one_step(carried, pieces):
        step_t, conv_t, in_t, out_t, keep_t = pieces
        decays = jnp.exp(step_t[:, None, :] * a_rates) * keep_t[:, None, None]
        carried = decays * carried + (step_t * conv_t)[:, None, :] * in_t[:, :, None]
        return (carried, lax.optimization_barrier(jnp.sum(carried * out_t[:, :, None], axis=1)))

    def one_block(carried, pieces):
        return lax.scan(one_step, carried, pieces)
    start_state = jnp.zeros((groups, a_rates.shape[0], chans), jnp.float32)
    pieces = tuple((time_major(v) for v in (step_size, conv_val, input_map, output_map, carry_keep)))
    _, outputs = lax.scan(jax.checkpoint(one_block), start_state, pieces)
    return jnp.moveaxis(outputs.reshape((length, groups, chans)), 0, 1)

def group_forward(weights, x_val, segs):
    norm_gain, in_proj_x, in_proj_z, x_proj, dt_proj, dt_bias, conv_weight, conv_bias, a_log, d_skip, out_proj = weights
    mean_square = lax.optimization_barrier(jnp.mean(x_val * x_val, axis=-1, keepdims=True))
    normed = low(x_val * lax.rsqrt(mean_square + eps_norm) * norm_gain)
    x_in = low_back(times_high(normed, in_proj_x))
    gate_in = low_back(times_high(normed, in_proj_z))
    conv_low = low(jax.nn.silu(conv_mix(x_in, segs, conv_weight, conv_bias)))
    x_dbl = low_back(times_high(conv_low, x_proj.T))
    step_size = jax.nn.softplus(times_high(x_dbl[..., :R], dt_proj) + dt_bias)
    input_map = x_dbl[..., R:R + N]
    output_map = x_dbl[..., R + N:]
    doc_starts = segs != jnp.pad(segs[:, :-1], ((0, 0), (1, 0)), constant_values=-1)
    carry_keep = 1.0 - doc_starts.astype(jnp.float32)
    a_rates = -jnp.exp(a_log)
    scanned = selective_scan(step_size, conv_low, input_map, output_map, carry_keep, a_rates) + d_skip * conv_low
    gated = low(scanned * jax.nn.silu(gate_in))
    return low_back(times_high(gated, out_proj.T))

def reference(residual, norm_gain, in_proj_x, in_proj_z, x_proj, dt_proj, dt_bias, conv_weight, conv_bias, a_log, d_skip, out_proj, doc_ids, cotangent):
    group_size = 1
    while SEQS % (group_size * 2) == 0 and group_size * 2 * TOK_DEV <= 4096:
        group_size = group_size * 2
    group_count = SEQS // group_size
    x_all = residual.reshape(group_count, group_size, TOK_DEV, D)
    id_all = doc_ids.reshape(group_count, group_size, TOK_DEV)
    cot_all = cotangent.reshape(group_count, group_size, TOK_DEV, D)
    weights = tuple((v.astype(jnp.float32) for v in (norm_gain, in_proj_x, in_proj_z, x_proj, dt_proj, dt_bias, conv_weight, conv_bias, a_log, d_skip, out_proj)))

    def forward(x_val, weight_val):

        def per_group(unused, pieces):
            return (unused, jax.checkpoint(group_forward)(weight_val, pieces[0], pieces[1]))
        _, mixed_all = lax.scan(per_group, jnp.zeros((), jnp.float32), (x_val, id_all))
        return mixed_all
    mixed_all, pullback = jax.vjp(forward, x_all, weights)
    grad_x, grad_weights = pullback(cot_all)
    mixed = mixed_all.reshape(TOKENS, D)
    block_out = residual + mixed
    grad_residual = cotangent + grad_x.reshape(TOKENS, D)
    rms_resid = jnp.sqrt(lax.optimization_barrier(jnp.mean((residual * residual).reshape(SEQS, TOK_DEV * D), axis=1)))
    rms_mixed = jnp.sqrt(lax.optimization_barrier(jnp.mean((mixed * mixed).reshape(SEQS, TOK_DEV * D), axis=1)))
    return (block_out, grad_residual, grad_weights[0], grad_weights[1], grad_weights[2], grad_weights[3], grad_weights[4], grad_weights[5], grad_weights[6], grad_weights[7], grad_weights[8], grad_weights[9], grad_weights[10], rms_resid, rms_mixed)
```

```python
import jax
import jax.numpy as jnp
from jax import lax
from jax.experimental import pallas as pl
from jax.experimental.pallas import tpu as pltpu
from jax.sharding import PartitionSpec as P

D = 2048
R = 128
N = 16

eps_norm = 1e-05

def sigmoid(v):
    return 1.0 / (1.0 + jnp.exp(-v))


def fold_rows(first, second, shift, lower):
    kept = jnp.where(lower, first, second)
    moved = jnp.where(lower, second, first)
    return kept + pltpu.roll(moved, shift, 0)


class RowSums:
    def __init__(self, masks):
        self.masks = masks
        self.held = {}
        self.result = None

    def add(self, token, value):
        level = 0
        while True:
            if level == 3:
                self.result = value
                return
            mate = (level, token ^ 1)
            if mate not in self.held:
                self.held[(level, token)] = value
                return
            other = self.held.pop(mate)
            first, second = (other, value) if token & 1 else (value, other)
            value = fold_rows(first, second, 1 << level, self.masks[level])
            token >>= 1
            level += 1


def split_dot(left, right_low, dims):
    high = left.astype(jnp.bfloat16)
    rest = (left - high.astype(jnp.float32)).astype(jnp.bfloat16)
    return lax.dot_general(high, right_low, dims, preferred_element_type=jnp.float32) + lax.dot_general(
        rest, right_low, dims, preferred_element_type=jnp.float32
    )


def scan_kernel(
    dbl_ref, conv_ref, gate_ref, gg_ref, dtp_ref, dtb_ref, alog_ref, skip_ref, keep_ref, in_ref, out_ref,
    gated_ref, ggate_ref, gconv_ref, gdbl_ref, gin_ref, gout_ref, gdtp_ref, gdtb_ref, galog_ref, gskip_ref,
    h_s, d_s, stepd_s, sc_s, gs_s, y_s, q_s, r_s, a_s,
):
    length, width = conv_ref.shape
    blocks = width // 128
    part = pl.program_id(0)
    sub = lax.broadcasted_iota(jnp.int32, (8, 128), 0)
    masks = [(sub & shift) == 0 for shift in (1, 2, 4)]
    lanes = [slice(b * 128, (b + 1) * 128) for b in range(blocks)]

    nn = (((1,), (0,)), ((), ()))
    step_raw = split_dot(dbl_ref[...], dtp_ref[...], nn) + dtb_ref[...]
    step = jnp.maximum(step_raw, 0.0) + jnp.log(1.0 + jnp.exp(-jnp.abs(step_raw)))
    stepd_s[...] = jnp.where(keep_ref[...] > 0.0, step, 1e30)
    sc_s[...] = step * conv_ref[...].astype(jnp.float32)
    gate = gate_ref[...]
    gs_s[...] = gg_ref[...] * gate * sigmoid(gate)
    a_s[...] = -jnp.exp(alog_ref[...])

    h_s[0] = jnp.zeros((N, width), jnp.float32)

    def forward(i, hs):
        base = pl.multiple_of(i * 8, 8)
        hs = list(hs)
        sums = [RowSums(masks) for _ in range(blocks)]
        stepd = [stepd_s[pl.ds(base, 8), lanes[b]] for b in range(blocks)]
        drive = [sc_s[pl.ds(base, 8), lanes[b]] for b in range(blocks)]
        for j in range(8):
            t = base + j
            in_t = in_ref[t]
            out_t = out_ref[t]
            for b in range(blocks):
                decay = jnp.exp(stepd[b][j : j + 1] * a_s[:, lanes[b]])
                hs[b] = decay * hs[b] + drive[b][j : j + 1] * in_t
                d_s[t, :, lanes[b]] = decay
                h_s[t + 1, :, lanes[b]] = hs[b]
                read = hs[b] * out_t
                sums[b].add(j, read[:8] + read[8:])
        for b in range(blocks):
            y_s[pl.ds(base, 8), lanes[b]] = sums[b].result
        return tuple(hs)

    zero = jnp.zeros((N, 128), jnp.float32)
    lax.fori_loop(0, length // 8, forward, (zero,) * blocks)

    conv = conv_ref[...].astype(jnp.float32)
    gate = gate_ref[...]
    sig = sigmoid(gate)
    scanned = y_s[...] + skip_ref[...] * conv
    gated_ref[...] = (scanned * gate * sig).astype(jnp.bfloat16)
    ggate_ref[...] = (gg_ref[...] * scanned * sig * (1.0 + gate * (1.0 - sig))).astype(jnp.bfloat16)

    @pl.when(part == 0)
    def _():
        gin_ref[...] = jnp.zeros_like(gin_ref)
        gout_ref[...] = jnp.zeros_like(gout_ref)
        gdbl_ref[...] = jnp.zeros_like(gdbl_ref)

    def backward(i, carried):
        base = pl.multiple_of(length - 8 - i * 8, 8)
        pulled, alog_sum = list(carried[0]), list(carried[1])
        q_sums = [RowSums(masks) for _ in range(blocks)]
        r_sums = [RowSums(masks) for _ in range(blocks)]
        stepd = [stepd_s[pl.ds(base, 8), lanes[b]] for b in range(blocks)]
        drive = [sc_s[pl.ds(base, 8), lanes[b]] for b in range(blocks)]
        gs = [gs_s[pl.ds(base, 8), lanes[b]] for b in range(blocks)]
        for j in reversed(range(8)):
            t = base + j
            in_t = in_ref[t]
            out_t = out_ref[t]
            gin_t = gin_ref[t]
            gout_t = gout_ref[t]
            for b in range(blocks):
                gs_t = gs[b][j : j + 1]
                adjoint = pulled[b] + out_t * gs_t
                gout_t = gout_t + gs_t * h_s[t + 1, :, lanes[b]]
                gin_t = gin_t + adjoint * drive[b][j : j + 1]
                q_t = adjoint * in_t
                q_sums[b].add(j, q_t[:8] + q_t[8:])
                pulled[b] = d_s[t, :, lanes[b]] * adjoint
                past = pulled[b] * h_s[t, :, lanes[b]]
                r_t = past * a_s[:, lanes[b]]
                r_sums[b].add(j, r_t[:8] + r_t[8:])
                alog_sum[b] = alog_sum[b] + past * stepd[b][j : j + 1]
            gin_ref[t] = gin_t
            gout_ref[t] = gout_t
        for b in range(blocks):
            q_s[pl.ds(base, 8), lanes[b]] = q_sums[b].result
            r_s[pl.ds(base, 8), lanes[b]] = r_sums[b].result
        return tuple(pulled), tuple(alog_sum)

    _, alog_sum = lax.fori_loop(0, length // 8, backward, ((zero,) * blocks, (zero,) * blocks))
    for b in range(blocks):
        galog_ref[:, lanes[b]] = alog_sum[b] * a_s[:, lanes[b]]

    conv = conv_ref[...].astype(jnp.float32)
    step_raw = split_dot(dbl_ref[...], dtp_ref[...], nn) + dtb_ref[...]
    step = jnp.maximum(step_raw, 0.0) + jnp.log(1.0 + jnp.exp(-jnp.abs(step_raw)))
    raw = (conv * q_s[...] + r_s[...]) * sigmoid(step_raw)
    gs = gs_s[...]
    gconv_ref[...] = step * q_s[...] + skip_ref[...] * gs
    gskip_ref[...] = jnp.sum(gs * conv, axis=0, keepdims=True)
    gdtb_ref[...] = jnp.sum(raw, axis=0, keepdims=True)
    raw_low = raw.astype(jnp.bfloat16)
    gdtp_ref[...] = lax.dot_general(
        dbl_ref[...].astype(jnp.bfloat16), raw_low, (((0,), (0,)), ((), ())), preferred_element_type=jnp.float32
    )
    gdbl_ref[...] += lax.dot_general(
        raw_low, dtp_ref[...], (((1,), (1,)), ((), ())), preferred_element_type=jnp.float32
    )


def scan_call(dbl, conv, gate, gg, dtp, dtb, alog, skip, keep, cb=512):
    length, chans = conv.shape
    cb = min(cb, chans)
    f32 = jnp.float32
    maps = jnp.broadcast_to(dbl[:, R:, None], (length, 2 * N, 128))
    tokens = lambda kind: (jax.ShapeDtypeStruct((length, chans), kind), pl.BlockSpec((length, cb), lambda i: (0, i)))
    whole = lambda *shape: (jax.ShapeDtypeStruct(shape, f32), pl.BlockSpec(shape, lambda i: (0,) * len(shape)))
    rows = lambda count: (jax.ShapeDtypeStruct((count, chans), f32), pl.BlockSpec((count, cb), lambda i: (0, i)))
    outs = [
        tokens(jnp.bfloat16), tokens(jnp.bfloat16), tokens(f32), whole(length, R), whole(length, N, 128), whole(length, N, 128),
        rows(R), rows(1), rows(N), rows(1),
    ]
    ins = [
        whole(length, R), tokens(f32), tokens(f32), tokens(f32), rows(R), rows(1), rows(N), rows(1),
        whole(length, 1),
    ]
    res = pl.pallas_call(
        scan_kernel,
        grid=(chans // cb,),
        in_specs=[spec for _, spec in ins] + [
            pl.BlockSpec((length, N, 128), lambda i: (0, 0, 0)), pl.BlockSpec((length, N, 128), lambda i: (0, 1, 0))],
        out_specs=[spec for _, spec in outs],
        out_shape=[shape for shape, _ in outs],
        scratch_shapes=[
            pltpu.VMEM((length + 1, N, cb), f32), pltpu.VMEM((length, N, cb), f32),
        ] + [pltpu.VMEM((length, cb), f32)] * 6 + [pltpu.VMEM((N, cb), f32)],
        name="selective_scan",
        compiler_params=pltpu.CompilerParams(vmem_limit_bytes=60 << 20),
    )(dbl[:, :R], conv, gate, gg, dtp, dtb[None], alog, skip[None], keep[:, None], maps, maps)
    gated, ggate, gconv, gdbl, gin, gout, gdtp, gdtb, galog, gskip = res
    gdbl_all = jnp.concatenate([gdbl, jnp.sum(gin, -1), jnp.sum(gout, -1)], axis=1)
    return gated, ggate, gconv, gdbl_all, gdtp, gdtb[0], galog, gskip[0]


def norm_rows(values, gain_val):
    mean_square = jnp.mean(values * values, axis=1, keepdims=True)
    return values * lax.rsqrt(mean_square + eps_norm) * gain_val


def conv_local(x_in, doc_ids, conv_weight, conv_bias):
    kernel_len = conv_weight.shape[0]
    length = x_in.shape[0]
    padded = jnp.pad(x_in, ((kernel_len - 1, 0), (0, 0)))
    id_pad = jnp.concatenate([jnp.full((kernel_len - 1,), -1, jnp.int32), doc_ids])
    summed = conv_bias + jnp.zeros_like(x_in)
    for offset in range(kernel_len):
        same_doc = (id_pad[offset : offset + length] == doc_ids).astype(jnp.float32)
        summed = summed + conv_weight[offset] * padded[offset : offset + length] * same_doc[:, None]
    return summed


def per_device(
    residual,
    norm_gain,
    in_proj_x,
    in_proj_z,
    x_proj,
    dt_proj,
    dt_bias,
    conv_weight,
    conv_bias,
    a_log,
    d_skip,
    out_proj,
    doc_ids,
    cotangent,
):
    gathered = (
        lax.all_gather(norm_gain, "dp", axis=0, tiled=True),
        lax.all_gather(in_proj_x, "dp", axis=0, tiled=True),
        lax.all_gather(in_proj_z, "dp", axis=0, tiled=True),
        lax.all_gather(dt_proj, "dp", axis=0, tiled=True),
        lax.all_gather(out_proj, "dp", axis=0, tiled=True),
    )
    gain_all, inx_all, inz_all, step_all, out_all = gathered
    seq_len = doc_ids.shape[0]
    normed_f32, norm_back = jax.vjp(norm_rows, residual, gain_all.astype(jnp.float32))
    normed = lax.all_gather(normed_f32.astype(jnp.bfloat16), "tensor", axis=0, tiled=True)
    x_in = jnp.dot(normed, inx_all, preferred_element_type=jnp.float32)
    gate_in = jnp.dot(normed, inz_all, preferred_element_type=jnp.float32)

    def conv_act(x_val, weight_val, bias_val):
        return jax.nn.silu(conv_local(x_val, doc_ids, weight_val, bias_val))

    conv_out, conv_back = jax.vjp(conv_act, x_in, conv_weight, conv_bias)
    conv_low = conv_out.astype(jnp.bfloat16)
    dbl_part = lax.dot_general(
        conv_low, x_proj, (((1,), (1,)), ((), ())), preferred_element_type=jnp.float32
    )
    x_dbl, resid_square = lax.psum((dbl_part, jnp.sum(residual * residual)), "tensor")
    doc_starts = doc_ids != jnp.concatenate([jnp.full((1,), -1, jnp.int32), doc_ids[:-1]])
    carry_keep = 1.0 - doc_starts.astype(jnp.float32)

    cot_all = lax.all_gather(cotangent.astype(jnp.bfloat16), "tensor", axis=0, tiled=True)
    grad_gated = jnp.dot(cot_all, out_all, preferred_element_type=jnp.float32)
    gated_low, grad_gate_low, grad_conv, grad_dbl_part, grad_step_w, grad_bias, grad_alog, grad_skip = scan_call(
        x_dbl, conv_low, gate_in, grad_gated, step_all, dt_bias, a_log, d_skip, carry_keep
    )
    mixed = lax.psum_scatter(
        lax.dot_general(
            gated_low, out_all, (((1,), (1,)), ((), ())), preferred_element_type=jnp.float32
        ),
        "tensor",
        scatter_dimension=0,
        tiled=True,
    )
    block_out = residual + mixed
    mixed_square = lax.psum(jnp.sum(mixed * mixed), "tensor")
    rms_resid = jnp.sqrt(resid_square / (seq_len * D)).reshape(1)
    rms_mixed = jnp.sqrt(mixed_square / (seq_len * D)).reshape(1)
    grad_out_w = lax.dot_general(
        cot_all, gated_low, (((0,), (0,)), ((), ())), preferred_element_type=jnp.float32
    )
    grad_dbl = lax.psum(grad_dbl_part, "tensor")
    grad_dbl_low = grad_dbl.astype(jnp.bfloat16)
    grad_conv = grad_conv + jnp.dot(grad_dbl_low, x_proj, preferred_element_type=jnp.float32)
    grad_xproj = lax.dot_general(
        grad_dbl_low, conv_low, (((0,), (0,)), ((), ())), preferred_element_type=jnp.float32
    )
    grad_xin, grad_convw, grad_convb = conv_back(grad_conv)
    grad_xin_low = grad_xin.astype(jnp.bfloat16)
    grad_inx = lax.dot_general(
        normed, grad_xin_low, (((0,), (0,)), ((), ())), preferred_element_type=jnp.float32
    )
    grad_inz = lax.dot_general(
        normed, grad_gate_low, (((0,), (0,)), ((), ())), preferred_element_type=jnp.float32
    )
    first_term = lax.dot_general(
        grad_xin_low, inx_all, (((1,), (1,)), ((), ())), preferred_element_type=jnp.float32
    )
    second_term = lax.dot_general(
        grad_gate_low, inz_all, (((1,), (1,)), ((), ())), preferred_element_type=jnp.float32
    )
    grad_normed = lax.psum_scatter(
        first_term + second_term, "tensor", scatter_dimension=0, tiled=True
    )
    grad_rows_x, grad_gain_part = norm_back(grad_normed)
    grad_residual = cotangent + grad_rows_x
    grad_gain = lax.psum(grad_gain_part, "tensor")
    if lax.axis_size("dp") <= 16:
        grad_inx, grad_inz, grad_out_w = (v.astype(jnp.bfloat16) for v in (grad_inx, grad_inz, grad_out_w))
    gain_shard, inx_shard, inz_shard, step_shard, out_shard = (
        lax.psum_scatter(grad_gain, "dp", scatter_dimension=0, tiled=True),
        lax.psum_scatter(grad_inx, "dp", scatter_dimension=0, tiled=True),
        lax.psum_scatter(grad_inz, "dp", scatter_dimension=0, tiled=True),
        lax.psum_scatter(grad_step_w, "dp", scatter_dimension=0, tiled=True),
        lax.psum_scatter(grad_out_w, "dp", scatter_dimension=0, tiled=True),
    )
    inx_shard, inz_shard, out_shard = (v.astype(jnp.float32) for v in (inx_shard, inz_shard, out_shard))
    small_sums = lax.psum(
        (grad_xproj, grad_bias, grad_convw, grad_convb, grad_alog, grad_skip), "dp"
    )
    xproj_sum, bias_sum, convw_sum, convb_sum, alog_sum, skip_sum = small_sums
    return (
        block_out,
        grad_residual,
        gain_shard,
        inx_shard,
        inz_shard,
        xproj_sum,
        step_shard,
        bias_sum,
        convw_sum,
        convb_sum,
        alog_sum,
        skip_sum,
        out_shard,
        rms_resid,
        rms_mixed,
    )


def solution(mesh):
    placed = (
        P(("dp", "tensor"), None),
        P("dp"),
        P("dp", "tensor"),
        P("dp", "tensor"),
        P(None, "tensor"),
        P("dp", "tensor"),
        P("tensor"),
        P(None, "tensor"),
        P("tensor"),
        P(None, "tensor"),
        P("tensor"),
        P("dp", "tensor"),
        P("dp"),
        P(("dp", "tensor"), None),
    )
    return jax.shard_map(
        per_device,
        mesh=mesh,
        in_specs=placed,
        out_specs=(
            P(("dp", "tensor"), None),
            P(("dp", "tensor"), None),
            P("dp"),
            P("dp", "tensor"),
            P("dp", "tensor"),
            P(None, "tensor"),
            P("dp", "tensor"),
            P("tensor"),
            P(None, "tensor"),
            P("tensor"),
            P(None, "tensor"),
            P("tensor"),
            P("dp", "tensor"),
            P("dp"),
            P("dp"),
        ),
        check_vma=False,
    )
```

```python
import jax
import jax.numpy as jnp
from jax import lax
from jax.experimental import pallas as pl
from jax.experimental.pallas import tpu as pltpu
from jax.sharding import PartitionSpec as P

D = 2048
R = 128
N = 16

eps_norm = 1e-05


def sigmoid(v):
    return 1.0 / (1.0 + jnp.exp(-v))


def fold_rows(first, second, shift, lower):
    kept = jnp.where(lower, first, second)
    moved = jnp.where(lower, second, first)
    return kept + pltpu.roll(moved, shift, 0)


class RowSums:
    def __init__(self, masks):
        self.masks = masks
        self.held = {}
        self.result = None

    def add(self, token, value):
        level = 0
        while True:
            if level == 3:
                self.result = value
                return
            mate = (level, token ^ 1)
            if mate not in self.held:
                self.held[(level, token)] = value
                return
            other = self.held.pop(mate)
            first, second = (other, value) if token & 1 else (value, other)
            value = fold_rows(first, second, 1 << level, self.masks[level])
            token >>= 1
            level += 1


def split_dot(left, right_low, dims):
    high = left.astype(jnp.bfloat16)
    rest = (left - high.astype(jnp.float32)).astype(jnp.bfloat16)
    return lax.dot_general(high, right_low, dims, preferred_element_type=jnp.float32) + lax.dot_general(
        rest, right_low, dims, preferred_element_type=jnp.float32
    )


def scan_kernel(
    dbl_ref, conv_ref, gate_ref, gg_ref, dtp_ref, dtb_ref, alog_ref, skip_ref, keep_ref, in_ref, out_ref,
    gated_ref, ggate_ref, gconv_ref, gdbl_ref, gin_ref, gout_ref, gdtp_ref, gdtb_ref, galog_ref, gskip_ref,
    h_s, d_s, stepd_s, sc_s, gs_s, y_s, q_s, r_s, a_s,
):
    length, width = conv_ref.shape
    blocks = width // 128
    part = pl.program_id(0)
    sub = lax.broadcasted_iota(jnp.int32, (8, 128), 0)
    masks = [(sub & shift) == 0 for shift in (1, 2, 4)]
    lanes = [slice(b * 128, (b + 1) * 128) for b in range(blocks)]

    nn = (((1,), (0,)), ((), ()))
    step_raw = split_dot(dbl_ref[...], dtp_ref[...], nn) + dtb_ref[...]
    step = jnp.maximum(step_raw, 0.0) + jnp.log(1.0 + jnp.exp(-jnp.abs(step_raw)))
    stepd_s[...] = jnp.where(keep_ref[...] > 0.0, step, 1e30)
    sc_s[...] = step * conv_ref[...].astype(jnp.float32)
    gate = gate_ref[...]
    gs_s[...] = gg_ref[...] * gate * sigmoid(gate)
    a_s[...] = -jnp.exp(alog_ref[...])

    h_s[0] = jnp.zeros((N, width), jnp.float32)

    def forward(i, hs):
        base = pl.multiple_of(i * 8, 8)
        hs = list(hs)
        sums = [RowSums(masks) for _ in range(blocks)]
        stepd = [stepd_s[pl.ds(base, 8), lanes[b]] for b in range(blocks)]
        drive = [sc_s[pl.ds(base, 8), lanes[b]] for b in range(blocks)]
        for j in range(8):
            t = base + j
            in_t = in_ref[t]
            out_t = out_ref[t]
            for b in range(blocks):
                decay = jnp.exp(stepd[b][j : j + 1] * a_s[:, lanes[b]])
                hs[b] = decay * hs[b] + drive[b][j : j + 1] * in_t
                d_s[t, :, lanes[b]] = decay
                h_s[t + 1, :, lanes[b]] = hs[b]
                read = hs[b] * out_t
                sums[b].add(j, read[:8] + read[8:])
        for b in range(blocks):
            y_s[pl.ds(base, 8), lanes[b]] = sums[b].result
        return tuple(hs)

    zero = jnp.zeros((N, 128), jnp.float32)
    lax.fori_loop(0, length // 8, forward, (zero,) * blocks)

    conv = conv_ref[...].astype(jnp.float32)
    gate = gate_ref[...]
    sig = sigmoid(gate)
    scanned = y_s[...] + skip_ref[...] * conv
    gated_ref[...] = (scanned * gate * sig).astype(jnp.bfloat16)
    ggate_ref[...] = (gg_ref[...] * scanned * sig * (1.0 + gate * (1.0 - sig))).astype(jnp.bfloat16)

    @pl.when(part == 0)
    def _():
        gin_ref[...] = jnp.zeros_like(gin_ref)
        gout_ref[...] = jnp.zeros_like(gout_ref)
        gdbl_ref[...] = jnp.zeros_like(gdbl_ref)

    def backward(i, carried):
        base = pl.multiple_of(length - 8 - i * 8, 8)
        pulled, alog_sum = list(carried[0]), list(carried[1])
        q_sums = [RowSums(masks) for _ in range(blocks)]
        r_sums = [RowSums(masks) for _ in range(blocks)]
        stepd = [stepd_s[pl.ds(base, 8), lanes[b]] for b in range(blocks)]
        drive = [sc_s[pl.ds(base, 8), lanes[b]] for b in range(blocks)]
        gs = [gs_s[pl.ds(base, 8), lanes[b]] for b in range(blocks)]
        for j in reversed(range(8)):
            t = base + j
            in_t = in_ref[t]
            out_t = out_ref[t]
            gin_t = gin_ref[t]
            gout_t = gout_ref[t]
            for b in range(blocks):
                gs_t = gs[b][j : j + 1]
                adjoint = pulled[b] + out_t * gs_t
                gout_t = gout_t + gs_t * h_s[t + 1, :, lanes[b]]
                gin_t = gin_t + adjoint * drive[b][j : j + 1]
                q_t = adjoint * in_t
                q_sums[b].add(j, q_t[:8] + q_t[8:])
                pulled[b] = d_s[t, :, lanes[b]] * adjoint
                past = pulled[b] * h_s[t, :, lanes[b]]
                r_t = past * a_s[:, lanes[b]]
                r_sums[b].add(j, r_t[:8] + r_t[8:])
                alog_sum[b] = alog_sum[b] + past * stepd[b][j : j + 1]
            gin_ref[t] = gin_t
            gout_ref[t] = gout_t
        for b in range(blocks):
            q_s[pl.ds(base, 8), lanes[b]] = q_sums[b].result
            r_s[pl.ds(base, 8), lanes[b]] = r_sums[b].result
        return tuple(pulled), tuple(alog_sum)

    _, alog_sum = lax.fori_loop(0, length // 8, backward, ((zero,) * blocks, (zero,) * blocks))
    for b in range(blocks):
        galog_ref[:, lanes[b]] = alog_sum[b] * a_s[:, lanes[b]]

    conv = conv_ref[...].astype(jnp.float32)
    step_raw = split_dot(dbl_ref[...], dtp_ref[...], nn) + dtb_ref[...]
    step = jnp.maximum(step_raw, 0.0) + jnp.log(1.0 + jnp.exp(-jnp.abs(step_raw)))
    raw = (conv * q_s[...] + r_s[...]) * sigmoid(step_raw)
    gs = gs_s[...]
    gconv_ref[...] = step * q_s[...] + skip_ref[...] * gs
    gskip_ref[...] = jnp.sum(gs * conv, axis=0, keepdims=True)
    gdtb_ref[...] = jnp.sum(raw, axis=0, keepdims=True)
    raw_low = raw.astype(jnp.bfloat16)
    gdtp_ref[...] = lax.dot_general(
        dbl_ref[...].astype(jnp.bfloat16), raw_low, (((0,), (0,)), ((), ())), preferred_element_type=jnp.float32
    )
    gdbl_ref[...] += lax.dot_general(
        dtp_ref[...], raw_low, (((1,), (1,)), ((), ())), preferred_element_type=jnp.float32
    )


def scan_call(dbl, conv, gate, gg, dtp, dtb, alog, skip, keep):
    length, chans = conv.shape
    cb = min(65536 // length, chans)
    f32 = jnp.float32
    maps = jnp.broadcast_to(dbl[:, R:, None], (length, 2 * N, 128))
    tokens = lambda kind: (jax.ShapeDtypeStruct((length, chans), kind), pl.BlockSpec((length, cb), lambda i: (0, i)))
    whole = lambda *shape: (jax.ShapeDtypeStruct(shape, f32), pl.BlockSpec(shape, lambda i: (0,) * len(shape)))
    rows = lambda count: (jax.ShapeDtypeStruct((count, chans), f32), pl.BlockSpec((count, cb), lambda i: (0, i)))
    outs = [
        tokens(jnp.bfloat16), tokens(jnp.bfloat16), tokens(f32), whole(R, length), whole(length, N, 128), whole(length, N, 128),
        rows(R), rows(1), rows(N), rows(1),
    ]
    ins = [
        whole(length, R), tokens(f32), tokens(f32), tokens(f32), rows(R), rows(1), rows(N), rows(1),
        whole(length, 1),
    ]
    res = pl.pallas_call(
        scan_kernel,
        grid=(chans // cb,),
        in_specs=[spec for _, spec in ins] + [
            pl.BlockSpec((length, N, 128), lambda i: (0, 0, 0)), pl.BlockSpec((length, N, 128), lambda i: (0, 1, 0))],
        out_specs=[spec for _, spec in outs],
        out_shape=[shape for shape, _ in outs],
        scratch_shapes=[
            pltpu.VMEM((length + 1, N, cb), f32), pltpu.VMEM((length, N, cb), f32),
        ] + [pltpu.VMEM((length, cb), f32)] * 6 + [pltpu.VMEM((N, cb), f32)],
        name="selective_scan",
        compiler_params=pltpu.CompilerParams(vmem_limit_bytes=60 << 20),
    )(dbl[:, :R], conv, gate, gg, dtp, dtb[None], alog, skip[None], keep[:, None], maps, maps)
    gated, ggate, gconv, gdbl, gin, gout, gdtp, gdtb, galog, gskip = res
    gdbl_all = jnp.concatenate([gdbl, jnp.sum(gin, -1).T, jnp.sum(gout, -1).T], axis=0)
    return gated, ggate, gconv, gdbl_all, gdtp, gdtb[0], galog, gskip[0]


MESH = pl.DeviceIdType.MESH
NZ = 4
F32 = jnp.float32
BF16 = jnp.bfloat16
NN = (((1,), (0,)), ((), ()))
NT = (((1,), (1,)), ((), ()))
TN = (((0,), (0,)), ((), ()))


def dot(left, right, dims=NN):
    return lax.dot_general(left, right, dims, preferred_element_type=F32)


def place(z, x, c):
    return (z * 2 + x) * 2 + c


class Spot:
    def __init__(self):
        self.dp = lax.axis_index("dp")
        self.y = lax.axis_index("tensor")
        self.z, self.x, self.c = self.dp // 4, (self.dp // 2) % 2, self.dp % 2
        self.x_mate = (place(self.z, 1 - self.x, self.c), self.y)
        self.c_mate = (place(self.z, self.x, 1 - self.c), self.y)
        self.y_mate = (self.dp, 1 - self.y)

    def z_at(self, offset):
        return lax.rem(self.z + offset + NZ, NZ)

    def on_line(self, z, y=None):
        return (place(z, self.x, self.c), self.y if y is None else y)


def greet(devices):
    barrier = pltpu.get_barrier_semaphore()
    for device in devices:
        pl.semaphore_signal(barrier, inc=1, device_id=device, device_id_type=MESH)
    pl.semaphore_wait(barrier, len(devices))


class Copies:
    def __init__(self, send_sems):
        self.send_sems = send_sems
        self.begun = []

    def send(self, src, dst, recv_sem, device):
        copy = pltpu.make_async_remote_copy(
            src_ref=src, dst_ref=dst, send_sem=self.send_sems.at[len(self.begun)], recv_sem=recv_sem,
            device_id=device, device_id_type=MESH,
        )
        copy.start()
        self.begun.append(copy)

    def wait_sent(self):
        for copy in self.begun:
            copy.wait_send()


def arrived(dst, recv_sem):
    pltpu.make_async_copy(dst, dst, recv_sem).wait()


class Gather:
    def __init__(self, spot, copies, src, dst, recv_sems, own_sem):
        self.spot, self.copies, self.src, self.dst, self.recv_sems, self.own_sem = spot, copies, src, dst, recv_sems, own_sem
        self.width = dst.shape[-1]

    def columns(self, z):
        return self.src.at[:, pl.ds(pl.multiple_of(z * self.width, self.width), self.width)]

    def push(self):
        spot, me = self.spot, self.spot.dp
        for offset in range(1, NZ):
            z = spot.z_at(offset)
            self.copies.send(self.columns(z), self.dst.at[me], self.recv_sems.at[me], spot.on_line(z))
        self.own = pltpu.make_async_copy(self.columns(spot.z), self.dst.at[me], self.own_sem)
        self.own.start()

    def pass_on(self, origin, device):
        self.copies.send(self.dst.at[origin], self.dst.at[origin], self.recv_sems.at[origin], device)

    def first(self):
        spot = self.spot
        for offset in range(NZ):
            origin = place(spot.z_at(-offset), spot.x, spot.c)
            if offset == 0:
                self.own.wait()
            else:
                arrived(self.dst.at[origin], self.recv_sems.at[origin])
            self.pass_on(origin, spot.x_mate)
            self.pass_on(origin, spot.c_mate)

    def second(self):
        spot = self.spot
        for offset in range(NZ):
            origin = place(spot.z_at(-offset), 1 - spot.x, spot.c)
            arrived(self.dst.at[origin], self.recv_sems.at[origin])
            self.pass_on(origin, spot.c_mate)

    def last(self):
        spot = self.spot
        for x in range(2):
            for offset in range(NZ):
                origin = place(spot.z_at(-offset), x, 1 - spot.c)
                arrived(self.dst.at[origin], self.recv_sems.at[origin])


class Share:
    def __init__(self, spot, copies, dst, recv_sems):
        self.spot, self.copies, self.dst, self.recv_sems = spot, copies, dst, recv_sems

    def send(self, z, device):
        y = self.spot.y
        self.copies.send(self.dst.at[z, y], self.dst.at[z, y], self.recv_sems.at[z, y], device)

    def push(self):
        spot = self.spot
        for offset in range(1, NZ):
            self.send(spot.z, spot.on_line(spot.z_at(offset)))
        self.send(spot.z, spot.y_mate)

    def first(self):
        spot = self.spot
        for offset in range(1, NZ):
            z = spot.z_at(-offset)
            arrived(self.dst.at[z, spot.y], self.recv_sems.at[z, spot.y])
            self.send(z, spot.y_mate)

    def last(self):
        spot = self.spot
        for offset in range(NZ):
            z = spot.z_at(-offset)
            arrived(self.dst.at[z, 1 - spot.y], self.recv_sems.at[z, 1 - spot.y])


class LineSum:
    def __init__(self, spot, copies, part, landing, total, part_sems, total_sems):
        self.spot, self.copies, self.part, self.landing, self.total = spot, copies, part, landing, total
        self.part_sems, self.total_sems = part_sems, total_sems
        self.offsets = [(dz, dy) for dz in range(NZ) for dy in range(2) if dz + dy > 0]

    def there(self, dz, dy):
        return self.spot.z_at(dz), lax.rem(self.spot.y + dy, 2)

    def push(self):
        for dz, dy in self.offsets:
            z, y = self.there(dz, dy)
            slot = dz * 2 + dy
            self.copies.send(self.part.at[z, y], self.landing.at[slot], self.part_sems.at[slot], self.spot.on_line(z, y))

    def middle(self):
        own_z, own_y = self.spot.z, self.spot.y
        summed = self.part[own_z, own_y]
        for dz, dy in self.offsets:
            slot = dz * 2 + dy
            arrived(self.landing.at[slot], self.part_sems.at[slot])
            summed = summed + self.landing[slot]
        self.total[own_z, own_y] = summed
        own = self.total.at[own_z, own_y]
        for dz, dy in self.offsets:
            z, y = self.there(dz, dy)
            self.copies.send(own, own, self.total_sems.at[own_z, own_y], self.spot.on_line(z, y))

    def last(self):
        for dz, dy in self.offsets:
            z, y = self.there(dz, dy)
            arrived(self.total.at[z, y], self.total_sems.at[z, y])


def column_masks(tile):
    return jnp.concatenate([tile] * 16, axis=0).T


def ahead_kernel(
    inx_ref, inz_ref, outp_ref, dtp_ref, resid_ref, cot_ref, info_ref, xproj_ref, chan_ref,
    w_ref, acts_ref, dtp_all, info_all, xin_ref, pre_ref, low_ref, gate_ref, gg_ref, total_ref, square_ref,
    part_s, landing_s, square_s, send_sems, w_sems, own_sems, act_sems, info_sems, part_sems, total_sems, square_sem,
):
    spot = Spot()
    plane = [lax.rem(spot.dp + offset, 4 * NZ) for offset in range(1, 4 * NZ)]
    greet([(dp, spot.y) for dp in plane] + [spot.on_line(spot.z_at(dz), 1 - spot.y) for dz in range(NZ)])
    copies = Copies(send_sems)
    chans = xin_ref.shape[1]
    lengths = resid_ref.shape[0] * 2

    info_all[spot.dp] = info_ref[...]
    for dp in plane:
        copies.send(info_ref, info_all.at[spot.dp], info_sems.at[spot.dp], (dp, spot.y))
    gathers = [
        Gather(spot, copies, src, dst, w_sems.at[k], own_sems.at[k])
        for k, (src, dst) in enumerate(
            ((inx_ref, w_ref.at[0]), (inz_ref, w_ref.at[1]), (outp_ref, w_ref.at[2]), (dtp_ref, dtp_all))
        )
    ]
    inx, inz, outp, dtp = gathers
    normed, cot = (Share(spot, copies, acts_ref.at[k], act_sems.at[k]) for k in range(2))
    inx.push()

    resid = resid_ref[...]
    row_square = jnp.sum(resid * resid, axis=1, keepdims=True)
    scaled = resid * lax.rsqrt(row_square / resid.shape[1] + eps_norm)
    square_s[0] = jnp.broadcast_to(jnp.sum(row_square, axis=0, keepdims=True), (8, 128))
    copies.send(square_s.at[0], square_s.at[1], square_sem, spot.y_mate)
    acts_ref[1, spot.z, spot.y] = cot_ref[...].astype(BF16)
    for dp in plane:
        arrived(info_all.at[dp], info_sems.at[dp])
    for k in range(4 * NZ):
        cols = slice(k * 128, (k + 1) * 128)
        acts_ref[0, spot.z, spot.y, :, cols] = (scaled[:, cols] * info_all[k, 0:1, :]).astype(BF16)
    normed.push()
    dtp.push()
    inx.first()
    inz.push()
    dtp.first()
    normed.first()
    inx.second()
    cot.push()
    dtp.second()
    inz.first()
    normed.last()
    inx.last()
    outp.push()

    x_in = dot(acts_ref[0].reshape(NZ * lengths, -1), w_ref[0].reshape(-1, chans))
    xin_ref[...] = x_in
    for k in range(NZ):
        rows = slice(k * lengths, (k + 1) * lengths)
        mask = column_masks(info_all[place(k, spot.x, spot.c)])
        one = x_in[rows]
        pre = chan_ref[4:5] + chan_ref[3:4] * one
        for back in range(1, 4):
            pre = pre + chan_ref[3 - back : 4 - back] * (pltpu.roll(one, back, 0) * mask[:, back : back + 1])
        pre_ref[rows] = pre
        low_ref[rows] = (pre * sigmoid(pre)).astype(BF16)
    columns = pl.ds(pl.multiple_of(spot.z * chans, chans), chans)
    dbl = dot(xproj_ref[:, columns], low_ref[...], NT)
    half = dbl.shape[0] // 2
    for k in range(NZ):
        for y in range(2):
            part_s[k, y] = dbl[y * half : (y + 1) * half, k * lengths : (k + 1) * lengths]
    x_dbl = LineSum(spot, copies, part_s, landing_s, total_ref, part_sems, total_sems)
    x_dbl.push()
    inz.second()
    cot.first()
    x_dbl.middle()
    inz.last()
    gate_ref[...] = dot(acts_ref[0].reshape(NZ * lengths, -1), w_ref[1].reshape(-1, chans))
    outp.first()
    x_dbl.last()
    outp.second()
    cot.last()
    outp.last()
    gg_ref[...] = dot(acts_ref[1].reshape(NZ * lengths, -1), w_ref[2].reshape(-1, chans))
    dtp.last()
    arrived(square_s.at[1], square_sem)
    square_ref[...] = square_s[0] + square_s[1]
    copies.wait_sent()


def ahead_call(in_x, in_z, out_p, dt_p, residual, cotangent, info, x_proj, chan):
    rows, width = in_x.shape
    n_dp = 4 * NZ
    half, feats = residual.shape
    chans = width // NZ
    tokens = NZ * 2 * half
    shape = jax.ShapeDtypeStruct
    outs = [
        shape((3, n_dp, rows, chans), BF16), shape((2, NZ, 2, half, feats), BF16), shape((n_dp, dt_p.shape[0], chans), F32),
        shape((n_dp, 8, 128), F32), shape((tokens, chans), F32), shape((tokens, chans), F32), shape((tokens, chans), BF16),
        shape((tokens, chans), F32), shape((tokens, chans), F32), shape((NZ, 2, x_proj.shape[0] // 2, 2 * half), F32),
        shape((8, 128), F32),
    ]
    in_any = pl.BlockSpec(memory_space=pl.ANY)
    in_vmem = pl.BlockSpec(memory_space=pltpu.VMEM)
    dma = pltpu.SemaphoreType.DMA
    return pl.pallas_call(
        ahead_kernel,
        out_shape=outs,
        in_specs=[in_any] * 4 + [in_vmem] * 5,
        out_specs=[in_vmem] * len(outs),
        scratch_shapes=[
            pltpu.VMEM(outs[9].shape, F32), pltpu.VMEM((2 * NZ,) + outs[9].shape[2:], F32), pltpu.VMEM((2, 8, 128), F32),
            dma((128,)), dma((4, n_dp)), dma((4,)), dma((2, NZ, 2)), dma((n_dp,)), dma((2 * NZ,)), dma((NZ, 2)), dma(()),
        ],
        name="ahead",
        compiler_params=pltpu.CompilerParams(collective_id=1, has_side_effects=True, vmem_limit_bytes=60 << 20),
    )(in_x, in_z, out_p, dt_p, residual, cotangent, info, x_proj, chan)


class TokenSum:
    def __init__(self, spot, copies, part, y_land, z_land, y_sems, z_sems):
        self.spot, self.copies, self.part, self.y_land, self.z_land = spot, copies, part, y_land, z_land
        self.y_sems, self.z_sems = y_sems, z_sems

    def push(self):
        spot = self.spot
        for offset in (1, 2, 3, 0):
            z = spot.z_at(offset)
            self.copies.send(self.part.at[z, 1 - spot.y], self.y_land.at[z], self.y_sems.at[z], spot.y_mate)

    def middle(self):
        spot = self.spot
        for offset in (1, 2, 3):
            z = spot.z_at(offset)
            arrived(self.y_land.at[z], self.y_sems.at[z])
            self.part[z, spot.y] = (self.part[z, spot.y].astype(F32) + self.y_land[z].astype(F32)).astype(BF16)
            self.copies.send(self.part.at[z, spot.y], self.z_land.at[offset - 1], self.z_sems.at[offset - 1], spot.on_line(z))

    def last(self):
        spot = self.spot
        arrived(self.y_land.at[spot.z], self.y_sems.at[spot.z])
        summed = self.part[spot.z, spot.y].astype(F32) + self.y_land[spot.z].astype(F32)
        for k in range(NZ - 1):
            arrived(self.z_land.at[k], self.z_sems.at[k])
            summed = summed + self.z_land[k].astype(F32)
        return summed


class RowSum:
    def __init__(self, spot, copies, part, c_land, x_land, z_land, c_sems, x_sems, z_sems, out):
        self.spot, self.copies, self.part, self.out = spot, copies, part, out
        self.c_land, self.x_land, self.z_land = c_land, x_land, z_land
        self.c_sems, self.x_sems, self.z_sems = c_sems, x_sems, z_sems

    def push(self):
        spot = self.spot
        for offset in (1, 2, 3, 0):
            z = spot.z_at(offset)
            for x in (1 - spot.x, spot.x):
                self.copies.send(self.part.at[z, x, 1 - spot.c], self.c_land.at[z, x], self.c_sems.at[z, x], spot.c_mate)

    def add(self, z, x, landed):
        part = self.part
        part[z, x, self.spot.c] = (part[z, x, self.spot.c].astype(F32) + landed.astype(F32)).astype(part.dtype)

    def second(self):
        spot = self.spot
        for offset in (1, 2, 3, 0):
            z = spot.z_at(offset)
            for x in (1 - spot.x, spot.x):
                arrived(self.c_land.at[z, x], self.c_sems.at[z, x])
                self.add(z, x, self.c_land[z, x])
            self.copies.send(self.part.at[z, 1 - spot.x, spot.c], self.x_land.at[z], self.x_sems.at[z], spot.x_mate)

    def columns(self, z):
        width = self.part.shape[-1]
        return pl.ds(pl.multiple_of(z * width, width), width)

    def third(self):
        spot = self.spot
        for offset in (1, 2, 3, 0):
            z = spot.z_at(offset)
            arrived(self.x_land.at[z], self.x_sems.at[z])
            self.add(z, spot.x, self.x_land[z])
            if offset:
                self.copies.send(
                    self.part.at[z, spot.x, spot.c], self.z_land.at[spot.z], self.z_sems.at[spot.z], spot.on_line(z)
                )
        self.out[:, self.columns(spot.z)] = self.part[spot.z, spot.x, spot.c].astype(F32)

    def last(self):
        spot = self.spot
        for offset in (1, 2, 3):
            z = spot.z_at(-offset)
            arrived(self.z_land.at[z], self.z_sems.at[z])
            self.out[:, self.columns(z)] = self.z_land[z].astype(F32)


class ChannelSum:
    def __init__(self, spot, copies, part, c_land, x_land, full, c_sem, x_sem, full_sems):
        self.spot, self.copies, self.part, self.full, self.full_sems = spot, copies, part, full, full_sems
        self.c_land, self.x_land, self.c_sem, self.x_sem = c_land, x_land, c_sem, x_sem

    def push(self):
        self.copies.send(self.part.at[1 - self.spot.c], self.c_land, self.c_sem, self.spot.c_mate)

    def second(self):
        spot = self.spot
        arrived(self.c_land, self.c_sem)
        self.part[spot.c] = self.part[spot.c] + self.c_land[...]
        self.copies.send(self.part.at[spot.c, 1 - spot.x], self.x_land, self.x_sem, spot.x_mate)

    def spread(self, origin, device):
        self.copies.send(self.full.at[origin], self.full.at[origin], self.full_sems.at[origin], device)

    def third(self):
        spot = self.spot
        arrived(self.x_land, self.x_sem)
        self.full[spot.dp] = self.part[spot.c, spot.x] + self.x_land[...]
        for offset in (1, 2, 3):
            self.spread(spot.dp, spot.on_line(spot.z_at(offset)))
        self.spread(spot.dp, spot.x_mate)
        self.spread(spot.dp, spot.c_mate)

    def fourth(self):
        spot = self.spot
        for offset in (1, 2, 3):
            origin = place(spot.z_at(-offset), spot.x, spot.c)
            arrived(self.full.at[origin], self.full_sems.at[origin])
            self.spread(origin, spot.x_mate)
            self.spread(origin, spot.c_mate)

    def fifth(self):
        spot = self.spot
        for offset in range(NZ):
            origin = place(spot.z_at(-offset), 1 - spot.x, spot.c)
            arrived(self.full.at[origin], self.full_sems.at[origin])
            self.spread(origin, spot.c_mate)

    def last(self):
        spot = self.spot
        for x in range(2):
            for offset in range(NZ):
                origin = place(spot.z_at(-offset), x, 1 - spot.c)
                arrived(self.full.at[origin], self.full_sems.at[origin])


def back_kernel(
    mixed_part, outw_part, inz_part, dtp_part, dbl_ref, small_ref,
    w_ref, normed_ref, xin_ref, pre_ref, low_ref, gconv_ref, ggate_ref, info_all, xproj_ref, chan_ref,
    resid_ref, cot_ref, gain_ref,
    block_ref, gresid_ref, ggain_ref, ginx_ref, ginz_ref, goutp_ref, gdtp_ref, full_ref, msquare_ref,
    mixed_s, normed_s, inx_s, inz_s, outw_s, dtp_s, chan_s, part_s, landing_s, total_s,
    y_land, z_land, wc_land, wx_land, wz_land, dc_land, dx_land, dz_land, fc_land, fx_land, square_s, gain_s, gain_land,
    send_sems, part_sems, total_sems, y_sems, z_sems, wc_sems, wx_sems, wz_sems, f_sems, full_sems, tile_sems, gain_sems,
    load_sems,
):
    spot = Spot()
    plane = [lax.rem(spot.dp + offset, 4 * NZ) for offset in range(1, 4 * NZ)]
    loads = [
        pltpu.make_async_copy(src, dst, load_sems.at[k])
        for k, (src, dst) in enumerate(((mixed_part, mixed_s), (outw_part, outw_s), (inz_part, inz_s), (dtp_part, dtp_s)))
    ]
    for load in loads:
        load.start()
    greet([(dp, spot.y) for dp in plane] + [spot.on_line(spot.z_at(dz), 1 - spot.y) for dz in range(NZ)])
    copies = Copies(send_sems)
    chans = xin_ref.shape[1]
    half = resid_ref.shape[0]
    length = 2 * half

    rows = dbl_ref.shape[0] // 2
    for k in range(NZ):
        for y in range(2):
            part_s[k, y] = dbl_ref[y * rows : (y + 1) * rows, k * length : (k + 1) * length]
    dbl_sum = LineSum(spot, copies, part_s, landing_s, total_s, part_sems, total_sems)
    dbl_sum.push()

    mixed_sum, normed_sum = (
        TokenSum(spot, copies, part, y_land.at[k], z_land.at[k], y_sems.at[k], z_sems.at[k])
        for k, part in enumerate((mixed_s, normed_s))
    )
    outw_sum, inz_sum, inx_sum = (
        RowSum(
            spot, copies, part, wc_land.at[k], wx_land.at[k], wz_land.at[k], wc_sems.at[k], wx_sems.at[k], wz_sems.at[k], out
        )
        for k, (part, out) in enumerate(((outw_s, goutp_ref), (inz_s, ginz_ref), (inx_s, ginx_ref)))
    )
    dtp_sum = RowSum(spot, copies, dtp_s, dc_land, dx_land, dz_land, wc_sems.at[3], wx_sems.at[3], wz_sems.at[3], gdtp_ref)
    for load in loads:
        load.wait()
    mixed_sum.push()
    outw_sum.push()
    inz_sum.push()
    dtp_sum.push()
    dbl_sum.middle()
    outw_sum.second()
    inz_sum.second()
    dtp_sum.second()
    mixed_sum.middle()
    dbl_sum.last()

    grad_dbl = jnp.concatenate(
        [jnp.concatenate([total_s[k, y] for k in range(NZ)], axis=1) for y in range(2)], axis=0
    ).astype(BF16)
    columns = pl.ds(pl.multiple_of(spot.z * chans, chans), chans)
    grad_conv = gconv_ref[...] + dot(grad_dbl, xproj_ref[:, columns], TN)
    pre = pre_ref[...]
    sig = sigmoid(pre)
    grad_pre = grad_conv * sig * (1.0 + pre * (1.0 - sig))
    taps = [jnp.zeros((1, chans), F32) for _ in range(4)]
    low_rows = []
    for k in range(NZ):
        here = slice(k * length, (k + 1) * length)
        mask = column_masks(info_all[place(k, spot.x, spot.c)])
        one, x_one = grad_pre[here], xin_ref[here]
        taps[3] = taps[3] + jnp.sum(one * x_one, axis=0, keepdims=True)
        grad_x = chan_ref[3:4] * one
        for back in range(1, 4):
            masked = one * mask[:, back : back + 1]
            taps[3 - back] = taps[3 - back] + jnp.sum(masked * pltpu.roll(x_one, back, 0), axis=0, keepdims=True)
            grad_x = grad_x + chan_ref[3 - back : 4 - back] * pltpu.roll(masked, length - back, 0)
        low_rows.append(grad_x.astype(BF16))
    grad_xin = jnp.concatenate(low_rows, axis=0)
    grad_bias = jnp.sum(grad_pre, axis=0, keepdims=True)
    chan_s[...] = jnp.concatenate(
        [dot(grad_dbl, low_ref[...]), small_ref[...], jnp.concatenate(taps + [grad_bias, jnp.zeros((3, chans), F32)], axis=0)], axis=0
    ).reshape(chan_s.shape)
    small_sum = ChannelSum(
        spot, copies, chan_s, fc_land, fx_land, full_ref, f_sems.at[0], f_sems.at[1], full_sems
    )
    small_sum.push()
    w_x, w_z = (w_ref[k].reshape(-1, chans) for k in range(2))
    grad_normed = dot(grad_xin, w_x, NT) + dot(ggate_ref[...], w_z, NT)
    normed_s[...] = grad_normed.astype(BF16).reshape(normed_s.shape)
    normed_sum.push()
    normed = normed_ref[...].reshape(NZ * length, -1)
    inx_s[...] = dot(normed, grad_xin, TN).astype(BF16).reshape(inx_s.shape)
    inx_sum.push()

    outw_sum.third()
    inz_sum.third()
    dtp_sum.third()
    small_sum.second()
    inx_sum.second()
    normed_sum.middle()
    small_sum.third()

    mixed = mixed_sum.last()
    resid = resid_ref[...]
    block_ref[...] = resid + mixed
    square_s[0] = jnp.broadcast_to(jnp.sum(jnp.sum(mixed * mixed, axis=1, keepdims=True), axis=0, keepdims=True), (8, 128))
    copies.send(square_s.at[0], square_s.at[1], tile_sems.at[0], spot.y_mate)
    inx_sum.third()
    small_sum.fourth()
    outw_sum.last()
    inz_sum.last()
    dtp_sum.last()
    small_sum.fifth()

    grad_rows = normed_sum.last()
    feats = resid.shape[1]
    inv = lax.rsqrt(jnp.sum(resid * resid, axis=1, keepdims=True) / feats + eps_norm)
    scaled = resid * inv
    gain_part = jnp.sum(grad_rows * scaled, axis=0, keepdims=True)
    for k in range(4 * NZ):
        gain_s[0, k] = jnp.broadcast_to(gain_part[:, k * 128 : (k + 1) * 128], (8, 128))
    copies.send(gain_s.at[0], gain_s.at[1], tile_sems.at[1], spot.y_mate)
    grad_scaled = grad_rows * gain_ref[...]
    mean = jnp.sum(grad_scaled * scaled, axis=1, keepdims=True) / feats
    gresid_ref[...] = cot_ref[...] + inv * (grad_scaled - scaled * mean)
    arrived(gain_s.at[1], tile_sems.at[1])
    gain_s[2] = gain_s[0] + gain_s[1]
    for offset, dp in enumerate(plane):
        copies.send(gain_s.at[2, dp], gain_land.at[offset], gain_sems.at[offset], (dp, spot.y))
    arrived(square_s.at[1], tile_sems.at[0])
    msquare_ref[...] = square_s[0] + square_s[1]
    inx_sum.last()
    small_sum.last()
    total = gain_s[2, spot.dp]
    for offset in range(4 * NZ - 1):
        arrived(gain_land.at[offset], gain_sems.at[offset])
        total = total + gain_land[offset]
    ggain_ref[...] = total
    copies.wait_sent()


def back_call(mixed_part, outw_part, inz_part, dtp_part, dbl, small, w, normed, x_in, pre, low, gconv, ggate, info_all, x_proj, chan, residual, cotangent, gain):
    half, feats = residual.shape
    tokens, chans = x_in.shape
    n_dp = 4 * NZ
    rows = outw_part.shape[0] // n_dp
    step_rows = dtp_part.shape[0] // n_dp
    wide = chans * NZ
    small_rows = dbl.shape[0] + small.shape[0] + 8
    shape = jax.ShapeDtypeStruct
    outs = [
        shape((half, feats), F32), shape((half, feats), F32), shape((8, 128), F32),
        shape((rows, wide), F32), shape((rows, wide), F32), shape((rows, wide), F32), shape((step_rows, wide), F32),
        shape((n_dp, small_rows // 4, chans), F32), shape((8, 128), F32),
    ]
    in_any = pl.BlockSpec(memory_space=pl.ANY)
    in_vmem = pl.BlockSpec(memory_space=pltpu.VMEM)
    vmem, dma = pltpu.VMEM, pltpu.SemaphoreType.DMA
    part = (NZ, 2, dbl.shape[0] // 2, 2 * half)
    tokens_of = (NZ, 2, half, feats)
    owners = (NZ, 2, 2, rows, chans)
    steps = (NZ, 2, 2, step_rows, chans)
    return pl.pallas_call(
        back_kernel,
        out_shape=outs,
        in_specs=[in_any] * 4 + [in_vmem] * 15,
        out_specs=[in_vmem] * len(outs),
        scratch_shapes=[
            vmem(tokens_of, BF16), vmem(tokens_of, BF16), vmem(owners, BF16), vmem(owners, BF16), vmem(owners, BF16),
            vmem(steps, F32), vmem((2, 2, small_rows // 4, chans), F32), vmem(part, F32), vmem((2 * NZ,) + part[2:], F32), vmem(part, F32),
            vmem((2, NZ) + tokens_of[2:], BF16), vmem((2, NZ - 1) + tokens_of[2:], BF16),
            vmem((3, NZ, 2) + owners[3:], BF16), vmem((3, NZ) + owners[3:], BF16), vmem((3, NZ) + owners[3:], BF16),
            vmem((NZ, 2) + steps[3:], F32), vmem((NZ,) + steps[3:], F32), vmem((NZ,) + steps[3:], F32),
            vmem((2, small_rows // 4, chans), F32), vmem((small_rows // 4, chans), F32),
            vmem((2, 8, 128), F32), vmem((3, n_dp, 8, 128), F32), vmem((n_dp - 1, 8, 128), F32),
            dma((192,)), dma((2 * NZ,)), dma((NZ, 2)), dma((2, NZ)), dma((2, NZ - 1)), dma((4, NZ, 2)), dma((4, NZ)), dma((4, NZ)),
            dma((2,)), dma((n_dp,)), dma((2,)), dma((n_dp - 1,)), dma((4,)),
        ],
        name="back",
        compiler_params=pltpu.CompilerParams(collective_id=2, has_side_effects=True, vmem_limit_bytes=62 << 20),
    )(
        mixed_part.reshape(tokens_of), outw_part.reshape(owners), inz_part.reshape(owners), dtp_part.reshape(steps), dbl, small,
        w, normed, x_in, pre, low, gconv, ggate, info_all, x_proj, chan, residual, cotangent, gain,
    )


def per_device_split(
    residual,
    norm_gain,
    in_proj_x,
    in_proj_z,
    x_proj,
    dt_proj,
    dt_bias,
    conv_weight,
    conv_bias,
    a_log,
    d_skip,
    out_proj,
    doc_ids,
    cotangent,
):
    dp = lax.axis_index("dp")
    z, group = dp // 4, dp % 4
    chans = in_proj_x.shape[1] // NZ
    seq_len = doc_ids.shape[0]
    tokens = NZ * seq_len

    def columns(*rows):
        return lax.dynamic_slice_in_dim(jnp.concatenate(rows, axis=0), z * chans, chans, 1)

    spare = jnp.zeros((3,) + conv_bias.shape, F32)
    chan = columns(conv_weight, conv_bias[None], spare)
    rates = columns(a_log, dt_bias[None], d_skip[None])
    position = jnp.arange(seq_len)
    same = [((jnp.roll(doc_ids, back) == doc_ids) & (position >= back)).astype(F32) for back in (1, 2, 3)]
    info = jnp.stack([norm_gain.astype(F32)] + same + [jnp.zeros((seq_len,), F32)] * 4)

    w_all, acts, step_all, info_all, x_in, conv_pre, conv_low, gate_in, grad_gated, dbl_total, resid_square = ahead_call(
        in_proj_x, in_proj_z, out_proj, dt_proj.astype(F32), residual, cotangent, info, x_proj, chan
    )
    dbl_rows = dbl_total.transpose(1, 2, 0, 3).reshape(x_proj.shape[0], tokens)
    keep = lax.dynamic_slice_in_dim(info_all.reshape(NZ, 4, 8, seq_len), group, 1, 1)[:, 0, 1].reshape(tokens)
    normed, cot_all = (v.reshape(tokens, -1) for v in (acts[0], acts[1]))
    gated, grad_gate, grad_conv, grad_dbl_part, grad_step_part, grad_bias, grad_alog, grad_skip = scan_call(
        dbl_rows.T, conv_low, gate_in, grad_gated, step_all.reshape(R, chans).astype(BF16),
        rates[N], rates[:N], rates[N + 1], keep,
    )
    mixed_part = dot(gated, w_all[2].reshape(-1, chans), NT).astype(BF16)
    outw_part = dot(cot_all, gated, TN).astype(BF16)
    inz_part = dot(normed, grad_gate, TN).astype(BF16)
    small = jnp.concatenate([grad_alog, grad_bias[None], grad_skip[None], jnp.zeros((6, chans), F32)], axis=0)
    gain_all = info_all[:, 0].reshape(1, -1)
    block_out, grad_residual, grad_gain, grad_inx, grad_inz, grad_outp, grad_dtp, full, mixed_square = back_call(
        mixed_part, outw_part, inz_part, grad_step_part, grad_dbl_part, small, w_all, acts[0], x_in, conv_pre, conv_low,
        grad_conv, grad_gate, info_all, x_proj, chan, residual, cotangent, gain_all,
    )
    rows = full.reshape(NZ, 2, 2, -1, chans).transpose(2, 1, 3, 0, 4).reshape(-1, NZ * chans)
    width = x_proj.shape[0]
    xproj_sum, alog_sum, bias_sum, skip_sum = rows[:width], rows[width : width + N], rows[width + N], rows[width + N + 1]
    convw_sum, convb_sum = rows[width + 24 : width + 28], rows[width + 28]
    rms_resid, rms_mixed = (jnp.sqrt(v[0, :1] / (seq_len * D)) for v in (resid_square, mixed_square))
    return (
        block_out,
        grad_residual,
        grad_gain[0],
        grad_inx,
        grad_inz,
        xproj_sum,
        grad_dtp,
        bias_sum,
        convw_sum,
        convb_sum,
        alog_sum,
        skip_sum,
        grad_outp,
        rms_resid,
        rms_mixed,
    )


def norm_rows(values, gain_val):
    mean_square = jnp.mean(values * values, axis=1, keepdims=True)
    return values * lax.rsqrt(mean_square + eps_norm) * gain_val


def conv_local(x_in, doc_ids, conv_weight, conv_bias):
    kernel_len = conv_weight.shape[0]
    length = x_in.shape[0]
    padded = jnp.pad(x_in, ((kernel_len - 1, 0), (0, 0)))
    id_pad = jnp.concatenate([jnp.full((kernel_len - 1,), -1, jnp.int32), doc_ids])
    summed = conv_bias + jnp.zeros_like(x_in)
    for offset in range(kernel_len):
        same_doc = (id_pad[offset : offset + length] == doc_ids).astype(jnp.float32)
        summed = summed + conv_weight[offset] * padded[offset : offset + length] * same_doc[:, None]
    return summed


def per_device(
    residual,
    norm_gain,
    in_proj_x,
    in_proj_z,
    x_proj,
    dt_proj,
    dt_bias,
    conv_weight,
    conv_bias,
    a_log,
    d_skip,
    out_proj,
    doc_ids,
    cotangent,
):
    gathered = (
        lax.all_gather(norm_gain, "dp", axis=0, tiled=True),
        lax.all_gather(in_proj_x, "dp", axis=0, tiled=True),
        lax.all_gather(in_proj_z, "dp", axis=0, tiled=True),
        lax.all_gather(dt_proj, "dp", axis=0, tiled=True),
        lax.all_gather(out_proj, "dp", axis=0, tiled=True),
    )
    gain_all, inx_all, inz_all, step_all, out_all = gathered
    seq_len = doc_ids.shape[0]
    normed_f32, norm_back = jax.vjp(norm_rows, residual, gain_all.astype(jnp.float32))
    normed = lax.all_gather(normed_f32.astype(jnp.bfloat16), "tensor", axis=0, tiled=True)
    x_in = jnp.dot(normed, inx_all, preferred_element_type=jnp.float32)
    gate_in = jnp.dot(normed, inz_all, preferred_element_type=jnp.float32)

    def conv_act(x_val, weight_val, bias_val):
        return jax.nn.silu(conv_local(x_val, doc_ids, weight_val, bias_val))

    conv_out, conv_back = jax.vjp(conv_act, x_in, conv_weight, conv_bias)
    conv_low = conv_out.astype(jnp.bfloat16)
    dbl_part = lax.dot_general(
        conv_low, x_proj, (((1,), (1,)), ((), ())), preferred_element_type=jnp.float32
    )
    x_dbl, resid_square = lax.psum((dbl_part, jnp.sum(residual * residual)), "tensor")
    doc_starts = doc_ids != jnp.concatenate([jnp.full((1,), -1, jnp.int32), doc_ids[:-1]])
    carry_keep = 1.0 - doc_starts.astype(jnp.float32)

    cot_all = lax.all_gather(cotangent.astype(jnp.bfloat16), "tensor", axis=0, tiled=True)
    grad_gated = jnp.dot(cot_all, out_all, preferred_element_type=jnp.float32)
    gated_low, grad_gate_low, grad_conv, grad_dbl_part, grad_step_w, grad_bias, grad_alog, grad_skip = scan_call(
        x_dbl, conv_low, gate_in, grad_gated, step_all, dt_bias, a_log, d_skip, carry_keep
    )
    mixed = lax.psum_scatter(
        lax.dot_general(
            gated_low, out_all, (((1,), (1,)), ((), ())), preferred_element_type=jnp.float32
        ),
        "tensor",
        scatter_dimension=0,
        tiled=True,
    )
    block_out = residual + mixed
    mixed_square = lax.psum(jnp.sum(mixed * mixed), "tensor")
    rms_resid = jnp.sqrt(resid_square / (seq_len * D)).reshape(1)
    rms_mixed = jnp.sqrt(mixed_square / (seq_len * D)).reshape(1)
    grad_out_w = lax.dot_general(
        cot_all, gated_low, (((0,), (0,)), ((), ())), preferred_element_type=jnp.float32
    )
    grad_dbl = lax.psum(grad_dbl_part.T, "tensor")
    grad_dbl_low = grad_dbl.astype(jnp.bfloat16)
    grad_conv = grad_conv + jnp.dot(grad_dbl_low, x_proj, preferred_element_type=jnp.float32)
    grad_xproj = lax.dot_general(
        grad_dbl_low, conv_low, (((0,), (0,)), ((), ())), preferred_element_type=jnp.float32
    )
    grad_xin, grad_convw, grad_convb = conv_back(grad_conv)
    grad_xin_low = grad_xin.astype(jnp.bfloat16)
    grad_inx = lax.dot_general(
        normed, grad_xin_low, (((0,), (0,)), ((), ())), preferred_element_type=jnp.float32
    )
    grad_inz = lax.dot_general(
        normed, grad_gate_low, (((0,), (0,)), ((), ())), preferred_element_type=jnp.float32
    )
    first_term = lax.dot_general(
        grad_xin_low, inx_all, (((1,), (1,)), ((), ())), preferred_element_type=jnp.float32
    )
    second_term = lax.dot_general(
        grad_gate_low, inz_all, (((1,), (1,)), ((), ())), preferred_element_type=jnp.float32
    )
    grad_normed = lax.psum_scatter(
        first_term + second_term, "tensor", scatter_dimension=0, tiled=True
    )
    grad_rows_x, grad_gain_part = norm_back(grad_normed)
    grad_residual = cotangent + grad_rows_x
    grad_gain = lax.psum(grad_gain_part, "tensor")
    gain_shard, inx_shard, inz_shard, step_shard, out_shard = (
        lax.psum_scatter(grad_gain, "dp", scatter_dimension=0, tiled=True),
        lax.psum_scatter(grad_inx, "dp", scatter_dimension=0, tiled=True),
        lax.psum_scatter(grad_inz, "dp", scatter_dimension=0, tiled=True),
        lax.psum_scatter(grad_step_w, "dp", scatter_dimension=0, tiled=True),
        lax.psum_scatter(grad_out_w, "dp", scatter_dimension=0, tiled=True),
    )
    small_sums = lax.psum(
        (grad_xproj, grad_bias, grad_convw, grad_convb, grad_alog, grad_skip), "dp"
    )
    xproj_sum, bias_sum, convw_sum, convb_sum, alog_sum, skip_sum = small_sums
    return (
        block_out,
        grad_residual,
        gain_shard,
        inx_shard,
        inz_shard,
        xproj_sum,
        step_shard,
        bias_sum,
        convw_sum,
        convb_sum,
        alog_sum,
        skip_sum,
        out_shard,
        rms_resid,
        rms_mixed,
    )


def solution(mesh):
    placed = (
        P(("dp", "tensor"), None),
        P("dp"),
        P("dp", "tensor"),
        P("dp", "tensor"),
        P(None, "tensor"),
        P("dp", "tensor"),
        P("tensor"),
        P(None, "tensor"),
        P("tensor"),
        P(None, "tensor"),
        P("tensor"),
        P("dp", "tensor"),
        P("dp"),
        P(("dp", "tensor"), None),
    )
    return jax.shard_map(
        per_device_split if mesh.shape["dp"] == 4 * NZ else per_device,
        mesh=mesh,
        in_specs=placed,
        out_specs=(
            P(("dp", "tensor"), None),
            P(("dp", "tensor"), None),
            P("dp"),
            P("dp", "tensor"),
            P("dp", "tensor"),
            P(None, "tensor"),
            P("dp", "tensor"),
            P("tensor"),
            P(None, "tensor"),
            P("tensor"),
            P(None, "tensor"),
            P("tensor"),
            P("dp", "tensor"),
            P("dp"),
            P("dp"),
        ),
        check_vma=False,
    )
```

```python
import functools

import jax
import jax.numpy as jnp
from jax import lax
from jax.experimental import pallas as pl
from jax.experimental.pallas import tpu as pltpu
from jax.sharding import PartitionSpec as P

D = 2048
R = 128
N = 16

eps_norm = 1e-05


def sigmoid(v):
    return 1.0 / (1.0 + jnp.exp(-v))


def softplus(v):
    return jnp.maximum(v, 0.0) + jnp.log(1.0 + jnp.exp(-jnp.abs(v)))


def fold_rows(first, second, shift, lower):
    kept = jnp.where(lower, first, second)
    moved = jnp.where(lower, second, first)
    return kept + pltpu.roll(moved, shift, 0)


class RowSums:
    def __init__(self, masks):
        self.masks = masks
        self.held = {}
        self.result = None

    def add(self, token, value):
        level = 0
        while True:
            if level == 3:
                self.result = value
                return
            mate = (level, token ^ 1)
            if mate not in self.held:
                self.held[(level, token)] = value
                return
            other = self.held.pop(mate)
            first, second = (other, value) if token & 1 else (value, other)
            value = fold_rows(first, second, 1 << level, self.masks[level])
            token >>= 1
            level += 1


def split_dot(left, right_low, dims):
    high = left.astype(jnp.bfloat16)
    rest = (left - high.astype(jnp.float32)).astype(jnp.bfloat16)
    return lax.dot_general(high, right_low, dims, preferred_element_type=jnp.float32) + lax.dot_general(
        rest, right_low, dims, preferred_element_type=jnp.float32
    )


def scan_kernel(
    dbl_ref, conv_ref, gate_ref, gg_ref, dtp_ref, dtb_ref, alog_ref, skip_ref, keep_ref, in_ref, out_ref,
    gated_ref, ggate_ref, gconv_ref, gdbl_ref, gin_ref, gout_ref, gdtp_ref, gdtb_ref, galog_ref, gskip_ref,
    h_s, d_s, stepd_s, sc_s, gs_s, y_s, q_s, r_s, a_s,
):
    length, width = conv_ref.shape
    blocks = width // 128
    part = pl.program_id(0)
    sub = lax.broadcasted_iota(jnp.int32, (8, 128), 0)
    masks = [(sub & shift) == 0 for shift in (1, 2, 4)]
    lanes = [slice(b * 128, (b + 1) * 128) for b in range(blocks)]

    nn = (((1,), (0,)), ((), ()))
    step_raw = split_dot(dbl_ref[...], dtp_ref[...], nn) + dtb_ref[...]
    step = jnp.maximum(step_raw, 0.0) + jnp.log(1.0 + jnp.exp(-jnp.abs(step_raw)))
    stepd_s[...] = jnp.where(keep_ref[...] > 0.0, step, 1e30)
    sc_s[...] = step * conv_ref[...].astype(jnp.float32)
    gate = gate_ref[...]
    gs_s[...] = gg_ref[...] * gate * sigmoid(gate)
    a_s[...] = -jnp.exp(alog_ref[...])

    h_s[0] = jnp.zeros((N, width), jnp.float32)

    def forward(i, hs):
        base = pl.multiple_of(i * 8, 8)
        hs = list(hs)
        sums = [RowSums(masks) for _ in range(blocks)]
        stepd = [stepd_s[pl.ds(base, 8), lanes[b]] for b in range(blocks)]
        drive = [sc_s[pl.ds(base, 8), lanes[b]] for b in range(blocks)]
        for j in range(8):
            t = base + j
            in_t = in_ref[t]
            out_t = out_ref[t]
            for b in range(blocks):
                decay = jnp.exp(stepd[b][j : j + 1] * a_s[:, lanes[b]])
                hs[b] = decay * hs[b] + drive[b][j : j + 1] * in_t
                d_s[t, :, lanes[b]] = decay
                h_s[t + 1, :, lanes[b]] = hs[b]
                read = hs[b] * out_t
                sums[b].add(j, read[:8] + read[8:])
        for b in range(blocks):
            y_s[pl.ds(base, 8), lanes[b]] = sums[b].result
        return tuple(hs)

    zero = jnp.zeros((N, 128), jnp.float32)
    lax.fori_loop(0, length // 8, forward, (zero,) * blocks)

    conv = conv_ref[...].astype(jnp.float32)
    gate = gate_ref[...]
    sig = sigmoid(gate)
    scanned = y_s[...] + skip_ref[...] * conv
    gated_ref[...] = (scanned * gate * sig).astype(jnp.bfloat16)
    ggate_ref[...] = (gg_ref[...] * scanned * sig * (1.0 + gate * (1.0 - sig))).astype(jnp.bfloat16)

    @pl.when(part == 0)
    def _():
        gin_ref[...] = jnp.zeros_like(gin_ref)
        gout_ref[...] = jnp.zeros_like(gout_ref)
        gdbl_ref[...] = jnp.zeros_like(gdbl_ref)

    def backward(i, carried):
        base = pl.multiple_of(length - 8 - i * 8, 8)
        pulled, alog_sum = list(carried[0]), list(carried[1])
        q_sums = [RowSums(masks) for _ in range(blocks)]
        r_sums = [RowSums(masks) for _ in range(blocks)]
        stepd = [stepd_s[pl.ds(base, 8), lanes[b]] for b in range(blocks)]
        drive = [sc_s[pl.ds(base, 8), lanes[b]] for b in range(blocks)]
        gs = [gs_s[pl.ds(base, 8), lanes[b]] for b in range(blocks)]
        for j in reversed(range(8)):
            t = base + j
            in_t = in_ref[t]
            out_t = out_ref[t]
            gin_t = gin_ref[t]
            gout_t = gout_ref[t]
            for b in range(blocks):
                gs_t = gs[b][j : j + 1]
                adjoint = pulled[b] + out_t * gs_t
                gout_t = gout_t + gs_t * h_s[t + 1, :, lanes[b]]
                gin_t = gin_t + adjoint * drive[b][j : j + 1]
                q_t = adjoint * in_t
                q_sums[b].add(j, q_t[:8] + q_t[8:])
                pulled[b] = d_s[t, :, lanes[b]] * adjoint
                past = pulled[b] * h_s[t, :, lanes[b]]
                r_t = past * a_s[:, lanes[b]]
                r_sums[b].add(j, r_t[:8] + r_t[8:])
                alog_sum[b] = alog_sum[b] + past * stepd[b][j : j + 1]
            gin_ref[t] = gin_t
            gout_ref[t] = gout_t
        for b in range(blocks):
            q_s[pl.ds(base, 8), lanes[b]] = q_sums[b].result
            r_s[pl.ds(base, 8), lanes[b]] = r_sums[b].result
        return tuple(pulled), tuple(alog_sum)

    _, alog_sum = lax.fori_loop(0, length // 8, backward, ((zero,) * blocks, (zero,) * blocks))
    for b in range(blocks):
        galog_ref[:, lanes[b]] = alog_sum[b] * a_s[:, lanes[b]]

    conv = conv_ref[...].astype(jnp.float32)
    step_raw = split_dot(dbl_ref[...], dtp_ref[...], nn) + dtb_ref[...]
    step = jnp.maximum(step_raw, 0.0) + jnp.log(1.0 + jnp.exp(-jnp.abs(step_raw)))
    raw = (conv * q_s[...] + r_s[...]) * sigmoid(step_raw)
    gs = gs_s[...]
    gconv_ref[...] = step * q_s[...] + skip_ref[...] * gs
    gskip_ref[...] = jnp.sum(gs * conv, axis=0, keepdims=True)
    gdtb_ref[...] = jnp.sum(raw, axis=0, keepdims=True)
    raw_low = raw.astype(jnp.bfloat16)
    gdtp_ref[...] = lax.dot_general(
        dbl_ref[...].astype(jnp.bfloat16), raw_low, (((0,), (0,)), ((), ())), preferred_element_type=jnp.float32
    )
    gdbl_ref[...] += lax.dot_general(
        dtp_ref[...], raw_low, (((1,), (1,)), ((), ())), preferred_element_type=jnp.float32
    )


def scan_call(dbl, conv, gate, gg, dtp, dtb, alog, skip, keep):
    length, chans = conv.shape
    cb = min(65536 // length, chans)
    f32 = jnp.float32
    maps = jnp.broadcast_to(dbl[:, R:, None], (length, 2 * N, 128))
    tokens = lambda kind: (jax.ShapeDtypeStruct((length, chans), kind), pl.BlockSpec((length, cb), lambda i: (0, i)))
    whole = lambda *shape: (jax.ShapeDtypeStruct(shape, f32), pl.BlockSpec(shape, lambda i: (0,) * len(shape)))
    rows = lambda count: (jax.ShapeDtypeStruct((count, chans), f32), pl.BlockSpec((count, cb), lambda i: (0, i)))
    outs = [
        tokens(jnp.bfloat16), tokens(jnp.bfloat16), tokens(f32), whole(R, length), whole(length, N, 128), whole(length, N, 128),
        rows(R), rows(1), rows(N), rows(1),
    ]
    ins = [
        whole(length, R), tokens(f32), tokens(f32), tokens(f32), rows(R), rows(1), rows(N), rows(1),
        whole(length, 1),
    ]
    res = pl.pallas_call(
        scan_kernel,
        grid=(chans // cb,),
        in_specs=[spec for _, spec in ins] + [
            pl.BlockSpec((length, N, 128), lambda i: (0, 0, 0)), pl.BlockSpec((length, N, 128), lambda i: (0, 1, 0))],
        out_specs=[spec for _, spec in outs],
        out_shape=[shape for shape, _ in outs],
        scratch_shapes=[
            pltpu.VMEM((length + 1, N, cb), f32), pltpu.VMEM((length, N, cb), f32),
        ] + [pltpu.VMEM((length, cb), f32)] * 6 + [pltpu.VMEM((N, cb), f32)],
        name="selective_scan",
        compiler_params=pltpu.CompilerParams(vmem_limit_bytes=60 << 20),
    )(dbl[:, :R], conv, gate, gg, dtp, dtb[None], alog, skip[None], keep[:, None], maps, maps)
    gated, ggate, gconv, gdbl, gin, gout, gdtp, gdtb, galog, gskip = res
    gdbl_all = jnp.concatenate([gdbl, jnp.sum(gin, -1).T, jnp.sum(gout, -1).T], axis=0)
    return gated, ggate, gconv, gdbl_all, gdtp, gdtb[0], galog, gskip[0]


MESH = pl.DeviceIdType.MESH
NZ = 4
F32 = jnp.float32
BF16 = jnp.bfloat16
NN = (((1,), (0,)), ((), ()))
NT = (((1,), (1,)), ((), ()))
TN = (((0,), (0,)), ((), ()))


def dot(left, right, dims=NN):
    return lax.dot_general(left, right, dims, preferred_element_type=F32)


def place(z, x, c):
    return (z * 2 + x) * 2 + c


class Spot:
    def __init__(self):
        self.dp = lax.axis_index("dp")
        self.y = lax.axis_index("tensor")
        self.z, self.x, self.c = self.dp // 4, (self.dp // 2) % 2, self.dp % 2
        self.x_mate = (place(self.z, 1 - self.x, self.c), self.y)
        self.c_mate = (place(self.z, self.x, 1 - self.c), self.y)
        self.y_mate = (self.dp, 1 - self.y)

    def z_at(self, offset):
        return lax.rem(self.z + offset + NZ, NZ)

    def on_line(self, z, y=None):
        return (place(z, self.x, self.c), self.y if y is None else y)


def greet(devices):
    barrier = pltpu.get_barrier_semaphore()
    for device in devices:
        pl.semaphore_signal(barrier, inc=1, device_id=device, device_id_type=MESH)
    pl.semaphore_wait(barrier, len(devices))


class Copies:
    def __init__(self, send_sems):
        self.send_sems = send_sems
        self.begun = []

    def send(self, src, dst, recv_sem, device, when=None):
        copy = pltpu.make_async_remote_copy(
            src_ref=src, dst_ref=dst, send_sem=self.send_sems.at[len(self.begun)], recv_sem=recv_sem,
            device_id=device, device_id_type=MESH,
        )
        self.begun.append((when, copy))
        if when is None:
            copy.start()
        else:
            pl.when(when)(copy.start)

    def wait_sent(self):
        for when, copy in self.begun:
            if when is None:
                copy.wait_send()
            else:
                pl.when(when)(copy.wait_send)


def arrived(dst, recv_sem, when=None):
    copy = pltpu.make_async_copy(dst, dst, recv_sem)
    if when is None:
        copy.wait()
    else:
        pl.when(when)(copy.wait)


class Gather:
    def __init__(self, spot, copies, src, dst, recv_sems, own_sem):
        self.spot, self.copies, self.src, self.dst, self.recv_sems, self.own_sem = spot, copies, src, dst, recv_sems, own_sem
        self.width = dst.shape[-1]

    def columns(self, z):
        return self.src.at[:, pl.ds(pl.multiple_of(z * self.width, self.width), self.width)]

    def push(self):
        spot, me = self.spot, self.spot.dp
        for offset in range(1, NZ):
            z = spot.z_at(offset)
            self.copies.send(self.columns(z), self.dst.at[me], self.recv_sems.at[me], spot.on_line(z))
        self.own = pltpu.make_async_copy(self.columns(spot.z), self.dst.at[me], self.own_sem)
        self.own.start()

    def pass_on(self, origin, device):
        self.copies.send(self.dst.at[origin], self.dst.at[origin], self.recv_sems.at[origin], device)

    def first(self):
        spot = self.spot
        for offset in range(NZ):
            origin = place(spot.z_at(-offset), spot.x, spot.c)
            if offset == 0:
                self.own.wait()
            else:
                arrived(self.dst.at[origin], self.recv_sems.at[origin])
            self.pass_on(origin, spot.x_mate)
            self.pass_on(origin, spot.c_mate)

    def second(self):
        spot = self.spot
        for offset in range(NZ):
            origin = place(spot.z_at(-offset), 1 - spot.x, spot.c)
            arrived(self.dst.at[origin], self.recv_sems.at[origin])
            self.pass_on(origin, spot.c_mate)

    def last(self):
        spot = self.spot
        for x in range(2):
            for offset in range(NZ):
                origin = place(spot.z_at(-offset), x, 1 - spot.c)
                arrived(self.dst.at[origin], self.recv_sems.at[origin])


class LineSum:
    def __init__(self, spot, copies, part, landing, total, part_sems, total_sems):
        self.spot, self.copies, self.part, self.landing, self.total = spot, copies, part, landing, total
        self.part_sems, self.total_sems = part_sems, total_sems
        self.offsets = [(dz, dy) for dz in range(NZ) for dy in range(2) if dz + dy > 0]

    def there(self, dz, dy):
        return self.spot.z_at(dz), lax.rem(self.spot.y + dy, 2)

    def push(self):
        for dz, dy in self.offsets:
            z, y = self.there(dz, dy)
            slot = dz * 2 + dy
            self.copies.send(self.part.at[z, y], self.landing.at[slot], self.part_sems.at[slot], self.spot.on_line(z, y))

    def middle(self):
        own_z, own_y = self.spot.z, self.spot.y
        summed = self.part[own_z, own_y]
        for dz, dy in self.offsets:
            slot = dz * 2 + dy
            arrived(self.landing.at[slot], self.part_sems.at[slot])
            summed = summed + self.landing[slot]
        self.total[own_z, own_y] = summed
        own = self.total.at[own_z, own_y]
        for dz, dy in self.offsets:
            z, y = self.there(dz, dy)
            self.copies.send(own, own, self.total_sems.at[own_z, own_y], self.spot.on_line(z, y))

    def last(self):
        for dz, dy in self.offsets:
            z, y = self.there(dz, dy)
            arrived(self.total.at[z, y], self.total_sems.at[z, y])


def column_masks(tile):
    return jnp.concatenate([tile] * 16, axis=0).T


class Share:
    def __init__(self, spot, copies, dst, recv_sems):
        self.spot, self.copies, self.dst, self.recv_sems = spot, copies, dst, recv_sems

    def send(self, z, device, when=None):
        y = self.spot.y
        self.copies.send(self.dst.at[z, y], self.dst.at[z, y], self.recv_sems.at[z, y], device, when)

    def push(self):
        spot = self.spot
        self.send(spot.z, spot.on_line(spot.z_at(1)), spot.z < NZ - 1)
        self.send(spot.z, spot.on_line(spot.z_at(-1)), spot.z > 0)
        self.send(spot.z, spot.y_mate)

    def first(self, far):
        spot = self.spot
        for way in (1, -1):
            origin = spot.z_at(-way * far)
            comes = spot.z >= far if way == 1 else spot.z < NZ - far
            goes = comes & (spot.z < NZ - 1 if way == 1 else spot.z > 0)
            arrived(self.dst.at[origin, spot.y], self.recv_sems.at[origin, spot.y], comes)
            if far < NZ - 1:
                self.send(origin, spot.on_line(spot.z_at(way)), goes)
            self.send(origin, spot.y_mate, comes)

    def last(self):
        spot = self.spot
        for offset in range(NZ):
            z = spot.z_at(-offset)
            arrived(self.dst.at[z, 1 - spot.y], self.recv_sems.at[z, 1 - spot.y])


class Scan:
    def __init__(self, maps, a_s, stepd_s, drive_s, gs_s, read_s, q_s, r_s, state_s, pulled_s, alog_s, spread_s, sum_s, gmap_s):
        self.maps, self.a_s, self.stepd_s, self.drive_s, self.gs_s = maps, a_s, stepd_s, drive_s, gs_s
        self.read_s, self.q_s, self.r_s, self.state_s = read_s, q_s, r_s, state_s
        self.pulled_s, self.alog_s, self.spread_s, self.sum_s, self.gmap_s = pulled_s, alog_s, spread_s, sum_s, gmap_s
        sub = lax.broadcasted_iota(jnp.int32, (8, 128), 0)
        self.masks = [(sub & shift) == 0 for shift in (1, 2, 4)]
        self.lane = lax.broadcasted_iota(jnp.int32, (N, 128), 1)
        self.blocks = [slice(b * 128, (b + 1) * 128) for b in range(a_s.shape[1] // 128)]

    def place(self, i):
        base = pl.multiple_of(i * 8, 8)
        tile = pl.ds(pl.multiple_of((base // 128) * 128, 128), 128)
        return base, tile, lax.rem(base, 128)

    def spread(self, tile, first):
        back = lax.rem(128 - first, 128)
        for k in range(2):
            moved = pltpu.roll(self.maps[k * N : (k + 1) * N, tile], back, 1)
            for j in range(8):
                self.spread_s[k, j] = jnp.broadcast_to(moved[:, j : j + 1], (N, 128))

    def forward(self, start, stop):
        def chunk(i, none):
            base, tile, first = self.place(i)
            self.spread(tile, first)
            for lanes in self.blocks:
                state = self.state_s[i, :, lanes]
                a = self.a_s[:, lanes]
                stepd, drive = self.stepd_s[pl.ds(base, 8), lanes], self.drive_s[pl.ds(base, 8), lanes]
                sums = RowSums(self.masks)
                for j in range(8):
                    state = jnp.exp(stepd[j : j + 1] * a) * state + drive[j : j + 1] * self.spread_s[0, j]
                    read = state * self.spread_s[1, j]
                    sums.add(j, read[:8] + read[8:])
                self.state_s[i + 1, :, lanes] = state
                self.read_s[pl.ds(base, 8), lanes] = sums.result
            return none

        lax.fori_loop(start, stop, chunk, 0)

    def backward(self, start, stop):
        def chunk(step, none):
            i = start + stop - 1 - step
            base, tile, first = self.place(i)
            self.spread(tile, first)
            for b, lanes in enumerate(self.blocks):
                a = self.a_s[:, lanes]
                stepd, drive = self.stepd_s[pl.ds(base, 8), lanes], self.drive_s[pl.ds(base, 8), lanes]
                gs = self.gs_s[pl.ds(base, 8), lanes]
                states, decays = [self.state_s[i, :, lanes]], []
                for j in range(8):
                    decays.append(jnp.exp(stepd[j : j + 1] * a))
                    states.append(decays[j] * states[j] + drive[j : j + 1] * self.spread_s[0, j])
                pulled, alog = self.pulled_s[:, lanes], self.alog_s[:, lanes]
                q_sums, r_sums = RowSums(self.masks), RowSums(self.masks)
                for j in reversed(range(8)):
                    adjoint = pulled + self.spread_s[1, j] * gs[j : j + 1]
                    g_in, g_out = adjoint * drive[j : j + 1], states[j + 1] * gs[j : j + 1]
                    if b > 0:
                        g_in, g_out = g_in + self.sum_s[0, j], g_out + self.sum_s[1, j]
                    self.sum_s[0, j], self.sum_s[1, j] = g_in, g_out
                    q_t = adjoint * self.spread_s[0, j]
                    q_sums.add(j, q_t[:8] + q_t[8:])
                    pulled = decays[j] * adjoint
                    past = pulled * states[j]
                    r_t = past * a
                    r_sums.add(j, r_t[:8] + r_t[8:])
                    alog = alog + past * stepd[j : j + 1]
                self.pulled_s[:, lanes], self.alog_s[:, lanes] = pulled, alog
                self.q_s[pl.ds(base, 8), lanes] = q_sums.result
                self.r_s[pl.ds(base, 8), lanes] = r_sums.result
            for k in range(2):
                row = self.gmap_s[k * N : (k + 1) * N, tile]
                for j in range(8):
                    row = jnp.where(self.lane == first + j, jnp.sum(self.sum_s[k, j], axis=1, keepdims=True), row)
                self.gmap_s[k * N : (k + 1) * N, tile] = row
            return none

        lax.fori_loop(start, stop, chunk, 0)


class TokenSum:
    def __init__(self, spot, copies, part, y_land, z_land, y_sems, z_sems):
        self.spot, self.copies, self.part, self.y_land, self.z_land = spot, copies, part, y_land, z_land
        self.y_sems, self.z_sems = y_sems, z_sems

    def push(self):
        spot = self.spot
        for offset in (1, 2, 3, 0):
            z = spot.z_at(offset)
            self.copies.send(self.part.at[z, 1 - spot.y], self.y_land.at[z], self.y_sems.at[z], spot.y_mate)

    def middle(self):
        spot = self.spot
        for offset in (1, 2, 3):
            z = spot.z_at(offset)
            arrived(self.y_land.at[z], self.y_sems.at[z])
            self.part[z, spot.y] = (self.part[z, spot.y].astype(F32) + self.y_land[z].astype(F32)).astype(BF16)
            self.copies.send(self.part.at[z, spot.y], self.z_land.at[offset - 1], self.z_sems.at[offset - 1], spot.on_line(z))

    def last(self):
        spot = self.spot
        arrived(self.y_land.at[spot.z], self.y_sems.at[spot.z])
        summed = self.part[spot.z, spot.y].astype(F32) + self.y_land[spot.z].astype(F32)
        for k in range(NZ - 1):
            arrived(self.z_land.at[k], self.z_sems.at[k])
            summed = summed + self.z_land[k].astype(F32)
        return summed


class RowSum:
    def __init__(self, spot, copies, part, c_land, x_land, z_land, c_sems, x_sems, z_sems):
        self.spot, self.copies, self.part = spot, copies, part
        self.c_land, self.x_land, self.z_land = c_land, x_land, z_land
        self.c_sems, self.x_sems, self.z_sems = c_sems, x_sems, z_sems

    def push(self):
        spot = self.spot
        for offset in (1, 2, 3, 0):
            z = spot.z_at(offset)
            for x in (1 - spot.x, spot.x):
                self.copies.send(self.part.at[z, x, 1 - spot.c], self.c_land.at[z, x], self.c_sems.at[z, x], spot.c_mate)

    def add(self, z, x, landed):
        part = self.part
        part[z, x, self.spot.c] = (part[z, x, self.spot.c].astype(F32) + landed.astype(F32)).astype(part.dtype)

    def second(self):
        spot = self.spot
        for offset in (1, 2, 3, 0):
            z = spot.z_at(offset)
            for x in (1 - spot.x, spot.x):
                arrived(self.c_land.at[z, x], self.c_sems.at[z, x])
                self.add(z, x, self.c_land[z, x])
            self.copies.send(self.part.at[z, 1 - spot.x, spot.c], self.x_land.at[z], self.x_sems.at[z], spot.x_mate)

    def third(self):
        spot = self.spot
        for offset in (1, 2, 3, 0):
            z = spot.z_at(offset)
            arrived(self.x_land.at[z], self.x_sems.at[z])
            self.add(z, spot.x, self.x_land[z])
            if offset:
                self.copies.send(
                    self.part.at[z, spot.x, spot.c], self.z_land.at[spot.z], self.z_sems.at[spot.z], spot.on_line(z)
                )
        self.z_land[spot.z] = self.part[spot.z, spot.x, spot.c]

    def last(self):
        spot = self.spot
        for offset in (1, 2, 3):
            z = spot.z_at(-offset)
            arrived(self.z_land.at[z], self.z_sems.at[z])


class ChannelSum:
    def __init__(self, spot, copies, part, c_land, x_land, full, c_sem, x_sem, full_sems):
        self.spot, self.copies, self.part, self.full, self.full_sems = spot, copies, part, full, full_sems
        self.c_land, self.x_land, self.c_sem, self.x_sem = c_land, x_land, c_sem, x_sem

    def push(self):
        self.copies.send(self.part.at[1 - self.spot.c], self.c_land, self.c_sem, self.spot.c_mate)

    def second(self):
        spot = self.spot
        arrived(self.c_land, self.c_sem)
        self.part[spot.c] = self.part[spot.c] + self.c_land[...]
        self.copies.send(self.part.at[spot.c, 1 - spot.x], self.x_land, self.x_sem, spot.x_mate)

    def spread(self, origin, device):
        self.copies.send(self.full.at[origin], self.full.at[origin], self.full_sems.at[origin], device)

    def third(self):
        spot = self.spot
        arrived(self.x_land, self.x_sem)
        self.full[spot.dp] = self.part[spot.c, spot.x] + self.x_land[...]
        for offset in (1, 2, 3):
            self.spread(spot.dp, spot.on_line(spot.z_at(offset)))
        self.spread(spot.dp, spot.x_mate)
        self.spread(spot.dp, spot.c_mate)

    def fourth(self):
        spot = self.spot
        for offset in (1, 2, 3):
            origin = place(spot.z_at(-offset), spot.x, spot.c)
            arrived(self.full.at[origin], self.full_sems.at[origin])
            self.spread(origin, spot.x_mate)
            self.spread(origin, spot.c_mate)

    def fifth(self):
        spot = self.spot
        for offset in range(NZ):
            origin = place(spot.z_at(-offset), 1 - spot.x, spot.c)
            arrived(self.full.at[origin], self.full_sems.at[origin])
            self.spread(origin, spot.c_mate)

    def last(self):
        spot = self.spot
        for x in range(2):
            for offset in range(NZ):
                origin = place(spot.z_at(-offset), x, 1 - spot.c)
                arrived(self.full.at[origin], self.full_sems.at[origin])


class Held:
    def __init__(self, names, refs):
        for name, ref in zip(names, refs, strict=True):
            setattr(self, name, ref)


def block_scratch(half, feats, rows, chans, step_rows, width):
    tokens, n_dp, length = 2 * half * NZ, 4 * NZ, 2 * half
    vmem, dma = pltpu.VMEM, pltpu.SemaphoreType.DMA
    owners, steps = (NZ, 2, 2, rows, chans), (NZ, 2, 2, step_rows, chans)
    part = (NZ, 2, width // 2, length)
    small = (width + 32) // 4
    held = {
        "w": vmem((3, n_dp, rows, chans), BF16),
        "acts": vmem((2, NZ, 2, half, feats), BF16),
        "dtp_own": vmem((step_rows, chans * NZ), F32),
        "dtp": vmem((n_dp, step_rows, chans), F32),
        "info": vmem((n_dp, 8, 128), F32),
        "mask": vmem((NZ, length, 128), F32),
        "low": vmem((tokens, chans), BF16),
        "gated": vmem((tokens, chans), BF16),
        "ggate": vmem((tokens, chans), BF16),
    }
    for name in ("x_in", "pre", "gate", "gg", "raw", "stepd", "drive", "gs", "read", "r"):
        held[name] = vmem((tokens, chans), F32)
    held |= {
        "a": vmem((N, chans), F32),
        "state": vmem((tokens // 8 + 1, N, chans), F32),
        "pulled": vmem((N, chans), F32),
        "alog": vmem((N, chans), F32),
        "spread": vmem((2, 8, N, 128), F32),
        "sum": vmem((2, 8, N, 128), F32),
        "gmap": vmem((2 * N, tokens), F32),
        "dbl": vmem((width, tokens), F32),
        "part": vmem(part, F32),
        "landing": vmem((2 * NZ,) + part[2:], F32),
        "total": vmem(part, F32),
        "gpart": vmem(part, F32),
        "glanding": vmem((2 * NZ,) + part[2:], F32),
        "gtotal": vmem(part, F32),
        "mixed": vmem((NZ, 2, half, feats), BF16),
        "normed": vmem((NZ, 2, half, feats), BF16),
        "outw": vmem(owners, BF16),
        "ginz": vmem(owners, BF16),
        "ginx": vmem(owners, BF16),
        "gdtp": vmem(steps, F32),
        "chan": vmem((2, 2, small, chans), F32),
        "y_land": vmem((2, NZ, half, feats), BF16),
        "z_land": vmem((2, NZ - 1, half, feats), BF16),
        "wc_land": vmem((3, NZ, 2, rows, chans), BF16),
        "wx_land": vmem((3, NZ, rows, chans), BF16),
        "dc_land": vmem((NZ, 2, step_rows, chans), F32),
        "dx_land": vmem((NZ, step_rows, chans), F32),
        "fc_land": vmem((2, small, chans), F32),
        "fx_land": vmem((small, chans), F32),
        "tile": vmem((4, 8, 128), F32),
        "gain": vmem((3, n_dp, 8, 128), F32),
        "gain_land": vmem((n_dp - 1, 8, 128), F32),
        "send_sems": dma((288,)),
        "own_sems": dma((4,)),
        "w_sems": dma((4, n_dp)),
        "act_sems": dma((2, NZ, 2)),
        "info_sems": dma((n_dp,)),
        "part_sems": dma((2, 2 * NZ)),
        "total_sems": dma((2, NZ, 2)),
        "y_sems": dma((2, NZ)),
        "z_sems": dma((2, NZ - 1)),
        "wc_sems": dma((4, NZ, 2)),
        "wx_sems": dma((4, NZ)),
        "wz_sems": dma((4, NZ)),
        "f_sems": dma((2,)),
        "full_sems": dma((n_dp,)),
        "tile_sems": dma((2,)),
        "gain_sems": dma((n_dp,)),
    }
    return held


def block_kernel(names, *refs):
    (
        inx_ref, inz_ref, outp_ref, resid_ref, cot_ref, gain_ref, ids_ref, dtp_ref, xproj_ref, convw_ref, convb_ref, dtb_ref,
        alog_ref, skip_ref,
        block_ref, gresid_ref, ggain_ref, ginx_ref, ginz_ref, goutp_ref, gdtp_ref, full_ref, square_ref, msquare_ref,
    ) = refs[:24]
    s = Held(names, refs[24:])
    spot = Spot()
    plane = [lax.rem(spot.dp + offset, 4 * NZ) for offset in range(1, 4 * NZ)]
    greet([(dp, spot.y) for dp in plane] + [spot.on_line(spot.z_at(dz), 1 - spot.y) for dz in range(NZ)])
    copies = Copies(s.send_sems)
    tokens, chans = s.x_in.shape
    half, feats = resid_ref.shape
    length = 2 * half
    columns = pl.ds(pl.multiple_of(spot.z * chans, chans), chans)
    sequences = [slice(k * length, (k + 1) * length) for k in range(NZ)]

    s.dtp_own[...] = dtp_ref[...].astype(F32)
    inx, inz, outp, dtp = (
        Gather(spot, copies, src, dst, s.w_sems.at[k], s.own_sems.at[k])
        for k, (src, dst) in enumerate(((inx_ref, s.w.at[0]), (inz_ref, s.w.at[1]), (outp_ref, s.w.at[2]), (s.dtp_own, s.dtp)))
    )
    normed, cot = (Share(spot, copies, s.acts.at[k], s.act_sems.at[k]) for k in range(2))

    ids = jnp.broadcast_to(ids_ref[...], (8, length))
    lane = lax.broadcasted_iota(jnp.int32, (8, length), 1)
    sub = lax.broadcasted_iota(jnp.int32, (8, length), 0)
    info = jnp.broadcast_to(gain_ref[...].astype(F32), (8, length))
    for back in range(1, 4):
        same = jnp.where((pltpu.roll(ids, back, 1) == ids) & (lane >= back), 1.0, 0.0)
        info = jnp.where(sub == back, same, info)
    s.info[spot.dp] = info
    for dp in plane:
        copies.send(s.info.at[spot.dp], s.info.at[spot.dp], s.info_sems.at[spot.dp], (dp, spot.y))
    inx.push()

    resid = resid_ref[...]
    row_square = jnp.sum(resid * resid, axis=1, keepdims=True)
    scaled = resid * lax.rsqrt(row_square / feats + eps_norm)
    s.tile[0] = jnp.broadcast_to(jnp.sum(row_square, axis=0, keepdims=True), (8, 128))
    copies.send(s.tile.at[0], s.tile.at[1], s.tile_sems.at[0], spot.y_mate)
    for dp in plane:
        arrived(s.info.at[dp], s.info_sems.at[dp])
    for k in range(4 * NZ):
        cols = slice(k * 128, (k + 1) * 128)
        s.acts[0, spot.z, spot.y, :, cols] = (scaled[:, cols] * s.info[k, 0:1, :]).astype(BF16)
    normed.push()
    dtp.push()
    s.acts[1, spot.z, spot.y] = cot_ref[...].astype(BF16)
    for k in range(NZ):
        s.mask[k] = column_masks(s.info[place(k, spot.x, spot.c)])
    inx.first()
    inz.push()
    normed.first(1)
    inx.second()
    cot.push()
    normed.first(2)
    dtp.first()
    dtp.second()
    normed.first(3)
    inz.first()
    outp.push()
    normed.last()
    inx.last()

    tokens_x = s.acts.at[0], s.acts.at[1]
    all_normed = s.acts[0].reshape(tokens, feats)
    s.x_in[...] = dot(all_normed, s.w[0].reshape(-1, chans))
    taps = convw_ref[:, columns]
    bias = convb_ref[:, columns]
    for k, rows in enumerate(sequences):
        one = s.x_in[rows]
        pre = bias + taps[3:4] * one
        for back in range(1, 4):
            pre = pre + taps[3 - back : 4 - back] * (pltpu.roll(one, back, 0) * s.mask[k, :, back : back + 1])
        s.pre[rows] = pre
        s.low[rows] = (pre * sigmoid(pre)).astype(BF16)
    x_proj = xproj_ref[:, columns]
    dbl = dot(x_proj, s.low[...], NT)
    blocks = [(k, y) for k in range(NZ) for y in range(2)]
    width = dbl.shape[0] // 2
    for k, y in blocks:
        s.part[k, y] = dbl[y * width : (y + 1) * width, sequences[k]]
    x_dbl = LineSum(spot, copies, s.part, s.landing, s.total, s.part_sems.at[0], s.total_sems.at[0])
    x_dbl.push()
    cot.first(1)
    inz.second()
    x_dbl.middle()
    cot.first(2)
    outp.first()
    dtp.last()
    x_dbl.last()

    for k, y in blocks:
        s.dbl[y * width : (y + 1) * width, sequences[k]] = s.total[k, y]
    step_w = s.dtp[...].reshape(R, chans).astype(BF16)
    s.raw[...] = split_dot(s.dbl[:R], step_w, TN) + dtb_ref[:, columns]
    for k, rows in enumerate(sequences):
        step = softplus(s.raw[rows])
        s.stepd[rows] = jnp.where(s.mask[k, :, 1:2] > 0.0, step, 1e30)
        s.drive[rows] = step * s.low[rows].astype(F32)
    s.a[...] = -jnp.exp(alog_ref[:, columns])
    s.state[0] = jnp.zeros((N, chans), F32)
    scan = Scan(
        s.dbl.at[R : R + 2 * N], s.a, s.stepd, s.drive, s.gs, s.read, s.read, s.r, s.state, s.pulled, s.alog, s.spread, s.sum, s.gmap
    )
    steps = tokens // 8
    scan.forward(0, steps // 4)
    cot.first(3)
    outp.second()
    scan.forward(steps // 4, steps)
    inz.last()
    s.gate[...] = dot(s.acts[0].reshape(tokens, feats), s.w[1].reshape(-1, chans))
    cot.last()
    outp.last()
    s.gg[...] = dot(s.acts[1].reshape(tokens, feats), s.w[2].reshape(-1, chans))
    skip = skip_ref[:, columns]
    for rows in sequences:
        gate, gg = s.gate[rows], s.gg[rows]
        sig = sigmoid(gate)
        scanned = s.read[rows] + skip * s.low[rows].astype(F32)
        s.gs[rows] = gg * gate * sig
        s.gated[rows] = (scanned * gate * sig).astype(BF16)
        s.ggate[rows] = (gg * scanned * sig * (1.0 + gate * (1.0 - sig))).astype(BF16)

    mixed_sum, normed_sum = (
        TokenSum(spot, copies, part, s.y_land.at[k], s.z_land.at[k], s.y_sems.at[k], s.z_sems.at[k])
        for k, part in enumerate((s.mixed, s.normed))
    )
    outw_sum, ginz_sum, ginx_sum, gdtp_sum = (
        RowSum(spot, copies, part, c_land, x_land, out, s.wc_sems.at[k], s.wx_sems.at[k], s.wz_sems.at[k])
        for k, (part, c_land, x_land, out) in enumerate((
            (s.outw, s.wc_land.at[0], s.wx_land.at[0], goutp_ref),
            (s.ginz, s.wc_land.at[1], s.wx_land.at[1], ginz_ref),
            (s.ginx, s.wc_land.at[2], s.wx_land.at[2], ginx_ref),
            (s.gdtp, s.dc_land, s.dx_land, gdtp_ref),
        ))
    )
    s.mixed[...] = dot(s.gated[...], s.w[2].reshape(-1, chans), NT).astype(BF16).reshape(s.mixed.shape)
    mixed_sum.push()
    s.outw[...] = dot(s.acts[1].reshape(tokens, feats), s.gated[...], TN).astype(BF16).reshape(s.outw.shape)
    outw_sum.push()
    s.ginz[...] = dot(s.acts[0].reshape(tokens, feats), s.ggate[...], TN).astype(BF16).reshape(s.ginz.shape)
    ginz_sum.push()

    s.pulled[...] = jnp.zeros_like(s.pulled)
    s.alog[...] = jnp.zeros_like(s.alog)
    outw_sum.second()
    scan.backward(steps - steps // 4, steps)
    ginz_sum.second()
    mixed_sum.middle()
    scan.backward(steps // 2, steps - steps // 4)
    outw_sum.third()
    scan.backward(steps // 4, steps // 2)
    ginz_sum.third()
    scan.backward(0, steps // 4)

    grad_bias = jnp.zeros((1, chans), F32)
    grad_skip = jnp.zeros((1, chans), F32)
    raw_rows = []
    for rows in sequences:
        conv, raw, gs, q = s.low[rows].astype(F32), s.raw[rows], s.gs[rows], s.read[rows]
        grad_raw = (conv * q + s.r[rows]) * sigmoid(raw)
        s.gg[rows] = softplus(raw) * q + skip * gs
        grad_bias = grad_bias + jnp.sum(grad_raw, axis=0, keepdims=True)
        grad_skip = grad_skip + jnp.sum(gs * conv, axis=0, keepdims=True)
        raw_rows.append(grad_raw.astype(BF16))
    raw_low = jnp.concatenate(raw_rows, axis=0)
    dbl = jnp.concatenate([dot(step_w, raw_low, NT), s.gmap[...]], axis=0)
    for k, y in blocks:
        s.gpart[k, y] = dbl[y * width : (y + 1) * width, sequences[k]]
    grad_dbl_sum = LineSum(spot, copies, s.gpart, s.glanding, s.gtotal, s.part_sems.at[1], s.total_sems.at[1])
    grad_dbl_sum.push()
    s.gdtp[...] = dot(s.dbl[:R].astype(BF16), raw_low).reshape(s.gdtp.shape)
    gdtp_sum.push()
    grad_dbl_sum.middle()
    gdtp_sum.second()
    grad_dbl_sum.last()

    grad_dbl = jnp.concatenate(
        [jnp.concatenate([s.gtotal[k, y] for k in range(NZ)], axis=1) for y in range(2)], axis=0
    ).astype(BF16)
    s.gg[...] += dot(grad_dbl, x_proj, TN)
    sums = [jnp.zeros((1, chans), F32) for _ in range(5)]
    low_rows = []
    for k, rows in enumerate(sequences):
        pre, x_one = s.pre[rows], s.x_in[rows]
        sig = sigmoid(pre)
        one = s.gg[rows] * sig * (1.0 + pre * (1.0 - sig))
        sums[3] = sums[3] + jnp.sum(one * x_one, axis=0, keepdims=True)
        sums[4] = sums[4] + jnp.sum(one, axis=0, keepdims=True)
        grad_x = taps[3:4] * one
        for back in range(1, 4):
            masked = one * s.mask[k, :, back : back + 1]
            sums[3 - back] = sums[3 - back] + jnp.sum(masked * pltpu.roll(x_one, back, 0), axis=0, keepdims=True)
            grad_x = grad_x + taps[3 - back : 4 - back] * pltpu.roll(masked, length - back, 0)
        low_rows.append(grad_x.astype(BF16))
    grad_xin = jnp.concatenate(low_rows, axis=0)
    s.normed[...] = (
        dot(grad_xin, s.w[0].reshape(-1, chans), NT) + dot(s.ggate[...], s.w[1].reshape(-1, chans), NT)
    ).astype(BF16).reshape(s.normed.shape)
    normed_sum.push()
    s.ginx[...] = dot(s.acts[0].reshape(tokens, feats), grad_xin, TN).astype(BF16).reshape(s.ginx.shape)
    ginx_sum.push()
    s.chan[...] = jnp.concatenate(
        [dot(grad_dbl, s.low[...]), s.alog[...] * s.a[...], grad_bias, grad_skip, jnp.zeros((6, chans), F32)]
        + sums + [jnp.zeros((3, chans), F32)], axis=0
    ).reshape(s.chan.shape)
    small_sum = ChannelSum(
        spot, copies, s.chan, s.fc_land, s.fx_land, full_ref, s.f_sems.at[0], s.f_sems.at[1], s.full_sems
    )
    small_sum.push()
    ginx_sum.second()
    gdtp_sum.third()
    small_sum.second()
    normed_sum.middle()
    small_sum.third()
    ginx_sum.third()

    mixed = mixed_sum.last()
    resid = resid_ref[...]
    block_ref[...] = resid + mixed
    s.tile[2] = jnp.broadcast_to(jnp.sum(jnp.sum(mixed * mixed, axis=1, keepdims=True), axis=0, keepdims=True), (8, 128))
    copies.send(s.tile.at[2], s.tile.at[3], s.tile_sems.at[1], spot.y_mate)
    small_sum.fourth()
    outw_sum.last()
    ginz_sum.last()
    gdtp_sum.last()
    small_sum.fifth()

    grad_rows = normed_sum.last()
    inv = lax.rsqrt(jnp.sum(resid * resid, axis=1, keepdims=True) / feats + eps_norm)
    scaled = resid * inv
    gain_part = jnp.sum(grad_rows * scaled, axis=0, keepdims=True)
    for k in range(4 * NZ):
        s.gain[0, k] = jnp.broadcast_to(gain_part[:, k * 128 : (k + 1) * 128], (8, 128))
    copies.send(s.gain.at[0], s.gain.at[1], s.gain_sems.at[4 * NZ - 1], spot.y_mate)
    gain = jnp.concatenate([s.info[k, 0:1] for k in range(4 * NZ)], axis=1)
    grad_scaled = grad_rows * gain
    mean = jnp.sum(grad_scaled * scaled, axis=1, keepdims=True) / feats
    gresid_ref[...] = cot_ref[...] + inv * (grad_scaled - scaled * mean)
    arrived(s.gain.at[1], s.gain_sems.at[4 * NZ - 1])
    s.gain[2] = s.gain[0] + s.gain[1]
    for offset, dp in enumerate(plane):
        copies.send(s.gain.at[2, dp], s.gain_land.at[offset], s.gain_sems.at[offset], (dp, spot.y))
    arrived(s.tile.at[1], s.tile_sems.at[0])
    square_ref[...] = s.tile[0] + s.tile[1]
    arrived(s.tile.at[3], s.tile_sems.at[1])
    msquare_ref[...] = s.tile[2] + s.tile[3]
    ginx_sum.last()
    small_sum.last()
    total = s.gain[2, spot.dp]
    for offset in range(4 * NZ - 1):
        arrived(s.gain_land.at[offset], s.gain_sems.at[offset])
        total = total + s.gain_land[offset]
    ggain_ref[...] = total
    copies.wait_sent()


def block_call(in_x, in_z, out_p, residual, cotangent, gain, ids, dt_p, x_proj, conv_w, conv_b, dt_b, a_log, d_skip):
    half, feats = residual.shape
    rows, wide = in_x.shape
    n_dp, chans = 4 * NZ, wide // NZ
    held = block_scratch(half, feats, rows, chans, dt_p.shape[0], x_proj.shape[0])
    shape = jax.ShapeDtypeStruct
    outs = [
        shape((half, feats), F32), shape((half, feats), F32), shape((8, 128), F32),
        shape((NZ, rows, chans), BF16), shape((NZ, rows, chans), BF16), shape((NZ, rows, chans), BF16),
        shape((NZ, dt_p.shape[0], chans), F32), shape((n_dp, (x_proj.shape[0] + 32) // 4, chans), F32),
        shape((8, 128), F32), shape((8, 128), F32),
    ]
    in_any = pl.BlockSpec(memory_space=pl.ANY)
    in_vmem = pl.BlockSpec(memory_space=pltpu.VMEM)
    return pl.pallas_call(
        functools.partial(block_kernel, list(held)),
        out_shape=outs,
        in_specs=[in_any] * 3 + [in_vmem] * 11,
        out_specs=[in_vmem] * len(outs),
        scratch_shapes=list(held.values()),
        name="block",
        compiler_params=pltpu.CompilerParams(collective_id=1, has_side_effects=True, vmem_limit_bytes=62 << 20),
    )(in_x, in_z, out_p, residual, cotangent, gain, ids, dt_p, x_proj, conv_w, conv_b, dt_b, a_log, d_skip)


def finish_kernel(
    block_in, gresid_in, ginx_in, ginz_in, goutp_in, gdtp_in, full_in,
    block_ref, gresid_ref, ginx_ref, ginz_ref, goutp_ref, gdtp_ref, xproj_ref, alog_ref, dtb_ref, skip_ref, convw_ref, convb_ref,
):
    block_ref[...] = block_in[...]
    gresid_ref[...] = gresid_in[...]
    chans = ginx_in.shape[2]
    for z in range(NZ):
        cols = slice(z * chans, (z + 1) * chans)
        for given, ref in ((ginx_in, ginx_ref), (ginz_in, ginz_ref), (goutp_in, goutp_ref), (gdtp_in, gdtp_ref)):
            ref[:, cols] = given[z].astype(F32)
        rows = full_in.shape[1]
        for k in range(4):
            origin = place(z, k % 2, k // 2)
            upto = min(rows, xproj_ref.shape[0] - k * rows)
            xproj_ref[k * rows : k * rows + upto, cols] = full_in[origin, :upto]
        last = place(z, 1, 1)
        alog_ref[:, cols] = full_in[last, upto : upto + N]
        dtb_ref[:, cols] = full_in[last, upto + N : upto + N + 1]
        skip_ref[:, cols] = full_in[last, upto + N + 1 : upto + N + 2]
        convw_ref[:, cols] = full_in[last, upto + 24 : upto + 28]
        convb_ref[:, cols] = full_in[last, upto + 28 : upto + 29]


def finish_call(block, gresid, ginx, ginz, goutp, gdtp, full, width):
    rows, wide = ginx.shape[1], ginx.shape[2] * NZ
    shape = lambda count: jax.ShapeDtypeStruct((count, wide), F32)
    outs = [
        jax.ShapeDtypeStruct(block.shape, F32), jax.ShapeDtypeStruct(gresid.shape, F32), shape(rows), shape(rows), shape(rows),
        shape(gdtp.shape[1]), shape(width), shape(N), shape(1), shape(1), shape(4), shape(1),
    ]
    spec = pl.BlockSpec(memory_space=pltpu.VMEM)
    return pl.pallas_call(
        finish_kernel, out_shape=outs, in_specs=[spec] * 7, out_specs=[spec] * len(outs), name="finish",
        compiler_params=pltpu.CompilerParams(vmem_limit_bytes=40 << 20),
    )(block, gresid, ginx, ginz, goutp, gdtp, full)


def per_device_split(
    residual,
    norm_gain,
    in_proj_x,
    in_proj_z,
    x_proj,
    dt_proj,
    dt_bias,
    conv_weight,
    conv_bias,
    a_log,
    d_skip,
    out_proj,
    doc_ids,
    cotangent,
):
    block, gresid, grad_gain, ginx, ginz, goutp, gdtp, full, resid_square, mixed_square = block_call(
        in_proj_x, in_proj_z, out_proj, residual, cotangent, norm_gain[None], doc_ids[None], dt_proj, x_proj, conv_weight,
        conv_bias[None], dt_bias[None], a_log, d_skip[None],
    )
    block, gresid, ginx, ginz, goutp, gdtp, g_xproj, g_alog, g_dtb, g_skip, g_convw, g_convb = finish_call(
        block, gresid, ginx, ginz, goutp, gdtp, full, x_proj.shape[0]
    )
    rms_resid, rms_mixed = (jnp.sqrt(v[0, :1] / (doc_ids.shape[0] * D)) for v in (resid_square, mixed_square))
    return (
        block,
        gresid,
        grad_gain[0],
        ginx,
        ginz,
        g_xproj,
        gdtp,
        g_dtb[0],
        g_convw,
        g_convb[0],
        g_alog,
        g_skip[0],
        goutp,
        rms_resid,
        rms_mixed,
    )


def norm_rows(values, gain_val):
    mean_square = jnp.mean(values * values, axis=1, keepdims=True)
    return values * lax.rsqrt(mean_square + eps_norm) * gain_val


def conv_local(x_in, doc_ids, conv_weight, conv_bias):
    kernel_len = conv_weight.shape[0]
    length = x_in.shape[0]
    padded = jnp.pad(x_in, ((kernel_len - 1, 0), (0, 0)))
    id_pad = jnp.concatenate([jnp.full((kernel_len - 1,), -1, jnp.int32), doc_ids])
    summed = conv_bias + jnp.zeros_like(x_in)
    for offset in range(kernel_len):
        same_doc = (id_pad[offset : offset + length] == doc_ids).astype(jnp.float32)
        summed = summed + conv_weight[offset] * padded[offset : offset + length] * same_doc[:, None]
    return summed


def per_device(
    residual,
    norm_gain,
    in_proj_x,
    in_proj_z,
    x_proj,
    dt_proj,
    dt_bias,
    conv_weight,
    conv_bias,
    a_log,
    d_skip,
    out_proj,
    doc_ids,
    cotangent,
):
    gathered = (
        lax.all_gather(norm_gain, "dp", axis=0, tiled=True),
        lax.all_gather(in_proj_x, "dp", axis=0, tiled=True),
        lax.all_gather(in_proj_z, "dp", axis=0, tiled=True),
        lax.all_gather(dt_proj, "dp", axis=0, tiled=True),
        lax.all_gather(out_proj, "dp", axis=0, tiled=True),
    )
    gain_all, inx_all, inz_all, step_all, out_all = gathered
    seq_len = doc_ids.shape[0]
    normed_f32, norm_back = jax.vjp(norm_rows, residual, gain_all.astype(jnp.float32))
    normed = lax.all_gather(normed_f32.astype(jnp.bfloat16), "tensor", axis=0, tiled=True)
    x_in = jnp.dot(normed, inx_all, preferred_element_type=jnp.float32)
    gate_in = jnp.dot(normed, inz_all, preferred_element_type=jnp.float32)

    def conv_act(x_val, weight_val, bias_val):
        return jax.nn.silu(conv_local(x_val, doc_ids, weight_val, bias_val))

    conv_out, conv_back = jax.vjp(conv_act, x_in, conv_weight, conv_bias)
    conv_low = conv_out.astype(jnp.bfloat16)
    dbl_part = lax.dot_general(
        conv_low, x_proj, (((1,), (1,)), ((), ())), preferred_element_type=jnp.float32
    )
    x_dbl, resid_square = lax.psum((dbl_part, jnp.sum(residual * residual)), "tensor")
    doc_starts = doc_ids != jnp.concatenate([jnp.full((1,), -1, jnp.int32), doc_ids[:-1]])
    carry_keep = 1.0 - doc_starts.astype(jnp.float32)

    cot_all = lax.all_gather(cotangent.astype(jnp.bfloat16), "tensor", axis=0, tiled=True)
    grad_gated = jnp.dot(cot_all, out_all, preferred_element_type=jnp.float32)
    gated_low, grad_gate_low, grad_conv, grad_dbl_part, grad_step_w, grad_bias, grad_alog, grad_skip = scan_call(
        x_dbl, conv_low, gate_in, grad_gated, step_all, dt_bias, a_log, d_skip, carry_keep
    )
    mixed = lax.psum_scatter(
        lax.dot_general(
            gated_low, out_all, (((1,), (1,)), ((), ())), preferred_element_type=jnp.float32
        ),
        "tensor",
        scatter_dimension=0,
        tiled=True,
    )
    block_out = residual + mixed
    mixed_square = lax.psum(jnp.sum(mixed * mixed), "tensor")
    rms_resid = jnp.sqrt(resid_square / (seq_len * D)).reshape(1)
    rms_mixed = jnp.sqrt(mixed_square / (seq_len * D)).reshape(1)
    grad_out_w = lax.dot_general(
        cot_all, gated_low, (((0,), (0,)), ((), ())), preferred_element_type=jnp.float32
    )
    grad_dbl = lax.psum(grad_dbl_part.T, "tensor")
    grad_dbl_low = grad_dbl.astype(jnp.bfloat16)
    grad_conv = grad_conv + jnp.dot(grad_dbl_low, x_proj, preferred_element_type=jnp.float32)
    grad_xproj = lax.dot_general(
        grad_dbl_low, conv_low, (((0,), (0,)), ((), ())), preferred_element_type=jnp.float32
    )
    grad_xin, grad_convw, grad_convb = conv_back(grad_conv)
    grad_xin_low = grad_xin.astype(jnp.bfloat16)
    grad_inx = lax.dot_general(
        normed, grad_xin_low, (((0,), (0,)), ((), ())), preferred_element_type=jnp.float32
    )
    grad_inz = lax.dot_general(
        normed, grad_gate_low, (((0,), (0,)), ((), ())), preferred_element_type=jnp.float32
    )
    first_term = lax.dot_general(
        grad_xin_low, inx_all, (((1,), (1,)), ((), ())), preferred_element_type=jnp.float32
    )
    second_term = lax.dot_general(
        grad_gate_low, inz_all, (((1,), (1,)), ((), ())), preferred_element_type=jnp.float32
    )
    grad_normed = lax.psum_scatter(
        first_term + second_term, "tensor", scatter_dimension=0, tiled=True
    )
    grad_rows_x, grad_gain_part = norm_back(grad_normed)
    grad_residual = cotangent + grad_rows_x
    grad_gain = lax.psum(grad_gain_part, "tensor")
    gain_shard, inx_shard, inz_shard, step_shard, out_shard = (
        lax.psum_scatter(grad_gain, "dp", scatter_dimension=0, tiled=True),
        lax.psum_scatter(grad_inx, "dp", scatter_dimension=0, tiled=True),
        lax.psum_scatter(grad_inz, "dp", scatter_dimension=0, tiled=True),
        lax.psum_scatter(grad_step_w, "dp", scatter_dimension=0, tiled=True),
        lax.psum_scatter(grad_out_w, "dp", scatter_dimension=0, tiled=True),
    )
    small_sums = lax.psum(
        (grad_xproj, grad_bias, grad_convw, grad_convb, grad_alog, grad_skip), "dp"
    )
    xproj_sum, bias_sum, convw_sum, convb_sum, alog_sum, skip_sum = small_sums
    return (
        block_out,
        grad_residual,
        gain_shard,
        inx_shard,
        inz_shard,
        xproj_sum,
        step_shard,
        bias_sum,
        convw_sum,
        convb_sum,
        alog_sum,
        skip_sum,
        out_shard,
        rms_resid,
        rms_mixed,
    )


def solution(mesh):
    placed = (
        P(("dp", "tensor"), None),
        P("dp"),
        P("dp", "tensor"),
        P("dp", "tensor"),
        P(None, "tensor"),
        P("dp", "tensor"),
        P("tensor"),
        P(None, "tensor"),
        P("tensor"),
        P(None, "tensor"),
        P("tensor"),
        P("dp", "tensor"),
        P("dp"),
        P(("dp", "tensor"), None),
    )
    return jax.shard_map(
        per_device_split if mesh.shape["dp"] == 4 * NZ else per_device,
        mesh=mesh,
        in_specs=placed,
        out_specs=(
            P(("dp", "tensor"), None),
            P(("dp", "tensor"), None),
            P("dp"),
            P("dp", "tensor"),
            P("dp", "tensor"),
            P(None, "tensor"),
            P("dp", "tensor"),
            P("tensor"),
            P(None, "tensor"),
            P("tensor"),
            P(None, "tensor"),
            P("tensor"),
            P("dp", "tensor"),
            P("dp"),
            P("dp"),
        ),
        check_vma=False,
    )
```

```python
import functools

import jax
import jax.numpy as jnp
from jax import lax
from jax.experimental import pallas as pl
from jax.experimental.pallas import tpu as pltpu
from jax.sharding import PartitionSpec as P

D = 2048
R = 128
N = 16

eps_norm = 1e-05


def sigmoid(v):
    return 1.0 / (1.0 + jnp.exp(-v))


def softplus(v):
    return jnp.maximum(v, 0.0) + jnp.log(1.0 + jnp.exp(-jnp.abs(v)))


def fold_rows(first, second, shift, lower):
    kept = jnp.where(lower, first, second)
    moved = jnp.where(lower, second, first)
    return kept + pltpu.roll(moved, shift, 0)


class RowSums:
    def __init__(self, masks):
        self.masks = masks
        self.held = {}
        self.result = None

    def add(self, token, value):
        level = 0
        while True:
            if level == 3:
                self.result = value
                return
            mate = (level, token ^ 1)
            if mate not in self.held:
                self.held[(level, token)] = value
                return
            other = self.held.pop(mate)
            first, second = (other, value) if token & 1 else (value, other)
            value = fold_rows(first, second, 1 << level, self.masks[level])
            token >>= 1
            level += 1


def split_dot(left, right_low, dims):
    high = left.astype(jnp.bfloat16)
    rest = (left - high.astype(jnp.float32)).astype(jnp.bfloat16)
    return lax.dot_general(high, right_low, dims, preferred_element_type=jnp.float32) + lax.dot_general(
        rest, right_low, dims, preferred_element_type=jnp.float32
    )


def scan_kernel(
    dbl_ref, conv_ref, gate_ref, gg_ref, dtp_ref, dtb_ref, alog_ref, skip_ref, keep_ref, in_ref, out_ref,
    gated_ref, ggate_ref, gconv_ref, gdbl_ref, gin_ref, gout_ref, gdtp_ref, gdtb_ref, galog_ref, gskip_ref,
    h_s, d_s, stepd_s, sc_s, gs_s, y_s, q_s, r_s, a_s,
):
    length, width = conv_ref.shape
    blocks = width // 128
    part = pl.program_id(0)
    sub = lax.broadcasted_iota(jnp.int32, (8, 128), 0)
    masks = [(sub & shift) == 0 for shift in (1, 2, 4)]
    lanes = [slice(b * 128, (b + 1) * 128) for b in range(blocks)]

    nn = (((1,), (0,)), ((), ()))
    step_raw = split_dot(dbl_ref[...], dtp_ref[...], nn) + dtb_ref[...]
    step = jnp.maximum(step_raw, 0.0) + jnp.log(1.0 + jnp.exp(-jnp.abs(step_raw)))
    stepd_s[...] = jnp.where(keep_ref[...] > 0.0, step, 1e30)
    sc_s[...] = step * conv_ref[...].astype(jnp.float32)
    gate = gate_ref[...]
    gs_s[...] = gg_ref[...] * gate * sigmoid(gate)
    a_s[...] = -jnp.exp(alog_ref[...])

    h_s[0] = jnp.zeros((N, width), jnp.float32)

    def forward(i, hs):
        base = pl.multiple_of(i * 8, 8)
        hs = list(hs)
        sums = [RowSums(masks) for _ in range(blocks)]
        stepd = [stepd_s[pl.ds(base, 8), lanes[b]] for b in range(blocks)]
        drive = [sc_s[pl.ds(base, 8), lanes[b]] for b in range(blocks)]
        for j in range(8):
            t = base + j
            in_t = in_ref[t]
            out_t = out_ref[t]
            for b in range(blocks):
                decay = jnp.exp(stepd[b][j : j + 1] * a_s[:, lanes[b]])
                hs[b] = decay * hs[b] + drive[b][j : j + 1] * in_t
                d_s[t, :, lanes[b]] = decay
                h_s[t + 1, :, lanes[b]] = hs[b]
                read = hs[b] * out_t
                sums[b].add(j, read[:8] + read[8:])
        for b in range(blocks):
            y_s[pl.ds(base, 8), lanes[b]] = sums[b].result
        return tuple(hs)

    zero = jnp.zeros((N, 128), jnp.float32)
    lax.fori_loop(0, length // 8, forward, (zero,) * blocks)

    conv = conv_ref[...].astype(jnp.float32)
    gate = gate_ref[...]
    sig = sigmoid(gate)
    scanned = y_s[...] + skip_ref[...] * conv
    gated_ref[...] = (scanned * gate * sig).astype(jnp.bfloat16)
    ggate_ref[...] = (gg_ref[...] * scanned * sig * (1.0 + gate * (1.0 - sig))).astype(jnp.bfloat16)

    @pl.when(part == 0)
    def _():
        gin_ref[...] = jnp.zeros_like(gin_ref)
        gout_ref[...] = jnp.zeros_like(gout_ref)
        gdbl_ref[...] = jnp.zeros_like(gdbl_ref)

    def backward(i, carried):
        base = pl.multiple_of(length - 8 - i * 8, 8)
        pulled, alog_sum = list(carried[0]), list(carried[1])
        q_sums = [RowSums(masks) for _ in range(blocks)]
        r_sums = [RowSums(masks) for _ in range(blocks)]
        stepd = [stepd_s[pl.ds(base, 8), lanes[b]] for b in range(blocks)]
        drive = [sc_s[pl.ds(base, 8), lanes[b]] for b in range(blocks)]
        gs = [gs_s[pl.ds(base, 8), lanes[b]] for b in range(blocks)]
        for j in reversed(range(8)):
            t = base + j
            in_t = in_ref[t]
            out_t = out_ref[t]
            gin_t = gin_ref[t]
            gout_t = gout_ref[t]
            for b in range(blocks):
                gs_t = gs[b][j : j + 1]
                adjoint = pulled[b] + out_t * gs_t
                gout_t = gout_t + gs_t * h_s[t + 1, :, lanes[b]]
                gin_t = gin_t + adjoint * drive[b][j : j + 1]
                q_t = adjoint * in_t
                q_sums[b].add(j, q_t[:8] + q_t[8:])
                pulled[b] = d_s[t, :, lanes[b]] * adjoint
                past = pulled[b] * h_s[t, :, lanes[b]]
                r_t = past * a_s[:, lanes[b]]
                r_sums[b].add(j, r_t[:8] + r_t[8:])
                alog_sum[b] = alog_sum[b] + past * stepd[b][j : j + 1]
            gin_ref[t] = gin_t
            gout_ref[t] = gout_t
        for b in range(blocks):
            q_s[pl.ds(base, 8), lanes[b]] = q_sums[b].result
            r_s[pl.ds(base, 8), lanes[b]] = r_sums[b].result
        return tuple(pulled), tuple(alog_sum)

    _, alog_sum = lax.fori_loop(0, length // 8, backward, ((zero,) * blocks, (zero,) * blocks))
    for b in range(blocks):
        galog_ref[:, lanes[b]] = alog_sum[b] * a_s[:, lanes[b]]

    conv = conv_ref[...].astype(jnp.float32)
    step_raw = split_dot(dbl_ref[...], dtp_ref[...], nn) + dtb_ref[...]
    step = jnp.maximum(step_raw, 0.0) + jnp.log(1.0 + jnp.exp(-jnp.abs(step_raw)))
    raw = (conv * q_s[...] + r_s[...]) * sigmoid(step_raw)
    gs = gs_s[...]
    gconv_ref[...] = step * q_s[...] + skip_ref[...] * gs
    gskip_ref[...] = jnp.sum(gs * conv, axis=0, keepdims=True)
    gdtb_ref[...] = jnp.sum(raw, axis=0, keepdims=True)
    raw_low = raw.astype(jnp.bfloat16)
    gdtp_ref[...] = lax.dot_general(
        dbl_ref[...].astype(jnp.bfloat16), raw_low, (((0,), (0,)), ((), ())), preferred_element_type=jnp.float32
    )
    gdbl_ref[...] += lax.dot_general(
        dtp_ref[...], raw_low, (((1,), (1,)), ((), ())), preferred_element_type=jnp.float32
    )


def scan_call(dbl, conv, gate, gg, dtp, dtb, alog, skip, keep):
    length, chans = conv.shape
    cb = min(65536 // length, chans)
    f32 = jnp.float32
    maps = jnp.broadcast_to(dbl[:, R:, None], (length, 2 * N, 128))
    tokens = lambda kind: (jax.ShapeDtypeStruct((length, chans), kind), pl.BlockSpec((length, cb), lambda i: (0, i)))
    whole = lambda *shape: (jax.ShapeDtypeStruct(shape, f32), pl.BlockSpec(shape, lambda i: (0,) * len(shape)))
    rows = lambda count: (jax.ShapeDtypeStruct((count, chans), f32), pl.BlockSpec((count, cb), lambda i: (0, i)))
    outs = [
        tokens(jnp.bfloat16), tokens(jnp.bfloat16), tokens(f32), whole(R, length), whole(length, N, 128), whole(length, N, 128),
        rows(R), rows(1), rows(N), rows(1),
    ]
    ins = [
        whole(length, R), tokens(f32), tokens(f32), tokens(f32), rows(R), rows(1), rows(N), rows(1),
        whole(length, 1),
    ]
    res = pl.pallas_call(
        scan_kernel,
        grid=(chans // cb,),
        in_specs=[spec for _, spec in ins] + [
            pl.BlockSpec((length, N, 128), lambda i: (0, 0, 0)), pl.BlockSpec((length, N, 128), lambda i: (0, 1, 0))],
        out_specs=[spec for _, spec in outs],
        out_shape=[shape for shape, _ in outs],
        scratch_shapes=[
            pltpu.VMEM((length + 1, N, cb), f32), pltpu.VMEM((length, N, cb), f32),
        ] + [pltpu.VMEM((length, cb), f32)] * 6 + [pltpu.VMEM((N, cb), f32)],
        name="selective_scan",
        compiler_params=pltpu.CompilerParams(vmem_limit_bytes=60 << 20),
    )(dbl[:, :R], conv, gate, gg, dtp, dtb[None], alog, skip[None], keep[:, None], maps, maps)
    gated, ggate, gconv, gdbl, gin, gout, gdtp, gdtb, galog, gskip = res
    gdbl_all = jnp.concatenate([gdbl, jnp.sum(gin, -1).T, jnp.sum(gout, -1).T], axis=0)
    return gated, ggate, gconv, gdbl_all, gdtp, gdtb[0], galog, gskip[0]


MESH = pl.DeviceIdType.MESH
NZ = 4
F32 = jnp.float32
BF16 = jnp.bfloat16
NN = (((1,), (0,)), ((), ()))
NT = (((1,), (1,)), ((), ()))
TN = (((0,), (0,)), ((), ()))


def dot(left, right, dims=NN):
    return lax.dot_general(left, right, dims, preferred_element_type=F32)


def place(z, x, c):
    return (z * 2 + x) * 2 + c


class Spot:
    def __init__(self):
        self.dp = lax.axis_index("dp")
        self.y = lax.axis_index("tensor")
        self.z, self.x, self.c = self.dp // 4, (self.dp // 2) % 2, self.dp % 2
        self.x_mate = (place(self.z, 1 - self.x, self.c), self.y)
        self.c_mate = (place(self.z, self.x, 1 - self.c), self.y)
        self.y_mate = (self.dp, 1 - self.y)

    def z_at(self, offset):
        return lax.rem(self.z + offset + NZ, NZ)

    def on_line(self, z, y=None):
        return (place(z, self.x, self.c), self.y if y is None else y)


def greet(devices):
    barrier = pltpu.get_barrier_semaphore()
    for device in devices:
        pl.semaphore_signal(barrier, inc=1, device_id=device, device_id_type=MESH)
    pl.semaphore_wait(barrier, len(devices))


class Copies:
    def __init__(self, send_sems, own_sems):
        self.send_sems, self.own_sems = send_sems, own_sems
        self.used, self.begun, self.kept = 0, [], []

    def new_sem(self):
        self.used += 1
        return self.send_sems.at[self.used - 1]

    def group(self, whole):
        sem = self.new_sem()
        self.begun.append((None, pltpu.make_async_copy(whole, whole, sem).wait))
        return sem

    def send(self, src, dst, recv_sem, device, when=None, group=None):
        copy = pltpu.make_async_remote_copy(
            src_ref=src, dst_ref=dst, send_sem=self.new_sem() if group is None else group, recv_sem=recv_sem,
            device_id=device, device_id_type=MESH,
        )
        if group is None:
            self.begun.append((when, copy.wait_send))
        if when is None:
            copy.start()
        else:
            pl.when(when)(copy.start)

    def keep(self, src, dst):
        copy = pltpu.make_async_copy(src, dst, self.own_sems.at[len(self.kept)])
        copy.start()
        self.kept.append(copy)

    def wait_sent(self):
        for when, wait in self.begun:
            if when is None:
                wait()
            else:
                pl.when(when)(wait)
        for copy in self.kept:
            copy.wait()


def arrived(dst, recv_sem, when=None):
    copy = pltpu.make_async_copy(dst, dst, recv_sem)
    if when is None:
        copy.wait()
    else:
        pl.when(when)(copy.wait)


class Gather:
    def __init__(self, spot, copies, src, dst, recv_sems, own_sem):
        self.spot, self.copies, self.src, self.dst, self.recv_sems, self.own_sem = spot, copies, src, dst, recv_sems, own_sem
        self.width = dst.shape[-1]
        self.group = copies.group(dst.at[pl.ds(0, 4 * NZ - 1)])

    def columns(self, z):
        return self.src.at[:, pl.ds(pl.multiple_of(z * self.width, self.width), self.width)]

    def push(self):
        spot, me = self.spot, self.spot.dp
        for offset in range(1, NZ):
            z = spot.z_at(offset)
            self.copies.send(self.columns(z), self.dst.at[me], self.recv_sems.at[me], spot.on_line(z), group=self.group)
        self.own = pltpu.make_async_copy(self.columns(spot.z), self.dst.at[me], self.own_sem)
        self.own.start()

    def pass_on(self, origin, device):
        sem = self.recv_sems.at[4 * NZ if device is self.spot.c_mate else origin]
        self.copies.send(self.dst.at[origin], self.dst.at[origin], sem, device, group=self.group)

    def first(self):
        spot = self.spot
        for offset in range(NZ):
            origin = place(spot.z_at(-offset), spot.x, spot.c)
            if offset == 0:
                self.own.wait()
            else:
                arrived(self.dst.at[origin], self.recv_sems.at[origin])
            self.pass_on(origin, spot.x_mate)
            self.pass_on(origin, spot.c_mate)

    def second(self):
        spot = self.spot
        for offset in range(NZ):
            origin = place(spot.z_at(-offset), 1 - spot.x, spot.c)
            arrived(self.dst.at[origin], self.recv_sems.at[origin])
            self.pass_on(origin, spot.c_mate)

    def last(self):
        arrived(self.dst.at[pl.ds(0, 2 * NZ)], self.recv_sems.at[4 * NZ])


class LineSum:
    def __init__(self, spot, copies, part, landing, total, sems):
        self.spot, self.copies, self.part, self.landing, self.total, self.sems = spot, copies, part, landing, total, sems
        self.offsets = [(dz, dy) for dz in range(NZ) for dy in range(2) if dz + dy > 0]
        self.all_others = landing.at[pl.ds(0, len(self.offsets))]
        self.groups = [copies.group(self.all_others) for _ in range(2)]

    def there(self, dz, dy):
        return self.spot.z_at(dz), lax.rem(self.spot.y + dy, 2)

    def push(self):
        for k, (dz, dy) in enumerate(self.offsets):
            z, y = self.there(dz, dy)
            self.copies.send(self.part.at[z, y], self.landing.at[k], self.sems.at[0], self.spot.on_line(z, y), group=self.groups[0])

    def middle(self):
        own_z, own_y = self.spot.z, self.spot.y
        arrived(self.all_others, self.sems.at[0])
        summed = self.part[own_z, own_y].astype(F32)
        for k in range(len(self.offsets)):
            summed = summed + self.landing[k].astype(F32)
        self.total[own_z, own_y] = summed.astype(BF16)
        own = self.total.at[own_z, own_y]
        for dz, dy in self.offsets:
            self.copies.send(own, own, self.sems.at[1], self.spot.on_line(*self.there(dz, dy)), group=self.groups[1])

    def last(self):
        arrived(self.all_others, self.sems.at[1])


def column_masks(tile):
    return jnp.concatenate([tile] * 16, axis=0).T


class Share:
    def __init__(self, spot, copies, dst, recv_sems):
        self.spot, self.copies, self.dst, self.recv_sems = spot, copies, dst, recv_sems
        self.over_y = copies.group(dst.at[pl.ds(0, NZ // 2)])

    def send(self, z, device, when=None):
        own = self.dst.at[z, self.spot.y]
        self.copies.send(own, own, self.recv_sems.at[z], device, when)

    def send_y(self, z, when=None):
        own = self.dst.at[z, self.spot.y]
        self.copies.send(own, own, self.recv_sems.at[NZ], self.spot.y_mate, when, self.over_y)

    def push(self):
        spot = self.spot
        self.send(spot.z, spot.on_line(spot.z_at(1)), spot.z < NZ - 1)
        self.send(spot.z, spot.on_line(spot.z_at(-1)), spot.z > 0)
        self.send_y(spot.z)

    def first(self, far):
        spot = self.spot
        for way in (1, -1):
            origin = spot.z_at(-way * far)
            comes = spot.z >= far if way == 1 else spot.z < NZ - far
            goes = comes & (spot.z < NZ - 1 if way == 1 else spot.z > 0)
            arrived(self.dst.at[origin, spot.y], self.recv_sems.at[origin], comes)
            if far < NZ - 1:
                self.send(origin, spot.on_line(spot.z_at(way)), goes)
            self.send_y(origin, comes)

    def last(self):
        arrived(self.dst.at[pl.ds(0, NZ // 2)], self.recv_sems.at[NZ])


class Scan:
    def __init__(self, maps, a_s, stepd_s, drive_s, gs_s, read_s, q_s, r_s, state_s, pulled_s, alog_s, spread_s, sum_s, gmap_s):
        self.maps, self.a_s, self.stepd_s, self.drive_s, self.gs_s = maps, a_s, stepd_s, drive_s, gs_s
        self.read_s, self.q_s, self.r_s, self.state_s = read_s, q_s, r_s, state_s
        self.pulled_s, self.alog_s, self.spread_s, self.sum_s, self.gmap_s = pulled_s, alog_s, spread_s, sum_s, gmap_s
        sub = lax.broadcasted_iota(jnp.int32, (8, 128), 0)
        self.masks = [(sub & shift) == 0 for shift in (1, 2, 4)]
        self.lane = lax.broadcasted_iota(jnp.int32, (N, 128), 1)
        self.blocks = [slice(b * 128, (b + 1) * 128) for b in range(a_s.shape[1] // 128)]

    def place(self, i):
        base = pl.multiple_of(i * 8, 8)
        tile = pl.ds(pl.multiple_of((base // 128) * 128, 128), 128)
        return base, tile, lax.rem(base, 128)

    def spread(self, tile, first):
        back = lax.rem(128 - first, 128)
        for k in range(2):
            moved = pltpu.roll(self.maps[k * N : (k + 1) * N, tile], back, 1)
            for j in range(8):
                self.spread_s[k, j] = jnp.broadcast_to(moved[:, j : j + 1], (N, 128))

    def forward(self, start, stop):
        def chunk(i, none):
            base, tile, first = self.place(i)
            self.spread(tile, first)
            for lanes in self.blocks:
                state = self.state_s[i, :, lanes]
                a = self.a_s[:, lanes]
                stepd, drive = self.stepd_s[pl.ds(base, 8), lanes], self.drive_s[pl.ds(base, 8), lanes]
                sums = RowSums(self.masks)
                for j in range(8):
                    state = jnp.exp(stepd[j : j + 1] * a) * state + drive[j : j + 1] * self.spread_s[0, j]
                    read = state * self.spread_s[1, j]
                    sums.add(j, read[:8] + read[8:])
                self.state_s[i + 1, :, lanes] = state
                self.read_s[pl.ds(base, 8), lanes] = sums.result
            return none

        lax.fori_loop(start, stop, chunk, 0)

    def backward(self, start, stop):
        def chunk(step, none):
            i = start + stop - 1 - step
            base, tile, first = self.place(i)
            self.spread(tile, first)
            for b, lanes in enumerate(self.blocks):
                a = self.a_s[:, lanes]
                stepd, drive = self.stepd_s[pl.ds(base, 8), lanes], self.drive_s[pl.ds(base, 8), lanes]
                gs = self.gs_s[pl.ds(base, 8), lanes]
                states, decays = [self.state_s[i, :, lanes]], []
                for j in range(8):
                    decays.append(jnp.exp(stepd[j : j + 1] * a))
                    states.append(decays[j] * states[j] + drive[j : j + 1] * self.spread_s[0, j])
                pulled, alog = self.pulled_s[:, lanes], self.alog_s[:, lanes]
                q_sums, r_sums = RowSums(self.masks), RowSums(self.masks)
                for j in reversed(range(8)):
                    adjoint = pulled + self.spread_s[1, j] * gs[j : j + 1]
                    g_in, g_out = adjoint * drive[j : j + 1], states[j + 1] * gs[j : j + 1]
                    if b > 0:
                        g_in, g_out = g_in + self.sum_s[0, j], g_out + self.sum_s[1, j]
                    self.sum_s[0, j], self.sum_s[1, j] = g_in, g_out
                    q_t = adjoint * self.spread_s[0, j]
                    q_sums.add(j, q_t[:8] + q_t[8:])
                    pulled = decays[j] * adjoint
                    past = pulled * states[j]
                    r_t = past * a
                    r_sums.add(j, r_t[:8] + r_t[8:])
                    alog = alog + past * stepd[j : j + 1]
                self.pulled_s[:, lanes], self.alog_s[:, lanes] = pulled, alog
                self.q_s[pl.ds(base, 8), lanes] = q_sums.result
                self.r_s[pl.ds(base, 8), lanes] = r_sums.result
            for k in range(2):
                row = self.gmap_s[k * N : (k + 1) * N, tile]
                for j in range(8):
                    row = jnp.where(self.lane == first + j, jnp.sum(self.sum_s[k, j], axis=1, keepdims=True), row)
                self.gmap_s[k * N : (k + 1) * N, tile] = row
            return none

        lax.fori_loop(start, stop, chunk, 0)


class TokenSum:
    def __init__(self, spot, copies, part, y_land, z_land, y_sems, z_sems):
        self.spot, self.copies, self.part, self.y_land, self.z_land = spot, copies, part, y_land, z_land
        self.y_sems, self.z_sems = y_sems, z_sems
        self.group = copies.group(y_land)

    def push(self):
        spot = self.spot
        for far in (3, 2, 1):
            for way in (1, -1):
                self.over_y(spot.z_at(way * far), self.within(way, far))
        self.over_y(spot.z, None)

    def within(self, way, far):
        return self.spot.z < NZ - far if way == 1 else self.spot.z >= far

    def over_y(self, z, when):
        self.copies.send(self.part.at[z, 1 - self.spot.y], self.y_land.at[z], self.y_sems.at[z], self.spot.y_mate, when, self.group)

    def add(self, z, landed):
        part, y = self.part, self.spot.y
        part[z, y] = (part[z, y].astype(F32) + landed[...].astype(F32)).astype(BF16)

    def stage(self, far):
        spot = self.spot
        for side, way in enumerate((1, -1)):
            z = spot.z_at(way * far)
            goes = self.within(way, far)
            grown = goes & self.within(-way, 1)
            land, sem = self.z_land.at[side, z], self.z_sems.at[side, z]

            @pl.when(goes)
            def _(z=z):
                arrived(self.y_land.at[z], self.y_sems.at[z])
                self.add(z, self.y_land.at[z])

            if far < NZ - 1:

                @pl.when(grown)
                def _(z=z, land=land, sem=sem):
                    arrived(land, sem)
                    self.add(z, land)

            self.copies.send(self.part.at[z, spot.y], land, sem, spot.on_line(spot.z_at(way)), goes)

    def last(self):
        spot = self.spot
        z = spot.z
        arrived(self.y_land.at[z], self.y_sems.at[z])
        self.add(z, self.y_land.at[z])
        for side, way in enumerate((1, -1)):

            @pl.when(self.within(-way, 1))
            def _(land=self.z_land.at[side, z], sem=self.z_sems.at[side, z]):
                arrived(land, sem)
                self.add(z, land)

        return self.part[z, spot.y].astype(F32)


class RowSum:
    def __init__(self, spot, copies, part, c_land, x_land, z_land, c_sems, x_sems, z_sem):
        self.spot, self.copies, self.part = spot, copies, part
        self.c_land, self.x_land, self.z_land = c_land, x_land, z_land
        self.c_sems, self.x_sems, self.z_sem = c_sems, x_sems, z_sem
        self.groups = [copies.group(whole) for whole in (c_land, x_land, z_land.at[pl.ds(0, NZ - 1)])]

    def push(self):
        spot = self.spot
        for offset in (1, 2, 3, 0):
            z = spot.z_at(offset)
            for x in range(2):
                self.copies.send(
                    self.part.at[z, x, 1 - spot.c], self.c_land.at[z, x], self.c_sems.at[z], spot.c_mate, group=self.groups[0]
                )

    def add(self, z, x, landed):
        part = self.part
        part[z, x, self.spot.c] = (part[z, x, self.spot.c].astype(F32) + landed.astype(F32)).astype(part.dtype)

    def second(self):
        spot = self.spot
        for offset in (1, 2, 3, 0):
            z = spot.z_at(offset)
            arrived(self.c_land.at[z], self.c_sems.at[z])
            for x in range(2):
                self.add(z, x, self.c_land[z, x])
            self.copies.send(
                self.part.at[z, 1 - spot.x, spot.c], self.x_land.at[z], self.x_sems.at[z], spot.x_mate, group=self.groups[1]
            )

    def third(self, offsets=(1, 2, 3, 0)):
        spot = self.spot
        for offset in offsets:
            z = spot.z_at(offset)
            arrived(self.x_land.at[z], self.x_sems.at[z])
            self.add(z, spot.x, self.x_land[z])
            own = self.part.at[z, spot.x, spot.c]
            if offset:
                self.copies.send(own, self.z_land.at[spot.z], self.z_sem, spot.on_line(z), group=self.groups[2])
            else:
                self.copies.keep(own, self.z_land.at[z])

    def last(self):
        arrived(self.z_land.at[pl.ds(0, NZ - 1)], self.z_sem)


class ChannelSum:
    def __init__(self, spot, copies, part, c_land, x_land, own, full, c_sem, x_sem, full_sems):
        self.spot, self.copies, self.part, self.own, self.full, self.full_sems = spot, copies, part, own, full, full_sems
        self.c_land, self.x_land, self.c_sem, self.x_sem = c_land, x_land, c_sem, x_sem
        self.group = copies.group(full.at[pl.ds(0, 4 * NZ - 1)])

    def push(self):
        self.copies.send(self.part.at[1 - self.spot.c], self.c_land, self.c_sem, self.spot.c_mate)

    def second(self):
        spot = self.spot
        arrived(self.c_land, self.c_sem)
        self.part[spot.c] = self.part[spot.c] + self.c_land[...]
        self.copies.send(self.part.at[spot.c, 1 - spot.x], self.x_land, self.x_sem, spot.x_mate)

    def spread(self, origin, device, src=None):
        src = self.full.at[origin] if src is None else src
        sem = self.full_sems.at[4 * NZ if device is self.spot.c_mate else origin]
        self.copies.send(src, self.full.at[origin], sem, device, group=self.group)

    def third(self):
        spot = self.spot
        arrived(self.x_land, self.x_sem)
        self.own[...] = (self.part[spot.c, spot.x] + self.x_land[...]).astype(BF16)
        for device in [spot.on_line(spot.z_at(offset)) for offset in (1, 2, 3)] + [spot.x_mate, spot.c_mate]:
            self.spread(spot.dp, device, self.own)
        self.copies.keep(self.own, self.full.at[spot.dp])

    def fourth(self):
        spot = self.spot
        for offset in (1, 2, 3):
            origin = place(spot.z_at(-offset), spot.x, spot.c)
            arrived(self.full.at[origin], self.full_sems.at[origin])
            self.spread(origin, spot.x_mate)
            self.spread(origin, spot.c_mate)

    def fifth(self):
        spot = self.spot
        for offset in range(NZ):
            origin = place(spot.z_at(-offset), 1 - spot.x, spot.c)
            arrived(self.full.at[origin], self.full_sems.at[origin])
            self.spread(origin, spot.c_mate)

    def last(self):
        arrived(self.full.at[pl.ds(0, 2 * NZ)], self.full_sems.at[4 * NZ])


class Held:
    def __init__(self, names, refs):
        for name, ref in zip(names, refs, strict=True):
            setattr(self, name, ref)


def block_scratch(half, feats, rows, chans, step_rows, width):
    tokens, n_dp, length = 2 * half * NZ, 4 * NZ, 2 * half
    vmem, dma = pltpu.VMEM, pltpu.SemaphoreType.DMA
    owners, steps = (NZ, 2, 2, rows, chans), (NZ, 2, 2, step_rows, chans)
    part = (NZ, 2, width // 2, length)
    small = (width + 32) // 4
    held = {
        "w": vmem((3, n_dp, rows, chans), BF16),
        "acts": vmem((2, NZ, 2, half, feats), BF16),
        "dtp_own": vmem((step_rows, chans * NZ), F32),
        "dtp": vmem((n_dp, step_rows, chans), F32),
        "info": vmem((n_dp, 8, 128), F32),
        "mask": vmem((NZ, length, 128), F32),
        "low": vmem((tokens, chans), BF16),
        "gated": vmem((tokens, chans), BF16),
        "ggate": vmem((tokens, chans), BF16),
    }
    for name in ("x_in", "pre", "gate", "gg", "raw", "stepd", "drive", "gs", "read", "r"):
        held[name] = vmem((tokens, chans), F32)
    held |= {
        "a": vmem((N, chans), F32),
        "state": vmem((tokens // 8 + 1, N, chans), F32),
        "pulled": vmem((N, chans), F32),
        "alog": vmem((N, chans), F32),
        "spread": vmem((2, 8, N, 128), F32),
        "sum": vmem((2, 8, N, 128), F32),
        "gmap": vmem((2 * N, tokens), F32),
        "dbl": vmem((width, tokens), F32),
        "part": vmem((2,) + part, BF16),
        "landing": vmem((2, 2 * NZ) + part[2:], BF16),
        "total": vmem((2,) + part, BF16),
        "mixed": vmem((NZ, 2, half, feats), BF16),
        "normed": vmem((NZ, 2, half, feats), BF16),
        "outw": vmem(owners, BF16),
        "ginz": vmem(owners, BF16),
        "ginx": vmem(owners, BF16),
        "gdtp": vmem(steps, F32),
        "chan": vmem((2, 2, small, chans), F32),
        "y_land": vmem((2, NZ, half, feats), BF16),
        "z_land": vmem((2, 2, NZ, half, feats), BF16),
        "wc_land": vmem((3, NZ, 2, rows, chans), BF16),
        "wx_land": vmem((3, NZ, rows, chans), BF16),
        "dc_land": vmem((NZ, 2, step_rows, chans), F32),
        "dx_land": vmem((NZ, step_rows, chans), F32),
        "fc_land": vmem((2, small, chans), F32),
        "fx_land": vmem((small, chans), F32),
        "f_own": vmem((small, chans), BF16),
        "block": vmem((half, feats), F32),
        "gresid": vmem((half, feats), F32),
        "tile": vmem((4, 8, 128), F32),
        "gain": vmem((3, n_dp, 8, 128), F32),
        "gain_land": vmem((n_dp - 1, 8, 128), F32),
        "send_sems": dma((56,)),
        "keep_sems": dma((7,)),
        "own_sems": dma((4,)),
        "w_sems": dma((4, n_dp + 1)),
        "act_sems": dma((2, NZ + 1)),
        "info_sem": dma(()),
        "dbl_sems": dma((2, 2)),
        "y_sems": dma((2, NZ)),
        "z_sems": dma((2, 2, NZ)),
        "wc_sems": dma((4, NZ)),
        "wx_sems": dma((4, NZ)),
        "wz_sems": dma((4,)),
        "f_sems": dma((2,)),
        "full_sems": dma((n_dp + 1,)),
        "tile_sems": dma((2,)),
        "gain_sems": dma((2,)),
    }
    return held


def block_kernel(names, *refs):
    (
        inx_ref, inz_ref, outp_ref, resid_ref, cot_ref, gain_ref, ids_ref, dtp_ref, xproj_ref, convw_ref, convb_ref, dtb_ref,
        alog_ref, skip_ref,
        block_ref, gresid_ref, ggain_ref, ginx_ref, ginz_ref, goutp_ref, gdtp_ref, full_ref, square_ref, msquare_ref,
    ) = refs[:24]
    s = Held(names, refs[24:])
    spot = Spot()
    plane = [lax.rem(spot.dp + offset, 4 * NZ) for offset in range(1, 4 * NZ)]
    greet([(dp, spot.y) for dp in plane] + [spot.on_line(spot.z_at(dz), 1 - spot.y) for dz in range(NZ)])
    copies = Copies(s.send_sems, s.keep_sems)
    tokens, chans = s.x_in.shape
    half, feats = resid_ref.shape
    length = 2 * half
    columns = pl.ds(pl.multiple_of(spot.z * chans, chans), chans)
    sequences = [slice(k * length, (k + 1) * length) for k in range(NZ)]

    s.dtp_own[...] = dtp_ref[...].astype(F32)
    inx, inz, outp, dtp = (
        Gather(spot, copies, src, dst, s.w_sems.at[k], s.own_sems.at[k])
        for k, (src, dst) in enumerate(((inx_ref, s.w.at[0]), (inz_ref, s.w.at[1]), (outp_ref, s.w.at[2]), (s.dtp_own, s.dtp)))
    )
    normed, cot = (Share(spot, copies, s.acts.at[k], s.act_sems.at[k]) for k in range(2))

    ids = jnp.broadcast_to(ids_ref[...], (8, length))
    lane = lax.broadcasted_iota(jnp.int32, (8, length), 1)
    sub = lax.broadcasted_iota(jnp.int32, (8, length), 0)
    info = jnp.broadcast_to(gain_ref[...].astype(F32), (8, length))
    for back in range(1, 4):
        same = jnp.where((pltpu.roll(ids, back, 1) == ids) & (lane >= back), 1.0, 0.0)
        info = jnp.where(sub == back, same, info)
    s.info[spot.dp] = info
    other_info = s.info.at[pl.ds(0, 4 * NZ - 1)]
    info_group = copies.group(other_info)
    for dp in plane:
        copies.send(s.info.at[spot.dp], s.info.at[spot.dp], s.info_sem, (dp, spot.y), group=info_group)
    inx.push()

    resid = resid_ref[...]
    row_square = jnp.sum(resid * resid, axis=1, keepdims=True)
    scaled = resid * lax.rsqrt(row_square / feats + eps_norm)
    s.tile[0] = jnp.broadcast_to(jnp.sum(row_square, axis=0, keepdims=True), (8, 128))
    copies.send(s.tile.at[0], s.tile.at[1], s.tile_sems.at[0], spot.y_mate)
    arrived(other_info, s.info_sem)
    for k in range(4 * NZ):
        cols = slice(k * 128, (k + 1) * 128)
        s.acts[0, spot.z, spot.y, :, cols] = (scaled[:, cols] * s.info[k, 0:1, :]).astype(BF16)
    normed.push()
    dtp.push()
    s.acts[1, spot.z, spot.y] = cot_ref[...].astype(BF16)
    for k in range(NZ):
        s.mask[k] = column_masks(s.info[place(k, spot.x, spot.c)])
    inx.first()
    normed.first(1)
    inx.second()
    inz.push()
    normed.first(2)
    dtp.first()
    dtp.second()
    cot.push()
    normed.first(3)
    normed.last()
    inx.last()

    tokens_x = s.acts.at[0], s.acts.at[1]
    all_normed = s.acts[0].reshape(tokens, feats)
    s.x_in[...] = dot(all_normed, s.w[0].reshape(-1, chans))
    taps = convw_ref[:, columns]
    bias = convb_ref[:, columns]
    for k, rows in enumerate(sequences):
        one = s.x_in[rows]
        pre = bias + taps[3:4] * one
        for back in range(1, 4):
            pre = pre + taps[3 - back : 4 - back] * (pltpu.roll(one, back, 0) * s.mask[k, :, back : back + 1])
        s.pre[rows] = pre
        s.low[rows] = (pre * sigmoid(pre)).astype(BF16)
    x_proj = xproj_ref[:, columns]
    dbl = dot(x_proj, s.low[...], NT)
    blocks = [(k, y) for k in range(NZ) for y in range(2)]
    width = dbl.shape[0] // 2
    for k, y in blocks:
        s.part[0, k, y] = dbl[y * width : (y + 1) * width, sequences[k]].astype(BF16)
    x_dbl = LineSum(
        spot, copies, s.part.at[0], s.landing.at[0], s.total.at[0], s.dbl_sems.at[0]
    )
    x_dbl.push()
    outp.push()
    cot.first(1)
    x_dbl.middle()
    inz.first()
    cot.first(2)
    x_dbl.last()

    dtp.last()
    for k, y in blocks:
        s.dbl[y * width : (y + 1) * width, sequences[k]] = s.total[0, k, y].astype(F32)
    step_w = s.dtp[...].reshape(R, chans).astype(BF16)
    s.raw[...] = dot(s.dbl[:R].astype(BF16), step_w, TN) + dtb_ref[:, columns]
    for k, rows in enumerate(sequences):
        step = softplus(s.raw[rows])
        s.stepd[rows] = jnp.where(s.mask[k, :, 1:2] > 0.0, step, 1e30)
        s.drive[rows] = step * s.low[rows].astype(F32)
    s.a[...] = -jnp.exp(alog_ref[:, columns])
    s.state[0] = jnp.zeros((N, chans), F32)
    scan = Scan(
        s.dbl.at[R : R + 2 * N], s.a, s.stepd, s.drive, s.gs, s.read, s.read, s.r, s.state, s.pulled, s.alog, s.spread, s.sum, s.gmap
    )
    steps = tokens // 8
    scan.forward(0, steps // 4)
    inz.second()
    scan.forward(steps // 4, steps // 2)
    cot.first(3)
    scan.forward(steps // 2, 3 * steps // 4)
    outp.first()
    scan.forward(3 * steps // 4, steps)
    outp.second()
    inz.last()
    s.gate[...] = dot(s.acts[0].reshape(tokens, feats), s.w[1].reshape(-1, chans))
    cot.last()
    outp.last()
    s.gg[...] = dot(s.acts[1].reshape(tokens, feats), s.w[2].reshape(-1, chans))
    skip = skip_ref[:, columns]
    for rows in sequences:
        gate, gg = s.gate[rows], s.gg[rows]
        sig = sigmoid(gate)
        scanned = s.read[rows] + skip * s.low[rows].astype(F32)
        s.gs[rows] = gg * gate * sig
        s.gated[rows] = (scanned * gate * sig).astype(BF16)
        s.ggate[rows] = (gg * scanned * sig * (1.0 + gate * (1.0 - sig))).astype(BF16)

    mixed_sum, normed_sum = (
        TokenSum(spot, copies, part, s.y_land.at[k], s.z_land.at[k], s.y_sems.at[k], s.z_sems.at[k])
        for k, part in enumerate((s.mixed, s.normed))
    )
    outw_sum, ginz_sum, ginx_sum, gdtp_sum = (
        RowSum(spot, copies, part, c_land, x_land, out, s.wc_sems.at[k], s.wx_sems.at[k], s.wz_sems.at[k])
        for k, (part, c_land, x_land, out) in enumerate((
            (s.outw, s.wc_land.at[0], s.wx_land.at[0], goutp_ref),
            (s.ginz, s.wc_land.at[1], s.wx_land.at[1], ginz_ref),
            (s.ginx, s.wc_land.at[2], s.wx_land.at[2], ginx_ref),
            (s.gdtp, s.dc_land, s.dx_land, gdtp_ref),
        ))
    )
    s.mixed[...] = dot(s.gated[...], s.w[2].reshape(-1, chans), NT).astype(BF16).reshape(s.mixed.shape)
    mixed_sum.push()
    s.outw[...] = dot(s.acts[1].reshape(tokens, feats), s.gated[...], TN).astype(BF16).reshape(s.outw.shape)
    outw_sum.push()
    s.ginz[...] = dot(s.acts[0].reshape(tokens, feats), s.ggate[...], TN).astype(BF16).reshape(s.ginz.shape)
    ginz_sum.push()

    s.pulled[...] = jnp.zeros_like(s.pulled)
    s.alog[...] = jnp.zeros_like(s.alog)
    outw_sum.second()
    scan.backward(steps - steps // 4, steps)
    ginz_sum.second()
    mixed_sum.stage(3)
    scan.backward(steps // 2, steps - steps // 4)
    outw_sum.third()
    mixed_sum.stage(2)
    scan.backward(steps // 4, steps // 2)
    scan.backward(0, steps // 4)

    grad_bias = jnp.zeros((1, chans), F32)
    grad_skip = jnp.zeros((1, chans), F32)
    raw_rows = []
    for rows in sequences:
        conv, raw, gs, q = s.low[rows].astype(F32), s.raw[rows], s.gs[rows], s.read[rows]
        grad_raw = (conv * q + s.r[rows]) * sigmoid(raw)
        s.gg[rows] = softplus(raw) * q + skip * gs
        grad_bias = grad_bias + jnp.sum(grad_raw, axis=0, keepdims=True)
        grad_skip = grad_skip + jnp.sum(gs * conv, axis=0, keepdims=True)
        raw_rows.append(grad_raw.astype(BF16))
    raw_low = jnp.concatenate(raw_rows, axis=0)
    dbl = jnp.concatenate([dot(step_w, raw_low, NT), s.gmap[...]], axis=0)
    for k, y in blocks:
        s.part[1, k, y] = dbl[y * width : (y + 1) * width, sequences[k]].astype(BF16)
    grad_dbl_sum = LineSum(
        spot, copies, s.part.at[1], s.landing.at[1], s.total.at[1], s.dbl_sems.at[1]
    )
    grad_dbl_sum.push()
    s.gdtp[...] = dot(s.dbl[:R].astype(BF16), raw_low).reshape(s.gdtp.shape)
    gdtp_sum.push()
    grad_dbl_sum.middle()
    mixed_sum.stage(1)
    ginz_sum.third()
    gdtp_sum.second()
    grad_dbl_sum.last()

    grad_dbl = jnp.concatenate(
        [jnp.concatenate([s.total[1, k, y] for k in range(NZ)], axis=1) for y in range(2)], axis=0
    )
    s.gg[...] += dot(grad_dbl, x_proj, TN)
    sums = [jnp.zeros((1, chans), F32) for _ in range(5)]
    low_rows = []
    for k, rows in enumerate(sequences):
        pre, x_one = s.pre[rows], s.x_in[rows]
        sig = sigmoid(pre)
        one = s.gg[rows] * sig * (1.0 + pre * (1.0 - sig))
        sums[3] = sums[3] + jnp.sum(one * x_one, axis=0, keepdims=True)
        sums[4] = sums[4] + jnp.sum(one, axis=0, keepdims=True)
        grad_x = taps[3:4] * one
        for back in range(1, 4):
            masked = one * s.mask[k, :, back : back + 1]
            sums[3 - back] = sums[3 - back] + jnp.sum(masked * pltpu.roll(x_one, back, 0), axis=0, keepdims=True)
            grad_x = grad_x + taps[3 - back : 4 - back] * pltpu.roll(masked, length - back, 0)
        low_rows.append(grad_x.astype(BF16))
    grad_xin = jnp.concatenate(low_rows, axis=0)
    grad_normed = dot(grad_xin, s.w[0].reshape(-1, chans), NT) + dot(s.ggate[...], s.w[1].reshape(-1, chans), NT)
    s.normed[...] = grad_normed.astype(BF16).reshape(s.normed.shape)
    normed_sum.push()
    s.chan[...] = jnp.concatenate(
        [dot(grad_dbl, s.low[...]), s.alog[...] * s.a[...], grad_bias, grad_skip, jnp.zeros((6, chans), F32)]
        + sums + [jnp.zeros((3, chans), F32)], axis=0
    ).reshape(s.chan.shape)
    small_sum = ChannelSum(
        spot, copies, s.chan, s.fc_land, s.fx_land, s.f_own, full_ref, s.f_sems.at[0], s.f_sems.at[1], s.full_sems
    )
    small_sum.push()
    s.ginx[...] = dot(s.acts[0].reshape(tokens, feats), grad_xin, TN).astype(BF16).reshape(s.ginx.shape)
    ginx_sum.push()
    small_sum.second()
    gain_part = jnp.sum(grad_normed * s.acts[0].reshape(tokens, feats).astype(F32), axis=0, keepdims=True)
    for k in range(4 * NZ):
        s.gain[0, k] = jnp.broadcast_to(gain_part[:, k * 128 : (k + 1) * 128], (8, 128)) / s.info[k, 0:1]
    copies.send(s.gain.at[0], s.gain.at[1], s.gain_sems.at[0], spot.y_mate)
    ginx_sum.second()
    gdtp_sum.third()
    normed_sum.stage(3)
    small_sum.third()
    normed_sum.stage(2)
    ginx_sum.third((1, 2))
    arrived(s.gain.at[1], s.gain_sems.at[0])
    s.gain[2] = s.gain[0] + s.gain[1]
    gain_group = copies.group(s.gain_land)
    for offset, dp in enumerate(plane):
        copies.send(s.gain.at[2, dp], s.gain_land.at[offset], s.gain_sems.at[1], (dp, spot.y), group=gain_group)
    normed_sum.stage(1)
    ginx_sum.third((3, 0))
    small_sum.fourth()

    mixed = mixed_sum.last()
    resid = resid_ref[...]
    s.block[...] = resid + mixed
    copies.keep(s.block, block_ref)
    s.tile[2] = jnp.broadcast_to(jnp.sum(jnp.sum(mixed * mixed, axis=1, keepdims=True), axis=0, keepdims=True), (8, 128))
    copies.send(s.tile.at[2], s.tile.at[3], s.tile_sems.at[1], spot.y_mate)
    arrived(s.gain_land, s.gain_sems.at[1])
    total = s.gain[2, spot.dp]
    for offset in range(4 * NZ - 1):
        total = total + s.gain_land[offset]
    ggain_ref[...] = total
    small_sum.fifth()
    outw_sum.last()
    ginz_sum.last()
    gdtp_sum.last()
    arrived(s.tile.at[1], s.tile_sems.at[0])
    square_ref[...] = s.tile[0] + s.tile[1]
    arrived(s.tile.at[3], s.tile_sems.at[1])
    msquare_ref[...] = s.tile[2] + s.tile[3]

    grad_rows = normed_sum.last()
    inv = lax.rsqrt(jnp.sum(resid * resid, axis=1, keepdims=True) / feats + eps_norm)
    scaled = resid * inv
    gain = jnp.concatenate([s.info[k, 0:1] for k in range(4 * NZ)], axis=1)
    grad_scaled = grad_rows * gain
    mean = jnp.sum(grad_scaled * scaled, axis=1, keepdims=True) / feats
    s.gresid[...] = cot_ref[...] + inv * (grad_scaled - scaled * mean)
    copies.keep(s.gresid, gresid_ref)
    ginx_sum.last()
    small_sum.last()
    copies.wait_sent()
    assert copies.used == s.send_sems.shape[0], copies.used


def block_call(in_x, in_z, out_p, residual, cotangent, gain, ids, dt_p, x_proj, conv_w, conv_b, dt_b, a_log, d_skip):
    half, feats = residual.shape
    rows, wide = in_x.shape
    n_dp, chans = 4 * NZ, wide // NZ
    held = block_scratch(half, feats, rows, chans, dt_p.shape[0], x_proj.shape[0])
    shape = jax.ShapeDtypeStruct
    outs = [
        shape((half, feats), F32), shape((half, feats), F32), shape((8, 128), F32),
        shape((NZ, rows, chans), BF16), shape((NZ, rows, chans), BF16), shape((NZ, rows, chans), BF16),
        shape((NZ, dt_p.shape[0], chans), F32), shape((n_dp, (x_proj.shape[0] + 32) // 4, chans), BF16),
        shape((8, 128), F32), shape((8, 128), F32),
    ]
    in_any = pl.BlockSpec(memory_space=pl.ANY)
    in_vmem = pl.BlockSpec(memory_space=pltpu.VMEM)
    return pl.pallas_call(
        functools.partial(block_kernel, list(held)),
        out_shape=outs,
        in_specs=[in_any] * 3 + [in_vmem] * 11,
        out_specs=[in_any] * 2 + [in_vmem] + [in_any] * 5 + [in_vmem] * 2,
        scratch_shapes=list(held.values()),
        name="block",
        compiler_params=pltpu.CompilerParams(collective_id=1, has_side_effects=True, vmem_limit_bytes=62 << 20),
    )(in_x, in_z, out_p, residual, cotangent, gain, ids, dt_p, x_proj, conv_w, conv_b, dt_b, a_log, d_skip)


def finish_kernel(
    scale, block_in, gresid_in, ginx_in, ginz_in, goutp_in, gdtp_in, full_in, ggain_in, square_in, msquare_in,
    block_ref, gresid_ref, ginx_ref, ginz_ref, goutp_ref, gdtp_ref, xproj_ref, alog_ref, dtb_ref, skip_ref, convw_ref, convb_ref,
    ggain_ref, rms_ref, mrms_ref,
):
    block_ref[...] = block_in[...]
    gresid_ref[...] = gresid_in[...]
    ggain_ref[...] = ggain_in[0:1]
    rms_ref[...] = jnp.sqrt(square_in[0:1, 0:1] * scale)
    mrms_ref[...] = jnp.sqrt(msquare_in[0:1, 0:1] * scale)
    chans = ginx_in.shape[2]
    for z in range(NZ):
        cols = slice(z * chans, (z + 1) * chans)
        for given, ref in ((ginx_in, ginx_ref), (ginz_in, ginz_ref), (goutp_in, goutp_ref), (gdtp_in, gdtp_ref)):
            ref[:, cols] = given[z].astype(F32)
        rows = full_in.shape[1]
        for k in range(4):
            found = full_in[place(z, k % 2, k // 2)].astype(F32)
            upto = min(rows, xproj_ref.shape[0] - k * rows)
            xproj_ref[k * rows : k * rows + upto, cols] = found[:upto]
        alog_ref[:, cols] = found[upto : upto + N]
        dtb_ref[:, cols] = found[upto + N : upto + N + 1]
        skip_ref[:, cols] = found[upto + N + 1 : upto + N + 2]
        convw_ref[:, cols] = found[upto + 24 : upto + 28]
        convb_ref[:, cols] = found[upto + 28 : upto + 29]


def finish_call(block, gresid, ginx, ginz, goutp, gdtp, full, ggain, square, msquare, width):
    rows, wide = ginx.shape[1], ginx.shape[2] * NZ
    shape = lambda count, columns=wide: jax.ShapeDtypeStruct((count, columns), F32)
    outs = [
        shape(*block.shape), shape(*gresid.shape), shape(rows), shape(rows), shape(rows),
        shape(gdtp.shape[1]), shape(width), shape(N), shape(1), shape(1), shape(4), shape(1), shape(1, 128), shape(1, 1), shape(1, 1),
    ]
    spec = pl.BlockSpec(memory_space=pltpu.VMEM)
    return pl.pallas_call(
        functools.partial(finish_kernel, 1.0 / (2 * block.shape[0] * block.shape[1])),
        out_shape=outs, in_specs=[spec] * 10, out_specs=[spec] * len(outs), name="finish",
        compiler_params=pltpu.CompilerParams(vmem_limit_bytes=60 << 20),
    )(block, gresid, ginx, ginz, goutp, gdtp, full, ggain, square, msquare)


def per_device_split(
    residual,
    norm_gain,
    in_proj_x,
    in_proj_z,
    x_proj,
    dt_proj,
    dt_bias,
    conv_weight,
    conv_bias,
    a_log,
    d_skip,
    out_proj,
    doc_ids,
    cotangent,
):
    parts = block_call(
        in_proj_x, in_proj_z, out_proj, residual, cotangent, norm_gain[None], doc_ids[None], dt_proj, x_proj, conv_weight,
        conv_bias[None], dt_bias[None], a_log, d_skip[None],
    )
    block, gresid, ggain, ginx, ginz, goutp, gdtp, full, square, msquare = parts
    block, gresid, ginx, ginz, goutp, gdtp, g_xproj, g_alog, g_dtb, g_skip, g_convw, g_convb, ggain, rms, mrms = finish_call(
        block, gresid, ginx, ginz, goutp, gdtp, full, ggain, square, msquare, x_proj.shape[0]
    )
    return (
        block,
        gresid,
        ggain[0],
        ginx,
        ginz,
        g_xproj,
        gdtp,
        g_dtb[0],
        g_convw,
        g_convb[0],
        g_alog,
        g_skip[0],
        goutp,
        rms[0],
        mrms[0],
    )


def norm_rows(values, gain_val):
    mean_square = jnp.mean(values * values, axis=1, keepdims=True)
    return values * lax.rsqrt(mean_square + eps_norm) * gain_val


def conv_local(x_in, doc_ids, conv_weight, conv_bias):
    kernel_len = conv_weight.shape[0]
    length = x_in.shape[0]
    padded = jnp.pad(x_in, ((kernel_len - 1, 0), (0, 0)))
    id_pad = jnp.concatenate([jnp.full((kernel_len - 1,), -1, jnp.int32), doc_ids])
    summed = conv_bias + jnp.zeros_like(x_in)
    for offset in range(kernel_len):
        same_doc = (id_pad[offset : offset + length] == doc_ids).astype(jnp.float32)
        summed = summed + conv_weight[offset] * padded[offset : offset + length] * same_doc[:, None]
    return summed


def per_device(
    residual,
    norm_gain,
    in_proj_x,
    in_proj_z,
    x_proj,
    dt_proj,
    dt_bias,
    conv_weight,
    conv_bias,
    a_log,
    d_skip,
    out_proj,
    doc_ids,
    cotangent,
):
    gathered = (
        lax.all_gather(norm_gain, "dp", axis=0, tiled=True),
        lax.all_gather(in_proj_x, "dp", axis=0, tiled=True),
        lax.all_gather(in_proj_z, "dp", axis=0, tiled=True),
        lax.all_gather(dt_proj, "dp", axis=0, tiled=True),
        lax.all_gather(out_proj, "dp", axis=0, tiled=True),
    )
    gain_all, inx_all, inz_all, step_all, out_all = gathered
    seq_len = doc_ids.shape[0]
    normed_f32, norm_back = jax.vjp(norm_rows, residual, gain_all.astype(jnp.float32))
    normed = lax.all_gather(normed_f32.astype(jnp.bfloat16), "tensor", axis=0, tiled=True)
    x_in = jnp.dot(normed, inx_all, preferred_element_type=jnp.float32)
    gate_in = jnp.dot(normed, inz_all, preferred_element_type=jnp.float32)

    def conv_act(x_val, weight_val, bias_val):
        return jax.nn.silu(conv_local(x_val, doc_ids, weight_val, bias_val))

    conv_out, conv_back = jax.vjp(conv_act, x_in, conv_weight, conv_bias)
    conv_low = conv_out.astype(jnp.bfloat16)
    dbl_part = lax.dot_general(
        conv_low, x_proj, (((1,), (1,)), ((), ())), preferred_element_type=jnp.float32
    )
    x_dbl, resid_square = lax.psum((dbl_part, jnp.sum(residual * residual)), "tensor")
    doc_starts = doc_ids != jnp.concatenate([jnp.full((1,), -1, jnp.int32), doc_ids[:-1]])
    carry_keep = 1.0 - doc_starts.astype(jnp.float32)

    cot_all = lax.all_gather(cotangent.astype(jnp.bfloat16), "tensor", axis=0, tiled=True)
    grad_gated = jnp.dot(cot_all, out_all, preferred_element_type=jnp.float32)
    gated_low, grad_gate_low, grad_conv, grad_dbl_part, grad_step_w, grad_bias, grad_alog, grad_skip = scan_call(
        x_dbl, conv_low, gate_in, grad_gated, step_all, dt_bias, a_log, d_skip, carry_keep
    )
    mixed = lax.psum_scatter(
        lax.dot_general(
            gated_low, out_all, (((1,), (1,)), ((), ())), preferred_element_type=jnp.float32
        ),
        "tensor",
        scatter_dimension=0,
        tiled=True,
    )
    block_out = residual + mixed
    mixed_square = lax.psum(jnp.sum(mixed * mixed), "tensor")
    rms_resid = jnp.sqrt(resid_square / (seq_len * D)).reshape(1)
    rms_mixed = jnp.sqrt(mixed_square / (seq_len * D)).reshape(1)
    grad_out_w = lax.dot_general(
        cot_all, gated_low, (((0,), (0,)), ((), ())), preferred_element_type=jnp.float32
    )
    grad_dbl = lax.psum(grad_dbl_part.T, "tensor")
    grad_dbl_low = grad_dbl.astype(jnp.bfloat16)
    grad_conv = grad_conv + jnp.dot(grad_dbl_low, x_proj, preferred_element_type=jnp.float32)
    grad_xproj = lax.dot_general(
        grad_dbl_low, conv_low, (((0,), (0,)), ((), ())), preferred_element_type=jnp.float32
    )
    grad_xin, grad_convw, grad_convb = conv_back(grad_conv)
    grad_xin_low = grad_xin.astype(jnp.bfloat16)
    grad_inx = lax.dot_general(
        normed, grad_xin_low, (((0,), (0,)), ((), ())), preferred_element_type=jnp.float32
    )
    grad_inz = lax.dot_general(
        normed, grad_gate_low, (((0,), (0,)), ((), ())), preferred_element_type=jnp.float32
    )
    first_term = lax.dot_general(
        grad_xin_low, inx_all, (((1,), (1,)), ((), ())), preferred_element_type=jnp.float32
    )
    second_term = lax.dot_general(
        grad_gate_low, inz_all, (((1,), (1,)), ((), ())), preferred_element_type=jnp.float32
    )
    grad_normed = lax.psum_scatter(
        first_term + second_term, "tensor", scatter_dimension=0, tiled=True
    )
    grad_rows_x, grad_gain_part = norm_back(grad_normed)
    grad_residual = cotangent + grad_rows_x
    grad_gain = lax.psum(grad_gain_part, "tensor")
    gain_shard, inx_shard, inz_shard, step_shard, out_shard = (
        lax.psum_scatter(grad_gain, "dp", scatter_dimension=0, tiled=True),
        lax.psum_scatter(grad_inx, "dp", scatter_dimension=0, tiled=True),
        lax.psum_scatter(grad_inz, "dp", scatter_dimension=0, tiled=True),
        lax.psum_scatter(grad_step_w, "dp", scatter_dimension=0, tiled=True),
        lax.psum_scatter(grad_out_w, "dp", scatter_dimension=0, tiled=True),
    )
    small_sums = lax.psum(
        (grad_xproj, grad_bias, grad_convw, grad_convb, grad_alog, grad_skip), "dp"
    )
    xproj_sum, bias_sum, convw_sum, convb_sum, alog_sum, skip_sum = small_sums
    return (
        block_out,
        grad_residual,
        gain_shard,
        inx_shard,
        inz_shard,
        xproj_sum,
        step_shard,
        bias_sum,
        convw_sum,
        convb_sum,
        alog_sum,
        skip_sum,
        out_shard,
        rms_resid,
        rms_mixed,
    )


def solution(mesh):
    placed = (
        P(("dp", "tensor"), None),
        P("dp"),
        P("dp", "tensor"),
        P("dp", "tensor"),
        P(None, "tensor"),
        P("dp", "tensor"),
        P("tensor"),
        P(None, "tensor"),
        P("tensor"),
        P(None, "tensor"),
        P("tensor"),
        P("dp", "tensor"),
        P("dp"),
        P(("dp", "tensor"), None),
    )
    return jax.shard_map(
        per_device_split if mesh.shape["dp"] == 4 * NZ else per_device,
        mesh=mesh,
        in_specs=placed,
        out_specs=(
            P(("dp", "tensor"), None),
            P(("dp", "tensor"), None),
            P("dp"),
            P("dp", "tensor"),
            P("dp", "tensor"),
            P(None, "tensor"),
            P("dp", "tensor"),
            P("tensor"),
            P(None, "tensor"),
            P("tensor"),
            P(None, "tensor"),
            P("tensor"),
            P("dp", "tensor"),
            P("dp"),
            P("dp"),
        ),
        check_vma=False,
    )
```

```python
import functools

import jax
import jax.numpy as jnp
from jax import lax
from jax.experimental import pallas as pl
from jax.experimental.pallas import tpu as pltpu
from jax.sharding import PartitionSpec as P

D = 2048
R = 128
N = 16

eps_norm = 1e-05


def sigmoid(v):
    return 1.0 / (1.0 + jnp.exp(-v))


def softplus(v):
    return jnp.maximum(v, 0.0) + jnp.log(1.0 + jnp.exp(-jnp.abs(v)))


def fold_rows(first, second, shift, lower):
    kept = jnp.where(lower, first, second)
    moved = jnp.where(lower, second, first)
    return kept + pltpu.roll(moved, shift, 0)


class RowSums:
    def __init__(self, masks):
        self.masks = masks
        self.held = {}
        self.result = None

    def add(self, token, value):
        level = 0
        while True:
            if level == 3:
                self.result = value
                return
            mate = (level, token ^ 1)
            if mate not in self.held:
                self.held[(level, token)] = value
                return
            other = self.held.pop(mate)
            first, second = (other, value) if token & 1 else (value, other)
            value = fold_rows(first, second, 1 << level, self.masks[level])
            token >>= 1
            level += 1


def split_dot(left, right_low, dims):
    high = left.astype(jnp.bfloat16)
    rest = (left - high.astype(jnp.float32)).astype(jnp.bfloat16)
    return lax.dot_general(high, right_low, dims, preferred_element_type=jnp.float32) + lax.dot_general(
        rest, right_low, dims, preferred_element_type=jnp.float32
    )


def scan_kernel(
    dbl_ref, conv_ref, gate_ref, gg_ref, dtp_ref, dtb_ref, alog_ref, skip_ref, keep_ref, in_ref, out_ref,
    gated_ref, ggate_ref, gconv_ref, gdbl_ref, gin_ref, gout_ref, gdtp_ref, gdtb_ref, galog_ref, gskip_ref,
    h_s, d_s, stepd_s, sc_s, gs_s, y_s, q_s, r_s, a_s,
):
    length, width = conv_ref.shape
    blocks = width // 128
    part = pl.program_id(0)
    sub = lax.broadcasted_iota(jnp.int32, (8, 128), 0)
    masks = [(sub & shift) == 0 for shift in (1, 2, 4)]
    lanes = [slice(b * 128, (b + 1) * 128) for b in range(blocks)]

    nn = (((1,), (0,)), ((), ()))
    step_raw = split_dot(dbl_ref[...], dtp_ref[...], nn) + dtb_ref[...]
    step = jnp.maximum(step_raw, 0.0) + jnp.log(1.0 + jnp.exp(-jnp.abs(step_raw)))
    stepd_s[...] = jnp.where(keep_ref[...] > 0.0, step, 1e30)
    sc_s[...] = step * conv_ref[...].astype(jnp.float32)
    gate = gate_ref[...]
    gs_s[...] = gg_ref[...] * gate * sigmoid(gate)
    a_s[...] = -jnp.exp(alog_ref[...])

    h_s[0] = jnp.zeros((N, width), jnp.float32)

    def forward(i, hs):
        base = pl.multiple_of(i * 8, 8)
        hs = list(hs)
        sums = [RowSums(masks) for _ in range(blocks)]
        stepd = [stepd_s[pl.ds(base, 8), lanes[b]] for b in range(blocks)]
        drive = [sc_s[pl.ds(base, 8), lanes[b]] for b in range(blocks)]
        for j in range(8):
            t = base + j
            in_t = in_ref[t]
            out_t = out_ref[t]
            for b in range(blocks):
                decay = jnp.exp(stepd[b][j : j + 1] * a_s[:, lanes[b]])
                hs[b] = decay * hs[b] + drive[b][j : j + 1] * in_t
                d_s[t, :, lanes[b]] = decay
                h_s[t + 1, :, lanes[b]] = hs[b]
                read = hs[b] * out_t
                sums[b].add(j, read[:8] + read[8:])
        for b in range(blocks):
            y_s[pl.ds(base, 8), lanes[b]] = sums[b].result
        return tuple(hs)

    zero = jnp.zeros((N, 128), jnp.float32)
    lax.fori_loop(0, length // 8, forward, (zero,) * blocks)

    conv = conv_ref[...].astype(jnp.float32)
    gate = gate_ref[...]
    sig = sigmoid(gate)
    scanned = y_s[...] + skip_ref[...] * conv
    gated_ref[...] = (scanned * gate * sig).astype(jnp.bfloat16)
    ggate_ref[...] = (gg_ref[...] * scanned * sig * (1.0 + gate * (1.0 - sig))).astype(jnp.bfloat16)

    @pl.when(part == 0)
    def _():
        gin_ref[...] = jnp.zeros_like(gin_ref)
        gout_ref[...] = jnp.zeros_like(gout_ref)
        gdbl_ref[...] = jnp.zeros_like(gdbl_ref)

    def backward(i, carried):
        base = pl.multiple_of(length - 8 - i * 8, 8)
        pulled, alog_sum = list(carried[0]), list(carried[1])
        q_sums = [RowSums(masks) for _ in range(blocks)]
        r_sums = [RowSums(masks) for _ in range(blocks)]
        stepd = [stepd_s[pl.ds(base, 8), lanes[b]] for b in range(blocks)]
        drive = [sc_s[pl.ds(base, 8), lanes[b]] for b in range(blocks)]
        gs = [gs_s[pl.ds(base, 8), lanes[b]] for b in range(blocks)]
        for j in reversed(range(8)):
            t = base + j
            in_t = in_ref[t]
            out_t = out_ref[t]
            gin_t = gin_ref[t]
            gout_t = gout_ref[t]
            for b in range(blocks):
                gs_t = gs[b][j : j + 1]
                adjoint = pulled[b] + out_t * gs_t
                gout_t = gout_t + gs_t * h_s[t + 1, :, lanes[b]]
                gin_t = gin_t + adjoint * drive[b][j : j + 1]
                q_t = adjoint * in_t
                q_sums[b].add(j, q_t[:8] + q_t[8:])
                pulled[b] = d_s[t, :, lanes[b]] * adjoint
                past = pulled[b] * h_s[t, :, lanes[b]]
                r_t = past * a_s[:, lanes[b]]
                r_sums[b].add(j, r_t[:8] + r_t[8:])
                alog_sum[b] = alog_sum[b] + past * stepd[b][j : j + 1]
            gin_ref[t] = gin_t
            gout_ref[t] = gout_t
        for b in range(blocks):
            q_s[pl.ds(base, 8), lanes[b]] = q_sums[b].result
            r_s[pl.ds(base, 8), lanes[b]] = r_sums[b].result
        return tuple(pulled), tuple(alog_sum)

    _, alog_sum = lax.fori_loop(0, length // 8, backward, ((zero,) * blocks, (zero,) * blocks))
    for b in range(blocks):
        galog_ref[:, lanes[b]] = alog_sum[b] * a_s[:, lanes[b]]

    conv = conv_ref[...].astype(jnp.float32)
    step_raw = split_dot(dbl_ref[...], dtp_ref[...], nn) + dtb_ref[...]
    step = jnp.maximum(step_raw, 0.0) + jnp.log(1.0 + jnp.exp(-jnp.abs(step_raw)))
    raw = (conv * q_s[...] + r_s[...]) * sigmoid(step_raw)
    gs = gs_s[...]
    gconv_ref[...] = step * q_s[...] + skip_ref[...] * gs
    gskip_ref[...] = jnp.sum(gs * conv, axis=0, keepdims=True)
    gdtb_ref[...] = jnp.sum(raw, axis=0, keepdims=True)
    raw_low = raw.astype(jnp.bfloat16)
    gdtp_ref[...] = lax.dot_general(
        dbl_ref[...].astype(jnp.bfloat16), raw_low, (((0,), (0,)), ((), ())), preferred_element_type=jnp.float32
    )
    gdbl_ref[...] += lax.dot_general(
        dtp_ref[...], raw_low, (((1,), (1,)), ((), ())), preferred_element_type=jnp.float32
    )


def scan_call(dbl, conv, gate, gg, dtp, dtb, alog, skip, keep):
    length, chans = conv.shape
    cb = min(65536 // length, chans)
    f32 = jnp.float32
    maps = jnp.broadcast_to(dbl[:, R:, None], (length, 2 * N, 128))
    tokens = lambda kind: (jax.ShapeDtypeStruct((length, chans), kind), pl.BlockSpec((length, cb), lambda i: (0, i)))
    whole = lambda *shape: (jax.ShapeDtypeStruct(shape, f32), pl.BlockSpec(shape, lambda i: (0,) * len(shape)))
    rows = lambda count: (jax.ShapeDtypeStruct((count, chans), f32), pl.BlockSpec((count, cb), lambda i: (0, i)))
    outs = [
        tokens(jnp.bfloat16), tokens(jnp.bfloat16), tokens(f32), whole(R, length), whole(length, N, 128), whole(length, N, 128),
        rows(R), rows(1), rows(N), rows(1),
    ]
    ins = [
        whole(length, R), tokens(f32), tokens(f32), tokens(f32), rows(R), rows(1), rows(N), rows(1),
        whole(length, 1),
    ]
    res = pl.pallas_call(
        scan_kernel,
        grid=(chans // cb,),
        in_specs=[spec for _, spec in ins] + [
            pl.BlockSpec((length, N, 128), lambda i: (0, 0, 0)), pl.BlockSpec((length, N, 128), lambda i: (0, 1, 0))],
        out_specs=[spec for _, spec in outs],
        out_shape=[shape for shape, _ in outs],
        scratch_shapes=[
            pltpu.VMEM((length + 1, N, cb), f32), pltpu.VMEM((length, N, cb), f32),
        ] + [pltpu.VMEM((length, cb), f32)] * 6 + [pltpu.VMEM((N, cb), f32)],
        name="selective_scan",
        compiler_params=pltpu.CompilerParams(vmem_limit_bytes=60 << 20),
    )(dbl[:, :R], conv, gate, gg, dtp, dtb[None], alog, skip[None], keep[:, None], maps, maps)
    gated, ggate, gconv, gdbl, gin, gout, gdtp, gdtb, galog, gskip = res
    gdbl_all = jnp.concatenate([gdbl, jnp.sum(gin, -1).T, jnp.sum(gout, -1).T], axis=0)
    return gated, ggate, gconv, gdbl_all, gdtp, gdtb[0], galog, gskip[0]


MESH = pl.DeviceIdType.MESH
NZ = 4
F32 = jnp.float32
BF16 = jnp.bfloat16
NN = (((1,), (0,)), ((), ()))
NT = (((1,), (1,)), ((), ()))
TN = (((0,), (0,)), ((), ()))


def dot(left, right, dims=NN):
    return lax.dot_general(left, right, dims, preferred_element_type=F32)


def place(z, x, c):
    return (z * 2 + x) * 2 + c


class Spot:
    def __init__(self):
        self.dp = lax.axis_index("dp")
        self.y = lax.axis_index("tensor")
        self.z, self.x, self.c = self.dp // 4, (self.dp // 2) % 2, self.dp % 2
        self.x_mate = (place(self.z, 1 - self.x, self.c), self.y)
        self.c_mate = (place(self.z, self.x, 1 - self.c), self.y)
        self.y_mate = (self.dp, 1 - self.y)

    def z_at(self, offset):
        return lax.rem(self.z + offset + NZ, NZ)

    def slot(self, origin, device):
        if device is self.c_mate:
            return 2 * NZ
        return origin // 4 + (NZ if device is self.x_mate else 0)

    def on_line(self, z, y=None):
        return (place(z, self.x, self.c), self.y if y is None else y)


def greet(devices):
    barrier = pltpu.get_barrier_semaphore()
    for device in devices:
        pl.semaphore_signal(barrier, inc=1, device_id=device, device_id_type=MESH)
    pl.semaphore_wait(barrier, len(devices))


class Copies:
    def __init__(self, send_sems, own_sems):
        self.send_sems, self.own_sems = send_sems, own_sems
        self.used, self.groups, self.begun, self.kept = 0, [], [], []

    def new_sem(self):
        self.used += 1
        return self.send_sems.at[self.used - 1]

    def group(self, whole):
        sem = self.new_sem()
        self.groups.append((sem, pltpu.make_async_copy(whole, whole, sem).wait))
        return sem

    def settle(self, *sems):
        for sem, wait in self.groups:
            if any(sem is one for one in sems):
                wait()
        self.groups = [(sem, wait) for sem, wait in self.groups if all(sem is not one for one in sems)]

    def send(self, src, dst, recv_sem, device, when=None, group=None):
        copy = pltpu.make_async_remote_copy(
            src_ref=src, dst_ref=dst, send_sem=self.new_sem() if group is None else group, recv_sem=recv_sem,
            device_id=device, device_id_type=MESH,
        )
        if group is None:
            self.begun.append((when, copy.wait_send))
        if when is None:
            copy.start()
        else:
            pl.when(when)(copy.start)

    def keep(self, src, dst):
        copy = pltpu.make_async_copy(src, dst, self.own_sems.at[len(self.kept)])
        copy.start()
        self.kept.append(copy)

    def wait_sent(self):
        self.settle(*[sem for sem, _ in self.groups])
        self.settle_alone(self.begun)
        for copy in self.kept:
            copy.wait()

    def settle_alone(self, begun):
        for when, wait in begun:
            if when is None:
                wait()
            else:
                pl.when(when)(wait)
        self.begun = [one for one in self.begun if all(one is not done for done in begun)]


def arrived(dst, recv_sem, when=None):
    copy = pltpu.make_async_copy(dst, dst, recv_sem)
    if when is None:
        copy.wait()
    else:
        pl.when(when)(copy.wait)


class Gather:
    def __init__(self, spot, copies, src, dst, recv_sems, own_sem):
        self.spot, self.copies, self.src, self.dst, self.recv_sems, self.own_sem = spot, copies, src, dst, recv_sems, own_sem
        self.width = dst.shape[-1]
        self.group = copies.group(dst.at[pl.ds(0, 4 * NZ - 1)])

    def columns(self, z):
        return self.src.at[:, pl.ds(pl.multiple_of(z * self.width, self.width), self.width)]

    def push(self, offsets=(1, 2, 3, 0)):
        spot, me = self.spot, self.spot.dp
        for offset in offsets:
            if offset == 0:
                self.push_own()
                continue
            z = spot.z_at(offset)
            self.copies.send(self.columns(z), self.dst.at[me], self.recv_sems.at[spot.z], spot.on_line(z), group=self.group)

    def push_own(self):
        spot, me = self.spot, self.spot.dp
        self.own = pltpu.make_async_copy(self.columns(spot.z), self.dst.at[me], self.own_sem)
        self.own.start()
        self.pass_on(me, spot.x_mate, self.columns(spot.z))
        self.pass_on(me, spot.c_mate, self.columns(spot.z))

    def pass_on(self, origin, device, src=None):
        sem = self.recv_sems.at[self.spot.slot(origin, device)]
        src = self.dst.at[origin] if src is None else src
        self.copies.send(src, self.dst.at[origin], sem, device, group=self.group)

    def first(self):
        spot = self.spot
        for offset in range(1, NZ):
            z = spot.z_at(-offset)
            origin = place(z, spot.x, spot.c)
            arrived(self.dst.at[origin], self.recv_sems.at[z])
            self.pass_on(origin, spot.x_mate)
            self.pass_on(origin, spot.c_mate)

    def second(self):
        spot = self.spot
        for offset in range(NZ):
            z = spot.z_at(-offset)
            origin = place(z, 1 - spot.x, spot.c)
            arrived(self.dst.at[origin], self.recv_sems.at[NZ + z])
            self.pass_on(origin, spot.c_mate)

    def last(self):
        self.own.wait()
        arrived(self.dst.at[pl.ds(0, 2 * NZ)], self.recv_sems.at[2 * NZ])


class LineSum:
    def __init__(self, spot, copies, part, landing, total, sems):
        self.spot, self.copies, self.part, self.landing, self.total, self.sems = spot, copies, part, landing, total, sems
        self.offsets = [(dz, dy) for dz in range(NZ) for dy in range(2) if dz + dy > 0]
        self.all_others = landing.at[pl.ds(0, len(self.offsets))]
        self.groups = [copies.group(self.all_others) for _ in range(2)]

    def there(self, dz, dy):
        return self.spot.z_at(dz), lax.rem(self.spot.y + dy, 2)

    def push(self):
        for k, (dz, dy) in enumerate(self.offsets):
            z, y = self.there(dz, dy)
            self.copies.send(self.part.at[z, y], self.landing.at[k], self.sems.at[0], self.spot.on_line(z, y), group=self.groups[0])

    def middle(self):
        own_z, own_y = self.spot.z, self.spot.y
        arrived(self.all_others, self.sems.at[0])
        summed = self.part[own_z, own_y].astype(F32)
        for k in range(len(self.offsets)):
            summed = summed + self.landing[k].astype(F32)
        self.total[own_z, own_y] = summed.astype(BF16)
        own = self.total.at[own_z, own_y]
        for dz, dy in self.offsets:
            self.copies.send(own, own, self.sems.at[1], self.spot.on_line(*self.there(dz, dy)), group=self.groups[1])

    def last(self):
        arrived(self.all_others, self.sems.at[1])


def column_masks(tile):
    return jnp.concatenate([tile] * 16, axis=0).T


class Share:
    def __init__(self, spot, copies, dst, recv_sems):
        self.spot, self.copies, self.dst, self.recv_sems = spot, copies, dst, recv_sems
        self.over_y, self.alone = copies.group(dst.at[pl.ds(0, NZ // 2)]), []

    def send(self, z, device, when=None):
        own = self.dst.at[z, self.spot.y]
        self.copies.send(own, own, self.recv_sems.at[z], device, when)
        self.alone.append(self.copies.begun[-1])

    def settle(self):
        self.copies.settle(self.over_y)
        self.copies.settle_alone(self.alone)

    def send_y(self, z, when=None):
        own = self.dst.at[z, self.spot.y]
        self.copies.send(own, own, self.recv_sems.at[NZ], self.spot.y_mate, when, self.over_y)

    def push(self):
        spot = self.spot
        self.send(spot.z, spot.on_line(spot.z_at(1)), spot.z < NZ - 1)
        self.send(spot.z, spot.on_line(spot.z_at(-1)), spot.z > 0)
        self.send_y(spot.z)

    def first(self, far):
        spot = self.spot
        for way in (1, -1):
            origin = spot.z_at(-way * far)
            comes = spot.z >= far if way == 1 else spot.z < NZ - far
            goes = comes & (spot.z < NZ - 1 if way == 1 else spot.z > 0)
            arrived(self.dst.at[origin, spot.y], self.recv_sems.at[origin], comes)
            if far < NZ - 1:
                self.send(origin, spot.on_line(spot.z_at(way)), goes)
            self.send_y(origin, comes)

    def last(self):
        arrived(self.dst.at[pl.ds(0, NZ // 2)], self.recv_sems.at[NZ])


class Scan:
    def __init__(self, a_s, stepd_s, drive_s, gs_s, read_s, q_s, r_s, state_s, pulled_s, alog_s, spread_s, sum_s, gmap_s):
        self.a_s, self.stepd_s, self.drive_s, self.gs_s = a_s, stepd_s, drive_s, gs_s
        self.read_s, self.q_s, self.r_s, self.state_s = read_s, q_s, r_s, state_s
        self.pulled_s, self.alog_s, self.spread_s, self.sum_s, self.gmap_s = pulled_s, alog_s, spread_s, sum_s, gmap_s
        sub = lax.broadcasted_iota(jnp.int32, (8, 128), 0)
        self.masks = [(sub & shift) == 0 for shift in (1, 2, 4)]
        self.lane = lax.broadcasted_iota(jnp.int32, (N, 128), 1)
        self.blocks = [slice(b * 128, (b + 1) * 128) for b in range(a_s.shape[1] // 128)]

    def place(self, i):
        base = pl.multiple_of(i * 8, 8)
        tile = pl.ds(pl.multiple_of((base // 128) * 128, 128), 128)
        return base, tile, lax.rem(base, 128)

    def spread(self, maps, shifted_s):
        rows = maps.shape[0]
        for i in range(maps.shape[1] // 8):
            tile, first = maps[:, i // 16 * 128 : (i // 16 + 1) * 128], i % 16 * 8
            shifted_s[i * rows : (i + 1) * rows] = pltpu.roll(tile, (128 - first) % 128, 1).astype(BF16)
        row = lax.broadcasted_iota(jnp.int32, (128, 8 * 128), 0)
        column = lax.broadcasted_iota(jnp.int32, (128, 8 * 128), 1)
        chosen = jnp.where(row == column // 128, 1.0, 0.0).astype(BF16)
        self.spread_s[...] = dot(shifted_s[...], chosen).reshape(self.spread_s.shape)

    def maps_at(self, i, j):
        lanes = slice(j * 128, (j + 1) * 128)
        return self.spread_s[i, :N, lanes], self.spread_s[i, N:, lanes]

    def forward(self, start, stop):
        def chunk(i, none):
            base = pl.multiple_of(i * 8, 8)
            for lanes in self.blocks:
                state = self.state_s[i, :, lanes]
                a = self.a_s[:, lanes]
                stepd, drive = self.stepd_s[pl.ds(base, 8), lanes], self.drive_s[pl.ds(base, 8), lanes]
                sums = RowSums(self.masks)
                for j in range(8):
                    in_map, out_map = self.maps_at(i, j)
                    state = jnp.exp(stepd[j : j + 1] * a) * state + drive[j : j + 1] * in_map
                    read = state * out_map
                    sums.add(j, read[:8] + read[8:])
                self.state_s[i + 1, :, lanes] = state
                self.read_s[pl.ds(base, 8), lanes] = sums.result
            return none

        lax.fori_loop(start, stop, chunk, 0)

    def backward(self, start, stop):
        def chunk(step, none):
            i = start + stop - 1 - step
            base, tile, first = self.place(i)
            for b, lanes in enumerate(self.blocks):
                a = self.a_s[:, lanes]
                stepd, drive = self.stepd_s[pl.ds(base, 8), lanes], self.drive_s[pl.ds(base, 8), lanes]
                gs = self.gs_s[pl.ds(base, 8), lanes]
                states, decays = [self.state_s[i, :, lanes]], []
                for j in range(8):
                    decays.append(jnp.exp(stepd[j : j + 1] * a))
                    states.append(decays[j] * states[j] + drive[j : j + 1] * self.maps_at(i, j)[0])
                pulled, alog = self.pulled_s[:, lanes], self.alog_s[:, lanes]
                q_sums, r_sums = RowSums(self.masks), RowSums(self.masks)
                for j in reversed(range(8)):
                    in_map, out_map = self.maps_at(i, j)
                    adjoint = pulled + out_map * gs[j : j + 1]
                    g_in, g_out = adjoint * drive[j : j + 1], states[j + 1] * gs[j : j + 1]
                    if b > 0:
                        g_in, g_out = g_in + self.sum_s[0, j], g_out + self.sum_s[1, j]
                    self.sum_s[0, j], self.sum_s[1, j] = g_in, g_out
                    q_t = adjoint * in_map
                    q_sums.add(j, q_t[:8] + q_t[8:])
                    pulled = decays[j] * adjoint
                    past = pulled * states[j]
                    r_t = past * a
                    r_sums.add(j, r_t[:8] + r_t[8:])
                    alog = alog + past * stepd[j : j + 1]
                self.pulled_s[:, lanes], self.alog_s[:, lanes] = pulled, alog
                self.q_s[pl.ds(base, 8), lanes] = q_sums.result
                self.r_s[pl.ds(base, 8), lanes] = r_sums.result
            for k in range(2):
                row = self.gmap_s[k * N : (k + 1) * N, tile]
                for j in range(8):
                    row = jnp.where(self.lane == first + j, jnp.sum(self.sum_s[k, j], axis=1, keepdims=True), row)
                self.gmap_s[k * N : (k + 1) * N, tile] = row
            return none

        lax.fori_loop(start, stop, chunk, 0)


class TokenSum:
    def __init__(self, spot, copies, part, y_land, z_land, y_sems, z_sems):
        self.spot, self.copies, self.part, self.y_land, self.z_land = spot, copies, part, y_land, z_land
        self.y_sems, self.z_sems = y_sems, z_sems
        self.group = copies.group(y_land)

    def push(self):
        spot = self.spot
        for far in (3, 2, 1):
            for way in (1, -1):
                self.over_y(spot.z_at(way * far), self.within(way, far))
        self.over_y(spot.z, None)

    def within(self, way, far):
        return self.spot.z < NZ - far if way == 1 else self.spot.z >= far

    def over_y(self, z, when):
        self.copies.send(self.part.at[z, 1 - self.spot.y], self.y_land.at[z], self.y_sems.at[z], self.spot.y_mate, when, self.group)

    def add(self, z, landed):
        part, y = self.part, self.spot.y
        part[z, y] = (part[z, y].astype(F32) + landed[...].astype(F32)).astype(BF16)

    def stage(self, far):
        spot = self.spot
        for side, way in enumerate((1, -1)):
            z = spot.z_at(way * far)
            goes = self.within(way, far)
            grown = goes & self.within(-way, 1)
            land, sem = self.z_land.at[side, z], self.z_sems.at[side, z]

            @pl.when(goes)
            def _(z=z):
                arrived(self.y_land.at[z], self.y_sems.at[z])
                self.add(z, self.y_land.at[z])

            if far < NZ - 1:

                @pl.when(grown)
                def _(z=z, land=land, sem=sem):
                    arrived(land, sem)
                    self.add(z, land)

            self.copies.send(self.part.at[z, spot.y], land, sem, spot.on_line(spot.z_at(way)), goes)

    def last(self):
        spot = self.spot
        z = spot.z
        arrived(self.y_land.at[z], self.y_sems.at[z])
        self.add(z, self.y_land.at[z])
        for side, way in enumerate((1, -1)):

            @pl.when(self.within(-way, 1))
            def _(land=self.z_land.at[side, z], sem=self.z_sems.at[side, z]):
                arrived(land, sem)
                self.add(z, land)

        return self.part[z, spot.y].astype(F32)


class RowSum:
    def __init__(self, spot, copies, part, c_land, x_land, z_land, c_sems, x_sems, z_sem):
        self.spot, self.copies, self.part = spot, copies, part
        self.c_land, self.x_land, self.z_land = c_land, x_land, z_land
        self.c_sems, self.x_sems, self.z_sem = c_sems, x_sems, z_sem
        self.groups = [copies.group(whole) for whole in (c_land, x_land, z_land.at[pl.ds(0, NZ - 1)])]

    def push(self):
        spot = self.spot
        for offset in (1, 2, 3, 0):
            z = spot.z_at(offset)
            for x in range(2):
                self.copies.send(
                    self.part.at[place(z, x, 1 - spot.c)], self.c_land.at[z, x], self.c_sems.at[z], spot.c_mate, group=self.groups[0]
                )

    def add(self, z, x, landed):
        part, owner = self.part, place(z, x, self.spot.c)
        part[owner] = (part[owner].astype(F32) + landed.astype(F32)).astype(part.dtype)

    def second(self):
        spot = self.spot
        for offset in (1, 2, 3, 0):
            z = spot.z_at(offset)
            arrived(self.c_land.at[z], self.c_sems.at[z])
            for x in range(2):
                self.add(z, x, self.c_land[z, x])
            self.copies.send(
                self.part.at[place(z, 1 - spot.x, spot.c)], self.x_land.at[z], self.x_sems.at[z], spot.x_mate, group=self.groups[1]
            )

    def third(self, offsets=(1, 2, 3, 0)):
        spot = self.spot
        for offset in offsets:
            z = spot.z_at(offset)
            arrived(self.x_land.at[z], self.x_sems.at[z])
            self.add(z, spot.x, self.x_land[z])
            own = self.part.at[place(z, spot.x, spot.c)]
            if offset:
                self.copies.send(own, self.z_land.at[spot.z], self.z_sem, spot.on_line(z), group=self.groups[2])
            else:
                self.copies.keep(own, self.z_land.at[z])

    def last(self):
        arrived(self.z_land.at[pl.ds(0, NZ - 1)], self.z_sem)


class ChannelSum:
    def __init__(self, spot, copies, part, c_land, x_land, own, full, c_sem, x_sem, full_sems):
        self.spot, self.copies, self.part, self.own, self.full, self.full_sems = spot, copies, part, own, full, full_sems
        self.c_land, self.x_land, self.c_sem, self.x_sem = c_land, x_land, c_sem, x_sem
        self.group = copies.group(full.at[pl.ds(0, 4 * NZ - 1)])

    def push(self):
        self.copies.send(self.part.at[1 - self.spot.c], self.c_land, self.c_sem, self.spot.c_mate)

    def second(self):
        spot = self.spot
        arrived(self.c_land, self.c_sem)
        self.part[spot.c] = self.part[spot.c] + self.c_land[...]
        self.copies.send(self.part.at[spot.c, 1 - spot.x], self.x_land, self.x_sem, spot.x_mate)

    def spread(self, origin, device, src=None):
        src = self.full.at[origin] if src is None else src
        sem = self.full_sems.at[self.spot.slot(origin, device)]
        self.copies.send(src, self.full.at[origin], sem, device, group=self.group)

    def third(self):
        spot = self.spot
        arrived(self.x_land, self.x_sem)
        self.own[...] = (self.part[spot.c, spot.x] + self.x_land[...]).astype(BF16)
        for device in [spot.on_line(spot.z_at(offset)) for offset in (1, 2, 3)] + [spot.x_mate, spot.c_mate]:
            self.spread(spot.dp, device, self.own)
        self.copies.keep(self.own, self.full.at[spot.dp])

    def fourth(self):
        spot = self.spot
        for offset in (1, 2, 3):
            z = spot.z_at(-offset)
            origin = place(z, spot.x, spot.c)
            arrived(self.full.at[origin], self.full_sems.at[z])
            self.spread(origin, spot.x_mate)
            self.spread(origin, spot.c_mate)

    def fifth(self):
        spot = self.spot
        for offset in range(NZ):
            z = spot.z_at(-offset)
            origin = place(z, 1 - spot.x, spot.c)
            arrived(self.full.at[origin], self.full_sems.at[NZ + z])
            self.spread(origin, spot.c_mate)

    def last(self):
        arrived(self.full.at[pl.ds(0, 2 * NZ)], self.full_sems.at[2 * NZ])


class Held:
    def __init__(self, names, refs):
        for name, ref in zip(names, refs, strict=True):
            setattr(self, name, ref)


def block_scratch(half, feats, rows, chans, step_rows, width):
    tokens, n_dp, length = 2 * half * NZ, 4 * NZ, 2 * half
    vmem, dma = pltpu.VMEM, pltpu.SemaphoreType.DMA
    owners, steps = (n_dp, rows, chans), (n_dp, step_rows, chans)
    part = (NZ, 2, width // 2, length)
    small = (width + 32) // 4
    held = {
        "w": vmem((3, n_dp, rows, chans), BF16),
        "acts": vmem((2, NZ, 2, half, feats), BF16),
        "dtp_own": vmem((step_rows, chans * NZ), F32),
        "dtp": vmem((n_dp, step_rows, chans), F32),
        "info": vmem((n_dp, 8, 128), F32),
        "mask": vmem((NZ, length, 128), F32),
        "low": vmem((tokens, chans), BF16),
        "gated": vmem((tokens, chans), BF16),
        "ggate": vmem((tokens, chans), BF16),
    }
    for name in ("x_in", "pre", "gate", "gg", "raw", "stepd", "drive", "gs", "read"):
        held[name] = vmem((tokens, chans), F32)
    held |= {
        "a": vmem((N, chans), F32),
        "state": vmem((tokens // 8 + 1, N, chans), F32),
        "pulled": vmem((N, chans), F32),
        "alog": vmem((N, chans), F32),
        "spread": vmem((tokens // 8, 2 * N, 8 * 128), F32),
        "shifted": vmem((tokens // 8 * 2 * N, 128), BF16),
        "sum": vmem((2, 8, N, 128), F32),
        "gmap": vmem((2 * N, tokens), F32),
        "dbl": vmem((width, tokens), F32),
        "part": vmem((2,) + part, BF16),
        "landing": vmem((2, 2 * NZ) + part[2:], BF16),
        "total": vmem((2,) + part, BF16),
        "mixed": vmem((NZ, 2, half, feats), BF16),
        "outw": vmem(owners, BF16),
        "ginz": vmem(owners, BF16),
        "gdtp": vmem(steps, F32),
        "chan": vmem((2, 2, small, chans), F32),
        "y_land": vmem((2, NZ, half, feats), BF16),
        "z_land": vmem((2, 2, NZ, half, feats), BF16),
        "wc_land": vmem((3, NZ, 2, rows, chans), BF16),
        "wx_land": vmem((3, NZ, rows, chans), BF16),
        "dc_land": vmem((NZ, 2, step_rows, chans), F32),
        "dx_land": vmem((NZ, step_rows, chans), F32),
        "fc_land": vmem((2, small, chans), F32),
        "fx_land": vmem((small, chans), F32),
        "f_own": vmem((small, chans), BF16),
        "block": vmem((half, feats), F32),
        "gresid": vmem((half, feats), F32),
        "tile": vmem((4, 8, 128), F32),
        "gain_part": vmem((2, n_dp, 128), F32),
        "gain": vmem((n_dp, 8, 128), F32),
        "gain_total": vmem((8, 128), F32),
        "squares": vmem((2, 8, 128), F32),
        "gain_land": vmem((n_dp - 1, 8, 128), F32),
        "resid": vmem((half, feats), F32),
        "cot": vmem((half, feats), F32),
        "xproj": vmem((width, chans * NZ), BF16),
        "load_sems": dma((3,)),
        "send_sems": dma((56,)),
        "keep_sems": dma((9,)),
        "own_sems": dma((4,)),
        "w_sems": dma((4, 2 * NZ + 1)),
        "act_sems": dma((2, NZ + 1)),
        "info_sem": dma(()),
        "dbl_sems": dma((2, 2)),
        "y_sems": dma((2, NZ)),
        "z_sems": dma((2, 2, NZ)),
        "wc_sems": dma((4, NZ)),
        "wx_sems": dma((4, NZ)),
        "wz_sems": dma((4,)),
        "f_sems": dma((2,)),
        "full_sems": dma((2 * NZ + 1,)),
        "tile_sems": dma((2,)),
        "gain_sems": dma((2,)),
    }
    return held


def block_kernel(names, *refs):
    (
        inx_ref, inz_ref, outp_ref, resid_in, cot_in, xproj_in, gain_ref, ids_ref, dtp_ref, convw_ref, convb_ref, dtb_ref,
        alog_ref, skip_ref,
        block_ref, gresid_ref, ggain_ref, ginx_ref, ginz_ref, goutp_ref, gdtp_ref, full_ref, squares_ref,
    ) = refs[:23]
    s = Held(names, refs[23:])
    spot = Spot()
    resid_ref, cot_ref, xproj_ref = s.resid, s.cot, s.xproj
    loads = [
        pltpu.make_async_copy(src, dst, s.load_sems.at[k])
        for k, (src, dst) in enumerate(((resid_in, s.resid), (cot_in, s.cot), (xproj_in, s.xproj)))
    ]
    for load in loads:
        load.start()
    plane = [lax.rem(spot.dp + offset, 4 * NZ) for offset in range(1, 4 * NZ)]
    greet([(dp, spot.y) for dp in plane] + [spot.on_line(spot.z_at(dz), 1 - spot.y) for dz in range(NZ)])
    copies = Copies(s.send_sems, s.keep_sems)
    tokens, chans = s.x_in.shape
    half, feats = resid_ref.shape
    length = 2 * half
    columns = pl.ds(pl.multiple_of(spot.z * chans, chans), chans)
    quarters = [
        (slice(k * feats // NZ, (k + 1) * feats // NZ), slice(k * NZ, (k + 1) * NZ)) for k in range(NZ)
    ]
    sequences = [slice(k * length, (k + 1) * length) for k in range(NZ)]

    s.dtp_own[...] = dtp_ref[...].astype(F32)
    inx, inz, outp, dtp = (
        Gather(spot, copies, src, dst, s.w_sems.at[k], s.own_sems.at[k])
        for k, (src, dst) in enumerate(((inx_ref, s.w.at[0]), (inz_ref, s.w.at[1]), (outp_ref, s.w.at[2]), (s.dtp_own, s.dtp)))
    )
    normed, cot = (Share(spot, copies, s.acts.at[k], s.act_sems.at[k]) for k in range(2))

    ids = jnp.broadcast_to(ids_ref[...], (8, length))
    lane = lax.broadcasted_iota(jnp.int32, (8, length), 1)
    sub = lax.broadcasted_iota(jnp.int32, (8, length), 0)
    info = jnp.broadcast_to(gain_ref[...].astype(F32), (8, length))
    for back in range(1, 4):
        same = jnp.where((pltpu.roll(ids, back, 1) == ids) & (lane >= back), 1.0, 0.0)
        info = jnp.where(sub == back, same, info)
    s.info[spot.dp] = info
    other_info = s.info.at[pl.ds(0, 4 * NZ - 1)]
    info_group = copies.group(other_info)
    for dp in plane:
        copies.send(s.info.at[spot.dp], s.info.at[spot.dp], s.info_sem, (dp, spot.y), group=info_group)
    inx.push()

    loads[0].wait()
    resid = resid_ref[...]
    row_square = jnp.sum(resid * resid, axis=1, keepdims=True)
    scaled = resid * lax.rsqrt(row_square / feats + eps_norm)
    s.tile[0] = jnp.broadcast_to(jnp.sum(row_square, axis=0, keepdims=True), (8, 128))
    copies.send(s.tile.at[0], s.tile.at[1], s.tile_sems.at[0], spot.y_mate)
    arrived(other_info, s.info_sem)
    for k in range(4 * NZ):
        cols = slice(k * 128, (k + 1) * 128)
        s.acts[0, spot.z, spot.y, :, cols] = (scaled[:, cols] * s.info[k, 0:1, :]).astype(BF16)
    normed.push()
    dtp.push()
    loads[1].wait()
    loads[2].wait()
    s.acts[1, spot.z, spot.y] = cot_ref[...].astype(BF16)
    for k in range(NZ):
        s.mask[k] = column_masks(s.info[place(k, spot.x, spot.c)])
    inx.first()
    normed.first(1)
    inx.second()
    normed.first(2)
    inz.push()
    dtp.first()
    dtp.second()
    normed.first(3)
    cot.push()
    normed.last()
    inx.last()

    all_normed = s.acts[0].reshape(tokens, feats)
    s.x_in[...] = dot(all_normed, s.w[0].reshape(-1, chans))
    taps = convw_ref[:, columns]
    bias = convb_ref[:, columns]
    for k, rows in enumerate(sequences):
        one = s.x_in[rows]
        pre = bias + taps[3:4] * one
        for back in range(1, 4):
            pre = pre + taps[3 - back : 4 - back] * (pltpu.roll(one, back, 0) * s.mask[k, :, back : back + 1])
        s.pre[rows] = pre
        s.low[rows] = (pre * sigmoid(pre)).astype(BF16)
    x_proj = xproj_ref[:, columns]
    dbl = dot(x_proj, s.low[...], NT)
    blocks = [(k, y) for k in range(NZ) for y in range(2)]
    width = dbl.shape[0] // 2
    for k, y in blocks:
        s.part[0, k, y] = dbl[y * width : (y + 1) * width, sequences[k]].astype(BF16)
    x_dbl = LineSum(
        spot, copies, s.part.at[0], s.landing.at[0], s.total.at[0], s.dbl_sems.at[0]
    )
    x_dbl.push()
    inz.first()
    cot.first(1)
    outp.push((1, 0))
    x_dbl.middle()
    outp.push((2, 3))
    cot.first(2)
    x_dbl.last()

    dtp.last()
    for k, y in blocks:
        s.dbl[y * width : (y + 1) * width, sequences[k]] = s.total[0, k, y].astype(F32)
    step_w = s.dtp[...].reshape(R, chans).astype(BF16)
    s.raw[...] = dot(s.dbl[:R].astype(BF16), step_w, TN) + dtb_ref[:, columns]
    for k, rows in enumerate(sequences):
        step = softplus(s.raw[rows])
        s.stepd[rows] = jnp.where(s.mask[k, :, 1:2] > 0.0, step, 1e30)
        s.drive[rows] = step * s.low[rows].astype(F32)
    s.a[...] = -jnp.exp(alog_ref[:, columns])
    s.state[0] = jnp.zeros((N, chans), F32)
    scan = Scan(
        s.a, s.stepd, s.drive, s.gs, s.read, s.read, s.gate, s.state, s.pulled, s.alog, s.spread, s.sum, s.gmap
    )
    scan.spread(s.dbl[R : R + 2 * N], s.shifted)
    steps = tokens // 8
    eighth = steps // 8
    inz.second()
    scan.forward(0, 4 * eighth)
    outp.first()
    cot.first(3)
    scan.forward(4 * eighth, steps)
    inz.last()
    s.gate[...] = dot(s.acts[0].reshape(tokens, feats), s.w[1].reshape(-1, chans))
    skip = skip_ref[:, columns]
    for rows in sequences:
        gate = s.gate[rows]
        scanned = s.read[rows] + skip * s.low[rows].astype(F32)
        s.gated[rows] = (scanned * gate * sigmoid(gate)).astype(BF16)

    mixed_sum, normed_sum = (
        TokenSum(spot, copies, part, s.y_land.at[k], s.z_land.at[k], s.y_sems.at[k], s.z_sems.at[k])
        for k, part in enumerate((s.mixed, s.acts.at[1]))
    )
    outw_sum, ginz_sum, ginx_sum, gdtp_sum = (
        RowSum(spot, copies, part, c_land, x_land, out, s.wc_sems.at[k], s.wx_sems.at[k], s.wz_sems.at[k])
        for k, (part, c_land, x_land, out) in enumerate((
            (s.outw, s.wc_land.at[0], s.wx_land.at[0], goutp_ref),
            (s.ginz, s.wc_land.at[1], s.wx_land.at[1], ginz_ref),
            (s.w.at[2], s.wc_land.at[2], s.wx_land.at[2], ginx_ref),
            (s.gdtp, s.dc_land, s.dx_land, gdtp_ref),
        ))
    )
    outp.second()
    cot.last()
    for cols, owners in quarters:
        given = s.acts[1, :, :, :, cols].reshape(tokens, -1)
        s.outw[owners] = dot(given, s.gated[...], TN).astype(BF16).reshape(-1, *s.outw.shape[1:])
    outw_sum.push()
    outp.last()
    s.gg[...] = dot(s.acts[1].reshape(tokens, feats), s.w[2].reshape(-1, chans))
    outw_sum.second()
    for cols, owners in quarters:
        part = dot(s.gated[...], s.w[2, owners].reshape(-1, chans), NT)
        s.mixed[:, :, :, cols] = part.astype(BF16).reshape(*s.mixed.shape[:3], -1)
    mixed_sum.push()
    for rows in sequences:
        gate, gg = s.gate[rows], s.gg[rows]
        sig = sigmoid(gate)
        scanned = s.read[rows] + skip * s.low[rows].astype(F32)
        s.gs[rows] = gg * gate * sig
        s.ggate[rows] = (gg * scanned * sig * (1.0 + gate * (1.0 - sig))).astype(BF16)
    outw_sum.third((1,))
    for cols, owners in quarters:
        given = s.acts[0, :, :, :, cols].reshape(tokens, -1)
        s.ginz[owners] = dot(given, s.ggate[...], TN).astype(BF16).reshape(-1, *s.ginz.shape[1:])
    ginz_sum.push()

    s.pulled[...] = jnp.zeros_like(s.pulled)
    s.alog[...] = jnp.zeros_like(s.alog)
    scan.backward(7 * eighth, steps)
    outw_sum.third((2,))
    ginz_sum.second()
    scan.backward(6 * eighth, 7 * eighth)
    outw_sum.third((3, 0))
    scan.backward(3 * eighth, 6 * eighth)
    ginz_sum.third((1,))
    mixed_sum.stage(3)
    scan.backward(0, 3 * eighth)
    grad_bias = jnp.zeros((1, chans), F32)
    grad_skip = jnp.zeros((1, chans), F32)
    raw_rows = []
    for rows in sequences:
        conv, raw, gs, q = s.low[rows].astype(F32), s.raw[rows], s.gs[rows], s.read[rows]
        grad_raw = (conv * q + s.gate[rows]) * sigmoid(raw)
        s.gg[rows] = softplus(raw) * q + skip * gs
        grad_bias = grad_bias + jnp.sum(grad_raw, axis=0, keepdims=True)
        grad_skip = grad_skip + jnp.sum(gs * conv, axis=0, keepdims=True)
        raw_rows.append(grad_raw.astype(BF16))
    raw_low = jnp.concatenate(raw_rows, axis=0)
    dbl = jnp.concatenate([dot(step_w, raw_low, NT), s.gmap[...]], axis=0)
    for k, y in blocks:
        s.part[1, k, y] = dbl[y * width : (y + 1) * width, sequences[k]].astype(BF16)
    grad_dbl_sum = LineSum(
        spot, copies, s.part.at[1], s.landing.at[1], s.total.at[1], s.dbl_sems.at[1]
    )
    grad_dbl_sum.push()
    s.gdtp[...] = dot(s.dbl[:R].astype(BF16), raw_low).reshape(s.gdtp.shape)
    gdtp_sum.push()
    grad_dbl_sum.middle()
    ginz_sum.third((2, 3, 0))
    mixed_sum.stage(2)
    gdtp_sum.second()
    grad_dbl_sum.last()

    grad_dbl = jnp.concatenate(
        [jnp.concatenate([s.total[1, k, y] for k in range(NZ)], axis=1) for y in range(2)], axis=0
    )
    s.gg[...] += dot(grad_dbl, x_proj, TN)
    sums = [jnp.zeros((1, chans), F32) for _ in range(5)]
    low_rows = []
    for k, rows in enumerate(sequences):
        pre, x_one = s.pre[rows], s.x_in[rows]
        sig = sigmoid(pre)
        one = s.gg[rows] * sig * (1.0 + pre * (1.0 - sig))
        sums[3] = sums[3] + jnp.sum(one * x_one, axis=0, keepdims=True)
        sums[4] = sums[4] + jnp.sum(one, axis=0, keepdims=True)
        grad_x = taps[3:4] * one
        for back in range(1, 4):
            masked = one * s.mask[k, :, back : back + 1]
            sums[3 - back] = sums[3 - back] + jnp.sum(masked * pltpu.roll(x_one, back, 0), axis=0, keepdims=True)
            grad_x = grad_x + taps[3 - back : 4 - back] * pltpu.roll(masked, length - back, 0)
        low_rows.append(grad_x.astype(BF16))
    grad_xin = jnp.concatenate(low_rows, axis=0)
    cot.settle()
    for cols, owners in quarters:
        part = dot(grad_xin, s.w[0, owners].reshape(-1, chans), NT) + dot(s.ggate[...], s.w[1, owners].reshape(-1, chans), NT)
        s.acts[1, :, :, :, cols] = part.astype(BF16).reshape(*s.mixed.shape[:3], -1)
        gain_part = jnp.sum(part * s.acts[0, :, :, :, cols].reshape(tokens, -1).astype(F32), axis=0, keepdims=True)
        for k in range(NZ):
            owner = owners.start + k
            s.gain_part[0, owner : owner + 1] = gain_part[:, k * 128 : (k + 1) * 128] / s.info[owner, 0:1]
    copies.send(s.gain_part.at[0], s.gain_part.at[1], s.gain_sems.at[0], spot.y_mate)
    normed_sum.push()
    s.chan[...] = jnp.concatenate(
        [dot(grad_dbl, s.low[...]), s.alog[...] * s.a[...], grad_bias, grad_skip, jnp.zeros((6, chans), F32)]
        + sums + [jnp.zeros((3, chans), F32)], axis=0
    ).reshape(s.chan.shape)
    small_sum = ChannelSum(
        spot, copies, s.chan, s.fc_land, s.fx_land, s.f_own, full_ref, s.f_sems.at[0], s.f_sems.at[1], s.full_sems
    )
    small_sum.push()
    copies.settle(outp.group)
    for cols, owners in quarters:
        given = s.acts[0, :, :, :, cols].reshape(tokens, -1)
        s.w[2, owners] = dot(given, grad_xin, TN).astype(BF16).reshape(-1, *s.outw.shape[1:])
    ginx_sum.push()
    small_sum.second()
    mixed_sum.stage(1)
    normed_sum.stage(3)
    ginx_sum.second()
    gdtp_sum.third()
    arrived(s.gain_part.at[1], s.gain_sems.at[0])
    for k in range(4 * NZ):
        s.gain[k] = jnp.broadcast_to(s.gain_part[0, k : k + 1] + s.gain_part[1, k : k + 1], (8, 128))
    gain_group = copies.group(s.gain_land)
    for offset, dp in enumerate(plane):
        copies.send(s.gain.at[dp], s.gain_land.at[offset], s.gain_sems.at[1], (dp, spot.y), group=gain_group)
    small_sum.third()
    normed_sum.stage(2)
    ginx_sum.third((1, 2))
    normed_sum.stage(1)
    ginx_sum.third((3, 0))
    small_sum.fourth()

    mixed = mixed_sum.last()
    resid = resid_ref[...]
    s.block[...] = resid + mixed
    copies.keep(s.block, block_ref)
    s.tile[2] = jnp.broadcast_to(jnp.sum(jnp.sum(mixed * mixed, axis=1, keepdims=True), axis=0, keepdims=True), (8, 128))
    copies.send(s.tile.at[2], s.tile.at[3], s.tile_sems.at[1], spot.y_mate)
    small_sum.fifth()
    outw_sum.last()
    ginz_sum.last()
    gdtp_sum.last()
    arrived(s.tile.at[1], s.tile_sems.at[0])
    s.squares[0] = s.tile[0] + s.tile[1]
    arrived(s.tile.at[3], s.tile_sems.at[1])
    s.squares[1] = s.tile[2] + s.tile[3]
    copies.keep(s.squares, squares_ref)

    grad_rows = normed_sum.last()
    inv = lax.rsqrt(jnp.sum(resid * resid, axis=1, keepdims=True) / feats + eps_norm)
    scaled = resid * inv
    gain = jnp.concatenate([s.info[k, 0:1] for k in range(4 * NZ)], axis=1)
    grad_scaled = grad_rows * gain
    mean = jnp.sum(grad_scaled * scaled, axis=1, keepdims=True) / feats
    s.gresid[...] = cot_ref[...] + inv * (grad_scaled - scaled * mean)
    copies.keep(s.gresid, gresid_ref)
    arrived(s.gain_land, s.gain_sems.at[1])
    total = s.gain[spot.dp]
    for offset in range(4 * NZ - 1):
        total = total + s.gain_land[offset]
    s.gain_total[...] = total
    copies.keep(s.gain_total, ggain_ref)
    ginx_sum.last()
    small_sum.last()
    copies.wait_sent()
    assert copies.used == s.send_sems.shape[0], copies.used


def block_call(in_x, in_z, out_p, residual, cotangent, gain, ids, dt_p, x_proj, conv_w, conv_b, dt_b, a_log, d_skip):
    half, feats = residual.shape
    rows, wide = in_x.shape
    n_dp, chans = 4 * NZ, wide // NZ
    held = block_scratch(half, feats, rows, chans, dt_p.shape[0], x_proj.shape[0])
    shape = jax.ShapeDtypeStruct
    outs = [
        shape((half, feats), F32), shape((half, feats), F32), shape((8, 128), F32),
        shape((NZ, rows, chans), BF16), shape((NZ, rows, chans), BF16), shape((NZ, rows, chans), BF16),
        shape((NZ, dt_p.shape[0], chans), F32), shape((n_dp, (x_proj.shape[0] + 32) // 4, chans), BF16),
        shape((2, 8, 128), F32),
    ]
    in_any = pl.BlockSpec(memory_space=pl.ANY)
    in_vmem = pl.BlockSpec(memory_space=pltpu.VMEM)
    return pl.pallas_call(
        functools.partial(block_kernel, list(held)),
        out_shape=outs,
        in_specs=[in_any] * 6 + [in_vmem] * 8,
        out_specs=[in_any] * len(outs),
        scratch_shapes=list(held.values()),
        name="block",
        compiler_params=pltpu.CompilerParams(collective_id=1, has_side_effects=True, vmem_limit_bytes=62 << 20),
    )(in_x, in_z, out_p, residual, cotangent, x_proj, gain, ids, dt_p, conv_w, conv_b, dt_b, a_log, d_skip)


def finish_kernel(
    scale, block_in, gresid_in, ginx_in, ginz_in, goutp_in, gdtp_in, full_in, ggain_in, squares_in,
    block_ref, gresid_ref, ginx_ref, ginz_ref, goutp_ref, gdtp_ref, xproj_ref, alog_ref, dtb_ref, skip_ref, convw_ref, convb_ref,
    ggain_ref, rms_ref, mrms_ref,
    token_s, low_s, wide_s, step_s, full_s, xproj_s, in_sems, out_sems,
):
    begun = []

    def out(src, dst):
        copy = pltpu.make_async_copy(src, dst, out_sems.at[len(begun)])
        copy.start()
        begun.append(copy)

    reads = [
        pltpu.make_async_copy(src, dst, in_sems.at[k])
        for k, (src, dst) in enumerate(
            (
                (block_in, token_s.at[0]), (gresid_in, token_s.at[1]),
                (ginx_in, low_s.at[0]), (ginz_in, low_s.at[1]), (goutp_in, low_s.at[2]), (full_in, full_s), (gdtp_in, step_s),
            )
        )
    ]
    for read in reads:
        read.start()
    for k, ref in enumerate((block_ref, gresid_ref)):
        reads[k].wait()
        out(token_s.at[k], ref)
    ggain_ref[...] = ggain_in[0:1]
    rms_ref[...] = jnp.sqrt(squares_in[0, 0:1, 0:1] * scale)
    mrms_ref[...] = jnp.sqrt(squares_in[1, 0:1, 0:1] * scale)
    chans = low_s.shape[3]
    columns = [slice(z * chans, (z + 1) * chans) for z in range(NZ)]
    for k, ref in enumerate((ginx_ref, ginz_ref, goutp_ref)):
        reads[k + 2].wait()
        for z, cols in enumerate(columns):
            wide_s[k, :, cols] = low_s[k, z].astype(F32)
        out(wide_s.at[k], ref)
    reads[5].wait()
    rows, width = full_s.shape[1], xproj_s.shape[0]
    for z, cols in enumerate(columns):
        for k in range(4):
            found = full_s[place(z, k % 2, k // 2)].astype(F32)
            upto = min(rows, width - k * rows)
            xproj_s[k * rows : k * rows + upto, cols] = found[:upto]
        alog_ref[:, cols] = found[upto : upto + N]
        dtb_ref[:, cols] = found[upto + N : upto + N + 1]
        skip_ref[:, cols] = found[upto + N + 1 : upto + N + 2]
        convw_ref[:, cols] = found[upto + 24 : upto + 28]
        convb_ref[:, cols] = found[upto + 28 : upto + 29]
    out(xproj_s, xproj_ref)
    reads[6].wait()
    for z, cols in enumerate(columns):
        gdtp_ref[:, cols] = step_s[z]
    for copy in begun:
        copy.wait()


def finish_call(block, gresid, ginx, ginz, goutp, gdtp, full, ggain, squares, width):
    rows, chans = ginx.shape[1:]
    wide = chans * NZ
    shape = lambda count, columns=wide: jax.ShapeDtypeStruct((count, columns), F32)
    vmem, dma = pltpu.VMEM, pltpu.SemaphoreType.DMA
    in_any, in_vmem = pl.BlockSpec(memory_space=pl.ANY), pl.BlockSpec(memory_space=vmem)
    return pl.pallas_call(
        functools.partial(finish_kernel, 1.0 / (2 * block.shape[0] * block.shape[1])),
        out_shape=[
            shape(*block.shape), shape(*gresid.shape), shape(rows), shape(rows), shape(rows), shape(gdtp.shape[1]), shape(width),
            shape(N), shape(1), shape(1), shape(4), shape(1), shape(1, 128), shape(1, 1), shape(1, 1),
        ],
        in_specs=[in_any] * 7 + [in_vmem] * 2,
        out_specs=[in_any] * 5 + [in_vmem] + [in_any] + [in_vmem] * 8,
        scratch_shapes=[
            vmem((2,) + block.shape, F32), vmem((3,) + ginx.shape, BF16), vmem((3, rows, wide), F32), vmem(gdtp.shape, F32), vmem(full.shape, BF16),
            vmem((width, wide), F32), dma((7,)), dma((6,)),
        ],
        name="finish",
        compiler_params=pltpu.CompilerParams(vmem_limit_bytes=60 << 20),
    )(block, gresid, ginx, ginz, goutp, gdtp, full, ggain, squares)


def per_device_split(
    residual,
    norm_gain,
    in_proj_x,
    in_proj_z,
    x_proj,
    dt_proj,
    dt_bias,
    conv_weight,
    conv_bias,
    a_log,
    d_skip,
    out_proj,
    doc_ids,
    cotangent,
):
    parts = block_call(
        in_proj_x, in_proj_z, out_proj, residual, cotangent, norm_gain[None], doc_ids[None], dt_proj, x_proj, conv_weight,
        conv_bias[None], dt_bias[None], a_log, d_skip[None],
    )
    block, gresid, ggain, ginx, ginz, goutp, gdtp, full, squares = parts
    block, gresid, ginx, ginz, goutp, gdtp, g_xproj, g_alog, g_dtb, g_skip, g_convw, g_convb, ggain, rms, mrms = finish_call(
        block, gresid, ginx, ginz, goutp, gdtp, full, ggain, squares, x_proj.shape[0]
    )
    return (
        block,
        gresid,
        ggain[0],
        ginx,
        ginz,
        g_xproj,
        gdtp,
        g_dtb[0],
        g_convw,
        g_convb[0],
        g_alog,
        g_skip[0],
        goutp,
        rms[0],
        mrms[0],
    )


def norm_rows(values, gain_val):
    mean_square = jnp.mean(values * values, axis=1, keepdims=True)
    return values * lax.rsqrt(mean_square + eps_norm) * gain_val


def conv_local(x_in, doc_ids, conv_weight, conv_bias):
    kernel_len = conv_weight.shape[0]
    length = x_in.shape[0]
    padded = jnp.pad(x_in, ((kernel_len - 1, 0), (0, 0)))
    id_pad = jnp.concatenate([jnp.full((kernel_len - 1,), -1, jnp.int32), doc_ids])
    summed = conv_bias + jnp.zeros_like(x_in)
    for offset in range(kernel_len):
        same_doc = (id_pad[offset : offset + length] == doc_ids).astype(jnp.float32)
        summed = summed + conv_weight[offset] * padded[offset : offset + length] * same_doc[:, None]
    return summed


def per_device(
    residual,
    norm_gain,
    in_proj_x,
    in_proj_z,
    x_proj,
    dt_proj,
    dt_bias,
    conv_weight,
    conv_bias,
    a_log,
    d_skip,
    out_proj,
    doc_ids,
    cotangent,
):
    gathered = (
        lax.all_gather(norm_gain, "dp", axis=0, tiled=True),
        lax.all_gather(in_proj_x, "dp", axis=0, tiled=True),
        lax.all_gather(in_proj_z, "dp", axis=0, tiled=True),
        lax.all_gather(dt_proj, "dp", axis=0, tiled=True),
        lax.all_gather(out_proj, "dp", axis=0, tiled=True),
    )
    gain_all, inx_all, inz_all, step_all, out_all = gathered
    seq_len = doc_ids.shape[0]
    normed_f32, norm_back = jax.vjp(norm_rows, residual, gain_all.astype(jnp.float32))
    normed = lax.all_gather(normed_f32.astype(jnp.bfloat16), "tensor", axis=0, tiled=True)
    x_in = jnp.dot(normed, inx_all, preferred_element_type=jnp.float32)
    gate_in = jnp.dot(normed, inz_all, preferred_element_type=jnp.float32)

    def conv_act(x_val, weight_val, bias_val):
        return jax.nn.silu(conv_local(x_val, doc_ids, weight_val, bias_val))

    conv_out, conv_back = jax.vjp(conv_act, x_in, conv_weight, conv_bias)
    conv_low = conv_out.astype(jnp.bfloat16)
    dbl_part = lax.dot_general(
        conv_low, x_proj, (((1,), (1,)), ((), ())), preferred_element_type=jnp.float32
    )
    x_dbl, resid_square = lax.psum((dbl_part, jnp.sum(residual * residual)), "tensor")
    doc_starts = doc_ids != jnp.concatenate([jnp.full((1,), -1, jnp.int32), doc_ids[:-1]])
    carry_keep = 1.0 - doc_starts.astype(jnp.float32)

    cot_all = lax.all_gather(cotangent.astype(jnp.bfloat16), "tensor", axis=0, tiled=True)
    grad_gated = jnp.dot(cot_all, out_all, preferred_element_type=jnp.float32)
    gated_low, grad_gate_low, grad_conv, grad_dbl_part, grad_step_w, grad_bias, grad_alog, grad_skip = scan_call(
        x_dbl, conv_low, gate_in, grad_gated, step_all, dt_bias, a_log, d_skip, carry_keep
    )
    mixed = lax.psum_scatter(
        lax.dot_general(
            gated_low, out_all, (((1,), (1,)), ((), ())), preferred_element_type=jnp.float32
        ),
        "tensor",
        scatter_dimension=0,
        tiled=True,
    )
    block_out = residual + mixed
    mixed_square = lax.psum(jnp.sum(mixed * mixed), "tensor")
    rms_resid = jnp.sqrt(resid_square / (seq_len * D)).reshape(1)
    rms_mixed = jnp.sqrt(mixed_square / (seq_len * D)).reshape(1)
    grad_out_w = lax.dot_general(
        cot_all, gated_low, (((0,), (0,)), ((), ())), preferred_element_type=jnp.float32
    )
    grad_dbl = lax.psum(grad_dbl_part.T, "tensor")
    grad_dbl_low = grad_dbl.astype(jnp.bfloat16)
    grad_conv = grad_conv + jnp.dot(grad_dbl_low, x_proj, preferred_element_type=jnp.float32)
    grad_xproj = lax.dot_general(
        grad_dbl_low, conv_low, (((0,), (0,)), ((), ())), preferred_element_type=jnp.float32
    )
    grad_xin, grad_convw, grad_convb = conv_back(grad_conv)
    grad_xin_low = grad_xin.astype(jnp.bfloat16)
    grad_inx = lax.dot_general(
        normed, grad_xin_low, (((0,), (0,)), ((), ())), preferred_element_type=jnp.float32
    )
    grad_inz = lax.dot_general(
        normed, grad_gate_low, (((0,), (0,)), ((), ())), preferred_element_type=jnp.float32
    )
    first_term = lax.dot_general(
        grad_xin_low, inx_all, (((1,), (1,)), ((), ())), preferred_element_type=jnp.float32
    )
    second_term = lax.dot_general(
        grad_gate_low, inz_all, (((1,), (1,)), ((), ())), preferred_element_type=jnp.float32
    )
    grad_normed = lax.psum_scatter(
        first_term + second_term, "tensor", scatter_dimension=0, tiled=True
    )
    grad_rows_x, grad_gain_part = norm_back(grad_normed)
    grad_residual = cotangent + grad_rows_x
    grad_gain = lax.psum(grad_gain_part, "tensor")
    gain_shard, inx_shard, inz_shard, step_shard, out_shard = (
        lax.psum_scatter(grad_gain, "dp", scatter_dimension=0, tiled=True),
        lax.psum_scatter(grad_inx, "dp", scatter_dimension=0, tiled=True),
        lax.psum_scatter(grad_inz, "dp", scatter_dimension=0, tiled=True),
        lax.psum_scatter(grad_step_w, "dp", scatter_dimension=0, tiled=True),
        lax.psum_scatter(grad_out_w, "dp", scatter_dimension=0, tiled=True),
    )
    small_sums = lax.psum(
        (grad_xproj, grad_bias, grad_convw, grad_convb, grad_alog, grad_skip), "dp"
    )
    xproj_sum, bias_sum, convw_sum, convb_sum, alog_sum, skip_sum = small_sums
    return (
        block_out,
        grad_residual,
        gain_shard,
        inx_shard,
        inz_shard,
        xproj_sum,
        step_shard,
        bias_sum,
        convw_sum,
        convb_sum,
        alog_sum,
        skip_sum,
        out_shard,
        rms_resid,
        rms_mixed,
    )


def solution(mesh):
    placed = (
        P(("dp", "tensor"), None),
        P("dp"),
        P("dp", "tensor"),
        P("dp", "tensor"),
        P(None, "tensor"),
        P("dp", "tensor"),
        P("tensor"),
        P(None, "tensor"),
        P("tensor"),
        P(None, "tensor"),
        P("tensor"),
        P("dp", "tensor"),
        P("dp"),
        P(("dp", "tensor"), None),
    )
    return jax.shard_map(
        per_device_split if mesh.shape["dp"] == 4 * NZ else per_device,
        mesh=mesh,
        in_specs=placed,
        out_specs=(
            P(("dp", "tensor"), None),
            P(("dp", "tensor"), None),
            P("dp"),
            P("dp", "tensor"),
            P("dp", "tensor"),
            P(None, "tensor"),
            P("dp", "tensor"),
            P("tensor"),
            P(None, "tensor"),
            P("tensor"),
            P(None, "tensor"),
            P("tensor"),
            P("dp", "tensor"),
            P("dp"),
            P("dp"),
        ),
        check_vma=False,
    )
```

```python
import functools

import jax
import jax.numpy as jnp
from jax import lax
from jax.experimental import pallas as pl
from jax.experimental.pallas import tpu as pltpu
from jax.sharding import PartitionSpec as P

D = 2048
R = 128
N = 16

eps_norm = 1e-05


def sigmoid(v):
    return 1.0 / (1.0 + jnp.exp(-v))


def softplus(v):
    return jnp.maximum(v, 0.0) + jnp.log(1.0 + jnp.exp(-jnp.abs(v)))


def fold_rows(first, second, shift, lower):
    kept = jnp.where(lower, first, second)
    moved = jnp.where(lower, second, first)
    return kept + pltpu.roll(moved, shift, 0)


class RowSums:
    def __init__(self, masks):
        self.masks = masks
        self.held = {}
        self.result = None

    def add(self, token, value):
        level = 0
        while True:
            if level == 3:
                self.result = value
                return
            mate = (level, token ^ 1)
            if mate not in self.held:
                self.held[(level, token)] = value
                return
            other = self.held.pop(mate)
            first, second = (other, value) if token & 1 else (value, other)
            value = fold_rows(first, second, 1 << level, self.masks[level])
            token >>= 1
            level += 1


def split_dot(left, right_low, dims):
    high = left.astype(jnp.bfloat16)
    rest = (left - high.astype(jnp.float32)).astype(jnp.bfloat16)
    return lax.dot_general(high, right_low, dims, preferred_element_type=jnp.float32) + lax.dot_general(
        rest, right_low, dims, preferred_element_type=jnp.float32
    )


def scan_kernel(
    dbl_ref, conv_ref, gate_ref, gg_ref, dtp_ref, dtb_ref, alog_ref, skip_ref, keep_ref, in_ref, out_ref,
    gated_ref, ggate_ref, gconv_ref, gdbl_ref, gin_ref, gout_ref, gdtp_ref, gdtb_ref, galog_ref, gskip_ref,
    h_s, d_s, stepd_s, sc_s, gs_s, y_s, q_s, r_s, a_s,
):
    length, width = conv_ref.shape
    blocks = width // 128
    part = pl.program_id(0)
    sub = lax.broadcasted_iota(jnp.int32, (8, 128), 0)
    masks = [(sub & shift) == 0 for shift in (1, 2, 4)]
    lanes = [slice(b * 128, (b + 1) * 128) for b in range(blocks)]

    nn = (((1,), (0,)), ((), ()))
    step_raw = split_dot(dbl_ref[...], dtp_ref[...], nn) + dtb_ref[...]
    step = jnp.maximum(step_raw, 0.0) + jnp.log(1.0 + jnp.exp(-jnp.abs(step_raw)))
    stepd_s[...] = jnp.where(keep_ref[...] > 0.0, step, 1e30)
    sc_s[...] = step * conv_ref[...].astype(jnp.float32)
    gate = gate_ref[...]
    gs_s[...] = gg_ref[...] * gate * sigmoid(gate)
    a_s[...] = -jnp.exp(alog_ref[...])

    h_s[0] = jnp.zeros((N, width), jnp.float32)

    def forward(i, hs):
        base = pl.multiple_of(i * 8, 8)
        hs = list(hs)
        sums = [RowSums(masks) for _ in range(blocks)]
        stepd = [stepd_s[pl.ds(base, 8), lanes[b]] for b in range(blocks)]
        drive = [sc_s[pl.ds(base, 8), lanes[b]] for b in range(blocks)]
        for j in range(8):
            t = base + j
            in_t = in_ref[t]
            out_t = out_ref[t]
            for b in range(blocks):
                decay = jnp.exp(stepd[b][j : j + 1] * a_s[:, lanes[b]])
                hs[b] = decay * hs[b] + drive[b][j : j + 1] * in_t
                d_s[t, :, lanes[b]] = decay
                h_s[t + 1, :, lanes[b]] = hs[b]
                read = hs[b] * out_t
                sums[b].add(j, read[:8] + read[8:])
        for b in range(blocks):
            y_s[pl.ds(base, 8), lanes[b]] = sums[b].result
        return tuple(hs)

    zero = jnp.zeros((N, 128), jnp.float32)
    lax.fori_loop(0, length // 8, forward, (zero,) * blocks)

    conv = conv_ref[...].astype(jnp.float32)
    gate = gate_ref[...]
    sig = sigmoid(gate)
    scanned = y_s[...] + skip_ref[...] * conv
    gated_ref[...] = (scanned * gate * sig).astype(jnp.bfloat16)
    ggate_ref[...] = (gg_ref[...] * scanned * sig * (1.0 + gate * (1.0 - sig))).astype(jnp.bfloat16)

    @pl.when(part == 0)
    def _():
        gin_ref[...] = jnp.zeros_like(gin_ref)
        gout_ref[...] = jnp.zeros_like(gout_ref)
        gdbl_ref[...] = jnp.zeros_like(gdbl_ref)

    def backward(i, carried):
        base = pl.multiple_of(length - 8 - i * 8, 8)
        pulled, alog_sum = list(carried[0]), list(carried[1])
        q_sums = [RowSums(masks) for _ in range(blocks)]
        r_sums = [RowSums(masks) for _ in range(blocks)]
        stepd = [stepd_s[pl.ds(base, 8), lanes[b]] for b in range(blocks)]
        drive = [sc_s[pl.ds(base, 8), lanes[b]] for b in range(blocks)]
        gs = [gs_s[pl.ds(base, 8), lanes[b]] for b in range(blocks)]
        for j in reversed(range(8)):
            t = base + j
            in_t = in_ref[t]
            out_t = out_ref[t]
            gin_t = gin_ref[t]
            gout_t = gout_ref[t]
            for b in range(blocks):
                gs_t = gs[b][j : j + 1]
                adjoint = pulled[b] + out_t * gs_t
                gout_t = gout_t + gs_t * h_s[t + 1, :, lanes[b]]
                gin_t = gin_t + adjoint * drive[b][j : j + 1]
                q_t = adjoint * in_t
                q_sums[b].add(j, q_t[:8] + q_t[8:])
                pulled[b] = d_s[t, :, lanes[b]] * adjoint
                past = pulled[b] * h_s[t, :, lanes[b]]
                r_t = past * a_s[:, lanes[b]]
                r_sums[b].add(j, r_t[:8] + r_t[8:])
                alog_sum[b] = alog_sum[b] + past * stepd[b][j : j + 1]
            gin_ref[t] = gin_t
            gout_ref[t] = gout_t
        for b in range(blocks):
            q_s[pl.ds(base, 8), lanes[b]] = q_sums[b].result
            r_s[pl.ds(base, 8), lanes[b]] = r_sums[b].result
        return tuple(pulled), tuple(alog_sum)

    _, alog_sum = lax.fori_loop(0, length // 8, backward, ((zero,) * blocks, (zero,) * blocks))
    for b in range(blocks):
        galog_ref[:, lanes[b]] = alog_sum[b] * a_s[:, lanes[b]]

    conv = conv_ref[...].astype(jnp.float32)
    step_raw = split_dot(dbl_ref[...], dtp_ref[...], nn) + dtb_ref[...]
    step = jnp.maximum(step_raw, 0.0) + jnp.log(1.0 + jnp.exp(-jnp.abs(step_raw)))
    raw = (conv * q_s[...] + r_s[...]) * sigmoid(step_raw)
    gs = gs_s[...]
    gconv_ref[...] = step * q_s[...] + skip_ref[...] * gs
    gskip_ref[...] = jnp.sum(gs * conv, axis=0, keepdims=True)
    gdtb_ref[...] = jnp.sum(raw, axis=0, keepdims=True)
    raw_low = raw.astype(jnp.bfloat16)
    gdtp_ref[...] = lax.dot_general(
        dbl_ref[...].astype(jnp.bfloat16), raw_low, (((0,), (0,)), ((), ())), preferred_element_type=jnp.float32
    )
    gdbl_ref[...] += lax.dot_general(
        dtp_ref[...], raw_low, (((1,), (1,)), ((), ())), preferred_element_type=jnp.float32
    )


def scan_call(dbl, conv, gate, gg, dtp, dtb, alog, skip, keep):
    length, chans = conv.shape
    cb = min(65536 // length, chans)
    f32 = jnp.float32
    maps = jnp.broadcast_to(dbl[:, R:, None], (length, 2 * N, 128))
    tokens = lambda kind: (jax.ShapeDtypeStruct((length, chans), kind), pl.BlockSpec((length, cb), lambda i: (0, i)))
    whole = lambda *shape: (jax.ShapeDtypeStruct(shape, f32), pl.BlockSpec(shape, lambda i: (0,) * len(shape)))
    rows = lambda count: (jax.ShapeDtypeStruct((count, chans), f32), pl.BlockSpec((count, cb), lambda i: (0, i)))
    outs = [
        tokens(jnp.bfloat16), tokens(jnp.bfloat16), tokens(f32), whole(R, length), whole(length, N, 128), whole(length, N, 128),
        rows(R), rows(1), rows(N), rows(1),
    ]
    ins = [
        whole(length, R), tokens(f32), tokens(f32), tokens(f32), rows(R), rows(1), rows(N), rows(1),
        whole(length, 1),
    ]
    res = pl.pallas_call(
        scan_kernel,
        grid=(chans // cb,),
        in_specs=[spec for _, spec in ins] + [
            pl.BlockSpec((length, N, 128), lambda i: (0, 0, 0)), pl.BlockSpec((length, N, 128), lambda i: (0, 1, 0))],
        out_specs=[spec for _, spec in outs],
        out_shape=[shape for shape, _ in outs],
        scratch_shapes=[
            pltpu.VMEM((length + 1, N, cb), f32), pltpu.VMEM((length, N, cb), f32),
        ] + [pltpu.VMEM((length, cb), f32)] * 6 + [pltpu.VMEM((N, cb), f32)],
        name="selective_scan",
        compiler_params=pltpu.CompilerParams(vmem_limit_bytes=60 << 20),
    )(dbl[:, :R], conv, gate, gg, dtp, dtb[None], alog, skip[None], keep[:, None], maps, maps)
    gated, ggate, gconv, gdbl, gin, gout, gdtp, gdtb, galog, gskip = res
    gdbl_all = jnp.concatenate([gdbl, jnp.sum(gin, -1).T, jnp.sum(gout, -1).T], axis=0)
    return gated, ggate, gconv, gdbl_all, gdtp, gdtb[0], galog, gskip[0]


MESH = pl.DeviceIdType.MESH
NZ = 4
F32 = jnp.float32
BF16 = jnp.bfloat16
NN = (((1,), (0,)), ((), ()))
NT = (((1,), (1,)), ((), ()))
TN = (((0,), (0,)), ((), ()))


def dot(left, right, dims=NN):
    return lax.dot_general(left, right, dims, preferred_element_type=F32)


def place(z, x, c):
    return (z * 2 + x) * 2 + c


class Spot:
    def __init__(self):
        self.dp = lax.axis_index("dp")
        self.y = lax.axis_index("tensor")
        self.z, self.x, self.c = self.dp // 4, (self.dp // 2) % 2, self.dp % 2
        self.x_mate = (place(self.z, 1 - self.x, self.c), self.y)
        self.c_mate = (place(self.z, self.x, 1 - self.c), self.y)
        self.y_mate = (self.dp, 1 - self.y)

        far, near = jnp.where(self.z < 2, 3, 0), 1 + self.z % 2
        self.others = [far, 6 - self.z - far - near, near]

    def turn(self, k):
        return self.others[k - 1] if k else self.z

    def z_at(self, offset):
        return lax.rem(self.z + offset + NZ, NZ)

    def slot(self, origin, device):
        if device is self.c_mate:
            return 2 * NZ
        return origin // 4 + (NZ if device is self.x_mate else 0)

    def on_line(self, z, y=None):
        return (place(z, self.x, self.c), self.y if y is None else y)


def greet(devices):
    barrier = pltpu.get_barrier_semaphore()
    for device in devices:
        pl.semaphore_signal(barrier, inc=1, device_id=device, device_id_type=MESH)
    pl.semaphore_wait(barrier, len(devices))


class Copies:
    def __init__(self, send_sems, own_sems):
        self.send_sems, self.own_sems = send_sems, own_sems
        self.used, self.groups, self.begun, self.kept = 0, [], [], []

    def new_sem(self):
        self.used += 1
        return self.send_sems.at[self.used - 1]

    def group(self, whole):
        sem = self.new_sem()
        self.groups.append((sem, pltpu.make_async_copy(whole, whole, sem).wait))
        return sem

    def settle(self, *sems):
        for sem, wait in self.groups:
            if any(sem is one for one in sems):
                wait()
        self.groups = [(sem, wait) for sem, wait in self.groups if all(sem is not one for one in sems)]

    def send(self, src, dst, recv_sem, device, when=None, group=None):
        copy = pltpu.make_async_remote_copy(
            src_ref=src, dst_ref=dst, send_sem=self.new_sem() if group is None else group, recv_sem=recv_sem,
            device_id=device, device_id_type=MESH,
        )
        if group is None:
            self.begun.append((when, copy.wait_send))
        if when is None:
            copy.start()
        else:
            pl.when(when)(copy.start)

    def keep(self, src, dst):
        copy = pltpu.make_async_copy(src, dst, self.own_sems.at[len(self.kept)])
        copy.start()
        self.kept.append(copy)

    def wait_sent(self):
        self.settle(*[sem for sem, _ in self.groups])
        self.settle_alone(self.begun)
        for copy in self.kept:
            copy.wait()

    def settle_alone(self, begun):
        for when, wait in begun:
            if when is None:
                wait()
            else:
                pl.when(when)(wait)
        self.begun = [one for one in self.begun if all(one is not done for done in begun)]


def arrived(dst, recv_sem, when=None):
    copy = pltpu.make_async_copy(dst, dst, recv_sem)
    if when is None:
        copy.wait()
    else:
        pl.when(when)(copy.wait)


class Gather:
    def __init__(self, spot, copies, src, dst, recv_sems, own_sem):
        self.spot, self.copies, self.src, self.dst, self.recv_sems, self.own_sem = spot, copies, src, dst, recv_sems, own_sem
        self.width = dst.shape[-1]
        self.group = copies.group(dst.at[pl.ds(0, 4 * NZ - 1)])

    def columns(self, z):
        return self.src.at[:, pl.ds(pl.multiple_of(z * self.width, self.width), self.width)]

    def push(self, offsets=(1, 2, 3, 0)):
        spot, me = self.spot, self.spot.dp
        for offset in offsets:
            if offset == 0:
                self.push_own()
                continue
            z = spot.turn(offset)
            self.copies.send(self.columns(z), self.dst.at[me], self.recv_sems.at[spot.z], spot.on_line(z), group=self.group)

    def push_own(self):
        spot, me = self.spot, self.spot.dp
        self.own = pltpu.make_async_copy(self.columns(spot.z), self.dst.at[me], self.own_sem)
        self.own.start()
        self.pass_on(me, spot.x_mate, self.columns(spot.z))
        self.pass_on(me, spot.c_mate, self.columns(spot.z))

    def pass_on(self, origin, device, src=None):
        sem = self.recv_sems.at[self.spot.slot(origin, device)]
        src = self.dst.at[origin] if src is None else src
        self.copies.send(src, self.dst.at[origin], sem, device, group=self.group)

    def first(self):
        spot = self.spot
        for offset in range(1, NZ):
            z = spot.turn(offset)
            origin = place(z, spot.x, spot.c)
            arrived(self.dst.at[origin], self.recv_sems.at[z])
            self.pass_on(origin, spot.x_mate)
            self.pass_on(origin, spot.c_mate)

    def second(self):
        spot = self.spot
        for offset in range(NZ):
            z = spot.turn(offset)
            origin = place(z, 1 - spot.x, spot.c)
            arrived(self.dst.at[origin], self.recv_sems.at[NZ + z])
            self.pass_on(origin, spot.c_mate)

    def last(self):
        self.own.wait()
        arrived(self.dst.at[pl.ds(0, 2 * NZ)], self.recv_sems.at[2 * NZ])


class LineSum:
    def __init__(self, spot, copies, part, landing, total, sems):
        self.spot, self.copies, self.part, self.landing, self.total, self.sems = spot, copies, part, landing, total, sems
        self.offsets = [(dz, dy) for dz in range(NZ) for dy in range(2) if dz + dy > 0]
        self.all_others = landing.at[pl.ds(0, len(self.offsets))]
        self.groups = [copies.group(self.all_others) for _ in range(2)]

    def there(self, dz, dy):
        return self.spot.z_at(dz), lax.rem(self.spot.y + dy, 2)

    def push(self):
        for k, (dz, dy) in enumerate(self.offsets):
            z, y = self.there(dz, dy)
            self.copies.send(self.part.at[z, y], self.landing.at[k], self.sems.at[0], self.spot.on_line(z, y), group=self.groups[0])

    def middle(self):
        own_z, own_y = self.spot.z, self.spot.y
        arrived(self.all_others, self.sems.at[0])
        summed = self.part[own_z, own_y].astype(F32)
        for k in range(len(self.offsets)):
            summed = summed + self.landing[k].astype(F32)
        self.total[own_z, own_y] = summed.astype(BF16)
        own = self.total.at[own_z, own_y]
        for dz, dy in self.offsets:
            self.copies.send(own, own, self.sems.at[1], self.spot.on_line(*self.there(dz, dy)), group=self.groups[1])

    def last(self):
        arrived(self.all_others, self.sems.at[1])


def column_masks(tile):
    return jnp.concatenate([tile] * 16, axis=0).T


class Share:
    def __init__(self, spot, copies, dst, recv_sems):
        self.spot, self.copies, self.dst, self.recv_sems = spot, copies, dst, recv_sems
        self.over_y, self.alone = copies.group(dst.at[pl.ds(0, NZ // 2)]), []

    def send(self, z, device, when=None):
        own = self.dst.at[z, self.spot.y]
        self.copies.send(own, own, self.recv_sems.at[z], device, when)
        self.alone.append(self.copies.begun[-1])

    def settle(self):
        self.copies.settle(self.over_y)
        self.copies.settle_alone(self.alone)

    def send_y(self, z, when=None):
        own = self.dst.at[z, self.spot.y]
        self.copies.send(own, own, self.recv_sems.at[NZ], self.spot.y_mate, when, self.over_y)

    def push(self):
        spot = self.spot
        self.send(spot.z, spot.on_line(spot.z_at(1)), spot.z < NZ - 1)
        self.send(spot.z, spot.on_line(spot.z_at(-1)), spot.z > 0)
        self.send_y(spot.z)

    def first(self, far):
        spot = self.spot
        for way in (1, -1):
            origin = spot.z_at(-way * far)
            comes = spot.z >= far if way == 1 else spot.z < NZ - far
            goes = comes & (spot.z < NZ - 1 if way == 1 else spot.z > 0)
            arrived(self.dst.at[origin, spot.y], self.recv_sems.at[origin], comes)
            if far < NZ - 1:
                self.send(origin, spot.on_line(spot.z_at(way)), goes)
            self.send_y(origin, comes)

    def last(self):
        arrived(self.dst.at[pl.ds(0, NZ // 2)], self.recv_sems.at[NZ])


class Scan:
    def __init__(self, a_s, stepd_s, drive_s, gs_s, read_s, q_s, r_s, state_s, pulled_s, alog_s, spread_s, sum_s, gmap_s):
        self.a_s, self.stepd_s, self.drive_s, self.gs_s = a_s, stepd_s, drive_s, gs_s
        self.read_s, self.q_s, self.r_s, self.state_s = read_s, q_s, r_s, state_s
        self.pulled_s, self.alog_s, self.spread_s, self.sum_s, self.gmap_s = pulled_s, alog_s, spread_s, sum_s, gmap_s
        sub = lax.broadcasted_iota(jnp.int32, (8, 128), 0)
        self.masks = [(sub & shift) == 0 for shift in (1, 2, 4)]
        self.lane = lax.broadcasted_iota(jnp.int32, (N, 128), 1)
        self.blocks = [slice(b * 128, (b + 1) * 128) for b in range(a_s.shape[1] // 128)]

    def place(self, i):
        base = pl.multiple_of(i * 8, 8)
        tile = pl.ds(pl.multiple_of((base // 128) * 128, 128), 128)
        return base, tile, lax.rem(base, 128)

    def spread(self, maps, shifted_s):
        rows = maps.shape[0]
        for i in range(maps.shape[1] // 8):
            tile, first = maps[:, i // 16 * 128 : (i // 16 + 1) * 128], i % 16 * 8
            shifted_s[i * rows : (i + 1) * rows] = pltpu.roll(tile, (128 - first) % 128, 1).astype(BF16)
        row = lax.broadcasted_iota(jnp.int32, (128, 8 * 128), 0)
        column = lax.broadcasted_iota(jnp.int32, (128, 8 * 128), 1)
        chosen = jnp.where(row == column // 128, 1.0, 0.0).astype(BF16)
        self.spread_s[...] = dot(shifted_s[...], chosen).reshape(self.spread_s.shape)

    def maps_at(self, i, j):
        lanes = slice(j * 128, (j + 1) * 128)
        return self.spread_s[i, :N, lanes], self.spread_s[i, N:, lanes]

    def forward(self, start, stop):
        def chunk(i, none):
            base = pl.multiple_of(i * 8, 8)
            for lanes in self.blocks:
                state = self.state_s[i, :, lanes]
                a = self.a_s[:, lanes]
                stepd, drive = self.stepd_s[pl.ds(base, 8), lanes], self.drive_s[pl.ds(base, 8), lanes]
                sums = RowSums(self.masks)
                for j in range(8):
                    in_map, out_map = self.maps_at(i, j)
                    state = jnp.exp(stepd[j : j + 1] * a) * state + drive[j : j + 1] * in_map
                    read = state * out_map
                    sums.add(j, read[:8] + read[8:])
                self.state_s[i + 1, :, lanes] = state
                self.read_s[pl.ds(base, 8), lanes] = sums.result
            return none

        lax.fori_loop(start, stop, chunk, 0)

    def backward(self, start, stop):
        def chunk(step, none):
            i = start + stop - 1 - step
            base, tile, first = self.place(i)
            for b, lanes in enumerate(self.blocks):
                a = self.a_s[:, lanes]
                stepd, drive = self.stepd_s[pl.ds(base, 8), lanes], self.drive_s[pl.ds(base, 8), lanes]
                gs = self.gs_s[pl.ds(base, 8), lanes]
                states, decays = [self.state_s[i, :, lanes]], []
                for j in range(8):
                    decays.append(jnp.exp(stepd[j : j + 1] * a))
                    states.append(decays[j] * states[j] + drive[j : j + 1] * self.maps_at(i, j)[0])
                pulled, alog = self.pulled_s[:, lanes], self.alog_s[:, lanes]
                q_sums, r_sums = RowSums(self.masks), RowSums(self.masks)
                for j in reversed(range(8)):
                    in_map, out_map = self.maps_at(i, j)
                    adjoint = pulled + out_map * gs[j : j + 1]
                    g_in, g_out = adjoint * drive[j : j + 1], states[j + 1] * gs[j : j + 1]
                    if b > 0:
                        g_in, g_out = g_in + self.sum_s[0, j], g_out + self.sum_s[1, j]
                    self.sum_s[0, j], self.sum_s[1, j] = g_in, g_out
                    q_t = adjoint * in_map
                    q_sums.add(j, q_t[:8] + q_t[8:])
                    pulled = decays[j] * adjoint
                    past = pulled * states[j]
                    r_t = past * a
                    r_sums.add(j, r_t[:8] + r_t[8:])
                    alog = alog + past * stepd[j : j + 1]
                self.pulled_s[:, lanes], self.alog_s[:, lanes] = pulled, alog
                self.q_s[pl.ds(base, 8), lanes] = q_sums.result
                self.r_s[pl.ds(base, 8), lanes] = r_sums.result
            for k in range(2):
                row = self.gmap_s[k * N : (k + 1) * N, tile]
                for j in range(8):
                    row = jnp.where(self.lane == first + j, jnp.sum(self.sum_s[k, j], axis=1, keepdims=True), row)
                self.gmap_s[k * N : (k + 1) * N, tile] = row
            return none

        lax.fori_loop(start, stop, chunk, 0)


class TokenSum:
    def __init__(self, spot, copies, part, y_land, z_land, y_sems, z_sems):
        self.spot, self.copies, self.part, self.y_land, self.z_land = spot, copies, part, y_land, z_land
        self.y_sems, self.z_sems = y_sems, z_sems
        self.group = copies.group(y_land)

    def push(self):
        spot = self.spot
        for far in (3, 2, 1):
            for way in (1, -1):
                self.over_y(spot.z_at(way * far), self.within(way, far))
        self.over_y(spot.z, None)

    def within(self, way, far):
        return self.spot.z < NZ - far if way == 1 else self.spot.z >= far

    def over_y(self, z, when):
        self.copies.send(self.part.at[z, 1 - self.spot.y], self.y_land.at[z], self.y_sems.at[z], self.spot.y_mate, when, self.group)

    def add(self, z, landed):
        part, y = self.part, self.spot.y
        part[z, y] = (part[z, y].astype(F32) + landed[...].astype(F32)).astype(BF16)

    def stage(self, far):
        spot = self.spot
        for side, way in enumerate((1, -1)):
            z = spot.z_at(way * far)
            goes = self.within(way, far)
            grown = goes & self.within(-way, 1)
            land, sem = self.z_land.at[side, z], self.z_sems.at[side, z]

            @pl.when(goes)
            def _(z=z):
                arrived(self.y_land.at[z], self.y_sems.at[z])
                self.add(z, self.y_land.at[z])

            if far < NZ - 1:

                @pl.when(grown)
                def _(z=z, land=land, sem=sem):
                    arrived(land, sem)
                    self.add(z, land)

            self.copies.send(self.part.at[z, spot.y], land, sem, spot.on_line(spot.z_at(way)), goes)

    def last(self):
        spot = self.spot
        z = spot.z
        arrived(self.y_land.at[z], self.y_sems.at[z])
        self.add(z, self.y_land.at[z])
        for side, way in enumerate((1, -1)):

            @pl.when(self.within(-way, 1))
            def _(land=self.z_land.at[side, z], sem=self.z_sems.at[side, z]):
                arrived(land, sem)
                self.add(z, land)

        return self.part[z, spot.y].astype(F32)


class RowSum:
    def __init__(self, spot, copies, part, c_land, x_land, z_land, c_sems, x_sems, z_sem):
        self.spot, self.copies, self.part = spot, copies, part
        self.c_land, self.x_land, self.z_land = c_land, x_land, z_land
        self.c_sems, self.x_sems, self.z_sem = c_sems, x_sems, z_sem
        self.groups = [copies.group(whole) for whole in (c_land, x_land, z_land.at[pl.ds(0, NZ - 1)])]

    def push(self):
        spot = self.spot
        for offset in (1, 2, 3, 0):
            z = spot.turn(offset)
            for x in range(2):
                self.copies.send(
                    self.part.at[place(z, x, 1 - spot.c)], self.c_land.at[z, x], self.c_sems.at[z], spot.c_mate, group=self.groups[0]
                )

    def add(self, z, x, landed):
        part, owner = self.part, place(z, x, self.spot.c)
        part[owner] = (part[owner].astype(F32) + landed.astype(F32)).astype(part.dtype)

    def second(self):
        spot = self.spot
        for offset in (1, 2, 3, 0):
            z = spot.turn(offset)
            arrived(self.c_land.at[z], self.c_sems.at[z])
            for x in range(2):
                self.add(z, x, self.c_land[z, x])
            self.copies.send(
                self.part.at[place(z, 1 - spot.x, spot.c)], self.x_land.at[z], self.x_sems.at[z], spot.x_mate, group=self.groups[1]
            )

    def third(self, offsets=(1, 2, 3, 0)):
        spot = self.spot
        for offset in offsets:
            z = spot.turn(offset)
            arrived(self.x_land.at[z], self.x_sems.at[z])
            self.add(z, spot.x, self.x_land[z])
            own = self.part.at[place(z, spot.x, spot.c)]
            if offset:
                self.copies.send(own, self.z_land.at[spot.z], self.z_sem, spot.on_line(z), group=self.groups[2])
            else:
                self.copies.keep(own, self.z_land.at[z])

    def last(self):
        arrived(self.z_land.at[pl.ds(0, NZ - 1)], self.z_sem)


class ChannelSum:
    def __init__(self, spot, copies, part, c_land, x_land, own, full, c_sem, x_sem, full_sems):
        self.spot, self.copies, self.part, self.own, self.full, self.full_sems = spot, copies, part, own, full, full_sems
        self.c_land, self.x_land, self.c_sem, self.x_sem = c_land, x_land, c_sem, x_sem
        self.group = copies.group(full.at[pl.ds(0, 4 * NZ - 1)])

    def push(self):
        self.copies.send(self.part.at[1 - self.spot.c], self.c_land, self.c_sem, self.spot.c_mate)

    def second(self):
        spot = self.spot
        arrived(self.c_land, self.c_sem)
        self.part[spot.c] = self.part[spot.c] + self.c_land[...]
        self.copies.send(self.part.at[spot.c, 1 - spot.x], self.x_land, self.x_sem, spot.x_mate)

    def spread(self, origin, device, src=None):
        src = self.full.at[origin] if src is None else src
        sem = self.full_sems.at[self.spot.slot(origin, device)]
        self.copies.send(src, self.full.at[origin], sem, device, group=self.group)

    def third(self):
        spot = self.spot
        arrived(self.x_land, self.x_sem)
        self.own[...] = (self.part[spot.c, spot.x] + self.x_land[...]).astype(BF16)
        for device in [spot.on_line(spot.z_at(offset)) for offset in (1, 2, 3)] + [spot.x_mate, spot.c_mate]:
            self.spread(spot.dp, device, self.own)
        self.copies.keep(self.own, self.full.at[spot.dp])

    def fourth(self):
        spot = self.spot
        for offset in (1, 2, 3):
            z = spot.z_at(-offset)
            origin = place(z, spot.x, spot.c)
            arrived(self.full.at[origin], self.full_sems.at[z])
            self.spread(origin, spot.x_mate)
            self.spread(origin, spot.c_mate)

    def fifth(self):
        spot = self.spot
        for offset in range(NZ):
            z = spot.z_at(-offset)
            origin = place(z, 1 - spot.x, spot.c)
            arrived(self.full.at[origin], self.full_sems.at[NZ + z])
            self.spread(origin, spot.c_mate)

    def last(self):
        arrived(self.full.at[pl.ds(0, 2 * NZ)], self.full_sems.at[2 * NZ])


class Held:
    def __init__(self, names, refs):
        for name, ref in zip(names, refs, strict=True):
            setattr(self, name, ref)


def block_scratch(half, feats, rows, chans, step_rows, width):
    tokens, n_dp, length = 2 * half * NZ, 4 * NZ, 2 * half
    vmem, dma = pltpu.VMEM, pltpu.SemaphoreType.DMA
    owners, steps = (n_dp, rows, chans), (n_dp, step_rows, chans)
    part = (NZ, 2, width // 2, length)
    small = (width + 32) // 4
    held = {
        "w": vmem((3, n_dp, rows, chans), BF16),
        "acts": vmem((2, NZ, 2, half, feats), BF16),
        "dtp_own": vmem((step_rows, chans * NZ), F32),
        "dtp": vmem((n_dp, step_rows, chans), F32),
        "info": vmem((n_dp, 8, 128), F32),
        "mask": vmem((NZ, length, 128), F32),
        "low": vmem((tokens, chans), BF16),
        "gated": vmem((tokens, chans), BF16),
        "ggate": vmem((tokens, chans), BF16),
    }
    for name in ("x_in", "pre", "gate", "gg", "raw", "stepd", "drive", "gs", "read"):
        held[name] = vmem((tokens, chans), F32)
    held |= {
        "a": vmem((N, chans), F32),
        "state": vmem((tokens // 8 + 1, N, chans), F32),
        "pulled": vmem((N, chans), F32),
        "alog": vmem((N, chans), F32),
        "spread": vmem((tokens // 8, 2 * N, 8 * 128), F32),
        "shifted": vmem((tokens // 8 * 2 * N, 128), BF16),
        "sum": vmem((2, 8, N, 128), F32),
        "gmap": vmem((2 * N, tokens), F32),
        "dbl": vmem((width, tokens), F32),
        "part": vmem((2,) + part, BF16),
        "landing": vmem((2, 2 * NZ) + part[2:], BF16),
        "total": vmem((2,) + part, BF16),
        "mixed": vmem((NZ, 2, half, feats), BF16),
        "outw": vmem(owners, BF16),
        "ginz": vmem(owners, BF16),
        "gdtp": vmem(steps, F32),
        "chan": vmem((2, 2, small, chans), F32),
        "y_land": vmem((2, NZ, half, feats), BF16),
        "z_land": vmem((2, 2, NZ, half, feats), BF16),
        "wc_land": vmem((3, NZ, 2, rows, chans), BF16),
        "wx_land": vmem((3, NZ, rows, chans), BF16),
        "dc_land": vmem((NZ, 2, step_rows, chans), F32),
        "dx_land": vmem((NZ, step_rows, chans), F32),
        "fc_land": vmem((2, small, chans), F32),
        "fx_land": vmem((small, chans), F32),
        "f_own": vmem((small, chans), BF16),
        "block": vmem((half, feats), F32),
        "gresid": vmem((half, feats), F32),
        "tile": vmem((4, 8, 128), F32),
        "gain_part": vmem((2, n_dp, 128), F32),
        "gain": vmem((n_dp, 8, 128), F32),
        "gain_total": vmem((8, 128), F32),
        "squares": vmem((2, 8, 128), F32),
        "gain_land": vmem((n_dp - 1, 8, 128), F32),
        "resid": vmem((half, feats), F32),
        "cot": vmem((half, feats), F32),
        "xproj": vmem((width, chans * NZ), BF16),
        "load_sems": dma((3,)),
        "send_sems": dma((56,)),
        "keep_sems": dma((9,)),
        "own_sems": dma((4,)),
        "w_sems": dma((4, 2 * NZ + 1)),
        "act_sems": dma((2, NZ + 1)),
        "info_sem": dma(()),
        "dbl_sems": dma((2, 2)),
        "y_sems": dma((2, NZ)),
        "z_sems": dma((2, 2, NZ)),
        "wc_sems": dma((4, NZ)),
        "wx_sems": dma((4, NZ)),
        "wz_sems": dma((4,)),
        "f_sems": dma((2,)),
        "full_sems": dma((2 * NZ + 1,)),
        "tile_sems": dma((2,)),
        "gain_sems": dma((2,)),
    }
    return held


def block_kernel(names, *refs):
    (
        inx_ref, inz_ref, outp_ref, resid_in, cot_in, xproj_in, gain_ref, ids_ref, dtp_ref, convw_ref, convb_ref, dtb_ref,
        alog_ref, skip_ref,
        block_ref, gresid_ref, ggain_ref, ginx_ref, ginz_ref, goutp_ref, gdtp_ref, full_ref, squares_ref,
    ) = refs[:23]
    s = Held(names, refs[23:])
    spot = Spot()
    resid_ref, cot_ref, xproj_ref = s.resid, s.cot, s.xproj
    loads = [
        pltpu.make_async_copy(src, dst, s.load_sems.at[k])
        for k, (src, dst) in enumerate(((resid_in, s.resid), (cot_in, s.cot), (xproj_in, s.xproj)))
    ]
    for load in loads:
        load.start()
    plane = [lax.rem(spot.dp + offset, 4 * NZ) for offset in range(1, 4 * NZ)]
    greet([(dp, spot.y) for dp in plane] + [spot.on_line(spot.z_at(dz), 1 - spot.y) for dz in range(NZ)])
    copies = Copies(s.send_sems, s.keep_sems)
    tokens, chans = s.x_in.shape
    half, feats = resid_ref.shape
    length = 2 * half
    columns = pl.ds(pl.multiple_of(spot.z * chans, chans), chans)
    quarters = [
        (slice(k * feats // NZ, (k + 1) * feats // NZ), slice(k * NZ, (k + 1) * NZ)) for k in range(NZ)
    ]
    sequences = [slice(k * length, (k + 1) * length) for k in range(NZ)]

    s.dtp_own[...] = dtp_ref[...].astype(F32)
    inx, inz, outp, dtp = (
        Gather(spot, copies, src, dst, s.w_sems.at[k], s.own_sems.at[k])
        for k, (src, dst) in enumerate(((inx_ref, s.w.at[0]), (inz_ref, s.w.at[1]), (outp_ref, s.w.at[2]), (s.dtp_own, s.dtp)))
    )
    normed, cot = (Share(spot, copies, s.acts.at[k], s.act_sems.at[k]) for k in range(2))

    ids = jnp.broadcast_to(ids_ref[...], (8, length))
    lane = lax.broadcasted_iota(jnp.int32, (8, length), 1)
    sub = lax.broadcasted_iota(jnp.int32, (8, length), 0)
    info = jnp.broadcast_to(gain_ref[...].astype(F32), (8, length))
    for back in range(1, 4):
        same = jnp.where((pltpu.roll(ids, back, 1) == ids) & (lane >= back), 1.0, 0.0)
        info = jnp.where(sub == back, same, info)
    s.info[spot.dp] = info
    other_info = s.info.at[pl.ds(0, 4 * NZ - 1)]
    info_group = copies.group(other_info)
    for dp in plane:
        copies.send(s.info.at[spot.dp], s.info.at[spot.dp], s.info_sem, (dp, spot.y), group=info_group)
    inx.push()

    loads[0].wait()
    resid = resid_ref[...]
    row_square = jnp.sum(resid * resid, axis=1, keepdims=True)
    scaled = resid * lax.rsqrt(row_square / feats + eps_norm)
    s.tile[0] = jnp.broadcast_to(jnp.sum(row_square, axis=0, keepdims=True), (8, 128))
    copies.send(s.tile.at[0], s.tile.at[1], s.tile_sems.at[0], spot.y_mate)
    arrived(other_info, s.info_sem)
    for k in range(4 * NZ):
        cols = slice(k * 128, (k + 1) * 128)
        s.acts[0, spot.z, spot.y, :, cols] = (scaled[:, cols] * s.info[k, 0:1, :]).astype(BF16)
    normed.push()
    dtp.push()
    loads[1].wait()
    loads[2].wait()
    s.acts[1, spot.z, spot.y] = cot_ref[...].astype(BF16)
    for k in range(NZ):
        s.mask[k] = column_masks(s.info[place(k, spot.x, spot.c)])
    inx.first()
    normed.first(1)
    inx.second()
    normed.first(2)
    inz.push()
    dtp.first()
    dtp.second()
    normed.first(3)
    cot.push()
    normed.last()
    inx.last()

    all_normed = s.acts[0].reshape(tokens, feats)
    s.x_in[...] = dot(all_normed, s.w[0].reshape(-1, chans))
    taps = convw_ref[:, columns]
    bias = convb_ref[:, columns]
    for k, rows in enumerate(sequences):
        one = s.x_in[rows]
        pre = bias + taps[3:4] * one
        for back in range(1, 4):
            pre = pre + taps[3 - back : 4 - back] * (pltpu.roll(one, back, 0) * s.mask[k, :, back : back + 1])
        s.pre[rows] = pre
        s.low[rows] = (pre * sigmoid(pre)).astype(BF16)
    x_proj = xproj_ref[:, columns]
    dbl = dot(x_proj, s.low[...], NT)
    blocks = [(k, y) for k in range(NZ) for y in range(2)]
    width = dbl.shape[0] // 2
    for k, y in blocks:
        s.part[0, k, y] = dbl[y * width : (y + 1) * width, sequences[k]].astype(BF16)
    x_dbl = LineSum(
        spot, copies, s.part.at[0], s.landing.at[0], s.total.at[0], s.dbl_sems.at[0]
    )
    x_dbl.push()
    inz.first()
    cot.first(1)
    x_dbl.middle()
    outp.push((1, 0))
    cot.first(2)
    x_dbl.last()
    outp.push((2, 3))

    dtp.last()
    for k, y in blocks:
        s.dbl[y * width : (y + 1) * width, sequences[k]] = s.total[0, k, y].astype(F32)
    step_w = s.dtp[...].reshape(R, chans).astype(BF16)
    s.raw[...] = dot(s.dbl[:R].astype(BF16), step_w, TN) + dtb_ref[:, columns]
    for k, rows in enumerate(sequences):
        step = softplus(s.raw[rows])
        s.stepd[rows] = jnp.where(s.mask[k, :, 1:2] > 0.0, step, 1e30)
        s.drive[rows] = step * s.low[rows].astype(F32)
    s.a[...] = -jnp.exp(alog_ref[:, columns])
    s.state[0] = jnp.zeros((N, chans), F32)
    scan = Scan(
        s.a, s.stepd, s.drive, s.gs, s.read, s.read, s.gate, s.state, s.pulled, s.alog, s.spread, s.sum, s.gmap
    )
    scan.spread(s.dbl[R : R + 2 * N], s.shifted)
    steps = tokens // 8
    eighth = steps // 8
    inz.second()
    scan.forward(0, 4 * eighth)
    cot.first(3)
    outp.first()
    scan.forward(4 * eighth, steps)
    inz.last()
    s.gate[...] = dot(s.acts[0].reshape(tokens, feats), s.w[1].reshape(-1, chans))
    skip = skip_ref[:, columns]
    for rows in sequences:
        gate = s.gate[rows]
        scanned = s.read[rows] + skip * s.low[rows].astype(F32)
        s.gated[rows] = (scanned * gate * sigmoid(gate)).astype(BF16)

    mixed_sum, normed_sum = (
        TokenSum(spot, copies, part, s.y_land.at[k], s.z_land.at[k], s.y_sems.at[k], s.z_sems.at[k])
        for k, part in enumerate((s.mixed, s.acts.at[1]))
    )
    outw_sum, ginz_sum, ginx_sum, gdtp_sum = (
        RowSum(spot, copies, part, c_land, x_land, out, s.wc_sems.at[k], s.wx_sems.at[k], s.wz_sems.at[k])
        for k, (part, c_land, x_land, out) in enumerate((
            (s.outw, s.wc_land.at[0], s.wx_land.at[0], goutp_ref),
            (s.ginz, s.wc_land.at[1], s.wx_land.at[1], ginz_ref),
            (s.w.at[2], s.wc_land.at[2], s.wx_land.at[2], ginx_ref),
            (s.gdtp, s.dc_land, s.dx_land, gdtp_ref),
        ))
    )
    cot.last()
    for cols, owners in quarters:
        given = s.acts[1, :, :, :, cols].reshape(tokens, -1)
        s.outw[owners] = dot(given, s.gated[...], TN).astype(BF16).reshape(-1, *s.outw.shape[1:])
    outw_sum.push()
    outp.second()
    outw_sum.second()
    outp.last()
    s.gg[...] = dot(s.acts[1].reshape(tokens, feats), s.w[2].reshape(-1, chans))
    outw_sum.third((1,))
    for cols, owners in quarters:
        part = dot(s.gated[...], s.w[2, owners].reshape(-1, chans), NT)
        s.mixed[:, :, :, cols] = part.astype(BF16).reshape(*s.mixed.shape[:3], -1)
    mixed_sum.push()
    for rows in sequences:
        gate, gg = s.gate[rows], s.gg[rows]
        sig = sigmoid(gate)
        scanned = s.read[rows] + skip * s.low[rows].astype(F32)
        s.gs[rows] = gg * gate * sig
        s.ggate[rows] = (gg * scanned * sig * (1.0 + gate * (1.0 - sig))).astype(BF16)
    for cols, owners in quarters:
        given = s.acts[0, :, :, :, cols].reshape(tokens, -1)
        s.ginz[owners] = dot(given, s.ggate[...], TN).astype(BF16).reshape(-1, *s.ginz.shape[1:])
    ginz_sum.push()

    s.pulled[...] = jnp.zeros_like(s.pulled)
    s.alog[...] = jnp.zeros_like(s.alog)
    scan.backward(7 * eighth, steps)
    outw_sum.third((2,))
    ginz_sum.second()
    scan.backward(6 * eighth, 7 * eighth)
    outw_sum.third((3, 0))
    mixed_sum.stage(3)
    scan.backward(4 * eighth, 6 * eighth)
    ginz_sum.third((1,))
    scan.backward(2 * eighth, 4 * eighth)
    ginz_sum.third((2,))
    scan.backward(0, 2 * eighth)
    grad_bias = jnp.zeros((1, chans), F32)
    grad_skip = jnp.zeros((1, chans), F32)
    raw_rows = []
    for rows in sequences:
        conv, raw, gs, q = s.low[rows].astype(F32), s.raw[rows], s.gs[rows], s.read[rows]
        grad_raw = (conv * q + s.gate[rows]) * sigmoid(raw)
        s.gg[rows] = softplus(raw) * q + skip * gs
        grad_bias = grad_bias + jnp.sum(grad_raw, axis=0, keepdims=True)
        grad_skip = grad_skip + jnp.sum(gs * conv, axis=0, keepdims=True)
        raw_rows.append(grad_raw.astype(BF16))
    raw_low = jnp.concatenate(raw_rows, axis=0)
    dbl = jnp.concatenate([dot(step_w, raw_low, NT), s.gmap[...]], axis=0)
    for k, y in blocks:
        s.part[1, k, y] = dbl[y * width : (y + 1) * width, sequences[k]].astype(BF16)
    grad_dbl_sum = LineSum(
        spot, copies, s.part.at[1], s.landing.at[1], s.total.at[1], s.dbl_sems.at[1]
    )
    grad_dbl_sum.push()
    s.gdtp[...] = dot(s.dbl[:R].astype(BF16), raw_low).reshape(s.gdtp.shape)
    gdtp_sum.push()
    grad_dbl_sum.middle()
    ginz_sum.third((3, 0))
    mixed_sum.stage(2)
    gdtp_sum.second()
    grad_dbl_sum.last()

    grad_dbl = jnp.concatenate(
        [jnp.concatenate([s.total[1, k, y] for k in range(NZ)], axis=1) for y in range(2)], axis=0
    )
    s.gg[...] += dot(grad_dbl, x_proj, TN)
    sums = [jnp.zeros((1, chans), F32) for _ in range(5)]
    low_rows = []
    for k, rows in enumerate(sequences):
        pre, x_one = s.pre[rows], s.x_in[rows]
        sig = sigmoid(pre)
        one = s.gg[rows] * sig * (1.0 + pre * (1.0 - sig))
        sums[3] = sums[3] + jnp.sum(one * x_one, axis=0, keepdims=True)
        sums[4] = sums[4] + jnp.sum(one, axis=0, keepdims=True)
        grad_x = taps[3:4] * one
        for back in range(1, 4):
            masked = one * s.mask[k, :, back : back + 1]
            sums[3 - back] = sums[3 - back] + jnp.sum(masked * pltpu.roll(x_one, back, 0), axis=0, keepdims=True)
            grad_x = grad_x + taps[3 - back : 4 - back] * pltpu.roll(masked, length - back, 0)
        low_rows.append(grad_x.astype(BF16))
    grad_xin = jnp.concatenate(low_rows, axis=0)
    copies.settle(outp.group)
    for cols, owners in quarters:
        given = s.acts[0, :, :, :, cols].reshape(tokens, -1)
        s.w[2, owners] = dot(given, grad_xin, TN).astype(BF16).reshape(-1, *s.outw.shape[1:])
    ginx_sum.push()
    cot.settle()
    for cols, owners in quarters:
        part = dot(grad_xin, s.w[0, owners].reshape(-1, chans), NT) + dot(s.ggate[...], s.w[1, owners].reshape(-1, chans), NT)
        s.acts[1, :, :, :, cols] = part.astype(BF16).reshape(*s.mixed.shape[:3], -1)
        gain_part = jnp.sum(part * s.acts[0, :, :, :, cols].reshape(tokens, -1).astype(F32), axis=0, keepdims=True)
        for k in range(NZ):
            owner = owners.start + k
            s.gain_part[0, owner : owner + 1] = gain_part[:, k * 128 : (k + 1) * 128] / s.info[owner, 0:1]
    copies.send(s.gain_part.at[0], s.gain_part.at[1], s.gain_sems.at[0], spot.y_mate)
    normed_sum.push()
    mixed_sum.stage(1)
    s.chan[...] = jnp.concatenate(
        [dot(grad_dbl, s.low[...]), s.alog[...] * s.a[...], grad_bias, grad_skip, jnp.zeros((6, chans), F32)]
        + sums + [jnp.zeros((3, chans), F32)], axis=0
    ).reshape(s.chan.shape)
    small_sum = ChannelSum(
        spot, copies, s.chan, s.fc_land, s.fx_land, s.f_own, full_ref, s.f_sems.at[0], s.f_sems.at[1], s.full_sems
    )
    small_sum.push()
    ginx_sum.second()
    gdtp_sum.third()
    ginx_sum.third((1,))
    normed_sum.stage(3)
    small_sum.second()
    ginx_sum.third((2,))
    arrived(s.gain_part.at[1], s.gain_sems.at[0])
    for k in range(4 * NZ):
        s.gain[k] = jnp.broadcast_to(s.gain_part[0, k : k + 1] + s.gain_part[1, k : k + 1], (8, 128))
    gain_group = copies.group(s.gain_land)
    for offset, dp in enumerate(plane):
        copies.send(s.gain.at[dp], s.gain_land.at[offset], s.gain_sems.at[1], (dp, spot.y), group=gain_group)
    normed_sum.stage(2)
    ginx_sum.third((3, 0))
    small_sum.third()
    normed_sum.stage(1)
    small_sum.fourth()

    mixed = mixed_sum.last()
    resid = resid_ref[...]
    s.block[...] = resid + mixed
    copies.keep(s.block, block_ref)
    s.tile[2] = jnp.broadcast_to(jnp.sum(jnp.sum(mixed * mixed, axis=1, keepdims=True), axis=0, keepdims=True), (8, 128))
    copies.send(s.tile.at[2], s.tile.at[3], s.tile_sems.at[1], spot.y_mate)
    small_sum.fifth()
    outw_sum.last()
    ginz_sum.last()
    gdtp_sum.last()
    arrived(s.tile.at[1], s.tile_sems.at[0])
    s.squares[0] = s.tile[0] + s.tile[1]
    arrived(s.tile.at[3], s.tile_sems.at[1])
    s.squares[1] = s.tile[2] + s.tile[3]
    copies.keep(s.squares, squares_ref)

    grad_rows = normed_sum.last()
    inv = lax.rsqrt(jnp.sum(resid * resid, axis=1, keepdims=True) / feats + eps_norm)
    scaled = resid * inv
    gain = jnp.concatenate([s.info[k, 0:1] for k in range(4 * NZ)], axis=1)
    grad_scaled = grad_rows * gain
    mean = jnp.sum(grad_scaled * scaled, axis=1, keepdims=True) / feats
    s.gresid[...] = cot_ref[...] + inv * (grad_scaled - scaled * mean)
    copies.keep(s.gresid, gresid_ref)
    arrived(s.gain_land, s.gain_sems.at[1])
    total = s.gain[spot.dp]
    for offset in range(4 * NZ - 1):
        total = total + s.gain_land[offset]
    s.gain_total[...] = total
    copies.keep(s.gain_total, ggain_ref)
    ginx_sum.last()
    small_sum.last()
    copies.wait_sent()
    assert copies.used == s.send_sems.shape[0], copies.used


def block_call(in_x, in_z, out_p, residual, cotangent, gain, ids, dt_p, x_proj, conv_w, conv_b, dt_b, a_log, d_skip):
    half, feats = residual.shape
    rows, wide = in_x.shape
    n_dp, chans = 4 * NZ, wide // NZ
    held = block_scratch(half, feats, rows, chans, dt_p.shape[0], x_proj.shape[0])
    shape = jax.ShapeDtypeStruct
    outs = [
        shape((half, feats), F32), shape((half, feats), F32), shape((8, 128), F32),
        shape((NZ, rows, chans), BF16), shape((NZ, rows, chans), BF16), shape((NZ, rows, chans), BF16),
        shape((NZ, dt_p.shape[0], chans), F32), shape((n_dp, (x_proj.shape[0] + 32) // 4, chans), BF16),
        shape((2, 8, 128), F32),
    ]
    in_any = pl.BlockSpec(memory_space=pl.ANY)
    in_vmem = pl.BlockSpec(memory_space=pltpu.VMEM)
    return pl.pallas_call(
        functools.partial(block_kernel, list(held)),
        out_shape=outs,
        in_specs=[in_any] * 6 + [in_vmem] * 8,
        out_specs=[in_any] * len(outs),
        scratch_shapes=list(held.values()),
        name="block",
        compiler_params=pltpu.CompilerParams(collective_id=1, has_side_effects=True, vmem_limit_bytes=62 << 20),
    )(in_x, in_z, out_p, residual, cotangent, x_proj, gain, ids, dt_p, conv_w, conv_b, dt_b, a_log, d_skip)


def finish_kernel(
    scale, block_in, gresid_in, ginx_in, ginz_in, goutp_in, gdtp_in, full_in, ggain_in, squares_in,
    block_ref, gresid_ref, ginx_ref, ginz_ref, goutp_ref, gdtp_ref, xproj_ref, alog_ref, dtb_ref, skip_ref, convw_ref, convb_ref,
    ggain_ref, rms_ref, mrms_ref,
    token_s, low_s, wide_s, step_s, full_s, xproj_s, in_sems, out_sems,
):
    begun = []

    def out(src, dst):
        copy = pltpu.make_async_copy(src, dst, out_sems.at[len(begun)])
        copy.start()
        begun.append(copy)

    reads = [
        pltpu.make_async_copy(src, dst, in_sems.at[k])
        for k, (src, dst) in enumerate(
            (
                (block_in, token_s.at[0]), (gresid_in, token_s.at[1]),
                (ginx_in, low_s.at[0]), (ginz_in, low_s.at[1]), (goutp_in, low_s.at[2]), (full_in, full_s), (gdtp_in, step_s),
            )
        )
    ]
    for read in reads:
        read.start()
    for k, ref in enumerate((block_ref, gresid_ref)):
        reads[k].wait()
        out(token_s.at[k], ref)
    ggain_ref[...] = ggain_in[0:1]
    rms_ref[...] = jnp.sqrt(squares_in[0, 0:1, 0:1] * scale)
    mrms_ref[...] = jnp.sqrt(squares_in[1, 0:1, 0:1] * scale)
    chans = low_s.shape[3]
    columns = [slice(z * chans, (z + 1) * chans) for z in range(NZ)]
    for k, ref in enumerate((ginx_ref, ginz_ref, goutp_ref)):
        reads[k + 2].wait()
        for z, cols in enumerate(columns):
            wide_s[k, :, cols] = low_s[k, z].astype(F32)
        out(wide_s.at[k], ref)
    reads[5].wait()
    rows, width = full_s.shape[1], xproj_s.shape[0]
    for z, cols in enumerate(columns):
        for k in range(4):
            found = full_s[place(z, k % 2, k // 2)].astype(F32)
            upto = min(rows, width - k * rows)
            xproj_s[k * rows : k * rows + upto, cols] = found[:upto]
        alog_ref[:, cols] = found[upto : upto + N]
        dtb_ref[:, cols] = found[upto + N : upto + N + 1]
        skip_ref[:, cols] = found[upto + N + 1 : upto + N + 2]
        convw_ref[:, cols] = found[upto + 24 : upto + 28]
        convb_ref[:, cols] = found[upto + 28 : upto + 29]
    out(xproj_s, xproj_ref)
    reads[6].wait()
    for z, cols in enumerate(columns):
        gdtp_ref[:, cols] = step_s[z]
    for copy in begun:
        copy.wait()


def finish_call(block, gresid, ginx, ginz, goutp, gdtp, full, ggain, squares, width):
    rows, chans = ginx.shape[1:]
    wide = chans * NZ
    shape = lambda count, columns=wide: jax.ShapeDtypeStruct((count, columns), F32)
    vmem, dma = pltpu.VMEM, pltpu.SemaphoreType.DMA
    in_any, in_vmem = pl.BlockSpec(memory_space=pl.ANY), pl.BlockSpec(memory_space=vmem)
    return pl.pallas_call(
        functools.partial(finish_kernel, 1.0 / (2 * block.shape[0] * block.shape[1])),
        out_shape=[
            shape(*block.shape), shape(*gresid.shape), shape(rows), shape(rows), shape(rows), shape(gdtp.shape[1]), shape(width),
            shape(N), shape(1), shape(1), shape(4), shape(1), shape(1, 128), shape(1, 1), shape(1, 1),
        ],
        in_specs=[in_any] * 7 + [in_vmem] * 2,
        out_specs=[in_any] * 5 + [in_vmem] + [in_any] + [in_vmem] * 8,
        scratch_shapes=[
            vmem((2,) + block.shape, F32), vmem((3,) + ginx.shape, BF16), vmem((3, rows, wide), F32), vmem(gdtp.shape, F32), vmem(full.shape, BF16),
            vmem((width, wide), F32), dma((7,)), dma((6,)),
        ],
        name="finish",
        compiler_params=pltpu.CompilerParams(vmem_limit_bytes=60 << 20),
    )(block, gresid, ginx, ginz, goutp, gdtp, full, ggain, squares)


def per_device_split(
    residual,
    norm_gain,
    in_proj_x,
    in_proj_z,
    x_proj,
    dt_proj,
    dt_bias,
    conv_weight,
    conv_bias,
    a_log,
    d_skip,
    out_proj,
    doc_ids,
    cotangent,
):
    parts = block_call(
        in_proj_x, in_proj_z, out_proj, residual, cotangent, norm_gain[None], doc_ids[None], dt_proj, x_proj, conv_weight,
        conv_bias[None], dt_bias[None], a_log, d_skip[None],
    )
    block, gresid, ggain, ginx, ginz, goutp, gdtp, full, squares = parts
    block, gresid, ginx, ginz, goutp, gdtp, g_xproj, g_alog, g_dtb, g_skip, g_convw, g_convb, ggain, rms, mrms = finish_call(
        block, gresid, ginx, ginz, goutp, gdtp, full, ggain, squares, x_proj.shape[0]
    )
    return (
        block,
        gresid,
        ggain[0],
        ginx,
        ginz,
        g_xproj,
        gdtp,
        g_dtb[0],
        g_convw,
        g_convb[0],
        g_alog,
        g_skip[0],
        goutp,
        rms[0],
        mrms[0],
    )


def norm_rows(values, gain_val):
    mean_square = jnp.mean(values * values, axis=1, keepdims=True)
    return values * lax.rsqrt(mean_square + eps_norm) * gain_val


def conv_local(x_in, doc_ids, conv_weight, conv_bias):
    kernel_len = conv_weight.shape[0]
    length = x_in.shape[0]
    padded = jnp.pad(x_in, ((kernel_len - 1, 0), (0, 0)))
    id_pad = jnp.concatenate([jnp.full((kernel_len - 1,), -1, jnp.int32), doc_ids])
    summed = conv_bias + jnp.zeros_like(x_in)
    for offset in range(kernel_len):
        same_doc = (id_pad[offset : offset + length] == doc_ids).astype(jnp.float32)
        summed = summed + conv_weight[offset] * padded[offset : offset + length] * same_doc[:, None]
    return summed


def per_device(
    residual,
    norm_gain,
    in_proj_x,
    in_proj_z,
    x_proj,
    dt_proj,
    dt_bias,
    conv_weight,
    conv_bias,
    a_log,
    d_skip,
    out_proj,
    doc_ids,
    cotangent,
):
    gathered = (
        lax.all_gather(norm_gain, "dp", axis=0, tiled=True),
        lax.all_gather(in_proj_x, "dp", axis=0, tiled=True),
        lax.all_gather(in_proj_z, "dp", axis=0, tiled=True),
        lax.all_gather(dt_proj, "dp", axis=0, tiled=True),
        lax.all_gather(out_proj, "dp", axis=0, tiled=True),
    )
    gain_all, inx_all, inz_all, step_all, out_all = gathered
    seq_len = doc_ids.shape[0]
    normed_f32, norm_back = jax.vjp(norm_rows, residual, gain_all.astype(jnp.float32))
    normed = lax.all_gather(normed_f32.astype(jnp.bfloat16), "tensor", axis=0, tiled=True)
    x_in = jnp.dot(normed, inx_all, preferred_element_type=jnp.float32)
    gate_in = jnp.dot(normed, inz_all, preferred_element_type=jnp.float32)

    def conv_act(x_val, weight_val, bias_val):
        return jax.nn.silu(conv_local(x_val, doc_ids, weight_val, bias_val))

    conv_out, conv_back = jax.vjp(conv_act, x_in, conv_weight, conv_bias)
    conv_low = conv_out.astype(jnp.bfloat16)
    dbl_part = lax.dot_general(
        conv_low, x_proj, (((1,), (1,)), ((), ())), preferred_element_type=jnp.float32
    )
    x_dbl, resid_square = lax.psum((dbl_part, jnp.sum(residual * residual)), "tensor")
    doc_starts = doc_ids != jnp.concatenate([jnp.full((1,), -1, jnp.int32), doc_ids[:-1]])
    carry_keep = 1.0 - doc_starts.astype(jnp.float32)

    cot_all = lax.all_gather(cotangent.astype(jnp.bfloat16), "tensor", axis=0, tiled=True)
    grad_gated = jnp.dot(cot_all, out_all, preferred_element_type=jnp.float32)
    gated_low, grad_gate_low, grad_conv, grad_dbl_part, grad_step_w, grad_bias, grad_alog, grad_skip = scan_call(
        x_dbl, conv_low, gate_in, grad_gated, step_all, dt_bias, a_log, d_skip, carry_keep
    )
    mixed = lax.psum_scatter(
        lax.dot_general(
            gated_low, out_all, (((1,), (1,)), ((), ())), preferred_element_type=jnp.float32
        ),
        "tensor",
        scatter_dimension=0,
        tiled=True,
    )
    block_out = residual + mixed
    mixed_square = lax.psum(jnp.sum(mixed * mixed), "tensor")
    rms_resid = jnp.sqrt(resid_square / (seq_len * D)).reshape(1)
    rms_mixed = jnp.sqrt(mixed_square / (seq_len * D)).reshape(1)
    grad_out_w = lax.dot_general(
        cot_all, gated_low, (((0,), (0,)), ((), ())), preferred_element_type=jnp.float32
    )
    grad_dbl = lax.psum(grad_dbl_part.T, "tensor")
    grad_dbl_low = grad_dbl.astype(jnp.bfloat16)
    grad_conv = grad_conv + jnp.dot(grad_dbl_low, x_proj, preferred_element_type=jnp.float32)
    grad_xproj = lax.dot_general(
        grad_dbl_low, conv_low, (((0,), (0,)), ((), ())), preferred_element_type=jnp.float32
    )
    grad_xin, grad_convw, grad_convb = conv_back(grad_conv)
    grad_xin_low = grad_xin.astype(jnp.bfloat16)
    grad_inx = lax.dot_general(
        normed, grad_xin_low, (((0,), (0,)), ((), ())), preferred_element_type=jnp.float32
    )
    grad_inz = lax.dot_general(
        normed, grad_gate_low, (((0,), (0,)), ((), ())), preferred_element_type=jnp.float32
    )
    first_term = lax.dot_general(
        grad_xin_low, inx_all, (((1,), (1,)), ((), ())), preferred_element_type=jnp.float32
    )
    second_term = lax.dot_general(
        grad_gate_low, inz_all, (((1,), (1,)), ((), ())), preferred_element_type=jnp.float32
    )
    grad_normed = lax.psum_scatter(
        first_term + second_term, "tensor", scatter_dimension=0, tiled=True
    )
    grad_rows_x, grad_gain_part = norm_back(grad_normed)
    grad_residual = cotangent + grad_rows_x
    grad_gain = lax.psum(grad_gain_part, "tensor")
    gain_shard, inx_shard, inz_shard, step_shard, out_shard = (
        lax.psum_scatter(grad_gain, "dp", scatter_dimension=0, tiled=True),
        lax.psum_scatter(grad_inx, "dp", scatter_dimension=0, tiled=True),
        lax.psum_scatter(grad_inz, "dp", scatter_dimension=0, tiled=True),
        lax.psum_scatter(grad_step_w, "dp", scatter_dimension=0, tiled=True),
        lax.psum_scatter(grad_out_w, "dp", scatter_dimension=0, tiled=True),
    )
    small_sums = lax.psum(
        (grad_xproj, grad_bias, grad_convw, grad_convb, grad_alog, grad_skip), "dp"
    )
    xproj_sum, bias_sum, convw_sum, convb_sum, alog_sum, skip_sum = small_sums
    return (
        block_out,
        grad_residual,
        gain_shard,
        inx_shard,
        inz_shard,
        xproj_sum,
        step_shard,
        bias_sum,
        convw_sum,
        convb_sum,
        alog_sum,
        skip_sum,
        out_shard,
        rms_resid,
        rms_mixed,
    )


def solution(mesh):
    placed = (
        P(("dp", "tensor"), None),
        P("dp"),
        P("dp", "tensor"),
        P("dp", "tensor"),
        P(None, "tensor"),
        P("dp", "tensor"),
        P("tensor"),
        P(None, "tensor"),
        P("tensor"),
        P(None, "tensor"),
        P("tensor"),
        P("dp", "tensor"),
        P("dp"),
        P(("dp", "tensor"), None),
    )
    return jax.shard_map(
        per_device_split if mesh.shape["dp"] == 4 * NZ else per_device,
        mesh=mesh,
        in_specs=placed,
        out_specs=(
            P(("dp", "tensor"), None),
            P(("dp", "tensor"), None),
            P("dp"),
            P("dp", "tensor"),
            P("dp", "tensor"),
            P(None, "tensor"),
            P("dp", "tensor"),
            P("tensor"),
            P(None, "tensor"),
            P("tensor"),
            P(None, "tensor"),
            P("tensor"),
            P("dp", "tensor"),
            P("dp"),
            P("dp"),
        ),
        check_vma=False,
    )
```

```python
import functools

import jax
import jax.numpy as jnp
from jax import lax
from jax.experimental import pallas as pl
from jax.experimental.pallas import tpu as pltpu
from jax.sharding import PartitionSpec as P

D = 2048
R = 128
N = 16

eps_norm = 1e-05


def sigmoid(v):
    return 1.0 / (1.0 + jnp.exp(-v))


def softplus(v):
    return jnp.maximum(v, 0.0) + jnp.log(1.0 + jnp.exp(-jnp.abs(v)))


def fold_rows(first, second, shift, lower):
    kept = jnp.where(lower, first, second)
    moved = jnp.where(lower, second, first)
    return kept + pltpu.roll(moved, shift, 0)


class RowSums:
    def __init__(self, masks):
        self.masks = masks
        self.held = {}
        self.result = None

    def add(self, token, value):
        level = 0
        while True:
            if level == 3:
                self.result = value
                return
            mate = (level, token ^ 1)
            if mate not in self.held:
                self.held[(level, token)] = value
                return
            other = self.held.pop(mate)
            first, second = (other, value) if token & 1 else (value, other)
            value = fold_rows(first, second, 1 << level, self.masks[level])
            token >>= 1
            level += 1


def split_dot(left, right_low, dims):
    high = left.astype(jnp.bfloat16)
    rest = (left - high.astype(jnp.float32)).astype(jnp.bfloat16)
    return lax.dot_general(high, right_low, dims, preferred_element_type=jnp.float32) + lax.dot_general(
        rest, right_low, dims, preferred_element_type=jnp.float32
    )


def scan_kernel(
    dbl_ref, conv_ref, gate_ref, gg_ref, dtp_ref, dtb_ref, alog_ref, skip_ref, keep_ref, in_ref, out_ref,
    gated_ref, ggate_ref, gconv_ref, gdbl_ref, gin_ref, gout_ref, gdtp_ref, gdtb_ref, galog_ref, gskip_ref,
    h_s, d_s, stepd_s, sc_s, gs_s, y_s, q_s, r_s, a_s,
):
    length, width = conv_ref.shape
    blocks = width // 128
    part = pl.program_id(0)
    sub = lax.broadcasted_iota(jnp.int32, (8, 128), 0)
    masks = [(sub & shift) == 0 for shift in (1, 2, 4)]
    lanes = [slice(b * 128, (b + 1) * 128) for b in range(blocks)]

    nn = (((1,), (0,)), ((), ()))
    step_raw = split_dot(dbl_ref[...], dtp_ref[...], nn) + dtb_ref[...]
    step = jnp.maximum(step_raw, 0.0) + jnp.log(1.0 + jnp.exp(-jnp.abs(step_raw)))
    stepd_s[...] = jnp.where(keep_ref[...] > 0.0, step, 1e30)
    sc_s[...] = step * conv_ref[...].astype(jnp.float32)
    gate = gate_ref[...]
    gs_s[...] = gg_ref[...] * gate * sigmoid(gate)
    a_s[...] = -jnp.exp(alog_ref[...])

    h_s[0] = jnp.zeros((N, width), jnp.float32)

    def forward(i, hs):
        base = pl.multiple_of(i * 8, 8)
        hs = list(hs)
        sums = [RowSums(masks) for _ in range(blocks)]
        stepd = [stepd_s[pl.ds(base, 8), lanes[b]] for b in range(blocks)]
        drive = [sc_s[pl.ds(base, 8), lanes[b]] for b in range(blocks)]
        for j in range(8):
            t = base + j
            in_t = in_ref[t]
            out_t = out_ref[t]
            for b in range(blocks):
                decay = jnp.exp(stepd[b][j : j + 1] * a_s[:, lanes[b]])
                hs[b] = decay * hs[b] + drive[b][j : j + 1] * in_t
                d_s[t, :, lanes[b]] = decay
                h_s[t + 1, :, lanes[b]] = hs[b]
                read = hs[b] * out_t
                sums[b].add(j, read[:8] + read[8:])
        for b in range(blocks):
            y_s[pl.ds(base, 8), lanes[b]] = sums[b].result
        return tuple(hs)

    zero = jnp.zeros((N, 128), jnp.float32)
    lax.fori_loop(0, length // 8, forward, (zero,) * blocks)

    conv = conv_ref[...].astype(jnp.float32)
    gate = gate_ref[...]
    sig = sigmoid(gate)
    scanned = y_s[...] + skip_ref[...] * conv
    gated_ref[...] = (scanned * gate * sig).astype(jnp.bfloat16)
    ggate_ref[...] = (gg_ref[...] * scanned * sig * (1.0 + gate * (1.0 - sig))).astype(jnp.bfloat16)

    @pl.when(part == 0)
    def _():
        gin_ref[...] = jnp.zeros_like(gin_ref)
        gout_ref[...] = jnp.zeros_like(gout_ref)
        gdbl_ref[...] = jnp.zeros_like(gdbl_ref)

    def backward(i, carried):
        base = pl.multiple_of(length - 8 - i * 8, 8)
        pulled, alog_sum = list(carried[0]), list(carried[1])
        q_sums = [RowSums(masks) for _ in range(blocks)]
        r_sums = [RowSums(masks) for _ in range(blocks)]
        stepd = [stepd_s[pl.ds(base, 8), lanes[b]] for b in range(blocks)]
        drive = [sc_s[pl.ds(base, 8), lanes[b]] for b in range(blocks)]
        gs = [gs_s[pl.ds(base, 8), lanes[b]] for b in range(blocks)]
        for j in reversed(range(8)):
            t = base + j
            in_t = in_ref[t]
            out_t = out_ref[t]
            gin_t = gin_ref[t]
            gout_t = gout_ref[t]
            for b in range(blocks):
                gs_t = gs[b][j : j + 1]
                adjoint = pulled[b] + out_t * gs_t
                gout_t = gout_t + gs_t * h_s[t + 1, :, lanes[b]]
                gin_t = gin_t + adjoint * drive[b][j : j + 1]
                q_t = adjoint * in_t
                q_sums[b].add(j, q_t[:8] + q_t[8:])
                pulled[b] = d_s[t, :, lanes[b]] * adjoint
                past = pulled[b] * h_s[t, :, lanes[b]]
                r_t = past * a_s[:, lanes[b]]
                r_sums[b].add(j, r_t[:8] + r_t[8:])
                alog_sum[b] = alog_sum[b] + past * stepd[b][j : j + 1]
            gin_ref[t] = gin_t
            gout_ref[t] = gout_t
        for b in range(blocks):
            q_s[pl.ds(base, 8), lanes[b]] = q_sums[b].result
            r_s[pl.ds(base, 8), lanes[b]] = r_sums[b].result
        return tuple(pulled), tuple(alog_sum)

    _, alog_sum = lax.fori_loop(0, length // 8, backward, ((zero,) * blocks, (zero,) * blocks))
    for b in range(blocks):
        galog_ref[:, lanes[b]] = alog_sum[b] * a_s[:, lanes[b]]

    conv = conv_ref[...].astype(jnp.float32)
    step_raw = split_dot(dbl_ref[...], dtp_ref[...], nn) + dtb_ref[...]
    step = jnp.maximum(step_raw, 0.0) + jnp.log(1.0 + jnp.exp(-jnp.abs(step_raw)))
    raw = (conv * q_s[...] + r_s[...]) * sigmoid(step_raw)
    gs = gs_s[...]
    gconv_ref[...] = step * q_s[...] + skip_ref[...] * gs
    gskip_ref[...] = jnp.sum(gs * conv, axis=0, keepdims=True)
    gdtb_ref[...] = jnp.sum(raw, axis=0, keepdims=True)
    raw_low = raw.astype(jnp.bfloat16)
    gdtp_ref[...] = lax.dot_general(
        dbl_ref[...].astype(jnp.bfloat16), raw_low, (((0,), (0,)), ((), ())), preferred_element_type=jnp.float32
    )
    gdbl_ref[...] += lax.dot_general(
        dtp_ref[...], raw_low, (((1,), (1,)), ((), ())), preferred_element_type=jnp.float32
    )


def scan_call(dbl, conv, gate, gg, dtp, dtb, alog, skip, keep):
    length, chans = conv.shape
    cb = min(65536 // length, chans)
    f32 = jnp.float32
    maps = jnp.broadcast_to(dbl[:, R:, None], (length, 2 * N, 128))
    tokens = lambda kind: (jax.ShapeDtypeStruct((length, chans), kind), pl.BlockSpec((length, cb), lambda i: (0, i)))
    whole = lambda *shape: (jax.ShapeDtypeStruct(shape, f32), pl.BlockSpec(shape, lambda i: (0,) * len(shape)))
    rows = lambda count: (jax.ShapeDtypeStruct((count, chans), f32), pl.BlockSpec((count, cb), lambda i: (0, i)))
    outs = [
        tokens(jnp.bfloat16), tokens(jnp.bfloat16), tokens(f32), whole(R, length), whole(length, N, 128), whole(length, N, 128),
        rows(R), rows(1), rows(N), rows(1),
    ]
    ins = [
        whole(length, R), tokens(f32), tokens(f32), tokens(f32), rows(R), rows(1), rows(N), rows(1),
        whole(length, 1),
    ]
    res = pl.pallas_call(
        scan_kernel,
        grid=(chans // cb,),
        in_specs=[spec for _, spec in ins] + [
            pl.BlockSpec((length, N, 128), lambda i: (0, 0, 0)), pl.BlockSpec((length, N, 128), lambda i: (0, 1, 0))],
        out_specs=[spec for _, spec in outs],
        out_shape=[shape for shape, _ in outs],
        scratch_shapes=[
            pltpu.VMEM((length + 1, N, cb), f32), pltpu.VMEM((length, N, cb), f32),
        ] + [pltpu.VMEM((length, cb), f32)] * 6 + [pltpu.VMEM((N, cb), f32)],
        name="selective_scan",
        compiler_params=pltpu.CompilerParams(vmem_limit_bytes=60 << 20),
    )(dbl[:, :R], conv, gate, gg, dtp, dtb[None], alog, skip[None], keep[:, None], maps, maps)
    gated, ggate, gconv, gdbl, gin, gout, gdtp, gdtb, galog, gskip = res
    gdbl_all = jnp.concatenate([gdbl, jnp.sum(gin, -1).T, jnp.sum(gout, -1).T], axis=0)
    return gated, ggate, gconv, gdbl_all, gdtp, gdtb[0], galog, gskip[0]


MESH = pl.DeviceIdType.MESH
NZ = 4
F32 = jnp.float32
BF16 = jnp.bfloat16
NN = (((1,), (0,)), ((), ()))
NT = (((1,), (1,)), ((), ()))
TN = (((0,), (0,)), ((), ()))


def dot(left, right, dims=NN):
    return lax.dot_general(left, right, dims, preferred_element_type=F32)


def place(z, x, c):
    return (z * 2 + x) * 2 + c


class Spot:
    def __init__(self):
        self.dp = lax.axis_index("dp")
        self.y = lax.axis_index("tensor")
        self.z, self.x, self.c = self.dp // 4, (self.dp // 2) % 2, self.dp % 2
        self.x_mate = (place(self.z, 1 - self.x, self.c), self.y)
        self.c_mate = (place(self.z, self.x, 1 - self.c), self.y)
        self.y_mate = (self.dp, 1 - self.y)

        far, near = jnp.where(self.z < 2, 3, 0), 1 + self.z % 2
        self.others = [far, 6 - self.z - far - near, near]

    def turn(self, k):
        return self.others[k - 1] if k else self.z

    def z_at(self, offset):
        return lax.rem(self.z + offset + NZ, NZ)

    def slot(self, origin, device):
        if device is self.c_mate:
            return 2 * NZ
        return origin // 4 + (NZ if device is self.x_mate else 0)

    def on_line(self, z, y=None):
        return (place(z, self.x, self.c), self.y if y is None else y)


def greet(devices):
    barrier = pltpu.get_barrier_semaphore()
    for device in devices:
        pl.semaphore_signal(barrier, inc=1, device_id=device, device_id_type=MESH)
    pl.semaphore_wait(barrier, len(devices))


class Copies:
    def __init__(self, send_sems, own_sems):
        self.send_sems, self.own_sems = send_sems, own_sems
        self.used, self.groups, self.begun, self.kept = 0, [], [], []

    def new_sem(self):
        self.used += 1
        return self.send_sems.at[self.used - 1]

    def group(self, whole):
        sem = self.new_sem()
        self.groups.append((sem, pltpu.make_async_copy(whole, whole, sem).wait))
        return sem

    def settle(self, *sems):
        for sem, wait in self.groups:
            if any(sem is one for one in sems):
                wait()
        self.groups = [(sem, wait) for sem, wait in self.groups if all(sem is not one for one in sems)]

    def send(self, src, dst, recv_sem, device, when=None, group=None):
        copy = pltpu.make_async_remote_copy(
            src_ref=src, dst_ref=dst, send_sem=self.new_sem() if group is None else group, recv_sem=recv_sem,
            device_id=device, device_id_type=MESH,
        )
        if group is None:
            self.begun.append((when, copy.wait_send))
        if when is None:
            copy.start()
        else:
            pl.when(when)(copy.start)

    def keep(self, src, dst):
        copy = pltpu.make_async_copy(src, dst, self.own_sems.at[len(self.kept)])
        copy.start()
        self.kept.append(copy)

    def wait_sent(self):
        self.settle(*[sem for sem, _ in self.groups])
        self.settle_alone(self.begun)
        for copy in self.kept:
            copy.wait()

    def settle_alone(self, begun):
        for when, wait in begun:
            if when is None:
                wait()
            else:
                pl.when(when)(wait)
        self.begun = [one for one in self.begun if all(one is not done for done in begun)]


def arrived(dst, recv_sem, when=None):
    copy = pltpu.make_async_copy(dst, dst, recv_sem)
    if when is None:
        copy.wait()
    else:
        pl.when(when)(copy.wait)


class Gather:
    def __init__(self, spot, copies, src, dst, recv_sems, own_sem):
        self.spot, self.copies, self.src, self.dst, self.recv_sems, self.own_sem = spot, copies, src, dst, recv_sems, own_sem
        self.width = dst.shape[-1]
        self.group = copies.group(dst.at[pl.ds(0, 4 * NZ - 1)])

    def columns(self, z):
        return self.src.at[:, pl.ds(pl.multiple_of(z * self.width, self.width), self.width)]

    def push(self, offsets=(1, 2, 3, 0)):
        spot, me = self.spot, self.spot.dp
        for offset in offsets:
            if offset == 0:
                self.push_own()
                continue
            z = spot.turn(offset)
            self.copies.send(self.columns(z), self.dst.at[me], self.recv_sems.at[spot.z], spot.on_line(z), group=self.group)

    def push_own(self):
        spot, me = self.spot, self.spot.dp
        self.own = pltpu.make_async_copy(self.columns(spot.z), self.dst.at[me], self.own_sem)
        self.own.start()
        self.pass_on(me, spot.x_mate, self.columns(spot.z))
        self.pass_on(me, spot.c_mate, self.columns(spot.z))

    def pass_on(self, origin, device, src=None):
        sem = self.recv_sems.at[self.spot.slot(origin, device)]
        src = self.dst.at[origin] if src is None else src
        self.copies.send(src, self.dst.at[origin], sem, device, group=self.group)

    def first(self):
        spot = self.spot
        for offset in range(1, NZ):
            z = spot.turn(offset)
            origin = place(z, spot.x, spot.c)
            arrived(self.dst.at[origin], self.recv_sems.at[z])
            self.pass_on(origin, spot.x_mate)
            self.pass_on(origin, spot.c_mate)

    def second(self):
        spot = self.spot
        for offset in range(NZ):
            z = spot.turn(offset)
            origin = place(z, 1 - spot.x, spot.c)
            arrived(self.dst.at[origin], self.recv_sems.at[NZ + z])
            self.pass_on(origin, spot.c_mate)

    def last(self):
        self.own.wait()
        arrived(self.dst.at[pl.ds(0, 2 * NZ)], self.recv_sems.at[2 * NZ])


class BlockGather(Gather):
    def columns(self, z):
        return self.src.at[z]


def fold_columns(values):
    half = values.shape[-1] // 2
    return jnp.concatenate([values[..., :half], values[..., half:]], axis=-2)


def unfold_columns(values):
    rows = values.shape[-2] // 2
    return jnp.concatenate([values[..., :rows, :], values[..., rows:, :]], axis=-1)


class LineSum:
    def __init__(self, spot, copies, part, landing, total, sems):
        self.spot, self.copies, self.part, self.landing, self.total, self.sems = spot, copies, part, landing, total, sems
        self.offsets = [(dz, dy) for dz in range(NZ) for dy in range(2) if dz + dy > 0]
        self.all_others = landing.at[pl.ds(0, len(self.offsets))]
        self.groups = [copies.group(self.all_others) for _ in range(2)]

    def there(self, dz, dy):
        return self.spot.z_at(dz), lax.rem(self.spot.y + dy, 2)

    def push(self):
        for k, (dz, dy) in enumerate(self.offsets):
            z, y = self.there(dz, dy)
            self.copies.send(self.part.at[z, y], self.landing.at[k], self.sems.at[0], self.spot.on_line(z, y), group=self.groups[0])

    def middle(self):
        own_z, own_y = self.spot.z, self.spot.y
        arrived(self.all_others, self.sems.at[0])
        summed = self.part[own_z, own_y].astype(F32)
        for k in range(len(self.offsets)):
            summed = summed + self.landing[k].astype(F32)
        self.total[own_z, own_y] = summed.astype(BF16)
        own = self.total.at[own_z, own_y]
        for dz, dy in self.offsets:
            self.copies.send(own, own, self.sems.at[1], self.spot.on_line(*self.there(dz, dy)), group=self.groups[1])

    def last(self):
        arrived(self.all_others, self.sems.at[1])


def column_masks(tile):
    return jnp.concatenate([tile] * 16, axis=0).T


class Share:
    def __init__(self, spot, copies, dst, recv_sems):
        self.spot, self.copies, self.dst, self.recv_sems = spot, copies, dst, recv_sems
        self.over_y, self.alone = copies.group(dst.at[pl.ds(0, NZ // 2)]), []

    def send(self, z, device, when=None):
        own = self.dst.at[z, self.spot.y]
        self.copies.send(own, own, self.recv_sems.at[z], device, when)
        self.alone.append(self.copies.begun[-1])

    def settle(self):
        self.copies.settle(self.over_y)
        self.copies.settle_alone(self.alone)

    def send_y(self, z, when=None):
        own = self.dst.at[z, self.spot.y]
        self.copies.send(own, own, self.recv_sems.at[NZ], self.spot.y_mate, when, self.over_y)

    def push(self, over_y=True):
        spot = self.spot
        self.send(spot.z, spot.on_line(spot.z_at(1)), spot.z < NZ - 1)
        self.send(spot.z, spot.on_line(spot.z_at(-1)), spot.z > 0)
        if over_y:
            self.send_y(spot.z)

    def first(self, far):
        spot = self.spot
        for way in (1, -1):
            origin = spot.z_at(-way * far)
            comes = spot.z >= far if way == 1 else spot.z < NZ - far
            goes = comes & (spot.z < NZ - 1 if way == 1 else spot.z > 0)
            arrived(self.dst.at[origin, spot.y], self.recv_sems.at[origin], comes)
            if far < NZ - 1:
                self.send(origin, spot.on_line(spot.z_at(way)), goes)
            self.send_y(origin, comes)

    def last(self):
        arrived(self.dst.at[pl.ds(0, NZ // 2)], self.recv_sems.at[NZ])


class Scan:
    def __init__(self, a_s, stepd_s, drive_s, gs_s, read_s, q_s, r_s, state_s, pulled_s, alog_s, spread_s, sum_s, gmap_s):
        self.a_s, self.stepd_s, self.drive_s, self.gs_s = a_s, stepd_s, drive_s, gs_s
        self.read_s, self.q_s, self.r_s, self.state_s = read_s, q_s, r_s, state_s
        self.pulled_s, self.alog_s, self.spread_s, self.sum_s, self.gmap_s = pulled_s, alog_s, spread_s, sum_s, gmap_s
        sub = lax.broadcasted_iota(jnp.int32, (8, 128), 0)
        self.masks = [(sub & shift) == 0 for shift in (1, 2, 4)]
        self.lane = lax.broadcasted_iota(jnp.int32, (N, 128), 1)
        self.blocks = [slice(b * 128, (b + 1) * 128) for b in range(a_s.shape[1] // 128)]

    def place(self, i):
        base = pl.multiple_of(i * 8, 8)
        tile = pl.ds(pl.multiple_of((base // 128) * 128, 128), 128)
        return base, tile, lax.rem(base, 128)

    def spread(self, maps, shifted_s):
        rows = maps.shape[0]
        for i in range(maps.shape[1] // 8):
            tile, first = maps[:, i // 16 * 128 : (i // 16 + 1) * 128], i % 16 * 8
            shifted_s[i * rows : (i + 1) * rows] = pltpu.roll(tile, (128 - first) % 128, 1).astype(BF16)
        row = lax.broadcasted_iota(jnp.int32, (128, 8 * 128), 0)
        column = lax.broadcasted_iota(jnp.int32, (128, 8 * 128), 1)
        chosen = jnp.where(row == column // 128, 1.0, 0.0).astype(BF16)
        self.spread_s[...] = dot(shifted_s[...], chosen).reshape(self.spread_s.shape)

    def maps_at(self, i, j):
        lanes = slice(j * 128, (j + 1) * 128)
        return self.spread_s[i, :N, lanes], self.spread_s[i, N:, lanes]

    def forward(self, start, stop):
        def chunk(i, none):
            base = pl.multiple_of(i * 8, 8)
            for lanes in self.blocks:
                state = self.state_s[i, :, lanes]
                a = self.a_s[:, lanes]
                stepd, drive = self.stepd_s[pl.ds(base, 8), lanes], self.drive_s[pl.ds(base, 8), lanes]
                sums = RowSums(self.masks)
                for j in range(8):
                    in_map, out_map = self.maps_at(i, j)
                    state = jnp.exp(stepd[j : j + 1] * a) * state + drive[j : j + 1] * in_map
                    read = state * out_map
                    sums.add(j, read[:8] + read[8:])
                self.state_s[i + 1, :, lanes] = state
                self.read_s[pl.ds(base, 8), lanes] = sums.result
            return none

        lax.fori_loop(start, stop, chunk, 0)

    def backward(self, start, stop):
        def chunk(step, none):
            i = start + stop - 1 - step
            base, tile, first = self.place(i)
            for b, lanes in enumerate(self.blocks):
                a = self.a_s[:, lanes]
                stepd, drive = self.stepd_s[pl.ds(base, 8), lanes], self.drive_s[pl.ds(base, 8), lanes]
                gs = self.gs_s[pl.ds(base, 8), lanes]
                states, decays = [self.state_s[i, :, lanes]], []
                for j in range(8):
                    decays.append(jnp.exp(stepd[j : j + 1] * a))
                    states.append(decays[j] * states[j] + drive[j : j + 1] * self.maps_at(i, j)[0])
                pulled, alog = self.pulled_s[:, lanes], self.alog_s[:, lanes]
                q_sums, r_sums = RowSums(self.masks), RowSums(self.masks)
                for j in reversed(range(8)):
                    in_map, out_map = self.maps_at(i, j)
                    adjoint = pulled + out_map * gs[j : j + 1]
                    g_in, g_out = adjoint * drive[j : j + 1], states[j + 1] * gs[j : j + 1]
                    if b > 0:
                        g_in, g_out = g_in + self.sum_s[0, j], g_out + self.sum_s[1, j]
                    self.sum_s[0, j], self.sum_s[1, j] = g_in, g_out
                    q_t = adjoint * in_map
                    q_sums.add(j, q_t[:8] + q_t[8:])
                    pulled = decays[j] * adjoint
                    past = pulled * states[j]
                    r_t = past * a
                    r_sums.add(j, r_t[:8] + r_t[8:])
                    alog = alog + past * stepd[j : j + 1]
                self.pulled_s[:, lanes], self.alog_s[:, lanes] = pulled, alog
                self.q_s[pl.ds(base, 8), lanes] = q_sums.result
                self.r_s[pl.ds(base, 8), lanes] = r_sums.result
            for k in range(2):
                row = self.gmap_s[k * N : (k + 1) * N, tile]
                for j in range(8):
                    row = jnp.where(self.lane == first + j, jnp.sum(self.sum_s[k, j], axis=1, keepdims=True), row)
                self.gmap_s[k * N : (k + 1) * N, tile] = row
            return none

        lax.fori_loop(start, stop, chunk, 0)


class TokenSum:
    def __init__(self, spot, copies, part, y_land, z_land, y_sems, z_sems):
        self.spot, self.copies, self.part, self.y_land, self.z_land = spot, copies, part, y_land, z_land
        self.y_sems, self.z_sems = y_sems, z_sems
        self.group = copies.group(y_land)

    def push(self):
        spot = self.spot
        for far in (3, 2, 1):
            for way in (1, -1):
                self.over_y(spot.z_at(way * far), self.within(way, far))
        self.over_y(spot.z, None)

    def within(self, way, far):
        return self.spot.z < NZ - far if way == 1 else self.spot.z >= far

    def over_y(self, z, when):
        self.copies.send(self.part.at[z, 1 - self.spot.y], self.y_land.at[z], self.y_sems.at[z], self.spot.y_mate, when, self.group)

    def add(self, z, landed):
        part, y = self.part, self.spot.y
        part[z, y] = (part[z, y].astype(F32) + landed[...].astype(F32)).astype(BF16)

    def stage(self, far):
        spot = self.spot
        for side, way in enumerate((1, -1)):
            z = spot.z_at(way * far)
            goes = self.within(way, far)
            grown = goes & self.within(-way, 1)
            land, sem = self.z_land.at[side, z], self.z_sems.at[side, z]

            @pl.when(goes)
            def _(z=z):
                arrived(self.y_land.at[z], self.y_sems.at[z])
                self.add(z, self.y_land.at[z])

            if far < NZ - 1:

                @pl.when(grown)
                def _(z=z, land=land, sem=sem):
                    arrived(land, sem)
                    self.add(z, land)

            self.copies.send(self.part.at[z, spot.y], land, sem, spot.on_line(spot.z_at(way)), goes)

    def last(self):
        spot = self.spot
        z = spot.z
        arrived(self.y_land.at[z], self.y_sems.at[z])
        self.add(z, self.y_land.at[z])
        for side, way in enumerate((1, -1)):

            @pl.when(self.within(-way, 1))
            def _(land=self.z_land.at[side, z], sem=self.z_sems.at[side, z]):
                arrived(land, sem)
                self.add(z, land)

        return self.part[z, spot.y].astype(F32)


class RowSum:
    def __init__(self, spot, copies, part, c_land, x_land, z_land, c_sems, x_sems, z_sem):
        self.spot, self.copies, self.part = spot, copies, part
        self.c_land, self.x_land, self.z_land = c_land, x_land, z_land
        self.c_sems, self.x_sems, self.z_sem = c_sems, x_sems, z_sem
        self.groups = [copies.group(whole) for whole in (c_land, x_land, z_land.at[pl.ds(0, NZ - 1)])]

    def push(self):
        spot = self.spot
        for offset in (1, 2, 3, 0):
            z = spot.turn(offset)
            for x in range(2):
                self.copies.send(
                    self.part.at[place(z, x, 1 - spot.c)], self.c_land.at[z, x], self.c_sems.at[z], spot.c_mate, group=self.groups[0]
                )

    def add(self, z, x, landed):
        part, owner = self.part, place(z, x, self.spot.c)
        part[owner] = (part[owner].astype(F32) + landed.astype(F32)).astype(part.dtype)

    def second(self):
        spot = self.spot
        for offset in (1, 2, 3, 0):
            z = spot.turn(offset)
            arrived(self.c_land.at[z], self.c_sems.at[z])
            for x in range(2):
                self.add(z, x, self.c_land[z, x])
            self.copies.send(
                self.part.at[place(z, 1 - spot.x, spot.c)], self.x_land.at[z], self.x_sems.at[z], spot.x_mate, group=self.groups[1]
            )

    def third(self, offsets=(1, 2, 3, 0)):
        spot = self.spot
        for offset in offsets:
            z = spot.turn(offset)
            arrived(self.x_land.at[z], self.x_sems.at[z])
            self.add(z, spot.x, self.x_land[z])
            own = self.part.at[place(z, spot.x, spot.c)]
            if offset:
                self.copies.send(own, self.z_land.at[spot.z], self.z_sem, spot.on_line(z), group=self.groups[2])
            else:
                self.copies.keep(own, self.z_land.at[z])

    def last(self):
        arrived(self.z_land.at[pl.ds(0, NZ - 1)], self.z_sem)


class ChannelSum:
    def __init__(self, spot, copies, part, c_land, x_land, own, full, c_sem, x_sem, full_sems):
        self.spot, self.copies, self.part, self.own, self.full, self.full_sems = spot, copies, part, own, full, full_sems
        self.c_land, self.x_land, self.c_sem, self.x_sem = c_land, x_land, c_sem, x_sem
        self.group = copies.group(full.at[pl.ds(0, 4 * NZ - 1)])

    def push(self):
        self.copies.send(self.part.at[1 - self.spot.c], self.c_land, self.c_sem, self.spot.c_mate)

    def second(self):
        spot = self.spot
        arrived(self.c_land, self.c_sem)
        self.part[spot.c] = self.part[spot.c] + self.c_land[...]
        self.copies.send(self.part.at[spot.c, 1 - spot.x], self.x_land, self.x_sem, spot.x_mate)

    def spread(self, origin, device, src=None):
        src = self.full.at[origin] if src is None else src
        sem = self.full_sems.at[self.spot.slot(origin, device)]
        self.copies.send(src, self.full.at[origin], sem, device, group=self.group)

    def third(self):
        spot = self.spot
        arrived(self.x_land, self.x_sem)
        self.own[...] = (self.part[spot.c, spot.x] + self.x_land[...]).astype(BF16)
        for device in [spot.on_line(spot.z_at(offset)) for offset in (1, 2, 3)] + [spot.x_mate, spot.c_mate]:
            self.spread(spot.dp, device, self.own)
        self.copies.keep(self.own, self.full.at[spot.dp])

    def fourth(self):
        spot = self.spot
        for offset in (1, 2, 3):
            z = spot.z_at(-offset)
            origin = place(z, spot.x, spot.c)
            arrived(self.full.at[origin], self.full_sems.at[z])
            self.spread(origin, spot.x_mate)
            self.spread(origin, spot.c_mate)

    def fifth(self):
        spot = self.spot
        for offset in range(NZ):
            z = spot.z_at(-offset)
            origin = place(z, 1 - spot.x, spot.c)
            arrived(self.full.at[origin], self.full_sems.at[NZ + z])
            self.spread(origin, spot.c_mate)

    def last(self):
        arrived(self.full.at[pl.ds(0, 2 * NZ)], self.full_sems.at[2 * NZ])


class Held:
    def __init__(self, names, refs):
        for name, ref in zip(names, refs, strict=True):
            setattr(self, name, ref)


def block_scratch(half, feats, rows, chans, step_rows, width):
    tokens, n_dp, length = 2 * half * NZ, 4 * NZ, 2 * half
    vmem, dma = pltpu.VMEM, pltpu.SemaphoreType.DMA
    owners, steps = (n_dp, rows, chans), (n_dp, 2 * step_rows, chans // 2)
    part = (NZ, 2, width // 2, length)
    small = (width + 32) // 4
    held = {
        "w": vmem((3, n_dp, rows, chans), BF16),
        "acts": vmem((2, NZ, 2, half, feats), BF16),
        "dtp_own": vmem((NZ,) + steps[1:], BF16),
        "dtp": vmem(steps, BF16),
        "info": vmem((n_dp, 8, 128), F32),
        "mask": vmem((NZ, length, 128), F32),
        "low": vmem((tokens, chans), BF16),
        "gated": vmem((tokens, chans), BF16),
        "ggate": vmem((tokens, chans), BF16),
    }
    for name in ("x_in", "pre", "gate", "gg", "raw", "stepd", "drive", "gs", "read"):
        held[name] = vmem((tokens, chans), F32)
    held |= {
        "a": vmem((N, chans), F32),
        "state": vmem((tokens // 8 + 1, N, chans), F32),
        "pulled": vmem((N, chans), F32),
        "alog": vmem((N, chans), F32),
        "spread": vmem((tokens // 8, 2 * N, 8 * 128), F32),
        "shifted": vmem((tokens // 8 * 2 * N, 128), BF16),
        "sum": vmem((2, 8, N, 128), F32),
        "gmap": vmem((2 * N, tokens), F32),
        "dbl": vmem((width, tokens), F32),
        "part": vmem((2,) + part, BF16),
        "landing": vmem((2, 2 * NZ) + part[2:], BF16),
        "total": vmem((2,) + part, BF16),
        "mixed": vmem((NZ, 2, half, feats), BF16),
        "outw": vmem(owners, BF16),
        "ginz": vmem(owners, BF16),
        "gdtp": vmem(steps, BF16),
        "chan": vmem((2, 2, small, chans), F32),
        "y_land": vmem((2, NZ, half, feats), BF16),
        "z_land": vmem((2, 2, NZ, half, feats), BF16),
        "wc_land": vmem((3, NZ, 2, rows, chans), BF16),
        "wx_land": vmem((3, NZ, rows, chans), BF16),
        "dc_land": vmem((NZ, 2) + steps[1:], BF16),
        "dx_land": vmem((NZ,) + steps[1:], BF16),
        "fc_land": vmem((2, small, chans), F32),
        "fx_land": vmem((small, chans), F32),
        "f_own": vmem((small, chans), BF16),
        "block": vmem((half, feats), F32),
        "gresid": vmem((half, feats), F32),
        "tile": vmem((4, 8, 128), F32),
        "gain_part": vmem((2, n_dp, 128), F32),
        "gain": vmem((n_dp, 8, 128), F32),
        "gain_total": vmem((8, 128), F32),
        "squares": vmem((2, 8, 128), F32),
        "gain_land": vmem((n_dp - 1, 8, 128), F32),
        "resid": vmem((half, feats), F32),
        "cot": vmem((half, feats), F32),
        "xproj": vmem((width, chans * NZ), BF16),
        "ids": vmem((1, length), jnp.int32),
        "convw": vmem((4, chans * NZ), F32),
        "convb": vmem((1, chans * NZ), F32),
        "dtb": vmem((1, chans * NZ), F32),
        "alog_in": vmem((N, chans * NZ), F32),
        "skip": vmem((1, chans * NZ), F32),
        "load_sems": dma((9,)),
        "send_sems": dma((56,)),
        "keep_sems": dma((9,)),
        "own_sems": dma((4,)),
        "w_sems": dma((4, 2 * NZ + 1)),
        "act_sems": dma((2, NZ + 1)),
        "info_sem": dma(()),
        "dbl_sems": dma((2, 2)),
        "y_sems": dma((2, NZ)),
        "z_sems": dma((2, 2, NZ)),
        "wc_sems": dma((4, NZ)),
        "wx_sems": dma((4, NZ)),
        "wz_sems": dma((4,)),
        "f_sems": dma((2,)),
        "full_sems": dma((2 * NZ + 1,)),
        "tile_sems": dma((2,)),
        "gain_sems": dma((2,)),
    }
    return held


def block_kernel(names, *refs):
    (
        inx_ref, inz_ref, outp_ref, resid_in, cot_in, xproj_in, ids_in, convw_in, convb_in, dtb_in, alog_in, skip_in, gain_ref, dtp_ref,
        block_ref, gresid_ref, ggain_ref, ginx_ref, ginz_ref, goutp_ref, gdtp_ref, full_ref, squares_ref,
    ) = refs[:23]
    s = Held(names, refs[23:])
    spot = Spot()
    resid_ref, cot_ref, xproj_ref, ids_ref = s.resid, s.cot, s.xproj, s.ids
    convw_ref, convb_ref, dtb_ref, alog_ref, skip_ref = s.convw, s.convb, s.dtb, s.alog_in, s.skip
    loads = [
        pltpu.make_async_copy(src, dst, s.load_sems.at[k])
        for k, (src, dst) in enumerate(
            (
                (ids_in, s.ids), (resid_in, s.resid), (cot_in, s.cot), (xproj_in, s.xproj), (convw_in, s.convw),
                (convb_in, s.convb), (dtb_in, s.dtb), (alog_in, s.alog_in), (skip_in, s.skip),
            )
        )
    ]
    for load in loads:
        load.start()
    plane = [lax.rem(spot.dp + offset, 4 * NZ) for offset in range(1, 4 * NZ)]
    greet([(dp, spot.y) for dp in plane] + [spot.on_line(spot.z_at(dz), 1 - spot.y) for dz in range(NZ)])
    copies = Copies(s.send_sems, s.keep_sems)
    tokens, chans = s.x_in.shape
    half, feats = resid_ref.shape
    length = 2 * half
    columns = pl.ds(pl.multiple_of(spot.z * chans, chans), chans)
    quarters = [
        (slice(k * feats // NZ, (k + 1) * feats // NZ), slice(k * NZ, (k + 1) * NZ)) for k in range(NZ)
    ]
    sequences = [slice(k * length, (k + 1) * length) for k in range(NZ)]

    step_rows = dtp_ref[...].astype(F32)
    for z in range(NZ):
        s.dtp_own[z] = fold_columns(step_rows[:, z * chans : (z + 1) * chans]).astype(BF16)
    inx, inz, outp = (
        Gather(spot, copies, src, s.w.at[k], s.w_sems.at[k], s.own_sems.at[k]) for k, src in enumerate((inx_ref, inz_ref, outp_ref))
    )
    dtp = BlockGather(spot, copies, s.dtp_own, s.dtp, s.w_sems.at[3], s.own_sems.at[3])
    normed, cot = (Share(spot, copies, s.acts.at[k], s.act_sems.at[k]) for k in range(2))

    loads[0].wait()
    ids = jnp.broadcast_to(ids_ref[...], (8, length))
    lane = lax.broadcasted_iota(jnp.int32, (8, length), 1)
    sub = lax.broadcasted_iota(jnp.int32, (8, length), 0)
    info = jnp.broadcast_to(gain_ref[...].astype(F32), (8, length))
    for back in range(1, 4):
        same = jnp.where((pltpu.roll(ids, back, 1) == ids) & (lane >= back), 1.0, 0.0)
        info = jnp.where(sub == back, same, info)
    s.info[spot.dp] = info
    other_info = s.info.at[pl.ds(0, 4 * NZ - 1)]
    info_group = copies.group(other_info)
    for dp in plane:
        copies.send(s.info.at[spot.dp], s.info.at[spot.dp], s.info_sem, (dp, spot.y), group=info_group)
    inx.push()

    loads[1].wait()
    resid = resid_ref[...]
    row_square = jnp.sum(resid * resid, axis=1, keepdims=True)
    scaled = resid * lax.rsqrt(row_square / feats + eps_norm)
    s.tile[0] = jnp.broadcast_to(jnp.sum(row_square, axis=0, keepdims=True), (8, 128))
    copies.send(s.tile.at[0], s.tile.at[1], s.tile_sems.at[0], spot.y_mate)
    arrived(other_info, s.info_sem)
    for k in range(4 * NZ):
        cols = slice(k * 128, (k + 1) * 128)
        s.acts[0, spot.z, spot.y, :, cols] = (scaled[:, cols] * s.info[k, 0:1, :]).astype(BF16)
    normed.push()
    dtp.push()
    for load in loads[2:]:
        load.wait()
    s.acts[1, spot.z, spot.y] = cot_ref[...].astype(BF16)
    for k in range(NZ):
        s.mask[k] = column_masks(s.info[place(k, spot.x, spot.c)])
    inx.first()
    normed.first(1)
    inx.second()
    normed.first(2)
    inz.push((3, 0))
    dtp.first()
    dtp.second()
    normed.first(3)
    inz.push((1, 2))
    cot.push(False)
    normed.last()
    cot.send_y(spot.z)
    inx.last()

    all_normed = s.acts[0].reshape(tokens, feats)
    s.x_in[...] = dot(all_normed, s.w[0].reshape(-1, chans))
    taps = convw_ref[:, columns]
    bias = convb_ref[:, columns]
    for k, rows in enumerate(sequences):
        one = s.x_in[rows]
        pre = bias + taps[3:4] * one
        for back in range(1, 4):
            pre = pre + taps[3 - back : 4 - back] * (pltpu.roll(one, back, 0) * s.mask[k, :, back : back + 1])
        s.pre[rows] = pre
        s.low[rows] = (pre * sigmoid(pre)).astype(BF16)
    x_proj = xproj_ref[:, columns]
    dbl = dot(x_proj, s.low[...], NT)
    blocks = [(k, y) for k in range(NZ) for y in range(2)]
    width = dbl.shape[0] // 2
    for k, y in blocks:
        s.part[0, k, y] = dbl[y * width : (y + 1) * width, sequences[k]].astype(BF16)
    x_dbl = LineSum(
        spot, copies, s.part.at[0], s.landing.at[0], s.total.at[0], s.dbl_sems.at[0]
    )
    x_dbl.push()
    inz.first()
    cot.first(1)
    x_dbl.middle()
    outp.push((1, 0))
    cot.first(2)
    x_dbl.last()
    outp.push((2, 3))

    dtp.last()
    for k, y in blocks:
        s.dbl[y * width : (y + 1) * width, sequences[k]] = s.total[0, k, y].astype(F32)
    step_w = unfold_columns(s.dtp[...].astype(F32)).reshape(R, chans).astype(BF16)
    s.raw[...] = dot(s.dbl[:R].astype(BF16), step_w, TN) + dtb_ref[:, columns]
    for k, rows in enumerate(sequences):
        step = softplus(s.raw[rows])
        s.stepd[rows] = jnp.where(s.mask[k, :, 1:2] > 0.0, step, 1e30)
        s.drive[rows] = step * s.low[rows].astype(F32)
    s.a[...] = -jnp.exp(alog_ref[:, columns])
    s.state[0] = jnp.zeros((N, chans), F32)
    scan = Scan(
        s.a, s.stepd, s.drive, s.gs, s.read, s.read, s.gate, s.state, s.pulled, s.alog, s.spread, s.sum, s.gmap
    )
    scan.spread(s.dbl[R : R + 2 * N], s.shifted)
    steps = tokens // 8
    eighth = steps // 8
    inz.second()
    scan.forward(0, 4 * eighth)
    cot.first(3)
    outp.first()
    scan.forward(4 * eighth, steps)
    inz.last()
    s.gate[...] = dot(s.acts[0].reshape(tokens, feats), s.w[1].reshape(-1, chans))
    skip = skip_ref[:, columns]
    for rows in sequences:
        gate = s.gate[rows]
        scanned = s.read[rows] + skip * s.low[rows].astype(F32)
        s.gated[rows] = (scanned * gate * sigmoid(gate)).astype(BF16)

    mixed_sum, normed_sum = (
        TokenSum(spot, copies, part, s.y_land.at[k], s.z_land.at[k], s.y_sems.at[k], s.z_sems.at[k])
        for k, part in enumerate((s.mixed, s.acts.at[1]))
    )
    outw_sum, ginz_sum, ginx_sum, gdtp_sum = (
        RowSum(spot, copies, part, c_land, x_land, out, s.wc_sems.at[k], s.wx_sems.at[k], s.wz_sems.at[k])
        for k, (part, c_land, x_land, out) in enumerate((
            (s.outw, s.wc_land.at[0], s.wx_land.at[0], goutp_ref),
            (s.ginz, s.wc_land.at[1], s.wx_land.at[1], ginz_ref),
            (s.w.at[2], s.wc_land.at[2], s.wx_land.at[2], ginx_ref),
            (s.gdtp, s.dc_land, s.dx_land, gdtp_ref),
        ))
    )
    cot.last()
    for cols, owners in quarters:
        given = s.acts[1, :, :, :, cols].reshape(tokens, -1)
        s.outw[owners] = dot(given, s.gated[...], TN).astype(BF16).reshape(-1, *s.outw.shape[1:])
    outw_sum.push()
    outp.second()
    outw_sum.second()
    outp.last()
    s.gg[...] = dot(s.acts[1].reshape(tokens, feats), s.w[2].reshape(-1, chans))
    outw_sum.third((1,))
    for cols, owners in quarters:
        part = dot(s.gated[...], s.w[2, owners].reshape(-1, chans), NT)
        s.mixed[:, :, :, cols] = part.astype(BF16).reshape(*s.mixed.shape[:3], -1)
    mixed_sum.push()
    for rows in sequences:
        gate, gg = s.gate[rows], s.gg[rows]
        sig = sigmoid(gate)
        scanned = s.read[rows] + skip * s.low[rows].astype(F32)
        s.gs[rows] = gg * gate * sig
        s.ggate[rows] = (gg * scanned * sig * (1.0 + gate * (1.0 - sig))).astype(BF16)
    for cols, owners in quarters:
        given = s.acts[0, :, :, :, cols].reshape(tokens, -1)
        s.ginz[owners] = dot(given, s.ggate[...], TN).astype(BF16).reshape(-1, *s.ginz.shape[1:])
    ginz_sum.push()

    s.pulled[...] = jnp.zeros_like(s.pulled)
    s.alog[...] = jnp.zeros_like(s.alog)
    scan.backward(7 * eighth, steps)
    outw_sum.third((2,))
    ginz_sum.second()
    scan.backward(6 * eighth, 7 * eighth)
    outw_sum.third((3, 0))
    mixed_sum.stage(3)
    scan.backward(4 * eighth, 6 * eighth)
    ginz_sum.third((1,))
    scan.backward(2 * eighth, 4 * eighth)
    ginz_sum.third((2,))
    scan.backward(0, 2 * eighth)
    grad_bias = jnp.zeros((1, chans), F32)
    grad_skip = jnp.zeros((1, chans), F32)
    raw_rows = []
    for rows in sequences:
        conv, raw, gs, q = s.low[rows].astype(F32), s.raw[rows], s.gs[rows], s.read[rows]
        grad_raw = (conv * q + s.gate[rows]) * sigmoid(raw)
        s.gg[rows] = softplus(raw) * q + skip * gs
        grad_bias = grad_bias + jnp.sum(grad_raw, axis=0, keepdims=True)
        grad_skip = grad_skip + jnp.sum(gs * conv, axis=0, keepdims=True)
        raw_rows.append(grad_raw.astype(BF16))
    raw_low = jnp.concatenate(raw_rows, axis=0)
    dbl = jnp.concatenate([dot(step_w, raw_low, NT), s.gmap[...]], axis=0)
    for k, y in blocks:
        s.part[1, k, y] = dbl[y * width : (y + 1) * width, sequences[k]].astype(BF16)
    grad_dbl_sum = LineSum(
        spot, copies, s.part.at[1], s.landing.at[1], s.total.at[1], s.dbl_sems.at[1]
    )
    grad_dbl_sum.push()
    grad_step = dot(s.dbl[:R].astype(BF16), raw_low).reshape(4 * NZ, -1, chans)
    s.gdtp[...] = fold_columns(grad_step).astype(BF16)
    gdtp_sum.push()
    grad_dbl_sum.middle()
    ginz_sum.third((3, 0))
    mixed_sum.stage(2)
    gdtp_sum.second()
    grad_dbl_sum.last()

    grad_dbl = jnp.concatenate(
        [jnp.concatenate([s.total[1, k, y] for k in range(NZ)], axis=1) for y in range(2)], axis=0
    )
    s.gg[...] += dot(grad_dbl, x_proj, TN)
    sums = [jnp.zeros((1, chans), F32) for _ in range(5)]
    low_rows = []
    for k, rows in enumerate(sequences):
        pre, x_one = s.pre[rows], s.x_in[rows]
        sig = sigmoid(pre)
        one = s.gg[rows] * sig * (1.0 + pre * (1.0 - sig))
        sums[3] = sums[3] + jnp.sum(one * x_one, axis=0, keepdims=True)
        sums[4] = sums[4] + jnp.sum(one, axis=0, keepdims=True)
        grad_x = taps[3:4] * one
        for back in range(1, 4):
            masked = one * s.mask[k, :, back : back + 1]
            sums[3 - back] = sums[3 - back] + jnp.sum(masked * pltpu.roll(x_one, back, 0), axis=0, keepdims=True)
            grad_x = grad_x + taps[3 - back : 4 - back] * pltpu.roll(masked, length - back, 0)
        low_rows.append(grad_x.astype(BF16))
    grad_xin = jnp.concatenate(low_rows, axis=0)
    copies.settle(outp.group)
    for cols, owners in quarters:
        given = s.acts[0, :, :, :, cols].reshape(tokens, -1)
        s.w[2, owners] = dot(given, grad_xin, TN).astype(BF16).reshape(-1, *s.outw.shape[1:])
    ginx_sum.push()
    cot.settle()
    for cols, owners in quarters:
        part = dot(grad_xin, s.w[0, owners].reshape(-1, chans), NT) + dot(s.ggate[...], s.w[1, owners].reshape(-1, chans), NT)
        s.acts[1, :, :, :, cols] = part.astype(BF16).reshape(*s.mixed.shape[:3], -1)
        gain_part = jnp.sum(part * s.acts[0, :, :, :, cols].reshape(tokens, -1).astype(F32), axis=0, keepdims=True)
        for k in range(NZ):
            owner = owners.start + k
            s.gain_part[0, owner : owner + 1] = gain_part[:, k * 128 : (k + 1) * 128] / s.info[owner, 0:1]
    copies.send(s.gain_part.at[0], s.gain_part.at[1], s.gain_sems.at[0], spot.y_mate)
    normed_sum.push()
    mixed_sum.stage(1)
    s.chan[...] = jnp.concatenate(
        [dot(grad_dbl, s.low[...]), s.alog[...] * s.a[...], grad_bias, grad_skip, jnp.zeros((6, chans), F32)]
        + sums + [jnp.zeros((3, chans), F32)], axis=0
    ).reshape(s.chan.shape)
    small_sum = ChannelSum(
        spot, copies, s.chan, s.fc_land, s.fx_land, s.f_own, full_ref, s.f_sems.at[0], s.f_sems.at[1], s.full_sems
    )
    small_sum.push()
    ginx_sum.second()
    gdtp_sum.third()
    ginx_sum.third((1,))
    normed_sum.stage(3)
    small_sum.second()
    ginx_sum.third((2,))
    arrived(s.gain_part.at[1], s.gain_sems.at[0])
    for k in range(4 * NZ):
        s.gain[k] = jnp.broadcast_to(s.gain_part[0, k : k + 1] + s.gain_part[1, k : k + 1], (8, 128))
    gain_group = copies.group(s.gain_land)
    for offset, dp in enumerate(plane):
        copies.send(s.gain.at[dp], s.gain_land.at[offset], s.gain_sems.at[1], (dp, spot.y), group=gain_group)
    normed_sum.stage(2)
    ginx_sum.third((3, 0))
    small_sum.third()
    normed_sum.stage(1)
    small_sum.fourth()

    mixed = mixed_sum.last()
    resid = resid_ref[...]
    s.block[...] = resid + mixed
    copies.keep(s.block, block_ref)
    s.tile[2] = jnp.broadcast_to(jnp.sum(jnp.sum(mixed * mixed, axis=1, keepdims=True), axis=0, keepdims=True), (8, 128))
    copies.send(s.tile.at[2], s.tile.at[3], s.tile_sems.at[1], spot.y_mate)
    small_sum.fifth()
    outw_sum.last()
    ginz_sum.last()
    gdtp_sum.last()
    arrived(s.tile.at[1], s.tile_sems.at[0])
    s.squares[0] = s.tile[0] + s.tile[1]
    arrived(s.tile.at[3], s.tile_sems.at[1])
    s.squares[1] = s.tile[2] + s.tile[3]
    copies.keep(s.squares, squares_ref)

    grad_rows = normed_sum.last()
    inv = lax.rsqrt(jnp.sum(resid * resid, axis=1, keepdims=True) / feats + eps_norm)
    scaled = resid * inv
    gain = jnp.concatenate([s.info[k, 0:1] for k in range(4 * NZ)], axis=1)
    grad_scaled = grad_rows * gain
    mean = jnp.sum(grad_scaled * scaled, axis=1, keepdims=True) / feats
    s.gresid[...] = cot_ref[...] + inv * (grad_scaled - scaled * mean)
    copies.keep(s.gresid, gresid_ref)
    arrived(s.gain_land, s.gain_sems.at[1])
    total = s.gain[spot.dp]
    for offset in range(4 * NZ - 1):
        total = total + s.gain_land[offset]
    s.gain_total[...] = total
    copies.keep(s.gain_total, ggain_ref)
    ginx_sum.last()
    small_sum.last()
    copies.wait_sent()
    assert copies.used == s.send_sems.shape[0], copies.used


def block_call(in_x, in_z, out_p, residual, cotangent, gain, ids, dt_p, x_proj, conv_w, conv_b, dt_b, a_log, d_skip):
    half, feats = residual.shape
    rows, wide = in_x.shape
    n_dp, chans = 4 * NZ, wide // NZ
    held = block_scratch(half, feats, rows, chans, dt_p.shape[0], x_proj.shape[0])
    shape = jax.ShapeDtypeStruct
    outs = [
        shape((half, feats), F32), shape((half, feats), F32), shape((8, 128), F32),
        shape((NZ, rows, chans), BF16), shape((NZ, rows, chans), BF16), shape((NZ, rows, chans), BF16),
        shape((NZ, 2 * dt_p.shape[0], chans // 2), BF16), shape((n_dp, (x_proj.shape[0] + 32) // 4, chans), BF16),
        shape((2, 8, 128), F32),
    ]
    in_any = pl.BlockSpec(memory_space=pl.ANY)
    in_vmem = pl.BlockSpec(memory_space=pltpu.VMEM)
    return pl.pallas_call(
        functools.partial(block_kernel, list(held)),
        out_shape=outs,
        in_specs=[in_any] * 12 + [in_vmem] * 2,
        out_specs=[in_any] * len(outs),
        scratch_shapes=list(held.values()),
        name="block",
        compiler_params=pltpu.CompilerParams(collective_id=1, has_side_effects=True, vmem_limit_bytes=62 << 20),
    )(in_x, in_z, out_p, residual, cotangent, x_proj, ids, conv_w, conv_b, dt_b, a_log, d_skip, gain, dt_p)


def finish_kernel(
    scale, block_in, gresid_in, ginx_in, ginz_in, goutp_in, gdtp_in, full_in, ggain_in, squares_in,
    block_ref, gresid_ref, ginx_ref, ginz_ref, goutp_ref, gdtp_ref, xproj_ref, alog_ref, dtb_ref, skip_ref, convw_ref, convb_ref,
    ggain_ref, rms_ref, mrms_ref,
    token_s, low_s, step_s, full_s, ggain_s, squares_s, wide_s, gdtp_s, xproj_s, rows_s, in_sems, out_sems,
):
    begun = []

    def out(src, dst):
        copy = pltpu.make_async_copy(src, dst, out_sems.at[len(begun)])
        copy.start()
        begun.append(copy)

    reads = [
        pltpu.make_async_copy(src, dst, in_sems.at[k])
        for k, (src, dst) in enumerate(
            (
                (ginx_in, low_s.at[0]), (ginz_in, low_s.at[1]), (goutp_in, low_s.at[2]), (full_in, full_s), (gdtp_in, step_s),
                (block_in, token_s.at[0]), (gresid_in, token_s.at[1]), (ggain_in, ggain_s), (squares_in, squares_s),
            )
        )
    ]
    for read in reads:
        read.start()
    chans = low_s.shape[3]
    columns = [slice(z * chans, (z + 1) * chans) for z in range(NZ)]
    for k, ref in enumerate((ginx_ref, ginz_ref, goutp_ref)):
        reads[k].wait()
        for z, cols in enumerate(columns):
            wide_s[k, :, cols] = low_s[k, z].astype(F32)
        out(wide_s.at[k], ref)
    reads[3].wait()
    rows, width = full_s.shape[1], xproj_s.shape[0]
    for z, cols in enumerate(columns):
        for k in range(4):
            found = full_s[place(z, k % 2, k // 2)].astype(F32)
            upto = min(rows, width - k * rows)
            xproj_s[k * rows : k * rows + upto, cols] = found[:upto]
        rows_s[:, cols] = found[upto:]
    out(xproj_s, xproj_ref)
    out(rows_s.at[pl.ds(0, N)], alog_ref)
    for at, ref in ((N, dtb_ref), (N + 1, skip_ref), (24, convw_ref), (28, convb_ref)):
        out(rows_s.at[pl.ds(at, ref.shape[0])], ref)
    reads[4].wait()
    for z, cols in enumerate(columns):
        gdtp_s[:, cols] = unfold_columns(step_s[z].astype(F32))
    out(gdtp_s, gdtp_ref)
    for k, ref in enumerate((block_ref, gresid_ref)):
        reads[5 + k].wait()
        out(token_s.at[k], ref)
    reads[7].wait()
    out(ggain_s.at[pl.ds(0, 1)], ggain_ref)
    reads[8].wait()
    for k, ref in enumerate((rms_ref, mrms_ref)):
        ref[...] = jnp.sqrt(squares_s[k, 0:1, 0:1] * scale)
    for copy in begun:
        copy.wait()


def finish_call(block, gresid, ginx, ginz, goutp, gdtp, full, ggain, squares, width):
    rows, chans = ginx.shape[1:]
    wide = chans * NZ
    shape = lambda count, columns=wide: jax.ShapeDtypeStruct((count, columns), F32)
    vmem, dma = pltpu.VMEM, pltpu.SemaphoreType.DMA
    in_any = pl.BlockSpec(memory_space=pl.ANY)
    outs = [
        shape(*block.shape), shape(*gresid.shape), shape(rows), shape(rows), shape(rows), shape(gdtp.shape[1] // 2), shape(width),
        shape(N), shape(1), shape(1), shape(4), shape(1), shape(1, 128), shape(1, 1), shape(1, 1),
    ]
    return pl.pallas_call(
        functools.partial(finish_kernel, 1.0 / (2 * block.shape[0] * block.shape[1])),
        out_shape=outs,
        in_specs=[in_any] * 9,
        out_specs=[in_any] * (len(outs) - 2) + [pl.BlockSpec(memory_space=vmem)] * 2,
        scratch_shapes=[
            vmem((2,) + block.shape, F32), vmem((3,) + ginx.shape, BF16), vmem(gdtp.shape, BF16), vmem(full.shape, BF16),
            vmem(ggain.shape, F32), vmem(squares.shape, F32), vmem((3, rows, wide), F32), vmem((gdtp.shape[1] // 2, wide), F32),
            vmem((width, wide), F32), vmem((32, wide), F32), dma((9,)), dma((len(outs) - 2,)),
        ],
        name="finish",
        compiler_params=pltpu.CompilerParams(vmem_limit_bytes=60 << 20),
    )(block, gresid, ginx, ginz, goutp, gdtp, full, ggain, squares)


def per_device_split(
    residual,
    norm_gain,
    in_proj_x,
    in_proj_z,
    x_proj,
    dt_proj,
    dt_bias,
    conv_weight,
    conv_bias,
    a_log,
    d_skip,
    out_proj,
    doc_ids,
    cotangent,
):
    parts = block_call(
        in_proj_x, in_proj_z, out_proj, residual, cotangent, norm_gain[None], doc_ids[None], dt_proj, x_proj, conv_weight,
        conv_bias[None], dt_bias[None], a_log, d_skip[None],
    )
    block, gresid, ggain, ginx, ginz, goutp, gdtp, full, squares = parts
    block, gresid, ginx, ginz, goutp, gdtp, g_xproj, g_alog, g_dtb, g_skip, g_convw, g_convb, ggain, rms, mrms = finish_call(
        block, gresid, ginx, ginz, goutp, gdtp, full, ggain, squares, x_proj.shape[0]
    )
    return (
        block,
        gresid,
        ggain[0],
        ginx,
        ginz,
        g_xproj,
        gdtp,
        g_dtb[0],
        g_convw,
        g_convb[0],
        g_alog,
        g_skip[0],
        goutp,
        rms[0],
        mrms[0],
    )


def norm_rows(values, gain_val):
    mean_square = jnp.mean(values * values, axis=1, keepdims=True)
    return values * lax.rsqrt(mean_square + eps_norm) * gain_val


def conv_local(x_in, doc_ids, conv_weight, conv_bias):
    kernel_len = conv_weight.shape[0]
    length = x_in.shape[0]
    padded = jnp.pad(x_in, ((kernel_len - 1, 0), (0, 0)))
    id_pad = jnp.concatenate([jnp.full((kernel_len - 1,), -1, jnp.int32), doc_ids])
    summed = conv_bias + jnp.zeros_like(x_in)
    for offset in range(kernel_len):
        same_doc = (id_pad[offset : offset + length] == doc_ids).astype(jnp.float32)
        summed = summed + conv_weight[offset] * padded[offset : offset + length] * same_doc[:, None]
    return summed


def per_device(
    residual,
    norm_gain,
    in_proj_x,
    in_proj_z,
    x_proj,
    dt_proj,
    dt_bias,
    conv_weight,
    conv_bias,
    a_log,
    d_skip,
    out_proj,
    doc_ids,
    cotangent,
):
    gathered = (
        lax.all_gather(norm_gain, "dp", axis=0, tiled=True),
        lax.all_gather(in_proj_x, "dp", axis=0, tiled=True),
        lax.all_gather(in_proj_z, "dp", axis=0, tiled=True),
        lax.all_gather(dt_proj, "dp", axis=0, tiled=True),
        lax.all_gather(out_proj, "dp", axis=0, tiled=True),
    )
    gain_all, inx_all, inz_all, step_all, out_all = gathered
    seq_len = doc_ids.shape[0]
    normed_f32, norm_back = jax.vjp(norm_rows, residual, gain_all.astype(jnp.float32))
    normed = lax.all_gather(normed_f32.astype(jnp.bfloat16), "tensor", axis=0, tiled=True)
    x_in = jnp.dot(normed, inx_all, preferred_element_type=jnp.float32)
    gate_in = jnp.dot(normed, inz_all, preferred_element_type=jnp.float32)

    def conv_act(x_val, weight_val, bias_val):
        return jax.nn.silu(conv_local(x_val, doc_ids, weight_val, bias_val))

    conv_out, conv_back = jax.vjp(conv_act, x_in, conv_weight, conv_bias)
    conv_low = conv_out.astype(jnp.bfloat16)
    dbl_part = lax.dot_general(
        conv_low, x_proj, (((1,), (1,)), ((), ())), preferred_element_type=jnp.float32
    )
    x_dbl, resid_square = lax.psum((dbl_part, jnp.sum(residual * residual)), "tensor")
    doc_starts = doc_ids != jnp.concatenate([jnp.full((1,), -1, jnp.int32), doc_ids[:-1]])
    carry_keep = 1.0 - doc_starts.astype(jnp.float32)

    cot_all = lax.all_gather(cotangent.astype(jnp.bfloat16), "tensor", axis=0, tiled=True)
    grad_gated = jnp.dot(cot_all, out_all, preferred_element_type=jnp.float32)
    gated_low, grad_gate_low, grad_conv, grad_dbl_part, grad_step_w, grad_bias, grad_alog, grad_skip = scan_call(
        x_dbl, conv_low, gate_in, grad_gated, step_all, dt_bias, a_log, d_skip, carry_keep
    )
    mixed = lax.psum_scatter(
        lax.dot_general(
            gated_low, out_all, (((1,), (1,)), ((), ())), preferred_element_type=jnp.float32
        ),
        "tensor",
        scatter_dimension=0,
        tiled=True,
    )
    block_out = residual + mixed
    mixed_square = lax.psum(jnp.sum(mixed * mixed), "tensor")
    rms_resid = jnp.sqrt(resid_square / (seq_len * D)).reshape(1)
    rms_mixed = jnp.sqrt(mixed_square / (seq_len * D)).reshape(1)
    grad_out_w = lax.dot_general(
        cot_all, gated_low, (((0,), (0,)), ((), ())), preferred_element_type=jnp.float32
    )
    grad_dbl = lax.psum(grad_dbl_part.T, "tensor")
    grad_dbl_low = grad_dbl.astype(jnp.bfloat16)
    grad_conv = grad_conv + jnp.dot(grad_dbl_low, x_proj, preferred_element_type=jnp.float32)
    grad_xproj = lax.dot_general(
        grad_dbl_low, conv_low, (((0,), (0,)), ((), ())), preferred_element_type=jnp.float32
    )
    grad_xin, grad_convw, grad_convb = conv_back(grad_conv)
    grad_xin_low = grad_xin.astype(jnp.bfloat16)
    grad_inx = lax.dot_general(
        normed, grad_xin_low, (((0,), (0,)), ((), ())), preferred_element_type=jnp.float32
    )
    grad_inz = lax.dot_general(
        normed, grad_gate_low, (((0,), (0,)), ((), ())), preferred_element_type=jnp.float32
    )
    first_term = lax.dot_general(
        grad_xin_low, inx_all, (((1,), (1,)), ((), ())), preferred_element_type=jnp.float32
    )
    second_term = lax.dot_general(
        grad_gate_low, inz_all, (((1,), (1,)), ((), ())), preferred_element_type=jnp.float32
    )
    grad_normed = lax.psum_scatter(
        first_term + second_term, "tensor", scatter_dimension=0, tiled=True
    )
    grad_rows_x, grad_gain_part = norm_back(grad_normed)
    grad_residual = cotangent + grad_rows_x
    grad_gain = lax.psum(grad_gain_part, "tensor")
    gain_shard, inx_shard, inz_shard, step_shard, out_shard = (
        lax.psum_scatter(grad_gain, "dp", scatter_dimension=0, tiled=True),
        lax.psum_scatter(grad_inx, "dp", scatter_dimension=0, tiled=True),
        lax.psum_scatter(grad_inz, "dp", scatter_dimension=0, tiled=True),
        lax.psum_scatter(grad_step_w, "dp", scatter_dimension=0, tiled=True),
        lax.psum_scatter(grad_out_w, "dp", scatter_dimension=0, tiled=True),
    )
    small_sums = lax.psum(
        (grad_xproj, grad_bias, grad_convw, grad_convb, grad_alog, grad_skip), "dp"
    )
    xproj_sum, bias_sum, convw_sum, convb_sum, alog_sum, skip_sum = small_sums
    return (
        block_out,
        grad_residual,
        gain_shard,
        inx_shard,
        inz_shard,
        xproj_sum,
        step_shard,
        bias_sum,
        convw_sum,
        convb_sum,
        alog_sum,
        skip_sum,
        out_shard,
        rms_resid,
        rms_mixed,
    )


def solution(mesh):
    placed = (
        P(("dp", "tensor"), None),
        P("dp"),
        P("dp", "tensor"),
        P("dp", "tensor"),
        P(None, "tensor"),
        P("dp", "tensor"),
        P("tensor"),
        P(None, "tensor"),
        P("tensor"),
        P(None, "tensor"),
        P("tensor"),
        P("dp", "tensor"),
        P("dp"),
        P(("dp", "tensor"), None),
    )
    return jax.shard_map(
        per_device_split if mesh.shape["dp"] == 4 * NZ else per_device,
        mesh=mesh,
        in_specs=placed,
        out_specs=(
            P(("dp", "tensor"), None),
            P(("dp", "tensor"), None),
            P("dp"),
            P("dp", "tensor"),
            P("dp", "tensor"),
            P(None, "tensor"),
            P("dp", "tensor"),
            P("tensor"),
            P(None, "tensor"),
            P("tensor"),
            P(None, "tensor"),
            P("tensor"),
            P("dp", "tensor"),
            P("dp"),
            P("dp"),
        ),
        check_vma=False,
    )
```

```python
import functools

import jax
import jax.numpy as jnp
from jax import lax
from jax.experimental import pallas as pl
from jax.experimental.pallas import tpu as pltpu
from jax.sharding import PartitionSpec as P

D = 2048
R = 128
N = 16

eps_norm = 1e-05


def sigmoid(v):
    return 1.0 / (1.0 + jnp.exp(-v))


def softplus(v):
    return jnp.maximum(v, 0.0) + jnp.log(1.0 + jnp.exp(-jnp.abs(v)))


def fold_rows(first, second, shift, lower):
    kept = jnp.where(lower, first, second)
    moved = jnp.where(lower, second, first)
    return kept + pltpu.roll(moved, shift, 0)


class RowSums:
    def __init__(self, masks):
        self.masks = masks
        self.held = {}
        self.result = None

    def add(self, token, value):
        level = 0
        while True:
            if level == 3:
                self.result = value
                return
            mate = (level, token ^ 1)
            if mate not in self.held:
                self.held[(level, token)] = value
                return
            other = self.held.pop(mate)
            first, second = (other, value) if token & 1 else (value, other)
            value = fold_rows(first, second, 1 << level, self.masks[level])
            token >>= 1
            level += 1


def split_dot(left, right_low, dims):
    high = left.astype(jnp.bfloat16)
    rest = (left - high.astype(jnp.float32)).astype(jnp.bfloat16)
    return lax.dot_general(high, right_low, dims, preferred_element_type=jnp.float32) + lax.dot_general(
        rest, right_low, dims, preferred_element_type=jnp.float32
    )


def scan_kernel(
    dbl_ref, conv_ref, gate_ref, gg_ref, dtp_ref, dtb_ref, alog_ref, skip_ref, keep_ref, in_ref, out_ref,
    gated_ref, ggate_ref, gconv_ref, gdbl_ref, gin_ref, gout_ref, gdtp_ref, gdtb_ref, galog_ref, gskip_ref,
    h_s, d_s, stepd_s, sc_s, gs_s, y_s, q_s, r_s, a_s,
):
    length, width = conv_ref.shape
    blocks = width // 128
    part = pl.program_id(0)
    sub = lax.broadcasted_iota(jnp.int32, (8, 128), 0)
    masks = [(sub & shift) == 0 for shift in (1, 2, 4)]
    lanes = [slice(b * 128, (b + 1) * 128) for b in range(blocks)]

    nn = (((1,), (0,)), ((), ()))
    step_raw = split_dot(dbl_ref[...], dtp_ref[...], nn) + dtb_ref[...]
    step = jnp.maximum(step_raw, 0.0) + jnp.log(1.0 + jnp.exp(-jnp.abs(step_raw)))
    stepd_s[...] = jnp.where(keep_ref[...] > 0.0, step, 1e30)
    sc_s[...] = step * conv_ref[...].astype(jnp.float32)
    gate = gate_ref[...]
    gs_s[...] = gg_ref[...] * gate * sigmoid(gate)
    a_s[...] = -jnp.exp(alog_ref[...])

    h_s[0] = jnp.zeros((N, width), jnp.float32)

    def forward(i, hs):
        base = pl.multiple_of(i * 8, 8)
        hs = list(hs)
        sums = [RowSums(masks) for _ in range(blocks)]
        stepd = [stepd_s[pl.ds(base, 8), lanes[b]] for b in range(blocks)]
        drive = [sc_s[pl.ds(base, 8), lanes[b]] for b in range(blocks)]
        for j in range(8):
            t = base + j
            in_t = in_ref[t]
            out_t = out_ref[t]
            for b in range(blocks):
                decay = jnp.exp(stepd[b][j : j + 1] * a_s[:, lanes[b]])
                hs[b] = decay * hs[b] + drive[b][j : j + 1] * in_t
                d_s[t, :, lanes[b]] = decay
                h_s[t + 1, :, lanes[b]] = hs[b]
                read = hs[b] * out_t
                sums[b].add(j, read[:8] + read[8:])
        for b in range(blocks):
            y_s[pl.ds(base, 8), lanes[b]] = sums[b].result
        return tuple(hs)

    zero = jnp.zeros((N, 128), jnp.float32)
    lax.fori_loop(0, length // 8, forward, (zero,) * blocks)

    conv = conv_ref[...].astype(jnp.float32)
    gate = gate_ref[...]
    sig = sigmoid(gate)
    scanned = y_s[...] + skip_ref[...] * conv
    gated_ref[...] = (scanned * gate * sig).astype(jnp.bfloat16)
    ggate_ref[...] = (gg_ref[...] * scanned * sig * (1.0 + gate * (1.0 - sig))).astype(jnp.bfloat16)

    @pl.when(part == 0)
    def _():
        gin_ref[...] = jnp.zeros_like(gin_ref)
        gout_ref[...] = jnp.zeros_like(gout_ref)
        gdbl_ref[...] = jnp.zeros_like(gdbl_ref)

    def backward(i, carried):
        base = pl.multiple_of(length - 8 - i * 8, 8)
        pulled, alog_sum = list(carried[0]), list(carried[1])
        q_sums = [RowSums(masks) for _ in range(blocks)]
        r_sums = [RowSums(masks) for _ in range(blocks)]
        stepd = [stepd_s[pl.ds(base, 8), lanes[b]] for b in range(blocks)]
        drive = [sc_s[pl.ds(base, 8), lanes[b]] for b in range(blocks)]
        gs = [gs_s[pl.ds(base, 8), lanes[b]] for b in range(blocks)]
        for j in reversed(range(8)):
            t = base + j
            in_t = in_ref[t]
            out_t = out_ref[t]
            gin_t = gin_ref[t]
            gout_t = gout_ref[t]
            for b in range(blocks):
                gs_t = gs[b][j : j + 1]
                adjoint = pulled[b] + out_t * gs_t
                gout_t = gout_t + gs_t * h_s[t + 1, :, lanes[b]]
                gin_t = gin_t + adjoint * drive[b][j : j + 1]
                q_t = adjoint * in_t
                q_sums[b].add(j, q_t[:8] + q_t[8:])
                pulled[b] = d_s[t, :, lanes[b]] * adjoint
                past = pulled[b] * h_s[t, :, lanes[b]]
                r_t = past * a_s[:, lanes[b]]
                r_sums[b].add(j, r_t[:8] + r_t[8:])
                alog_sum[b] = alog_sum[b] + past * stepd[b][j : j + 1]
            gin_ref[t] = gin_t
            gout_ref[t] = gout_t
        for b in range(blocks):
            q_s[pl.ds(base, 8), lanes[b]] = q_sums[b].result
            r_s[pl.ds(base, 8), lanes[b]] = r_sums[b].result
        return tuple(pulled), tuple(alog_sum)

    _, alog_sum = lax.fori_loop(0, length // 8, backward, ((zero,) * blocks, (zero,) * blocks))
    for b in range(blocks):
        galog_ref[:, lanes[b]] = alog_sum[b] * a_s[:, lanes[b]]

    conv = conv_ref[...].astype(jnp.float32)
    step_raw = split_dot(dbl_ref[...], dtp_ref[...], nn) + dtb_ref[...]
    step = jnp.maximum(step_raw, 0.0) + jnp.log(1.0 + jnp.exp(-jnp.abs(step_raw)))
    raw = (conv * q_s[...] + r_s[...]) * sigmoid(step_raw)
    gs = gs_s[...]
    gconv_ref[...] = step * q_s[...] + skip_ref[...] * gs
    gskip_ref[...] = jnp.sum(gs * conv, axis=0, keepdims=True)
    gdtb_ref[...] = jnp.sum(raw, axis=0, keepdims=True)
    raw_low = raw.astype(jnp.bfloat16)
    gdtp_ref[...] = lax.dot_general(
        dbl_ref[...].astype(jnp.bfloat16), raw_low, (((0,), (0,)), ((), ())), preferred_element_type=jnp.float32
    )
    gdbl_ref[...] += lax.dot_general(
        dtp_ref[...], raw_low, (((1,), (1,)), ((), ())), preferred_element_type=jnp.float32
    )


def scan_call(dbl, conv, gate, gg, dtp, dtb, alog, skip, keep):
    length, chans = conv.shape
    cb = min(65536 // length, chans)
    f32 = jnp.float32
    maps = jnp.broadcast_to(dbl[:, R:, None], (length, 2 * N, 128))
    tokens = lambda kind: (jax.ShapeDtypeStruct((length, chans), kind), pl.BlockSpec((length, cb), lambda i: (0, i)))
    whole = lambda *shape: (jax.ShapeDtypeStruct(shape, f32), pl.BlockSpec(shape, lambda i: (0,) * len(shape)))
    rows = lambda count: (jax.ShapeDtypeStruct((count, chans), f32), pl.BlockSpec((count, cb), lambda i: (0, i)))
    outs = [
        tokens(jnp.bfloat16), tokens(jnp.bfloat16), tokens(f32), whole(R, length), whole(length, N, 128), whole(length, N, 128),
        rows(R), rows(1), rows(N), rows(1),
    ]
    ins = [
        whole(length, R), tokens(f32), tokens(f32), tokens(f32), rows(R), rows(1), rows(N), rows(1),
        whole(length, 1),
    ]
    res = pl.pallas_call(
        scan_kernel,
        grid=(chans // cb,),
        in_specs=[spec for _, spec in ins] + [
            pl.BlockSpec((length, N, 128), lambda i: (0, 0, 0)), pl.BlockSpec((length, N, 128), lambda i: (0, 1, 0))],
        out_specs=[spec for _, spec in outs],
        out_shape=[shape for shape, _ in outs],
        scratch_shapes=[
            pltpu.VMEM((length + 1, N, cb), f32), pltpu.VMEM((length, N, cb), f32),
        ] + [pltpu.VMEM((length, cb), f32)] * 6 + [pltpu.VMEM((N, cb), f32)],
        name="selective_scan",
        compiler_params=pltpu.CompilerParams(vmem_limit_bytes=60 << 20),
    )(dbl[:, :R], conv, gate, gg, dtp, dtb[None], alog, skip[None], keep[:, None], maps, maps)
    gated, ggate, gconv, gdbl, gin, gout, gdtp, gdtb, galog, gskip = res
    gdbl_all = jnp.concatenate([gdbl, jnp.sum(gin, -1).T, jnp.sum(gout, -1).T], axis=0)
    return gated, ggate, gconv, gdbl_all, gdtp, gdtb[0], galog, gskip[0]


MESH = pl.DeviceIdType.MESH
NZ = 4
F32 = jnp.float32
BF16 = jnp.bfloat16
NN = (((1,), (0,)), ((), ()))
NT = (((1,), (1,)), ((), ()))
TN = (((0,), (0,)), ((), ()))


def dot(left, right, dims=NN):
    return lax.dot_general(left, right, dims, preferred_element_type=F32)


def place(z, x, c):
    return (z * 2 + x) * 2 + c


class Spot:
    def __init__(self):
        self.dp = lax.axis_index("dp")
        self.y = lax.axis_index("tensor")
        self.z, self.x, self.c = self.dp // 4, (self.dp // 2) % 2, self.dp % 2
        self.x_mate = (place(self.z, 1 - self.x, self.c), self.y)
        self.c_mate = (place(self.z, self.x, 1 - self.c), self.y)
        self.y_mate = (self.dp, 1 - self.y)

        far, near = jnp.where(self.z < 2, 3, 0), 1 + self.z % 2
        self.others = [far, 6 - self.z - far - near, near]

    def turn(self, k):
        return self.others[k - 1] if k else self.z

    def z_at(self, offset):
        return lax.rem(self.z + offset + NZ, NZ)

    def slot(self, origin, device):
        if device is self.c_mate:
            return 2 * NZ
        return origin // 4 + (NZ if device is self.x_mate else 0)

    def on_line(self, z, y=None):
        return (place(z, self.x, self.c), self.y if y is None else y)


def greet(devices):
    barrier = pltpu.get_barrier_semaphore()
    for device in devices:
        pl.semaphore_signal(barrier, inc=1, device_id=device, device_id_type=MESH)
    pl.semaphore_wait(barrier, len(devices))


class Copies:
    def __init__(self, send_sems, own_sems):
        self.send_sems, self.own_sems = send_sems, own_sems
        self.used, self.groups, self.begun, self.kept = 0, [], [], []

    def new_sem(self):
        self.used += 1
        return self.send_sems.at[self.used - 1]

    def group(self, whole):
        sem = self.new_sem()
        self.groups.append((sem, pltpu.make_async_copy(whole, whole, sem).wait))
        return sem

    def settle(self, *sems):
        for sem, wait in self.groups:
            if any(sem is one for one in sems):
                wait()
        self.groups = [(sem, wait) for sem, wait in self.groups if all(sem is not one for one in sems)]

    def send(self, src, dst, recv_sem, device, when=None, group=None):
        copy = pltpu.make_async_remote_copy(
            src_ref=src, dst_ref=dst, send_sem=self.new_sem() if group is None else group, recv_sem=recv_sem,
            device_id=device, device_id_type=MESH,
        )
        if group is None:
            self.begun.append((when, copy.wait_send))
        if when is None:
            copy.start()
        else:
            pl.when(when)(copy.start)

    def keep(self, src, dst):
        copy = pltpu.make_async_copy(src, dst, self.own_sems.at[len(self.kept)])
        copy.start()
        self.kept.append(copy)

    def wait_sent(self):
        self.settle(*[sem for sem, _ in self.groups])
        self.settle_alone(self.begun)
        for copy in self.kept:
            copy.wait()

    def settle_alone(self, begun):
        for when, wait in begun:
            if when is None:
                wait()
            else:
                pl.when(when)(wait)
        self.begun = [one for one in self.begun if all(one is not done for done in begun)]


def arrived(dst, recv_sem, when=None):
    copy = pltpu.make_async_copy(dst, dst, recv_sem)
    if when is None:
        copy.wait()
    else:
        pl.when(when)(copy.wait)


class Gather:
    def __init__(self, spot, copies, src, dst, recv_sems, own_sem):
        self.spot, self.copies, self.src, self.dst, self.recv_sems, self.own_sem = spot, copies, src, dst, recv_sems, own_sem
        self.width = dst.shape[-1]
        self.group = copies.group(dst.at[pl.ds(0, 4 * NZ - 1)])

    def columns(self, z):
        return self.src.at[:, pl.ds(pl.multiple_of(z * self.width, self.width), self.width)]

    def push(self, offsets=(1, 2, 3, 0)):
        spot, me = self.spot, self.spot.dp
        for offset in offsets:
            if offset == 0:
                self.push_own()
                continue
            z = spot.turn(offset)
            self.copies.send(self.columns(z), self.dst.at[me], self.recv_sems.at[spot.z], spot.on_line(z), group=self.group)

    def push_own(self):
        spot, me = self.spot, self.spot.dp
        self.own = pltpu.make_async_copy(self.columns(spot.z), self.dst.at[me], self.own_sem)
        self.own.start()
        self.pass_on(me, spot.x_mate, self.columns(spot.z))
        self.pass_on(me, spot.c_mate, self.columns(spot.z))

    def pass_on(self, origin, device, src=None):
        sem = self.recv_sems.at[self.spot.slot(origin, device)]
        src = self.dst.at[origin] if src is None else src
        self.copies.send(src, self.dst.at[origin], sem, device, group=self.group)

    def first(self):
        spot = self.spot
        for offset in range(1, NZ):
            z = spot.turn(offset)
            origin = place(z, spot.x, spot.c)
            arrived(self.dst.at[origin], self.recv_sems.at[z])
            self.pass_on(origin, spot.x_mate)
            self.pass_on(origin, spot.c_mate)

    def second(self):
        spot = self.spot
        for offset in range(NZ):
            z = spot.turn(offset)
            origin = place(z, 1 - spot.x, spot.c)
            arrived(self.dst.at[origin], self.recv_sems.at[NZ + z])
            self.pass_on(origin, spot.c_mate)

    def last(self):
        self.own.wait()
        arrived(self.dst.at[pl.ds(0, 2 * NZ)], self.recv_sems.at[2 * NZ])


class BlockGather(Gather):
    def columns(self, z):
        return self.src.at[z]


def fold_columns(values):
    half = values.shape[-1] // 2
    return jnp.concatenate([values[..., :half], values[..., half:]], axis=-2)


def unfold_columns(values):
    rows = values.shape[-2] // 2
    return jnp.concatenate([values[..., :rows, :], values[..., rows:, :]], axis=-1)


class LineSum:
    def __init__(self, spot, copies, part, landing, total, sems):
        self.spot, self.copies, self.part, self.landing, self.total, self.sems = spot, copies, part, landing, total, sems
        self.offsets = [(dz, dy) for dz in range(NZ) for dy in range(2) if dz + dy > 0]
        self.all_others = landing.at[pl.ds(0, len(self.offsets))]
        self.groups = [copies.group(self.all_others) for _ in range(2)]

    def there(self, dz, dy):
        return self.spot.z_at(dz), lax.rem(self.spot.y + dy, 2)

    def push(self):
        for k, (dz, dy) in enumerate(self.offsets):
            z, y = self.there(dz, dy)
            self.copies.send(self.part.at[z, y], self.landing.at[k], self.sems.at[0], self.spot.on_line(z, y), group=self.groups[0])

    def middle(self):
        own_z, own_y = self.spot.z, self.spot.y
        arrived(self.all_others, self.sems.at[0])
        summed = self.part[own_z, own_y].astype(F32)
        for k in range(len(self.offsets)):
            summed = summed + self.landing[k].astype(F32)
        self.total[own_z, own_y] = summed.astype(BF16)
        own = self.total.at[own_z, own_y]
        for dz, dy in self.offsets:
            self.copies.send(own, own, self.sems.at[1], self.spot.on_line(*self.there(dz, dy)), group=self.groups[1])

    def last(self):
        arrived(self.all_others, self.sems.at[1])


def column_masks(tile):
    return jnp.concatenate([tile] * 16, axis=0).T


class Share:
    def __init__(self, spot, copies, dst, recv_sems):
        self.spot, self.copies, self.dst, self.recv_sems = spot, copies, dst, recv_sems
        self.over_y, self.alone = copies.group(dst.at[pl.ds(0, NZ // 2)]), []

    def send(self, z, device, when=None):
        own = self.dst.at[z, self.spot.y]
        self.copies.send(own, own, self.recv_sems.at[z], device, when)
        self.alone.append(self.copies.begun[-1])

    def settle(self):
        self.copies.settle(self.over_y)
        self.copies.settle_alone(self.alone)

    def send_y(self, z, when=None):
        own = self.dst.at[z, self.spot.y]
        self.copies.send(own, own, self.recv_sems.at[NZ], self.spot.y_mate, when, self.over_y)

    def push(self, over_y=True):
        spot = self.spot
        self.send(spot.z, spot.on_line(spot.z_at(1)), spot.z < NZ - 1)
        self.send(spot.z, spot.on_line(spot.z_at(-1)), spot.z > 0)
        if over_y:
            self.send_y(spot.z)

    def first(self, far):
        spot = self.spot
        for way in (1, -1):
            origin = spot.z_at(-way * far)
            comes = spot.z >= far if way == 1 else spot.z < NZ - far
            goes = comes & (spot.z < NZ - 1 if way == 1 else spot.z > 0)
            arrived(self.dst.at[origin, spot.y], self.recv_sems.at[origin], comes)
            if far < NZ - 1:
                self.send(origin, spot.on_line(spot.z_at(way)), goes)
            self.send_y(origin, comes)

    def last(self):
        arrived(self.dst.at[pl.ds(0, NZ // 2)], self.recv_sems.at[NZ])


class Scan:
    def __init__(self, a_s, stepd_s, drive_s, gs_s, read_s, q_s, r_s, state_s, pulled_s, alog_s, spread_s, sum_s, gmap_s):
        self.a_s, self.stepd_s, self.drive_s, self.gs_s = a_s, stepd_s, drive_s, gs_s
        self.read_s, self.q_s, self.r_s, self.state_s = read_s, q_s, r_s, state_s
        self.pulled_s, self.alog_s, self.spread_s, self.sum_s, self.gmap_s = pulled_s, alog_s, spread_s, sum_s, gmap_s
        sub = lax.broadcasted_iota(jnp.int32, (8, 128), 0)
        self.masks = [(sub & shift) == 0 for shift in (1, 2, 4)]
        self.lane = lax.broadcasted_iota(jnp.int32, (N, 128), 1)
        self.blocks = [slice(b * 128, (b + 1) * 128) for b in range(a_s.shape[1] // 128)]

    def place(self, i):
        base = pl.multiple_of(i * 8, 8)
        tile = pl.ds(pl.multiple_of((base // 128) * 128, 128), 128)
        return base, tile, lax.rem(base, 128)

    def spread(self, maps, shifted_s):
        rows = maps.shape[0]
        for i in range(maps.shape[1] // 8):
            tile, first = maps[:, i // 16 * 128 : (i // 16 + 1) * 128], i % 16 * 8
            shifted_s[i * rows : (i + 1) * rows] = pltpu.roll(tile, (128 - first) % 128, 1).astype(BF16)
        row = lax.broadcasted_iota(jnp.int32, (128, 8 * 128), 0)
        column = lax.broadcasted_iota(jnp.int32, (128, 8 * 128), 1)
        chosen = jnp.where(row == column // 128, 1.0, 0.0).astype(BF16)
        self.spread_s[...] = dot(shifted_s[...], chosen).reshape(self.spread_s.shape)

    def maps_at(self, i, j):
        lanes = slice(j * 128, (j + 1) * 128)
        return self.spread_s[i, :N, lanes], self.spread_s[i, N:, lanes]

    def forward(self, start, stop):
        def chunk(i, none):
            base = pl.multiple_of(i * 8, 8)
            for lanes in self.blocks:
                state = self.state_s[i, :, lanes]
                a = self.a_s[:, lanes]
                stepd, drive = self.stepd_s[pl.ds(base, 8), lanes], self.drive_s[pl.ds(base, 8), lanes]
                sums = RowSums(self.masks)
                for j in range(8):
                    in_map, out_map = self.maps_at(i, j)
                    state = jnp.exp(stepd[j : j + 1] * a) * state + drive[j : j + 1] * in_map
                    read = state * out_map
                    sums.add(j, read[:8] + read[8:])
                self.state_s[i + 1, :, lanes] = state
                self.read_s[pl.ds(base, 8), lanes] = sums.result
            return none

        lax.fori_loop(start, stop, chunk, 0)

    def backward(self, start, stop):
        def chunk(step, none):
            i = start + stop - 1 - step
            base, tile, first = self.place(i)
            for b, lanes in enumerate(self.blocks):
                a = self.a_s[:, lanes]
                stepd, drive = self.stepd_s[pl.ds(base, 8), lanes], self.drive_s[pl.ds(base, 8), lanes]
                gs = self.gs_s[pl.ds(base, 8), lanes]
                states, decays = [self.state_s[i, :, lanes]], []
                for j in range(8):
                    decays.append(jnp.exp(stepd[j : j + 1] * a))
                    states.append(decays[j] * states[j] + drive[j : j + 1] * self.maps_at(i, j)[0])
                pulled, alog = self.pulled_s[:, lanes], self.alog_s[:, lanes]
                q_sums, r_sums = RowSums(self.masks), RowSums(self.masks)
                for j in reversed(range(8)):
                    in_map, out_map = self.maps_at(i, j)
                    adjoint = pulled + out_map * gs[j : j + 1]
                    g_in, g_out = adjoint * drive[j : j + 1], states[j + 1] * gs[j : j + 1]
                    if b > 0:
                        g_in, g_out = g_in + self.sum_s[0, j], g_out + self.sum_s[1, j]
                    self.sum_s[0, j], self.sum_s[1, j] = g_in, g_out
                    q_t = adjoint * in_map
                    q_sums.add(j, q_t[:8] + q_t[8:])
                    pulled = decays[j] * adjoint
                    past = pulled * states[j]
                    r_t = past * a
                    r_sums.add(j, r_t[:8] + r_t[8:])
                    alog = alog + past * stepd[j : j + 1]
                self.pulled_s[:, lanes], self.alog_s[:, lanes] = pulled, alog
                self.q_s[pl.ds(base, 8), lanes] = q_sums.result
                self.r_s[pl.ds(base, 8), lanes] = r_sums.result
            for k in range(2):
                row = self.gmap_s[k * N : (k + 1) * N, tile]
                for j in range(8):
                    row = jnp.where(self.lane == first + j, jnp.sum(self.sum_s[k, j], axis=1, keepdims=True), row)
                self.gmap_s[k * N : (k + 1) * N, tile] = row
            return none

        lax.fori_loop(start, stop, chunk, 0)


class TokenSum:
    def __init__(self, spot, copies, part, y_land, z_land, y_sems, z_sems):
        self.spot, self.copies, self.part, self.y_land, self.z_land = spot, copies, part, y_land, z_land
        self.y_sems, self.z_sems = y_sems, z_sems
        self.group = copies.group(y_land)

    def push(self):
        spot = self.spot
        for far in (3, 2, 1):
            for way in (1, -1):
                self.over_y(spot.z_at(way * far), self.within(way, far))
        self.over_y(spot.z, None)

    def within(self, way, far):
        return self.spot.z < NZ - far if way == 1 else self.spot.z >= far

    def over_y(self, z, when):
        self.copies.send(self.part.at[z, 1 - self.spot.y], self.y_land.at[z], self.y_sems.at[z], self.spot.y_mate, when, self.group)

    def add(self, z, landed):
        part, y = self.part, self.spot.y
        part[z, y] = (part[z, y].astype(F32) + landed[...].astype(F32)).astype(BF16)

    def stage(self, far):
        spot = self.spot
        for side, way in enumerate((1, -1)):
            z = spot.z_at(way * far)
            goes = self.within(way, far)
            grown = goes & self.within(-way, 1)
            land, sem = self.z_land.at[side, z], self.z_sems.at[side, z]

            @pl.when(goes)
            def _(z=z):
                arrived(self.y_land.at[z], self.y_sems.at[z])
                self.add(z, self.y_land.at[z])

            if far < NZ - 1:

                @pl.when(grown)
                def _(z=z, land=land, sem=sem):
                    arrived(land, sem)
                    self.add(z, land)

            self.copies.send(self.part.at[z, spot.y], land, sem, spot.on_line(spot.z_at(way)), goes)

    def last(self):
        spot = self.spot
        z = spot.z
        arrived(self.y_land.at[z], self.y_sems.at[z])
        self.add(z, self.y_land.at[z])
        for side, way in enumerate((1, -1)):

            @pl.when(self.within(-way, 1))
            def _(land=self.z_land.at[side, z], sem=self.z_sems.at[side, z]):
                arrived(land, sem)
                self.add(z, land)

        return self.part[z, spot.y].astype(F32)


class RowSum:
    def __init__(self, spot, copies, part, c_land, x_land, z_land, c_sems, x_sems, z_sem):
        self.spot, self.copies, self.part = spot, copies, part
        self.c_land, self.x_land, self.z_land = c_land, x_land, z_land
        self.c_sems, self.x_sems, self.z_sem = c_sems, x_sems, z_sem
        self.groups = [copies.group(whole) for whole in (c_land, x_land, z_land.at[pl.ds(0, NZ - 1)])]

    def push(self):
        spot = self.spot
        for offset in (1, 2, 3, 0):
            z = spot.turn(offset)
            for x in range(2):
                self.copies.send(
                    self.part.at[place(z, x, 1 - spot.c)], self.c_land.at[z, x], self.c_sems.at[z], spot.c_mate, group=self.groups[0]
                )

    def add(self, z, x, landed):
        part, owner = self.part, place(z, x, self.spot.c)
        part[owner] = (part[owner].astype(F32) + landed.astype(F32)).astype(part.dtype)

    def second(self):
        spot = self.spot
        for offset in (1, 2, 3, 0):
            z = spot.turn(offset)
            arrived(self.c_land.at[z], self.c_sems.at[z])
            for x in range(2):
                self.add(z, x, self.c_land[z, x])
            self.copies.send(
                self.part.at[place(z, 1 - spot.x, spot.c)], self.x_land.at[z], self.x_sems.at[z], spot.x_mate, group=self.groups[1]
            )

    def third(self, offsets=(1, 2, 3, 0)):
        spot = self.spot
        for offset in offsets:
            z = spot.turn(offset)
            arrived(self.x_land.at[z], self.x_sems.at[z])
            self.add(z, spot.x, self.x_land[z])
            own = self.part.at[place(z, spot.x, spot.c)]
            if offset:
                self.copies.send(own, self.z_land.at[spot.z], self.z_sem, spot.on_line(z), group=self.groups[2])
            else:
                self.copies.keep(own, self.z_land.at[z])

    def last(self):
        arrived(self.z_land.at[pl.ds(0, NZ - 1)], self.z_sem)


class ChannelSum:
    def __init__(self, spot, copies, part, c_land, x_land, own, full, c_sem, x_sem, full_sems):
        self.spot, self.copies, self.part, self.own, self.full, self.full_sems = spot, copies, part, own, full, full_sems
        self.c_land, self.x_land, self.c_sem, self.x_sem = c_land, x_land, c_sem, x_sem
        self.group = copies.group(full.at[pl.ds(0, 4 * NZ - 1)])

    def push(self):
        self.copies.send(self.part.at[1 - self.spot.c], self.c_land, self.c_sem, self.spot.c_mate)

    def second(self):
        spot = self.spot
        arrived(self.c_land, self.c_sem)
        self.part[spot.c] = self.part[spot.c] + self.c_land[...]
        self.copies.send(self.part.at[spot.c, 1 - spot.x], self.x_land, self.x_sem, spot.x_mate)

    def spread(self, origin, device, src=None):
        src = self.full.at[origin] if src is None else src
        sem = self.full_sems.at[self.spot.slot(origin, device)]
        self.copies.send(src, self.full.at[origin], sem, device, group=self.group)

    def third(self):
        spot = self.spot
        arrived(self.x_land, self.x_sem)
        self.own[...] = (self.part[spot.c, spot.x] + self.x_land[...]).astype(BF16)
        for device in [spot.on_line(spot.z_at(offset)) for offset in (1, 2, 3)] + [spot.x_mate, spot.c_mate]:
            self.spread(spot.dp, device, self.own)
        self.copies.keep(self.own, self.full.at[spot.dp])

    def fourth(self):
        spot = self.spot
        for offset in (1, 2, 3):
            z = spot.z_at(-offset)
            origin = place(z, spot.x, spot.c)
            arrived(self.full.at[origin], self.full_sems.at[z])
            self.spread(origin, spot.x_mate)
            self.spread(origin, spot.c_mate)

    def fifth(self):
        spot = self.spot
        for offset in range(NZ):
            z = spot.z_at(-offset)
            origin = place(z, 1 - spot.x, spot.c)
            arrived(self.full.at[origin], self.full_sems.at[NZ + z])
            self.spread(origin, spot.c_mate)

    def last(self):
        arrived(self.full.at[pl.ds(0, 2 * NZ)], self.full_sems.at[2 * NZ])


class Held:
    def __init__(self, names, refs):
        for name, ref in zip(names, refs, strict=True):
            setattr(self, name, ref)


def block_scratch(half, feats, rows, chans, step_rows, width):
    tokens, n_dp, length = 2 * half * NZ, 4 * NZ, 2 * half
    vmem, dma = pltpu.VMEM, pltpu.SemaphoreType.DMA
    owners, steps = (n_dp, rows, chans), (n_dp, 2 * step_rows, chans // 2)
    part = (NZ, 2, width // 2, length)
    small = (width + 32) // 4
    held = {
        "w": vmem((3, n_dp, rows, chans), BF16),
        "acts": vmem((2, NZ, 2, half, feats), BF16),
        "dtp_own": vmem((NZ,) + steps[1:], BF16),
        "dtp": vmem(steps, BF16),
        "info": vmem((n_dp, 8, 128), F32),
        "mask": vmem((NZ, length, 128), F32),
        "low": vmem((tokens, chans), BF16),
        "gated": vmem((tokens, chans), BF16),
        "ggate": vmem((tokens, chans), BF16),
    }
    for name in ("x_in", "pre", "gate", "gg", "raw", "stepd", "drive", "gs", "read"):
        held[name] = vmem((tokens, chans), F32)
    held |= {
        "a": vmem((N, chans), F32),
        "state": vmem((tokens // 8 + 1, N, chans), F32),
        "pulled": vmem((N, chans), F32),
        "alog": vmem((N, chans), F32),
        "spread": vmem((tokens // 8, 2 * N, 8 * 128), F32),
        "shifted": vmem((tokens // 8 * 2 * N, 128), BF16),
        "sum": vmem((2, 8, N, 128), F32),
        "gmap": vmem((2 * N, tokens), F32),
        "dbl": vmem((width, tokens), F32),
        "part": vmem((2,) + part, BF16),
        "landing": vmem((2, 2 * NZ) + part[2:], BF16),
        "total": vmem((2,) + part, BF16),
        "mixed": vmem((NZ, 2, half, feats), BF16),
        "outw": vmem(owners, BF16),
        "ginz": vmem(owners, BF16),
        "gdtp": vmem(steps, BF16),
        "chan": vmem((2, 2, small, chans), F32),
        "y_land": vmem((2, NZ, half, feats), BF16),
        "z_land": vmem((2, 2, NZ, half, feats), BF16),
        "wc_land": vmem((3, NZ, 2, rows, chans), BF16),
        "wx_land": vmem((3, NZ, rows, chans), BF16),
        "dc_land": vmem((NZ, 2) + steps[1:], BF16),
        "dx_land": vmem((NZ,) + steps[1:], BF16),
        "fc_land": vmem((2, small, chans), F32),
        "fx_land": vmem((small, chans), F32),
        "f_own": vmem((small, chans), BF16),
        "block": vmem((half, feats), F32),
        "gresid": vmem((half, feats), F32),
        "tile": vmem((4, 8, 128), F32),
        "gain_part": vmem((2, n_dp, 128), F32),
        "gain": vmem((n_dp, 8, 128), F32),
        "gain_total": vmem((8, 128), F32),
        "squares": vmem((2, 8, 128), F32),
        "gain_land": vmem((n_dp - 1, 8, 128), F32),
        "resid": vmem((half, feats), F32),
        "cot": vmem((half, feats), F32),
        "xproj": vmem((width, chans * NZ), BF16),
        "ids": vmem((1, length), jnp.int32),
        "convw": vmem((4, chans * NZ), F32),
        "convb": vmem((1, chans * NZ), F32),
        "dtb": vmem((1, chans * NZ), F32),
        "alog_in": vmem((N, chans * NZ), F32),
        "skip": vmem((1, chans * NZ), F32),
        "load_sems": dma((9,)),
        "send_sems": dma((56,)),
        "keep_sems": dma((9,)),
        "own_sems": dma((4,)),
        "w_sems": dma((4, 2 * NZ + 1)),
        "act_sems": dma((2, NZ + 1)),
        "info_sem": dma(()),
        "dbl_sems": dma((2, 2)),
        "y_sems": dma((2, NZ)),
        "z_sems": dma((2, 2, NZ)),
        "wc_sems": dma((4, NZ)),
        "wx_sems": dma((4, NZ)),
        "wz_sems": dma((4,)),
        "f_sems": dma((2,)),
        "full_sems": dma((2 * NZ + 1,)),
        "tile_sems": dma((2,)),
        "gain_sems": dma((2,)),
    }
    return held


def block_kernel(names, *refs):
    (
        inx_ref, inz_ref, outp_ref, resid_in, cot_in, xproj_in, ids_in, convw_in, convb_in, dtb_in, alog_in, skip_in, gain_ref, dtp_ref,
        block_ref, gresid_ref, ggain_ref, ginx_ref, ginz_ref, goutp_ref, gdtp_ref, full_ref, squares_ref,
    ) = refs[:23]
    s = Held(names, refs[23:])
    spot = Spot()
    resid_ref, cot_ref, xproj_ref, ids_ref = s.resid, s.cot, s.xproj, s.ids
    convw_ref, convb_ref, dtb_ref, alog_ref, skip_ref = s.convw, s.convb, s.dtb, s.alog_in, s.skip
    loads = [
        pltpu.make_async_copy(src, dst, s.load_sems.at[k])
        for k, (src, dst) in enumerate(
            (
                (ids_in, s.ids), (resid_in, s.resid), (cot_in, s.cot), (xproj_in, s.xproj), (convw_in, s.convw),
                (convb_in, s.convb), (dtb_in, s.dtb), (alog_in, s.alog_in), (skip_in, s.skip),
            )
        )
    ]
    for load in loads:
        load.start()
    plane = [lax.rem(spot.dp + offset, 4 * NZ) for offset in range(1, 4 * NZ)]
    greet([(dp, spot.y) for dp in plane] + [spot.on_line(spot.z_at(dz), 1 - spot.y) for dz in range(NZ)])
    copies = Copies(s.send_sems, s.keep_sems)
    tokens, chans = s.x_in.shape
    half, feats = resid_ref.shape
    length = 2 * half
    columns = pl.ds(pl.multiple_of(spot.z * chans, chans), chans)
    quarters = [
        (slice(k * feats // NZ, (k + 1) * feats // NZ), slice(k * NZ, (k + 1) * NZ)) for k in range(NZ)
    ]
    sequences = [slice(k * length, (k + 1) * length) for k in range(NZ)]

    step_rows = dtp_ref[...].astype(F32)
    for z in range(NZ):
        s.dtp_own[z] = fold_columns(step_rows[:, z * chans : (z + 1) * chans]).astype(BF16)
    inx, inz, outp = (
        Gather(spot, copies, src, s.w.at[k], s.w_sems.at[k], s.own_sems.at[k]) for k, src in enumerate((inx_ref, inz_ref, outp_ref))
    )
    dtp = BlockGather(spot, copies, s.dtp_own, s.dtp, s.w_sems.at[3], s.own_sems.at[3])
    normed, cot = (Share(spot, copies, s.acts.at[k], s.act_sems.at[k]) for k in range(2))

    loads[0].wait()
    ids = jnp.broadcast_to(ids_ref[...], (8, length))
    lane = lax.broadcasted_iota(jnp.int32, (8, length), 1)
    sub = lax.broadcasted_iota(jnp.int32, (8, length), 0)
    info = jnp.broadcast_to(gain_ref[...].astype(F32), (8, length))
    for back in range(1, 4):
        same = jnp.where((pltpu.roll(ids, back, 1) == ids) & (lane >= back), 1.0, 0.0)
        info = jnp.where(sub == back, same, info)
    s.info[spot.dp] = info
    other_info = s.info.at[pl.ds(0, 4 * NZ - 1)]
    info_group = copies.group(other_info)
    for dp in plane:
        copies.send(s.info.at[spot.dp], s.info.at[spot.dp], s.info_sem, (dp, spot.y), group=info_group)
    inx.push()

    loads[1].wait()
    resid = resid_ref[...]
    row_square = jnp.sum(resid * resid, axis=1, keepdims=True)
    scaled = resid * lax.rsqrt(row_square / feats + eps_norm)
    s.tile[0] = jnp.broadcast_to(jnp.sum(row_square, axis=0, keepdims=True), (8, 128))
    copies.send(s.tile.at[0], s.tile.at[1], s.tile_sems.at[0], spot.y_mate)
    arrived(other_info, s.info_sem)
    for k in range(4 * NZ):
        cols = slice(k * 128, (k + 1) * 128)
        s.acts[0, spot.z, spot.y, :, cols] = (scaled[:, cols] * s.info[k, 0:1, :]).astype(BF16)
    normed.push()
    dtp.push()
    for load in loads[2:]:
        load.wait()
    s.acts[1, spot.z, spot.y] = cot_ref[...].astype(BF16)
    for k in range(NZ):
        s.mask[k] = column_masks(s.info[place(k, spot.x, spot.c)])
    inx.first()
    normed.first(1)
    inx.second()
    normed.first(2)
    inz.push((3, 0))
    dtp.first()
    dtp.second()
    normed.first(3)
    inz.push((1, 2))
    cot.push(False)
    normed.last()
    cot.send_y(spot.z)
    inx.last()

    all_normed = s.acts[0].reshape(tokens, feats)
    s.x_in[...] = dot(all_normed, s.w[0].reshape(-1, chans))
    taps = convw_ref[:, columns]
    bias = convb_ref[:, columns]
    for k, rows in enumerate(sequences):
        one = s.x_in[rows]
        pre = bias + taps[3:4] * one
        for back in range(1, 4):
            pre = pre + taps[3 - back : 4 - back] * (pltpu.roll(one, back, 0) * s.mask[k, :, back : back + 1])
        s.pre[rows] = pre
        s.low[rows] = (pre * sigmoid(pre)).astype(BF16)
    x_proj = xproj_ref[:, columns]
    dbl = dot(x_proj, s.low[...], NT)
    blocks = [(k, y) for k in range(NZ) for y in range(2)]
    width = dbl.shape[0] // 2
    for k, y in blocks:
        s.part[0, k, y] = dbl[y * width : (y + 1) * width, sequences[k]].astype(BF16)
    x_dbl = LineSum(
        spot, copies, s.part.at[0], s.landing.at[0], s.total.at[0], s.dbl_sems.at[0]
    )
    x_dbl.push()
    inz.first()
    cot.first(1)
    x_dbl.middle()
    outp.push((1, 0))
    cot.first(2)
    x_dbl.last()
    outp.push((2, 3))

    dtp.last()
    for k, y in blocks:
        s.dbl[y * width : (y + 1) * width, sequences[k]] = s.total[0, k, y].astype(F32)
    step_w = unfold_columns(s.dtp[...].astype(F32)).reshape(R, chans).astype(BF16)
    s.raw[...] = dot(s.dbl[:R].astype(BF16), step_w, TN) + dtb_ref[:, columns]
    for k, rows in enumerate(sequences):
        step = softplus(s.raw[rows])
        s.stepd[rows] = jnp.where(s.mask[k, :, 1:2] > 0.0, step, 1e30)
        s.drive[rows] = step * s.low[rows].astype(F32)
    s.a[...] = -jnp.exp(alog_ref[:, columns])
    s.state[0] = jnp.zeros((N, chans), F32)
    scan = Scan(
        s.a, s.stepd, s.drive, s.gs, s.read, s.read, s.gate, s.state, s.pulled, s.alog, s.spread, s.sum, s.gmap
    )
    scan.spread(s.dbl[R : R + 2 * N], s.shifted)
    steps = tokens // 8
    eighth = steps // 8
    inz.second()
    scan.forward(0, 4 * eighth)
    cot.first(3)
    outp.first()
    scan.forward(4 * eighth, steps)
    inz.last()
    s.gate[...] = dot(s.acts[0].reshape(tokens, feats), s.w[1].reshape(-1, chans))
    skip = skip_ref[:, columns]
    for rows in sequences:
        gate = s.gate[rows]
        scanned = s.read[rows] + skip * s.low[rows].astype(F32)
        s.gated[rows] = (scanned * gate * sigmoid(gate)).astype(BF16)

    mixed_sum, normed_sum = (
        TokenSum(spot, copies, part, s.y_land.at[k], s.z_land.at[k], s.y_sems.at[k], s.z_sems.at[k])
        for k, part in enumerate((s.mixed, s.acts.at[1]))
    )
    outw_sum, ginz_sum, ginx_sum, gdtp_sum = (
        RowSum(spot, copies, part, c_land, x_land, out, s.wc_sems.at[k], s.wx_sems.at[k], s.wz_sems.at[k])
        for k, (part, c_land, x_land, out) in enumerate((
            (s.outw, s.wc_land.at[0], s.wx_land.at[0], goutp_ref),
            (s.ginz, s.wc_land.at[1], s.wx_land.at[1], ginz_ref),
            (s.w.at[2], s.wc_land.at[2], s.wx_land.at[2], ginx_ref),
            (s.gdtp, s.dc_land, s.dx_land, gdtp_ref),
        ))
    )
    cot.last()
    for cols, owners in quarters:
        given = s.acts[1, :, :, :, cols].reshape(tokens, -1)
        s.outw[owners] = dot(given, s.gated[...], TN).astype(BF16).reshape(-1, *s.outw.shape[1:])
    outw_sum.push()
    outp.second()
    outw_sum.second()
    outp.last()
    s.gg[...] = dot(s.acts[1].reshape(tokens, feats), s.w[2].reshape(-1, chans))
    outw_sum.third((1,))
    for cols, owners in quarters:
        part = dot(s.gated[...], s.w[2, owners].reshape(-1, chans), NT)
        s.mixed[:, :, :, cols] = part.astype(BF16).reshape(*s.mixed.shape[:3], -1)
    mixed_sum.push()
    for rows in sequences:
        gate, gg = s.gate[rows], s.gg[rows]
        sig = sigmoid(gate)
        scanned = s.read[rows] + skip * s.low[rows].astype(F32)
        s.gs[rows] = gg * gate * sig
        s.ggate[rows] = (gg * scanned * sig * (1.0 + gate * (1.0 - sig))).astype(BF16)
    for cols, owners in quarters:
        given = s.acts[0, :, :, :, cols].reshape(tokens, -1)
        s.ginz[owners] = dot(given, s.ggate[...], TN).astype(BF16).reshape(-1, *s.ginz.shape[1:])
    ginz_sum.push()

    s.pulled[...] = jnp.zeros_like(s.pulled)
    s.alog[...] = jnp.zeros_like(s.alog)
    scan.backward(7 * eighth, steps)
    outw_sum.third((2,))
    ginz_sum.second()
    scan.backward(6 * eighth, 7 * eighth)
    outw_sum.third((3, 0))
    mixed_sum.stage(3)
    scan.backward(4 * eighth, 6 * eighth)
    ginz_sum.third((1,))
    scan.backward(2 * eighth, 4 * eighth)
    ginz_sum.third((2,))
    scan.backward(0, 2 * eighth)
    grad_bias = jnp.zeros((1, chans), F32)
    grad_skip = jnp.zeros((1, chans), F32)
    raw_rows = []
    for rows in sequences:
        conv, raw, gs, q = s.low[rows].astype(F32), s.raw[rows], s.gs[rows], s.read[rows]
        grad_raw = (conv * q + s.gate[rows]) * sigmoid(raw)
        s.gg[rows] = softplus(raw) * q + skip * gs
        grad_bias = grad_bias + jnp.sum(grad_raw, axis=0, keepdims=True)
        grad_skip = grad_skip + jnp.sum(gs * conv, axis=0, keepdims=True)
        raw_rows.append(grad_raw.astype(BF16))
    raw_low = jnp.concatenate(raw_rows, axis=0)
    dbl = jnp.concatenate([dot(step_w, raw_low, NT), s.gmap[...]], axis=0)
    for k, y in blocks:
        s.part[1, k, y] = dbl[y * width : (y + 1) * width, sequences[k]].astype(BF16)
    grad_dbl_sum = LineSum(
        spot, copies, s.part.at[1], s.landing.at[1], s.total.at[1], s.dbl_sems.at[1]
    )
    grad_dbl_sum.push()
    grad_step = dot(s.dbl[:R].astype(BF16), raw_low).reshape(4 * NZ, -1, chans)
    s.gdtp[...] = fold_columns(grad_step).astype(BF16)
    gdtp_sum.push()
    grad_dbl_sum.middle()
    mixed_sum.stage(2)
    ginz_sum.third((3, 0))
    gdtp_sum.second()
    grad_dbl_sum.last()

    grad_dbl = jnp.concatenate(
        [jnp.concatenate([s.total[1, k, y] for k in range(NZ)], axis=1) for y in range(2)], axis=0
    )
    s.gg[...] += dot(grad_dbl, x_proj, TN)
    sums = [jnp.zeros((1, chans), F32) for _ in range(5)]
    low_rows = []
    for k, rows in enumerate(sequences):
        pre, x_one = s.pre[rows], s.x_in[rows]
        sig = sigmoid(pre)
        one = s.gg[rows] * sig * (1.0 + pre * (1.0 - sig))
        sums[3] = sums[3] + jnp.sum(one * x_one, axis=0, keepdims=True)
        sums[4] = sums[4] + jnp.sum(one, axis=0, keepdims=True)
        grad_x = taps[3:4] * one
        for back in range(1, 4):
            masked = one * s.mask[k, :, back : back + 1]
            sums[3 - back] = sums[3 - back] + jnp.sum(masked * pltpu.roll(x_one, back, 0), axis=0, keepdims=True)
            grad_x = grad_x + taps[3 - back : 4 - back] * pltpu.roll(masked, length - back, 0)
        low_rows.append(grad_x.astype(BF16))
    grad_xin = jnp.concatenate(low_rows, axis=0)
    s.chan[...] = jnp.concatenate(
        [dot(grad_dbl, s.low[...]), s.alog[...] * s.a[...], grad_bias, grad_skip, jnp.zeros((6, chans), F32)]
        + sums + [jnp.zeros((3, chans), F32)], axis=0
    ).reshape(s.chan.shape)
    small_sum = ChannelSum(
        spot, copies, s.chan, s.fc_land, s.fx_land, s.f_own, full_ref, s.f_sems.at[0], s.f_sems.at[1], s.full_sems
    )
    small_sum.push()
    copies.settle(outp.group)
    for cols, owners in quarters:
        given = s.acts[0, :, :, :, cols].reshape(tokens, -1)
        s.w[2, owners] = dot(given, grad_xin, TN).astype(BF16).reshape(-1, *s.outw.shape[1:])
    ginx_sum.push()
    small_sum.second()
    cot.settle()
    for cols, owners in quarters:
        part = dot(grad_xin, s.w[0, owners].reshape(-1, chans), NT) + dot(s.ggate[...], s.w[1, owners].reshape(-1, chans), NT)
        s.acts[1, :, :, :, cols] = part.astype(BF16).reshape(*s.mixed.shape[:3], -1)
        gain_part = jnp.sum(part * s.acts[0, :, :, :, cols].reshape(tokens, -1).astype(F32), axis=0, keepdims=True)
        for k in range(NZ):
            owner = owners.start + k
            s.gain_part[0, owner : owner + 1] = gain_part[:, k * 128 : (k + 1) * 128] / s.info[owner, 0:1]
    copies.send(s.gain_part.at[0], s.gain_part.at[1], s.gain_sems.at[0], spot.y_mate)
    normed_sum.push()
    mixed_sum.stage(1)
    ginx_sum.second()
    gdtp_sum.third()
    ginx_sum.third((1,))
    normed_sum.stage(3)
    small_sum.third()
    ginx_sum.third((2,))
    arrived(s.gain_part.at[1], s.gain_sems.at[0])
    for k in range(4 * NZ):
        s.gain[k] = jnp.broadcast_to(s.gain_part[0, k : k + 1] + s.gain_part[1, k : k + 1], (8, 128))
    gain_group = copies.group(s.gain_land)
    for offset, dp in enumerate(plane):
        copies.send(s.gain.at[dp], s.gain_land.at[offset], s.gain_sems.at[1], (dp, spot.y), group=gain_group)
    normed_sum.stage(2)
    ginx_sum.third((3, 0))
    normed_sum.stage(1)
    small_sum.fourth()

    mixed = mixed_sum.last()
    resid = resid_ref[...]
    s.block[...] = resid + mixed
    copies.keep(s.block, block_ref)
    s.tile[2] = jnp.broadcast_to(jnp.sum(jnp.sum(mixed * mixed, axis=1, keepdims=True), axis=0, keepdims=True), (8, 128))
    copies.send(s.tile.at[2], s.tile.at[3], s.tile_sems.at[1], spot.y_mate)
    small_sum.fifth()
    outw_sum.last()
    ginz_sum.last()
    gdtp_sum.last()
    arrived(s.tile.at[1], s.tile_sems.at[0])
    s.squares[0] = s.tile[0] + s.tile[1]
    arrived(s.tile.at[3], s.tile_sems.at[1])
    s.squares[1] = s.tile[2] + s.tile[3]
    copies.keep(s.squares, squares_ref)

    grad_rows = normed_sum.last()
    inv = lax.rsqrt(jnp.sum(resid * resid, axis=1, keepdims=True) / feats + eps_norm)
    scaled = resid * inv
    gain = jnp.concatenate([s.info[k, 0:1] for k in range(4 * NZ)], axis=1)
    grad_scaled = grad_rows * gain
    mean = jnp.sum(grad_scaled * scaled, axis=1, keepdims=True) / feats
    s.gresid[...] = cot_ref[...] + inv * (grad_scaled - scaled * mean)
    copies.keep(s.gresid, gresid_ref)
    arrived(s.gain_land, s.gain_sems.at[1])
    total = s.gain[spot.dp]
    for offset in range(4 * NZ - 1):
        total = total + s.gain_land[offset]
    s.gain_total[...] = total
    copies.keep(s.gain_total, ggain_ref)
    ginx_sum.last()
    small_sum.last()
    copies.wait_sent()
    assert copies.used == s.send_sems.shape[0], copies.used


def block_call(in_x, in_z, out_p, residual, cotangent, gain, ids, dt_p, x_proj, conv_w, conv_b, dt_b, a_log, d_skip):
    half, feats = residual.shape
    rows, wide = in_x.shape
    n_dp, chans = 4 * NZ, wide // NZ
    held = block_scratch(half, feats, rows, chans, dt_p.shape[0], x_proj.shape[0])
    shape = jax.ShapeDtypeStruct
    outs = [
        shape((half, feats), F32), shape((half, feats), F32), shape((8, 128), F32),
        shape((NZ, rows, chans), BF16), shape((NZ, rows, chans), BF16), shape((NZ, rows, chans), BF16),
        shape((NZ, 2 * dt_p.shape[0], chans // 2), BF16), shape((n_dp, (x_proj.shape[0] + 32) // 4, chans), BF16),
        shape((2, 8, 128), F32),
    ]
    in_any = pl.BlockSpec(memory_space=pl.ANY)
    in_vmem = pl.BlockSpec(memory_space=pltpu.VMEM)
    return pl.pallas_call(
        functools.partial(block_kernel, list(held)),
        out_shape=outs,
        in_specs=[in_any] * 12 + [in_vmem] * 2,
        out_specs=[in_any] * len(outs),
        scratch_shapes=list(held.values()),
        name="block",
        compiler_params=pltpu.CompilerParams(collective_id=1, has_side_effects=True, vmem_limit_bytes=62 << 20),
    )(in_x, in_z, out_p, residual, cotangent, x_proj, ids, conv_w, conv_b, dt_b, a_log, d_skip, gain, dt_p)


def finish_kernel(
    scale, block_in, gresid_in, ginx_in, ginz_in, goutp_in, gdtp_in, full_in, ggain_in, squares_in,
    block_ref, gresid_ref, ginx_ref, ginz_ref, goutp_ref, gdtp_ref, xproj_ref, alog_ref, dtb_ref, skip_ref, convw_ref, convb_ref,
    ggain_ref, rms_ref, mrms_ref,
    token_s, low_s, step_s, full_s, ggain_s, squares_s, wide_s, gdtp_s, xproj_s, rows_s, in_sems, out_sems,
):
    begun = []

    def out(src, dst):
        copy = pltpu.make_async_copy(src, dst, out_sems.at[len(begun)])
        copy.start()
        begun.append(copy)

    reads = [
        pltpu.make_async_copy(src, dst, in_sems.at[k])
        for k, (src, dst) in enumerate(
            (
                (ginx_in, low_s.at[0]), (ginz_in, low_s.at[1]), (goutp_in, low_s.at[2]), (full_in, full_s), (gdtp_in, step_s),
                (block_in, token_s.at[0]), (gresid_in, token_s.at[1]), (ggain_in, ggain_s), (squares_in, squares_s),
            )
        )
    ]
    for read in reads:
        read.start()
    chans = low_s.shape[3]
    columns = [slice(z * chans, (z + 1) * chans) for z in range(NZ)]
    for k, ref in enumerate((ginx_ref, ginz_ref, goutp_ref)):
        reads[k].wait()
        for z, cols in enumerate(columns):
            wide_s[k, :, cols] = low_s[k, z].astype(F32)
        out(wide_s.at[k], ref)
    reads[3].wait()
    rows, width = full_s.shape[1], xproj_s.shape[0]
    for z, cols in enumerate(columns):
        for k in range(4):
            found = full_s[place(z, k % 2, k // 2)].astype(F32)
            upto = min(rows, width - k * rows)
            xproj_s[k * rows : k * rows + upto, cols] = found[:upto]
        rows_s[:, cols] = found[upto:]
    out(xproj_s, xproj_ref)
    out(rows_s.at[pl.ds(0, N)], alog_ref)
    for at, ref in ((N, dtb_ref), (N + 1, skip_ref), (24, convw_ref), (28, convb_ref)):
        out(rows_s.at[pl.ds(at, ref.shape[0])], ref)
    reads[4].wait()
    for z, cols in enumerate(columns):
        gdtp_s[:, cols] = unfold_columns(step_s[z].astype(F32))
    out(gdtp_s, gdtp_ref)
    for k, ref in enumerate((block_ref, gresid_ref)):
        reads[5 + k].wait()
        out(token_s.at[k], ref)
    reads[7].wait()
    out(ggain_s.at[pl.ds(0, 1)], ggain_ref)
    reads[8].wait()
    for k, ref in enumerate((rms_ref, mrms_ref)):
        ref[...] = jnp.sqrt(squares_s[k, 0:1, 0:1] * scale)
    for copy in begun:
        copy.wait()


def finish_call(block, gresid, ginx, ginz, goutp, gdtp, full, ggain, squares, width):
    rows, chans = ginx.shape[1:]
    wide = chans * NZ
    shape = lambda count, columns=wide: jax.ShapeDtypeStruct((count, columns), F32)
    vmem, dma = pltpu.VMEM, pltpu.SemaphoreType.DMA
    in_any = pl.BlockSpec(memory_space=pl.ANY)
    outs = [
        shape(*block.shape), shape(*gresid.shape), shape(rows), shape(rows), shape(rows), shape(gdtp.shape[1] // 2), shape(width),
        shape(N), shape(1), shape(1), shape(4), shape(1), shape(1, 128), shape(1, 1), shape(1, 1),
    ]
    return pl.pallas_call(
        functools.partial(finish_kernel, 1.0 / (2 * block.shape[0] * block.shape[1])),
        out_shape=outs,
        in_specs=[in_any] * 9,
        out_specs=[in_any] * (len(outs) - 2) + [pl.BlockSpec(memory_space=vmem)] * 2,
        scratch_shapes=[
            vmem((2,) + block.shape, F32), vmem((3,) + ginx.shape, BF16), vmem(gdtp.shape, BF16), vmem(full.shape, BF16),
            vmem(ggain.shape, F32), vmem(squares.shape, F32), vmem((3, rows, wide), F32), vmem((gdtp.shape[1] // 2, wide), F32),
            vmem((width, wide), F32), vmem((32, wide), F32), dma((9,)), dma((len(outs) - 2,)),
        ],
        name="finish",
        compiler_params=pltpu.CompilerParams(vmem_limit_bytes=60 << 20),
    )(block, gresid, ginx, ginz, goutp, gdtp, full, ggain, squares)


def per_device_split(
    residual,
    norm_gain,
    in_proj_x,
    in_proj_z,
    x_proj,
    dt_proj,
    dt_bias,
    conv_weight,
    conv_bias,
    a_log,
    d_skip,
    out_proj,
    doc_ids,
    cotangent,
):
    parts = block_call(
        in_proj_x, in_proj_z, out_proj, residual, cotangent, norm_gain[None], doc_ids[None], dt_proj, x_proj, conv_weight,
        conv_bias[None], dt_bias[None], a_log, d_skip[None],
    )
    block, gresid, ggain, ginx, ginz, goutp, gdtp, full, squares = parts
    block, gresid, ginx, ginz, goutp, gdtp, g_xproj, g_alog, g_dtb, g_skip, g_convw, g_convb, ggain, rms, mrms = finish_call(
        block, gresid, ginx, ginz, goutp, gdtp, full, ggain, squares, x_proj.shape[0]
    )
    return (
        block,
        gresid,
        ggain[0],
        ginx,
        ginz,
        g_xproj,
        gdtp,
        g_dtb[0],
        g_convw,
        g_convb[0],
        g_alog,
        g_skip[0],
        goutp,
        rms[0],
        mrms[0],
    )


def norm_rows(values, gain_val):
    mean_square = jnp.mean(values * values, axis=1, keepdims=True)
    return values * lax.rsqrt(mean_square + eps_norm) * gain_val


def conv_local(x_in, doc_ids, conv_weight, conv_bias):
    kernel_len = conv_weight.shape[0]
    length = x_in.shape[0]
    padded = jnp.pad(x_in, ((kernel_len - 1, 0), (0, 0)))
    id_pad = jnp.concatenate([jnp.full((kernel_len - 1,), -1, jnp.int32), doc_ids])
    summed = conv_bias + jnp.zeros_like(x_in)
    for offset in range(kernel_len):
        same_doc = (id_pad[offset : offset + length] == doc_ids).astype(jnp.float32)
        summed = summed + conv_weight[offset] * padded[offset : offset + length] * same_doc[:, None]
    return summed


def per_device(
    residual,
    norm_gain,
    in_proj_x,
    in_proj_z,
    x_proj,
    dt_proj,
    dt_bias,
    conv_weight,
    conv_bias,
    a_log,
    d_skip,
    out_proj,
    doc_ids,
    cotangent,
):
    gathered = (
        lax.all_gather(norm_gain, "dp", axis=0, tiled=True),
        lax.all_gather(in_proj_x, "dp", axis=0, tiled=True),
        lax.all_gather(in_proj_z, "dp", axis=0, tiled=True),
        lax.all_gather(dt_proj, "dp", axis=0, tiled=True),
        lax.all_gather(out_proj, "dp", axis=0, tiled=True),
    )
    gain_all, inx_all, inz_all, step_all, out_all = gathered
    seq_len = doc_ids.shape[0]
    normed_f32, norm_back = jax.vjp(norm_rows, residual, gain_all.astype(jnp.float32))
    normed = lax.all_gather(normed_f32.astype(jnp.bfloat16), "tensor", axis=0, tiled=True)
    x_in = jnp.dot(normed, inx_all, preferred_element_type=jnp.float32)
    gate_in = jnp.dot(normed, inz_all, preferred_element_type=jnp.float32)

    def conv_act(x_val, weight_val, bias_val):
        return jax.nn.silu(conv_local(x_val, doc_ids, weight_val, bias_val))

    conv_out, conv_back = jax.vjp(conv_act, x_in, conv_weight, conv_bias)
    conv_low = conv_out.astype(jnp.bfloat16)
    dbl_part = lax.dot_general(
        conv_low, x_proj, (((1,), (1,)), ((), ())), preferred_element_type=jnp.float32
    )
    x_dbl, resid_square = lax.psum((dbl_part, jnp.sum(residual * residual)), "tensor")
    doc_starts = doc_ids != jnp.concatenate([jnp.full((1,), -1, jnp.int32), doc_ids[:-1]])
    carry_keep = 1.0 - doc_starts.astype(jnp.float32)

    cot_all = lax.all_gather(cotangent.astype(jnp.bfloat16), "tensor", axis=0, tiled=True)
    grad_gated = jnp.dot(cot_all, out_all, preferred_element_type=jnp.float32)
    gated_low, grad_gate_low, grad_conv, grad_dbl_part, grad_step_w, grad_bias, grad_alog, grad_skip = scan_call(
        x_dbl, conv_low, gate_in, grad_gated, step_all, dt_bias, a_log, d_skip, carry_keep
    )
    mixed = lax.psum_scatter(
        lax.dot_general(
            gated_low, out_all, (((1,), (1,)), ((), ())), preferred_element_type=jnp.float32
        ),
        "tensor",
        scatter_dimension=0,
        tiled=True,
    )
    block_out = residual + mixed
    mixed_square = lax.psum(jnp.sum(mixed * mixed), "tensor")
    rms_resid = jnp.sqrt(resid_square / (seq_len * D)).reshape(1)
    rms_mixed = jnp.sqrt(mixed_square / (seq_len * D)).reshape(1)
    grad_out_w = lax.dot_general(
        cot_all, gated_low, (((0,), (0,)), ((), ())), preferred_element_type=jnp.float32
    )
    grad_dbl = lax.psum(grad_dbl_part.T, "tensor")
    grad_dbl_low = grad_dbl.astype(jnp.bfloat16)
    grad_conv = grad_conv + jnp.dot(grad_dbl_low, x_proj, preferred_element_type=jnp.float32)
    grad_xproj = lax.dot_general(
        grad_dbl_low, conv_low, (((0,), (0,)), ((), ())), preferred_element_type=jnp.float32
    )
    grad_xin, grad_convw, grad_convb = conv_back(grad_conv)
    grad_xin_low = grad_xin.astype(jnp.bfloat16)
    grad_inx = lax.dot_general(
        normed, grad_xin_low, (((0,), (0,)), ((), ())), preferred_element_type=jnp.float32
    )
    grad_inz = lax.dot_general(
        normed, grad_gate_low, (((0,), (0,)), ((), ())), preferred_element_type=jnp.float32
    )
    first_term = lax.dot_general(
        grad_xin_low, inx_all, (((1,), (1,)), ((), ())), preferred_element_type=jnp.float32
    )
    second_term = lax.dot_general(
        grad_gate_low, inz_all, (((1,), (1,)), ((), ())), preferred_element_type=jnp.float32
    )
    grad_normed = lax.psum_scatter(
        first_term + second_term, "tensor", scatter_dimension=0, tiled=True
    )
    grad_rows_x, grad_gain_part = norm_back(grad_normed)
    grad_residual = cotangent + grad_rows_x
    grad_gain = lax.psum(grad_gain_part, "tensor")
    gain_shard, inx_shard, inz_shard, step_shard, out_shard = (
        lax.psum_scatter(grad_gain, "dp", scatter_dimension=0, tiled=True),
        lax.psum_scatter(grad_inx, "dp", scatter_dimension=0, tiled=True),
        lax.psum_scatter(grad_inz, "dp", scatter_dimension=0, tiled=True),
        lax.psum_scatter(grad_step_w, "dp", scatter_dimension=0, tiled=True),
        lax.psum_scatter(grad_out_w, "dp", scatter_dimension=0, tiled=True),
    )
    small_sums = lax.psum(
        (grad_xproj, grad_bias, grad_convw, grad_convb, grad_alog, grad_skip), "dp"
    )
    xproj_sum, bias_sum, convw_sum, convb_sum, alog_sum, skip_sum = small_sums
    return (
        block_out,
        grad_residual,
        gain_shard,
        inx_shard,
        inz_shard,
        xproj_sum,
        step_shard,
        bias_sum,
        convw_sum,
        convb_sum,
        alog_sum,
        skip_sum,
        out_shard,
        rms_resid,
        rms_mixed,
    )


def solution(mesh):
    placed = (
        P(("dp", "tensor"), None),
        P("dp"),
        P("dp", "tensor"),
        P("dp", "tensor"),
        P(None, "tensor"),
        P("dp", "tensor"),
        P("tensor"),
        P(None, "tensor"),
        P("tensor"),
        P(None, "tensor"),
        P("tensor"),
        P("dp", "tensor"),
        P("dp"),
        P(("dp", "tensor"), None),
    )
    return jax.shard_map(
        per_device_split if mesh.shape["dp"] == 4 * NZ else per_device,
        mesh=mesh,
        in_specs=placed,
        out_specs=(
            P(("dp", "tensor"), None),
            P(("dp", "tensor"), None),
            P("dp"),
            P("dp", "tensor"),
            P("dp", "tensor"),
            P(None, "tensor"),
            P("dp", "tensor"),
            P("tensor"),
            P(None, "tensor"),
            P("tensor"),
            P(None, "tensor"),
            P("tensor"),
            P("dp", "tensor"),
            P("dp"),
            P("dp"),
        ),
        check_vma=False,
    )
```

```python
import functools

import jax
import jax.numpy as jnp
from jax import lax
from jax.experimental import pallas as pl
from jax.experimental.pallas import tpu as pltpu
from jax.sharding import PartitionSpec as P

D = 2048
R = 128
N = 16

eps_norm = 1e-05


def sigmoid(v):
    return 1.0 / (1.0 + jnp.exp(-v))


def softplus(v):
    return jnp.maximum(v, 0.0) + jnp.log(1.0 + jnp.exp(-jnp.abs(v)))


def fold_rows(first, second, shift, lower):
    kept = jnp.where(lower, first, second)
    moved = jnp.where(lower, second, first)
    return kept + pltpu.roll(moved, shift, 0)


class RowSums:
    def __init__(self, masks):
        self.masks = masks
        self.held = {}
        self.result = None

    def add(self, token, value):
        level = 0
        while True:
            if level == 3:
                self.result = value
                return
            mate = (level, token ^ 1)
            if mate not in self.held:
                self.held[(level, token)] = value
                return
            other = self.held.pop(mate)
            first, second = (other, value) if token & 1 else (value, other)
            value = fold_rows(first, second, 1 << level, self.masks[level])
            token >>= 1
            level += 1


def split_dot(left, right_low, dims):
    high = left.astype(jnp.bfloat16)
    rest = (left - high.astype(jnp.float32)).astype(jnp.bfloat16)
    return lax.dot_general(high, right_low, dims, preferred_element_type=jnp.float32) + lax.dot_general(
        rest, right_low, dims, preferred_element_type=jnp.float32
    )


def scan_kernel(
    dbl_ref, conv_ref, gate_ref, gg_ref, dtp_ref, dtb_ref, alog_ref, skip_ref, keep_ref, in_ref, out_ref,
    gated_ref, ggate_ref, gconv_ref, gdbl_ref, gin_ref, gout_ref, gdtp_ref, gdtb_ref, galog_ref, gskip_ref,
    h_s, d_s, stepd_s, sc_s, gs_s, y_s, q_s, r_s, a_s,
):
    length, width = conv_ref.shape
    blocks = width // 128
    part = pl.program_id(0)
    sub = lax.broadcasted_iota(jnp.int32, (8, 128), 0)
    masks = [(sub & shift) == 0 for shift in (1, 2, 4)]
    lanes = [slice(b * 128, (b + 1) * 128) for b in range(blocks)]

    nn = (((1,), (0,)), ((), ()))
    step_raw = split_dot(dbl_ref[...], dtp_ref[...], nn) + dtb_ref[...]
    step = jnp.maximum(step_raw, 0.0) + jnp.log(1.0 + jnp.exp(-jnp.abs(step_raw)))
    stepd_s[...] = jnp.where(keep_ref[...] > 0.0, step, 1e30)
    sc_s[...] = step * conv_ref[...].astype(jnp.float32)
    gate = gate_ref[...]
    gs_s[...] = gg_ref[...] * gate * sigmoid(gate)
    a_s[...] = -jnp.exp(alog_ref[...])

    h_s[0] = jnp.zeros((N, width), jnp.float32)

    def forward(i, hs):
        base = pl.multiple_of(i * 8, 8)
        hs = list(hs)
        sums = [RowSums(masks) for _ in range(blocks)]
        stepd = [stepd_s[pl.ds(base, 8), lanes[b]] for b in range(blocks)]
        drive = [sc_s[pl.ds(base, 8), lanes[b]] for b in range(blocks)]
        for j in range(8):
            t = base + j
            in_t = in_ref[t]
            out_t = out_ref[t]
            for b in range(blocks):
                decay = jnp.exp(stepd[b][j : j + 1] * a_s[:, lanes[b]])
                hs[b] = decay * hs[b] + drive[b][j : j + 1] * in_t
                d_s[t, :, lanes[b]] = decay
                h_s[t + 1, :, lanes[b]] = hs[b]
                read = hs[b] * out_t
                sums[b].add(j, read[:8] + read[8:])
        for b in range(blocks):
            y_s[pl.ds(base, 8), lanes[b]] = sums[b].result
        return tuple(hs)

    zero = jnp.zeros((N, 128), jnp.float32)
    lax.fori_loop(0, length // 8, forward, (zero,) * blocks)

    conv = conv_ref[...].astype(jnp.float32)
    gate = gate_ref[...]
    sig = sigmoid(gate)
    scanned = y_s[...] + skip_ref[...] * conv
    gated_ref[...] = (scanned * gate * sig).astype(jnp.bfloat16)
    ggate_ref[...] = (gg_ref[...] * scanned * sig * (1.0 + gate * (1.0 - sig))).astype(jnp.bfloat16)

    @pl.when(part == 0)
    def _():
        gin_ref[...] = jnp.zeros_like(gin_ref)
        gout_ref[...] = jnp.zeros_like(gout_ref)
        gdbl_ref[...] = jnp.zeros_like(gdbl_ref)

    def backward(i, carried):
        base = pl.multiple_of(length - 8 - i * 8, 8)
        pulled, alog_sum = list(carried[0]), list(carried[1])
        q_sums = [RowSums(masks) for _ in range(blocks)]
        r_sums = [RowSums(masks) for _ in range(blocks)]
        stepd = [stepd_s[pl.ds(base, 8), lanes[b]] for b in range(blocks)]
        drive = [sc_s[pl.ds(base, 8), lanes[b]] for b in range(blocks)]
        gs = [gs_s[pl.ds(base, 8), lanes[b]] for b in range(blocks)]
        for j in reversed(range(8)):
            t = base + j
            in_t = in_ref[t]
            out_t = out_ref[t]
            gin_t = gin_ref[t]
            gout_t = gout_ref[t]
            for b in range(blocks):
                gs_t = gs[b][j : j + 1]
                adjoint = pulled[b] + out_t * gs_t
                gout_t = gout_t + gs_t * h_s[t + 1, :, lanes[b]]
                gin_t = gin_t + adjoint * drive[b][j : j + 1]
                q_t = adjoint * in_t
                q_sums[b].add(j, q_t[:8] + q_t[8:])
                pulled[b] = d_s[t, :, lanes[b]] * adjoint
                past = pulled[b] * h_s[t, :, lanes[b]]
                r_t = past * a_s[:, lanes[b]]
                r_sums[b].add(j, r_t[:8] + r_t[8:])
                alog_sum[b] = alog_sum[b] + past * stepd[b][j : j + 1]
            gin_ref[t] = gin_t
            gout_ref[t] = gout_t
        for b in range(blocks):
            q_s[pl.ds(base, 8), lanes[b]] = q_sums[b].result
            r_s[pl.ds(base, 8), lanes[b]] = r_sums[b].result
        return tuple(pulled), tuple(alog_sum)

    _, alog_sum = lax.fori_loop(0, length // 8, backward, ((zero,) * blocks, (zero,) * blocks))
    for b in range(blocks):
        galog_ref[:, lanes[b]] = alog_sum[b] * a_s[:, lanes[b]]

    conv = conv_ref[...].astype(jnp.float32)
    step_raw = split_dot(dbl_ref[...], dtp_ref[...], nn) + dtb_ref[...]
    step = jnp.maximum(step_raw, 0.0) + jnp.log(1.0 + jnp.exp(-jnp.abs(step_raw)))
    raw = (conv * q_s[...] + r_s[...]) * sigmoid(step_raw)
    gs = gs_s[...]
    gconv_ref[...] = step * q_s[...] + skip_ref[...] * gs
    gskip_ref[...] = jnp.sum(gs * conv, axis=0, keepdims=True)
    gdtb_ref[...] = jnp.sum(raw, axis=0, keepdims=True)
    raw_low = raw.astype(jnp.bfloat16)
    gdtp_ref[...] = lax.dot_general(
        dbl_ref[...].astype(jnp.bfloat16), raw_low, (((0,), (0,)), ((), ())), preferred_element_type=jnp.float32
    )
    gdbl_ref[...] += lax.dot_general(
        dtp_ref[...], raw_low, (((1,), (1,)), ((), ())), preferred_element_type=jnp.float32
    )


def scan_call(dbl, conv, gate, gg, dtp, dtb, alog, skip, keep):
    length, chans = conv.shape
    cb = min(65536 // length, chans)
    f32 = jnp.float32
    maps = jnp.broadcast_to(dbl[:, R:, None], (length, 2 * N, 128))
    tokens = lambda kind: (jax.ShapeDtypeStruct((length, chans), kind), pl.BlockSpec((length, cb), lambda i: (0, i)))
    whole = lambda *shape: (jax.ShapeDtypeStruct(shape, f32), pl.BlockSpec(shape, lambda i: (0,) * len(shape)))
    rows = lambda count: (jax.ShapeDtypeStruct((count, chans), f32), pl.BlockSpec((count, cb), lambda i: (0, i)))
    outs = [
        tokens(jnp.bfloat16), tokens(jnp.bfloat16), tokens(f32), whole(R, length), whole(length, N, 128), whole(length, N, 128),
        rows(R), rows(1), rows(N), rows(1),
    ]
    ins = [
        whole(length, R), tokens(f32), tokens(f32), tokens(f32), rows(R), rows(1), rows(N), rows(1),
        whole(length, 1),
    ]
    res = pl.pallas_call(
        scan_kernel,
        grid=(chans // cb,),
        in_specs=[spec for _, spec in ins] + [
            pl.BlockSpec((length, N, 128), lambda i: (0, 0, 0)), pl.BlockSpec((length, N, 128), lambda i: (0, 1, 0))],
        out_specs=[spec for _, spec in outs],
        out_shape=[shape for shape, _ in outs],
        scratch_shapes=[
            pltpu.VMEM((length + 1, N, cb), f32), pltpu.VMEM((length, N, cb), f32),
        ] + [pltpu.VMEM((length, cb), f32)] * 6 + [pltpu.VMEM((N, cb), f32)],
        name="selective_scan",
        compiler_params=pltpu.CompilerParams(vmem_limit_bytes=60 << 20),
    )(dbl[:, :R], conv, gate, gg, dtp, dtb[None], alog, skip[None], keep[:, None], maps, maps)
    gated, ggate, gconv, gdbl, gin, gout, gdtp, gdtb, galog, gskip = res
    gdbl_all = jnp.concatenate([gdbl, jnp.sum(gin, -1).T, jnp.sum(gout, -1).T], axis=0)
    return gated, ggate, gconv, gdbl_all, gdtp, gdtb[0], galog, gskip[0]


MESH = pl.DeviceIdType.MESH
NZ = 4
F32 = jnp.float32
BF16 = jnp.bfloat16
NN = (((1,), (0,)), ((), ()))
NT = (((1,), (1,)), ((), ()))
TN = (((0,), (0,)), ((), ()))


def dot(left, right, dims=NN):
    return lax.dot_general(left, right, dims, preferred_element_type=F32)


def place(z, x, c):
    return (z * 2 + x) * 2 + c


class Spot:
    def __init__(self):
        self.dp = lax.axis_index("dp")
        self.y = lax.axis_index("tensor")
        self.z, self.x, self.c = self.dp // 4, (self.dp // 2) % 2, self.dp % 2
        self.x_mate = (place(self.z, 1 - self.x, self.c), self.y)
        self.c_mate = (place(self.z, self.x, 1 - self.c), self.y)
        self.y_mate = (self.dp, 1 - self.y)

        far, near = jnp.where(self.z < 2, 3, 0), 1 + self.z % 2
        self.others = [far, 6 - self.z - far - near, near]

    def turn(self, k):
        return self.others[k - 1] if k else self.z

    def z_at(self, offset):
        return lax.rem(self.z + offset + NZ, NZ)

    def slot(self, origin, device):
        if device is self.c_mate:
            return 2 * NZ
        return origin // 4 + (NZ if device is self.x_mate else 0)

    def on_line(self, z, y=None):
        return (place(z, self.x, self.c), self.y if y is None else y)


def greet(devices):
    barrier = pltpu.get_barrier_semaphore()
    for device in devices:
        pl.semaphore_signal(barrier, inc=1, device_id=device, device_id_type=MESH)
    pl.semaphore_wait(barrier, len(devices))


class Copies:
    def __init__(self, send_sems, own_sems):
        self.send_sems, self.own_sems = send_sems, own_sems
        self.used, self.groups, self.begun, self.kept = 0, [], [], []

    def new_sem(self):
        self.used += 1
        return self.send_sems.at[self.used - 1]

    def group(self, whole):
        sem = self.new_sem()
        self.groups.append((sem, pltpu.make_async_copy(whole, whole, sem).wait))
        return sem

    def settle(self, *sems):
        for sem, wait in self.groups:
            if any(sem is one for one in sems):
                wait()
        self.groups = [(sem, wait) for sem, wait in self.groups if all(sem is not one for one in sems)]

    def send(self, src, dst, recv_sem, device, when=None, group=None):
        copy = pltpu.make_async_remote_copy(
            src_ref=src, dst_ref=dst, send_sem=self.new_sem() if group is None else group, recv_sem=recv_sem,
            device_id=device, device_id_type=MESH,
        )
        if group is None:
            self.begun.append((when, copy.wait_send))
        if when is None:
            copy.start()
        else:
            pl.when(when)(copy.start)

    def keep(self, src, dst):
        copy = pltpu.make_async_copy(src, dst, self.own_sems.at[len(self.kept)])
        copy.start()
        self.kept.append(copy)

    def wait_sent(self):
        self.settle(*[sem for sem, _ in self.groups])
        self.settle_alone(self.begun)
        for copy in self.kept:
            copy.wait()

    def settle_alone(self, begun):
        for when, wait in begun:
            if when is None:
                wait()
            else:
                pl.when(when)(wait)
        self.begun = [one for one in self.begun if all(one is not done for done in begun)]


def arrived(dst, recv_sem, when=None):
    copy = pltpu.make_async_copy(dst, dst, recv_sem)
    if when is None:
        copy.wait()
    else:
        pl.when(when)(copy.wait)


class Gather:
    def __init__(self, spot, copies, src, dst, recv_sems, own_sem):
        self.spot, self.copies, self.src, self.dst, self.recv_sems, self.own_sem = spot, copies, src, dst, recv_sems, own_sem
        self.width = dst.shape[-1]
        self.group = copies.group(dst.at[pl.ds(0, 4 * NZ - 1)])

    def columns(self, z):
        return self.src.at[:, pl.ds(pl.multiple_of(z * self.width, self.width), self.width)]

    def push(self, offsets=(1, 2, 3, 0)):
        spot, me = self.spot, self.spot.dp
        for offset in offsets:
            if offset == 0:
                self.push_own()
                continue
            z = spot.turn(offset)
            self.copies.send(self.columns(z), self.dst.at[me], self.recv_sems.at[spot.z], spot.on_line(z), group=self.group)

    def push_own(self):
        spot, me = self.spot, self.spot.dp
        self.own = pltpu.make_async_copy(self.columns(spot.z), self.dst.at[me], self.own_sem)
        self.own.start()
        self.pass_on(me, spot.x_mate, self.columns(spot.z))
        self.pass_on(me, spot.c_mate, self.columns(spot.z))

    def pass_on(self, origin, device, src=None):
        sem = self.recv_sems.at[self.spot.slot(origin, device)]
        src = self.dst.at[origin] if src is None else src
        self.copies.send(src, self.dst.at[origin], sem, device, group=self.group)

    def first(self):
        spot = self.spot
        for offset in range(1, NZ):
            z = spot.turn(offset)
            origin = place(z, spot.x, spot.c)
            arrived(self.dst.at[origin], self.recv_sems.at[z])
            self.pass_on(origin, spot.x_mate)
            self.pass_on(origin, spot.c_mate)

    def second(self):
        spot = self.spot
        for offset in range(NZ):
            z = spot.turn(offset)
            origin = place(z, 1 - spot.x, spot.c)
            arrived(self.dst.at[origin], self.recv_sems.at[NZ + z])
            self.pass_on(origin, spot.c_mate)

    def last(self):
        self.own.wait()
        arrived(self.dst.at[pl.ds(0, 2 * NZ)], self.recv_sems.at[2 * NZ])


class BlockGather(Gather):
    def columns(self, z):
        return self.src.at[z]


def fold_columns(values):
    half = values.shape[-1] // 2
    return jnp.concatenate([values[..., :half], values[..., half:]], axis=-2)


def unfold_columns(values):
    rows = values.shape[-2] // 2
    return jnp.concatenate([values[..., :rows, :], values[..., rows:, :]], axis=-1)


class LineSum:
    def __init__(self, spot, copies, part, landing, total, sems):
        self.spot, self.copies, self.part, self.landing, self.total, self.sems = spot, copies, part, landing, total, sems
        self.offsets = [(dz, dy) for dz in range(NZ) for dy in range(2) if dz + dy > 0]
        self.all_others = landing.at[pl.ds(0, len(self.offsets))]
        self.groups = [copies.group(self.all_others) for _ in range(2)]

    def there(self, dz, dy):
        return self.spot.z_at(dz), lax.rem(self.spot.y + dy, 2)

    def push(self):
        for k, (dz, dy) in enumerate(self.offsets):
            z, y = self.there(dz, dy)
            self.copies.send(self.part.at[z, y], self.landing.at[k], self.sems.at[0], self.spot.on_line(z, y), group=self.groups[0])

    def middle(self):
        own_z, own_y = self.spot.z, self.spot.y
        arrived(self.all_others, self.sems.at[0])
        summed = self.part[own_z, own_y].astype(F32)
        for k in range(len(self.offsets)):
            summed = summed + self.landing[k].astype(F32)
        self.total[own_z, own_y] = summed.astype(BF16)
        own = self.total.at[own_z, own_y]
        for dz, dy in self.offsets:
            self.copies.send(own, own, self.sems.at[1], self.spot.on_line(*self.there(dz, dy)), group=self.groups[1])

    def last(self):
        arrived(self.all_others, self.sems.at[1])


def column_masks(tile):
    return jnp.concatenate([tile] * 16, axis=0).T


class Share:
    def __init__(self, spot, copies, dst, recv_sems):
        self.spot, self.copies, self.dst, self.recv_sems = spot, copies, dst, recv_sems
        self.over_y, self.alone = copies.group(dst.at[pl.ds(0, NZ // 2)]), []

    def send(self, z, device, when=None):
        own = self.dst.at[z, self.spot.y]
        self.copies.send(own, own, self.recv_sems.at[z], device, when)
        self.alone.append(self.copies.begun[-1])

    def settle(self):
        self.copies.settle(self.over_y)
        self.copies.settle_alone(self.alone)

    def send_y(self, z, when=None):
        own = self.dst.at[z, self.spot.y]
        self.copies.send(own, own, self.recv_sems.at[NZ], self.spot.y_mate, when, self.over_y)

    def push(self, over_y=True):
        spot = self.spot
        self.send(spot.z, spot.on_line(spot.z_at(1)), spot.z < NZ - 1)
        self.send(spot.z, spot.on_line(spot.z_at(-1)), spot.z > 0)
        if over_y:
            self.send_y(spot.z)

    def first(self, far):
        spot = self.spot
        for way in (1, -1):
            origin = spot.z_at(-way * far)
            comes = spot.z >= far if way == 1 else spot.z < NZ - far
            goes = comes & (spot.z < NZ - 1 if way == 1 else spot.z > 0)
            arrived(self.dst.at[origin, spot.y], self.recv_sems.at[origin], comes)
            if far < NZ - 1:
                self.send(origin, spot.on_line(spot.z_at(way)), goes)
            self.send_y(origin, comes)

    def last(self):
        arrived(self.dst.at[pl.ds(0, NZ // 2)], self.recv_sems.at[NZ])


class Scan:
    def __init__(self, a_s, stepd_s, drive_s, gs_s, read_s, q_s, r_s, state_s, pulled_s, alog_s, spread_s, sum_s, gmap_s):
        self.a_s, self.stepd_s, self.drive_s, self.gs_s = a_s, stepd_s, drive_s, gs_s
        self.read_s, self.q_s, self.r_s, self.state_s = read_s, q_s, r_s, state_s
        self.pulled_s, self.alog_s, self.spread_s, self.sum_s, self.gmap_s = pulled_s, alog_s, spread_s, sum_s, gmap_s
        sub = lax.broadcasted_iota(jnp.int32, (8, 128), 0)
        self.masks = [(sub & shift) == 0 for shift in (1, 2, 4)]
        self.lane = lax.broadcasted_iota(jnp.int32, (N, 128), 1)
        self.blocks = [slice(b * 128, (b + 1) * 128) for b in range(a_s.shape[1] // 128)]

    def place(self, i):
        base = pl.multiple_of(i * 8, 8)
        tile = pl.ds(pl.multiple_of((base // 128) * 128, 128), 128)
        return base, tile, lax.rem(base, 128)

    def spread(self, maps, shifted_s):
        rows = maps.shape[0]
        for i in range(maps.shape[1] // 8):
            tile, first = maps[:, i // 16 * 128 : (i // 16 + 1) * 128], i % 16 * 8
            shifted_s[i * rows : (i + 1) * rows] = pltpu.roll(tile, (128 - first) % 128, 1).astype(BF16)
        row = lax.broadcasted_iota(jnp.int32, (128, 8 * 128), 0)
        column = lax.broadcasted_iota(jnp.int32, (128, 8 * 128), 1)
        chosen = jnp.where(row == column // 128, 1.0, 0.0).astype(BF16)
        self.spread_s[...] = dot(shifted_s[...], chosen).reshape(self.spread_s.shape)

    def maps_at(self, i, j):
        lanes = slice(j * 128, (j + 1) * 128)
        return self.spread_s[i, :N, lanes], self.spread_s[i, N:, lanes]

    def forward(self, start, stop):
        def chunk(i, none):
            base = pl.multiple_of(i * 8, 8)
            for lanes in self.blocks:
                state = self.state_s[i, :, lanes]
                a = self.a_s[:, lanes]
                stepd, drive = self.stepd_s[pl.ds(base, 8), lanes], self.drive_s[pl.ds(base, 8), lanes]
                sums = RowSums(self.masks)
                for j in range(8):
                    in_map, out_map = self.maps_at(i, j)
                    state = jnp.exp(stepd[j : j + 1] * a) * state + drive[j : j + 1] * in_map
                    read = state * out_map
                    sums.add(j, read[:8] + read[8:])
                self.state_s[i + 1, :, lanes] = state
                self.read_s[pl.ds(base, 8), lanes] = sums.result
            return none

        lax.fori_loop(start, stop, chunk, 0)

    def backward(self, start, stop):
        def chunk(step, none):
            i = start + stop - 1 - step
            base, tile, first = self.place(i)
            for b, lanes in enumerate(self.blocks):
                a = self.a_s[:, lanes]
                stepd, drive = self.stepd_s[pl.ds(base, 8), lanes], self.drive_s[pl.ds(base, 8), lanes]
                gs = self.gs_s[pl.ds(base, 8), lanes]
                states, decays = [self.state_s[i, :, lanes]], []
                for j in range(8):
                    decays.append(jnp.exp(stepd[j : j + 1] * a))
                    states.append(decays[j] * states[j] + drive[j : j + 1] * self.maps_at(i, j)[0])
                pulled, alog = self.pulled_s[:, lanes], self.alog_s[:, lanes]
                q_sums, r_sums = RowSums(self.masks), RowSums(self.masks)
                for j in reversed(range(8)):
                    in_map, out_map = self.maps_at(i, j)
                    adjoint = pulled + out_map * gs[j : j + 1]
                    g_in, g_out = adjoint * drive[j : j + 1], states[j + 1] * gs[j : j + 1]
                    if b > 0:
                        g_in, g_out = g_in + self.sum_s[0, j], g_out + self.sum_s[1, j]
                    self.sum_s[0, j], self.sum_s[1, j] = g_in, g_out
                    q_t = adjoint * in_map
                    q_sums.add(j, q_t[:8] + q_t[8:])
                    pulled = decays[j] * adjoint
                    past = pulled * states[j]
                    r_t = past * a
                    r_sums.add(j, r_t[:8] + r_t[8:])
                    alog = alog + past * stepd[j : j + 1]
                self.pulled_s[:, lanes], self.alog_s[:, lanes] = pulled, alog
                self.q_s[pl.ds(base, 8), lanes] = q_sums.result
                self.r_s[pl.ds(base, 8), lanes] = r_sums.result
            for k in range(2):
                row = self.gmap_s[k * N : (k + 1) * N, tile]
                for j in range(8):
                    row = jnp.where(self.lane == first + j, jnp.sum(self.sum_s[k, j], axis=1, keepdims=True), row)
                self.gmap_s[k * N : (k + 1) * N, tile] = row
            return none

        lax.fori_loop(start, stop, chunk, 0)


class TokenSum:
    def __init__(self, spot, copies, part, y_land, z_land, y_sems, z_sems):
        self.spot, self.copies, self.part, self.y_land, self.z_land = spot, copies, part, y_land, z_land
        self.y_sems, self.z_sems = y_sems, z_sems
        self.group = copies.group(y_land)

    def push(self):
        spot = self.spot
        for far in (3, 2, 1):
            for way in (1, -1):
                self.over_y(spot.z_at(way * far), self.within(way, far))
        self.over_y(spot.z, None)

    def within(self, way, far):
        return self.spot.z < NZ - far if way == 1 else self.spot.z >= far

    def over_y(self, z, when):
        self.copies.send(self.part.at[z, 1 - self.spot.y], self.y_land.at[z], self.y_sems.at[z], self.spot.y_mate, when, self.group)

    def add(self, z, landed):
        part, y = self.part, self.spot.y
        part[z, y] = (part[z, y].astype(F32) + landed[...].astype(F32)).astype(BF16)

    def stage(self, far):
        spot = self.spot
        for side, way in enumerate((1, -1)):
            z = spot.z_at(way * far)
            goes = self.within(way, far)
            grown = goes & self.within(-way, 1)
            land, sem = self.z_land.at[side, z], self.z_sems.at[side, z]

            @pl.when(goes)
            def _(z=z):
                arrived(self.y_land.at[z], self.y_sems.at[z])
                self.add(z, self.y_land.at[z])

            if far < NZ - 1:

                @pl.when(grown)
                def _(z=z, land=land, sem=sem):
                    arrived(land, sem)
                    self.add(z, land)

            self.copies.send(self.part.at[z, spot.y], land, sem, spot.on_line(spot.z_at(way)), goes)

    def last(self):
        spot = self.spot
        z = spot.z
        arrived(self.y_land.at[z], self.y_sems.at[z])
        self.add(z, self.y_land.at[z])
        for side, way in enumerate((1, -1)):

            @pl.when(self.within(-way, 1))
            def _(land=self.z_land.at[side, z], sem=self.z_sems.at[side, z]):
                arrived(land, sem)
                self.add(z, land)

        return self.part[z, spot.y].astype(F32)


class RowSum:
    def __init__(self, spot, copies, part, c_land, x_land, z_land, c_sems, x_sems, z_sem):
        self.spot, self.copies, self.part = spot, copies, part
        self.c_land, self.x_land, self.z_land = c_land, x_land, z_land
        self.c_sems, self.x_sems, self.z_sem = c_sems, x_sems, z_sem
        self.groups = [copies.group(whole) for whole in (c_land, x_land, z_land.at[pl.ds(0, NZ - 1)])]

    def push(self):
        spot = self.spot
        for offset in (1, 2, 3, 0):
            z = spot.turn(offset)
            for x in range(2):
                self.copies.send(
                    self.part.at[place(z, x, 1 - spot.c)], self.c_land.at[z, x], self.c_sems.at[z], spot.c_mate, group=self.groups[0]
                )

    def add(self, z, x, landed):
        part, owner = self.part, place(z, x, self.spot.c)
        part[owner] = (part[owner].astype(F32) + landed.astype(F32)).astype(part.dtype)

    def second(self):
        spot = self.spot
        for offset in (1, 2, 3, 0):
            z = spot.turn(offset)
            arrived(self.c_land.at[z], self.c_sems.at[z])
            for x in range(2):
                self.add(z, x, self.c_land[z, x])
            self.copies.send(
                self.part.at[place(z, 1 - spot.x, spot.c)], self.x_land.at[z], self.x_sems.at[z], spot.x_mate, group=self.groups[1]
            )

    def third(self, offsets=(1, 2, 3, 0)):
        spot = self.spot
        for offset in offsets:
            z = spot.turn(offset)
            arrived(self.x_land.at[z], self.x_sems.at[z])
            self.add(z, spot.x, self.x_land[z])
            own = self.part.at[place(z, spot.x, spot.c)]
            if offset:
                self.copies.send(own, self.z_land.at[spot.z], self.z_sem, spot.on_line(z), group=self.groups[2])
            else:
                self.copies.keep(own, self.z_land.at[z])

    def last(self):
        arrived(self.z_land.at[pl.ds(0, NZ - 1)], self.z_sem)


class ChannelSum:
    def __init__(self, spot, copies, part, c_land, x_land, own, full, c_sem, x_sem, full_sems):
        self.spot, self.copies, self.part, self.own, self.full, self.full_sems = spot, copies, part, own, full, full_sems
        self.c_land, self.x_land, self.c_sem, self.x_sem = c_land, x_land, c_sem, x_sem
        self.group = copies.group(full.at[pl.ds(0, 4 * NZ - 1)])

    def push(self):
        self.copies.send(self.part.at[1 - self.spot.c], self.c_land, self.c_sem, self.spot.c_mate)

    def second(self):
        spot = self.spot
        arrived(self.c_land, self.c_sem)
        self.part[spot.c] = self.part[spot.c] + self.c_land[...]
        self.copies.send(self.part.at[spot.c, 1 - spot.x], self.x_land, self.x_sem, spot.x_mate)

    def spread(self, origin, device, src=None):
        src = self.full.at[origin] if src is None else src
        sem = self.full_sems.at[self.spot.slot(origin, device)]
        self.copies.send(src, self.full.at[origin], sem, device, group=self.group)

    def third(self):
        spot = self.spot
        arrived(self.x_land, self.x_sem)
        self.own[...] = (self.part[spot.c, spot.x] + self.x_land[...]).astype(BF16)
        for device in [spot.on_line(spot.z_at(offset)) for offset in (1, 2, 3)] + [spot.x_mate, spot.c_mate]:
            self.spread(spot.dp, device, self.own)
        self.copies.keep(self.own, self.full.at[spot.dp])

    def fourth(self):
        spot = self.spot
        for offset in (1, 2, 3):
            z = spot.z_at(-offset)
            origin = place(z, spot.x, spot.c)
            arrived(self.full.at[origin], self.full_sems.at[z])
            self.spread(origin, spot.x_mate)
            self.spread(origin, spot.c_mate)

    def fifth(self):
        spot = self.spot
        for offset in range(NZ):
            z = spot.z_at(-offset)
            origin = place(z, 1 - spot.x, spot.c)
            arrived(self.full.at[origin], self.full_sems.at[NZ + z])
            self.spread(origin, spot.c_mate)

    def last(self):
        arrived(self.full.at[pl.ds(0, 2 * NZ)], self.full_sems.at[2 * NZ])


class Held:
    def __init__(self, names, refs):
        for name, ref in zip(names, refs, strict=True):
            setattr(self, name, ref)


def block_scratch(half, feats, rows, chans, step_rows, width):
    tokens, n_dp, length = 2 * half * NZ, 4 * NZ, 2 * half
    vmem, dma = pltpu.VMEM, pltpu.SemaphoreType.DMA
    owners, steps = (n_dp, rows, chans), (n_dp, 2 * step_rows, chans // 2)
    part = (NZ, 2, width // 2, length)
    small = (width + 32) // 4
    held = {
        "w": vmem((3, n_dp, rows, chans), BF16),
        "acts": vmem((2, NZ, 2, half, feats), BF16),
        "dtp_own": vmem((NZ,) + steps[1:], BF16),
        "dtp": vmem(steps, BF16),
        "info": vmem((n_dp, 8, 128), F32),
        "mask": vmem((NZ, length, 128), F32),
        "low": vmem((tokens, chans), BF16),
        "gated": vmem((tokens, chans), BF16),
        "ggate": vmem((tokens, chans), BF16),
    }
    for name in ("x_in", "pre", "gate", "gg", "raw", "stepd", "drive", "gs", "read"):
        held[name] = vmem((tokens, chans), F32)
    held |= {
        "a": vmem((N, chans), F32),
        "state": vmem((tokens // 8 + 1, N, chans), F32),
        "pulled": vmem((N, chans), F32),
        "alog": vmem((N, chans), F32),
        "spread": vmem((tokens // 8, 2 * N, 8 * 128), F32),
        "shifted": vmem((tokens // 8 * 2 * N, 128), BF16),
        "sum": vmem((2, 8, N, 128), F32),
        "gmap": vmem((2 * N, tokens), F32),
        "dbl": vmem((width, tokens), F32),
        "part": vmem((2,) + part, BF16),
        "landing": vmem((2, 2 * NZ) + part[2:], BF16),
        "total": vmem((2,) + part, BF16),
        "mixed": vmem((NZ, 2, half, feats), BF16),
        "outw": vmem(owners, BF16),
        "ginz": vmem(owners, BF16),
        "gdtp": vmem(steps, BF16),
        "chan": vmem((2, 2, small, chans), F32),
        "y_land": vmem((2, NZ, half, feats), BF16),
        "z_land": vmem((2, 2, NZ, half, feats), BF16),
        "wc_land": vmem((3, NZ, 2, rows, chans), BF16),
        "wx_land": vmem((3, NZ, rows, chans), BF16),
        "dc_land": vmem((NZ, 2) + steps[1:], BF16),
        "dx_land": vmem((NZ,) + steps[1:], BF16),
        "fc_land": vmem((2, small, chans), F32),
        "fx_land": vmem((small, chans), F32),
        "f_own": vmem((small, chans), BF16),
        "block": vmem((half, feats), F32),
        "gresid": vmem((half, feats), F32),
        "tile": vmem((4, 8, 128), F32),
        "gain_part": vmem((2, n_dp, 128), F32),
        "gain": vmem((n_dp, 8, 128), F32),
        "gain_total": vmem((8, 128), F32),
        "squares": vmem((2, 8, 128), F32),
        "gain_land": vmem((n_dp - 1, 8, 128), F32),
        "resid": vmem((half, feats), F32),
        "cot": vmem((half, feats), F32),
        "xproj": vmem((width, chans * NZ), BF16),
        "ids": vmem((1, length), jnp.int32),
        "convw": vmem((4, chans * NZ), F32),
        "convb": vmem((1, chans * NZ), F32),
        "dtb": vmem((1, chans * NZ), F32),
        "alog_in": vmem((N, chans * NZ), F32),
        "skip": vmem((1, chans * NZ), F32),
        "load_sems": dma((9,)),
        "send_sems": dma((56,)),
        "keep_sems": dma((9,)),
        "own_sems": dma((4,)),
        "w_sems": dma((4, 2 * NZ + 1)),
        "act_sems": dma((2, NZ + 1)),
        "info_sem": dma(()),
        "dbl_sems": dma((2, 2)),
        "y_sems": dma((2, NZ)),
        "z_sems": dma((2, 2, NZ)),
        "wc_sems": dma((4, NZ)),
        "wx_sems": dma((4, NZ)),
        "wz_sems": dma((4,)),
        "f_sems": dma((2,)),
        "full_sems": dma((2 * NZ + 1,)),
        "tile_sems": dma((2,)),
        "gain_sems": dma((2,)),
    }
    return held


def block_kernel(names, *refs):
    (
        inx_ref, inz_ref, outp_ref, resid_in, cot_in, xproj_in, ids_in, convw_in, convb_in, dtb_in, alog_in, skip_in, gain_ref, dtp_ref,
        block_ref, gresid_ref, ggain_ref, ginx_ref, ginz_ref, goutp_ref, gdtp_ref, full_ref, squares_ref,
    ) = refs[:23]
    s = Held(names, refs[23:])
    spot = Spot()
    resid_ref, cot_ref, xproj_ref, ids_ref = s.resid, s.cot, s.xproj, s.ids
    convw_ref, convb_ref, dtb_ref, alog_ref, skip_ref = s.convw, s.convb, s.dtb, s.alog_in, s.skip
    loads = [
        pltpu.make_async_copy(src, dst, s.load_sems.at[k])
        for k, (src, dst) in enumerate(
            (
                (ids_in, s.ids), (resid_in, s.resid), (cot_in, s.cot), (xproj_in, s.xproj), (convw_in, s.convw),
                (convb_in, s.convb), (dtb_in, s.dtb), (alog_in, s.alog_in), (skip_in, s.skip),
            )
        )
    ]
    for load in loads:
        load.start()
    plane = [lax.rem(spot.dp + offset, 4 * NZ) for offset in range(1, 4 * NZ)]
    greet([(dp, spot.y) for dp in plane] + [spot.on_line(spot.z_at(dz), 1 - spot.y) for dz in range(NZ)])
    copies = Copies(s.send_sems, s.keep_sems)
    tokens, chans = s.x_in.shape
    half, feats = resid_ref.shape
    length = 2 * half
    columns = pl.ds(pl.multiple_of(spot.z * chans, chans), chans)
    quarters = [
        (slice(k * feats // NZ, (k + 1) * feats // NZ), slice(k * NZ, (k + 1) * NZ)) for k in range(NZ)
    ]
    sequences = [slice(k * length, (k + 1) * length) for k in range(NZ)]

    step_rows = dtp_ref[...].astype(F32)
    for z in range(NZ):
        s.dtp_own[z] = fold_columns(step_rows[:, z * chans : (z + 1) * chans]).astype(BF16)
    inx, inz, outp = (
        Gather(spot, copies, src, s.w.at[k], s.w_sems.at[k], s.own_sems.at[k]) for k, src in enumerate((inx_ref, inz_ref, outp_ref))
    )
    dtp = BlockGather(spot, copies, s.dtp_own, s.dtp, s.w_sems.at[3], s.own_sems.at[3])
    normed, cot = (Share(spot, copies, s.acts.at[k], s.act_sems.at[k]) for k in range(2))

    loads[0].wait()
    ids = jnp.broadcast_to(ids_ref[...], (8, length))
    lane = lax.broadcasted_iota(jnp.int32, (8, length), 1)
    sub = lax.broadcasted_iota(jnp.int32, (8, length), 0)
    info = jnp.broadcast_to(gain_ref[...].astype(F32), (8, length))
    for back in range(1, 4):
        same = jnp.where((pltpu.roll(ids, back, 1) == ids) & (lane >= back), 1.0, 0.0)
        info = jnp.where(sub == back, same, info)
    s.info[spot.dp] = info
    other_info = s.info.at[pl.ds(0, 4 * NZ - 1)]
    info_group = copies.group(other_info)
    for dp in plane:
        copies.send(s.info.at[spot.dp], s.info.at[spot.dp], s.info_sem, (dp, spot.y), group=info_group)
    inx.push()

    loads[1].wait()
    resid = resid_ref[...]
    row_square = jnp.sum(resid * resid, axis=1, keepdims=True)
    scaled = resid * lax.rsqrt(row_square / feats + eps_norm)
    s.tile[0] = jnp.broadcast_to(jnp.sum(row_square, axis=0, keepdims=True), (8, 128))
    copies.send(s.tile.at[0], s.tile.at[1], s.tile_sems.at[0], spot.y_mate)
    arrived(other_info, s.info_sem)
    for k in range(4 * NZ):
        cols = slice(k * 128, (k + 1) * 128)
        s.acts[0, spot.z, spot.y, :, cols] = (scaled[:, cols] * s.info[k, 0:1, :]).astype(BF16)
    normed.push()
    dtp.push()
    for load in loads[2:]:
        load.wait()
    s.acts[1, spot.z, spot.y] = cot_ref[...].astype(BF16)
    for k in range(NZ):
        s.mask[k] = column_masks(s.info[place(k, spot.x, spot.c)])
    inx.first()
    normed.first(1)
    inx.second()
    normed.first(2)
    inz.push((3, 0))
    dtp.first()
    dtp.second()
    normed.first(3)
    inz.push((1, 2))
    cot.push(False)
    normed.last()
    cot.send_y(spot.z)
    inx.last()

    all_normed = s.acts[0].reshape(tokens, feats)
    s.x_in[...] = dot(all_normed, s.w[0].reshape(-1, chans))
    taps = convw_ref[:, columns]
    bias = convb_ref[:, columns]
    for k, rows in enumerate(sequences):
        one = s.x_in[rows]
        pre = bias + taps[3:4] * one
        for back in range(1, 4):
            pre = pre + taps[3 - back : 4 - back] * (pltpu.roll(one, back, 0) * s.mask[k, :, back : back + 1])
        s.pre[rows] = pre
        s.low[rows] = (pre * sigmoid(pre)).astype(BF16)
    x_proj = xproj_ref[:, columns]
    dbl = dot(x_proj, s.low[...], NT)
    blocks = [(k, y) for k in range(NZ) for y in range(2)]
    width = dbl.shape[0] // 2
    for k, y in blocks:
        s.part[0, k, y] = dbl[y * width : (y + 1) * width, sequences[k]].astype(BF16)
    x_dbl = LineSum(
        spot, copies, s.part.at[0], s.landing.at[0], s.total.at[0], s.dbl_sems.at[0]
    )
    x_dbl.push()
    inz.first()
    cot.first(1)
    x_dbl.middle()
    outp.push((1, 0))
    cot.first(2)
    x_dbl.last()
    outp.push((2, 3))

    dtp.last()
    for k, y in blocks:
        s.dbl[y * width : (y + 1) * width, sequences[k]] = s.total[0, k, y].astype(F32)
    step_w = unfold_columns(s.dtp[...].astype(F32)).reshape(R, chans).astype(BF16)
    s.raw[...] = dot(s.dbl[:R].astype(BF16), step_w, TN) + dtb_ref[:, columns]
    for k, rows in enumerate(sequences):
        step = softplus(s.raw[rows])
        s.stepd[rows] = jnp.where(s.mask[k, :, 1:2] > 0.0, step, 1e30)
        s.drive[rows] = step * s.low[rows].astype(F32)
    s.a[...] = -jnp.exp(alog_ref[:, columns])
    s.state[0] = jnp.zeros((N, chans), F32)
    scan = Scan(
        s.a, s.stepd, s.drive, s.gs, s.read, s.read, s.gate, s.state, s.pulled, s.alog, s.spread, s.sum, s.gmap
    )
    scan.spread(s.dbl[R : R + 2 * N], s.shifted)
    steps = tokens // 8
    eighth = steps // 8
    inz.second()
    scan.forward(0, 4 * eighth)
    cot.first(3)
    outp.first()
    scan.forward(4 * eighth, steps)
    inz.last()
    s.gate[...] = dot(s.acts[0].reshape(tokens, feats), s.w[1].reshape(-1, chans))
    skip = skip_ref[:, columns]
    for rows in sequences:
        gate = s.gate[rows]
        scanned = s.read[rows] + skip * s.low[rows].astype(F32)
        s.gated[rows] = (scanned * gate * sigmoid(gate)).astype(BF16)

    mixed_sum, normed_sum = (
        TokenSum(spot, copies, part, s.y_land.at[k], s.z_land.at[k], s.y_sems.at[k], s.z_sems.at[k])
        for k, part in enumerate((s.mixed, s.acts.at[1]))
    )
    outw_sum, ginz_sum, ginx_sum, gdtp_sum = (
        RowSum(spot, copies, part, c_land, x_land, out, s.wc_sems.at[k], s.wx_sems.at[k], s.wz_sems.at[k])
        for k, (part, c_land, x_land, out) in enumerate((
            (s.outw, s.wc_land.at[0], s.wx_land.at[0], goutp_ref),
            (s.ginz, s.wc_land.at[1], s.wx_land.at[1], ginz_ref),
            (s.w.at[2], s.wc_land.at[2], s.wx_land.at[2], ginx_ref),
            (s.gdtp, s.dc_land, s.dx_land, gdtp_ref),
        ))
    )
    cot.last()
    for cols, owners in quarters:
        given = s.acts[1, :, :, :, cols].reshape(tokens, -1)
        s.outw[owners] = dot(given, s.gated[...], TN).astype(BF16).reshape(-1, *s.outw.shape[1:])
    outw_sum.push()
    outp.second()
    outw_sum.second()
    outp.last()
    s.gg[...] = dot(s.acts[1].reshape(tokens, feats), s.w[2].reshape(-1, chans))
    for cols, owners in quarters:
        part = dot(s.gated[...], s.w[2, owners].reshape(-1, chans), NT)
        s.mixed[:, :, :, cols] = part.astype(BF16).reshape(*s.mixed.shape[:3], -1)
    mixed_sum.push()
    outw_sum.third((1,))
    for rows in sequences:
        gate, gg = s.gate[rows], s.gg[rows]
        sig = sigmoid(gate)
        scanned = s.read[rows] + skip * s.low[rows].astype(F32)
        s.gs[rows] = gg * gate * sig
        s.ggate[rows] = (gg * scanned * sig * (1.0 + gate * (1.0 - sig))).astype(BF16)
    for cols, owners in quarters:
        given = s.acts[0, :, :, :, cols].reshape(tokens, -1)
        s.ginz[owners] = dot(given, s.ggate[...], TN).astype(BF16).reshape(-1, *s.ginz.shape[1:])
    ginz_sum.push()

    s.pulled[...] = jnp.zeros_like(s.pulled)
    s.alog[...] = jnp.zeros_like(s.alog)
    scan.backward(7 * eighth, steps)
    outw_sum.third((2,))
    ginz_sum.second()
    scan.backward(6 * eighth, 7 * eighth)
    outw_sum.third((3, 0))
    mixed_sum.stage(3)
    scan.backward(4 * eighth, 6 * eighth)
    ginz_sum.third((1,))
    scan.backward(2 * eighth, 4 * eighth)
    ginz_sum.third((2,))
    scan.backward(0, 2 * eighth)
    grad_bias = jnp.zeros((1, chans), F32)
    grad_skip = jnp.zeros((1, chans), F32)
    raw_rows = []
    for rows in sequences:
        conv, raw, gs, q = s.low[rows].astype(F32), s.raw[rows], s.gs[rows], s.read[rows]
        grad_raw = (conv * q + s.gate[rows]) * sigmoid(raw)
        s.gg[rows] = softplus(raw) * q + skip * gs
        grad_bias = grad_bias + jnp.sum(grad_raw, axis=0, keepdims=True)
        grad_skip = grad_skip + jnp.sum(gs * conv, axis=0, keepdims=True)
        raw_rows.append(grad_raw.astype(BF16))
    raw_low = jnp.concatenate(raw_rows, axis=0)
    dbl = jnp.concatenate([dot(step_w, raw_low, NT), s.gmap[...]], axis=0)
    for k, y in blocks:
        s.part[1, k, y] = dbl[y * width : (y + 1) * width, sequences[k]].astype(BF16)
    grad_dbl_sum = LineSum(
        spot, copies, s.part.at[1], s.landing.at[1], s.total.at[1], s.dbl_sems.at[1]
    )
    grad_dbl_sum.push()
    grad_step = dot(s.dbl[:R].astype(BF16), raw_low).reshape(4 * NZ, -1, chans)
    s.gdtp[...] = fold_columns(grad_step).astype(BF16)
    gdtp_sum.push()
    grad_dbl_sum.middle()
    mixed_sum.stage(2)
    ginz_sum.third((3, 0))
    gdtp_sum.second()
    grad_dbl_sum.last()

    grad_dbl = jnp.concatenate(
        [jnp.concatenate([s.total[1, k, y] for k in range(NZ)], axis=1) for y in range(2)], axis=0
    )
    s.gg[...] += dot(grad_dbl, x_proj, TN)
    sums = [jnp.zeros((1, chans), F32) for _ in range(5)]
    low_rows = []
    for k, rows in enumerate(sequences):
        pre, x_one = s.pre[rows], s.x_in[rows]
        sig = sigmoid(pre)
        one = s.gg[rows] * sig * (1.0 + pre * (1.0 - sig))
        sums[3] = sums[3] + jnp.sum(one * x_one, axis=0, keepdims=True)
        sums[4] = sums[4] + jnp.sum(one, axis=0, keepdims=True)
        grad_x = taps[3:4] * one
        for back in range(1, 4):
            masked = one * s.mask[k, :, back : back + 1]
            sums[3 - back] = sums[3 - back] + jnp.sum(masked * pltpu.roll(x_one, back, 0), axis=0, keepdims=True)
            grad_x = grad_x + taps[3 - back : 4 - back] * pltpu.roll(masked, length - back, 0)
        low_rows.append(grad_x.astype(BF16))
    grad_xin = jnp.concatenate(low_rows, axis=0)
    s.chan[...] = jnp.concatenate(
        [dot(grad_dbl, s.low[...]), s.alog[...] * s.a[...], grad_bias, grad_skip, jnp.zeros((6, chans), F32)]
        + sums + [jnp.zeros((3, chans), F32)], axis=0
    ).reshape(s.chan.shape)
    small_sum = ChannelSum(
        spot, copies, s.chan, s.fc_land, s.fx_land, s.f_own, full_ref, s.f_sems.at[0], s.f_sems.at[1], s.full_sems
    )
    small_sum.push()
    copies.settle(outp.group)
    for cols, owners in quarters:
        given = s.acts[0, :, :, :, cols].reshape(tokens, -1)
        s.w[2, owners] = dot(given, grad_xin, TN).astype(BF16).reshape(-1, *s.outw.shape[1:])
    ginx_sum.push()
    small_sum.second()
    cot.settle()
    for cols, owners in quarters:
        part = dot(grad_xin, s.w[0, owners].reshape(-1, chans), NT) + dot(s.ggate[...], s.w[1, owners].reshape(-1, chans), NT)
        s.acts[1, :, :, :, cols] = part.astype(BF16).reshape(*s.mixed.shape[:3], -1)
        gain_part = jnp.sum(part * s.acts[0, :, :, :, cols].reshape(tokens, -1).astype(F32), axis=0, keepdims=True)
        for k in range(NZ):
            owner = owners.start + k
            s.gain_part[0, owner : owner + 1] = gain_part[:, k * 128 : (k + 1) * 128] / s.info[owner, 0:1]
    copies.send(s.gain_part.at[0], s.gain_part.at[1], s.gain_sems.at[0], spot.y_mate)
    normed_sum.push()
    mixed_sum.stage(1)
    ginx_sum.second()
    gdtp_sum.third()
    ginx_sum.third((1,))
    normed_sum.stage(3)
    small_sum.third()
    ginx_sum.third((2,))
    arrived(s.gain_part.at[1], s.gain_sems.at[0])
    for k in range(4 * NZ):
        s.gain[k] = jnp.broadcast_to(s.gain_part[0, k : k + 1] + s.gain_part[1, k : k + 1], (8, 128))
    gain_group = copies.group(s.gain_land)
    for offset, dp in enumerate(plane):
        copies.send(s.gain.at[dp], s.gain_land.at[offset], s.gain_sems.at[1], (dp, spot.y), group=gain_group)
    normed_sum.stage(2)
    ginx_sum.third((3, 0))
    normed_sum.stage(1)
    small_sum.fourth()

    mixed = mixed_sum.last()
    resid = resid_ref[...]
    s.block[...] = resid + mixed
    copies.keep(s.block, block_ref)
    s.tile[2] = jnp.broadcast_to(jnp.sum(jnp.sum(mixed * mixed, axis=1, keepdims=True), axis=0, keepdims=True), (8, 128))
    copies.send(s.tile.at[2], s.tile.at[3], s.tile_sems.at[1], spot.y_mate)
    small_sum.fifth()
    outw_sum.last()
    ginz_sum.last()
    gdtp_sum.last()
    arrived(s.tile.at[1], s.tile_sems.at[0])
    s.squares[0] = s.tile[0] + s.tile[1]
    arrived(s.tile.at[3], s.tile_sems.at[1])
    s.squares[1] = s.tile[2] + s.tile[3]
    copies.keep(s.squares, squares_ref)

    grad_rows = normed_sum.last()
    inv = lax.rsqrt(jnp.sum(resid * resid, axis=1, keepdims=True) / feats + eps_norm)
    scaled = resid * inv
    gain = jnp.concatenate([s.info[k, 0:1] for k in range(4 * NZ)], axis=1)
    grad_scaled = grad_rows * gain
    mean = jnp.sum(grad_scaled * scaled, axis=1, keepdims=True) / feats
    s.gresid[...] = cot_ref[...] + inv * (grad_scaled - scaled * mean)
    copies.keep(s.gresid, gresid_ref)
    arrived(s.gain_land, s.gain_sems.at[1])
    total = s.gain[spot.dp]
    for offset in range(4 * NZ - 1):
        total = total + s.gain_land[offset]
    s.gain_total[...] = total
    copies.keep(s.gain_total, ggain_ref)
    ginx_sum.last()
    small_sum.last()
    copies.wait_sent()
    assert copies.used == s.send_sems.shape[0], copies.used


def block_call(in_x, in_z, out_p, residual, cotangent, gain, ids, dt_p, x_proj, conv_w, conv_b, dt_b, a_log, d_skip):
    half, feats = residual.shape
    rows, wide = in_x.shape
    n_dp, chans = 4 * NZ, wide // NZ
    held = block_scratch(half, feats, rows, chans, dt_p.shape[0], x_proj.shape[0])
    shape = jax.ShapeDtypeStruct
    outs = [
        shape((half, feats), F32), shape((half, feats), F32), shape((8, 128), F32),
        shape((NZ, rows, chans), BF16), shape((NZ, rows, chans), BF16), shape((NZ, rows, chans), BF16),
        shape((NZ, 2 * dt_p.shape[0], chans // 2), BF16), shape((n_dp, (x_proj.shape[0] + 32) // 4, chans), BF16),
        shape((2, 8, 128), F32),
    ]
    in_any = pl.BlockSpec(memory_space=pl.ANY)
    in_vmem = pl.BlockSpec(memory_space=pltpu.VMEM)
    return pl.pallas_call(
        functools.partial(block_kernel, list(held)),
        out_shape=outs,
        in_specs=[in_any] * 12 + [in_vmem] * 2,
        out_specs=[in_any] * len(outs),
        scratch_shapes=list(held.values()),
        name="block",
        compiler_params=pltpu.CompilerParams(collective_id=1, has_side_effects=True, vmem_limit_bytes=62 << 20),
    )(in_x, in_z, out_p, residual, cotangent, x_proj, ids, conv_w, conv_b, dt_b, a_log, d_skip, gain, dt_p)


def finish_kernel(
    scale, block_in, gresid_in, ginx_in, ginz_in, goutp_in, gdtp_in, full_in, ggain_in, squares_in,
    block_ref, gresid_ref, ginx_ref, ginz_ref, goutp_ref, gdtp_ref, xproj_ref, alog_ref, dtb_ref, skip_ref, convw_ref, convb_ref,
    ggain_ref, rms_ref, mrms_ref,
    token_s, low_s, step_s, full_s, ggain_s, squares_s, wide_s, gdtp_s, xproj_s, rows_s, in_sems, out_sems,
):
    begun = []

    def out(src, dst):
        copy = pltpu.make_async_copy(src, dst, out_sems.at[len(begun)])
        copy.start()
        begun.append(copy)

    reads = [
        pltpu.make_async_copy(src, dst, in_sems.at[k])
        for k, (src, dst) in enumerate(
            (
                (ginx_in, low_s.at[0]), (ginz_in, low_s.at[1]), (goutp_in, low_s.at[2]), (full_in, full_s), (gdtp_in, step_s),
                (block_in, token_s.at[0]), (gresid_in, token_s.at[1]), (ggain_in, ggain_s), (squares_in, squares_s),
            )
        )
    ]
    for read in reads:
        read.start()
    chans = low_s.shape[3]
    columns = [slice(z * chans, (z + 1) * chans) for z in range(NZ)]
    for k, ref in enumerate((ginx_ref, ginz_ref, goutp_ref)):
        reads[k].wait()
        for z, cols in enumerate(columns):
            wide_s[k, :, cols] = low_s[k, z].astype(F32)
        out(wide_s.at[k], ref)
    reads[3].wait()
    rows, width = full_s.shape[1], xproj_s.shape[0]
    for z, cols in enumerate(columns):
        for k in range(4):
            found = full_s[place(z, k % 2, k // 2)].astype(F32)
            upto = min(rows, width - k * rows)
            xproj_s[k * rows : k * rows + upto, cols] = found[:upto]
        rows_s[:, cols] = found[upto:]
    out(xproj_s, xproj_ref)
    out(rows_s.at[pl.ds(0, N)], alog_ref)
    for at, ref in ((N, dtb_ref), (N + 1, skip_ref), (24, convw_ref), (28, convb_ref)):
        out(rows_s.at[pl.ds(at, ref.shape[0])], ref)
    reads[4].wait()
    for z, cols in enumerate(columns):
        gdtp_s[:, cols] = unfold_columns(step_s[z].astype(F32))
    out(gdtp_s, gdtp_ref)
    for k, ref in enumerate((block_ref, gresid_ref)):
        reads[5 + k].wait()
        out(token_s.at[k], ref)
    reads[7].wait()
    out(ggain_s.at[pl.ds(0, 1)], ggain_ref)
    reads[8].wait()
    for k, ref in enumerate((rms_ref, mrms_ref)):
        ref[...] = jnp.sqrt(squares_s[k, 0:1, 0:1] * scale)
    for copy in begun:
        copy.wait()


def finish_call(block, gresid, ginx, ginz, goutp, gdtp, full, ggain, squares, width):
    rows, chans = ginx.shape[1:]
    wide = chans * NZ
    shape = lambda count, columns=wide: jax.ShapeDtypeStruct((count, columns), F32)
    vmem, dma = pltpu.VMEM, pltpu.SemaphoreType.DMA
    in_any = pl.BlockSpec(memory_space=pl.ANY)
    outs = [
        shape(*block.shape), shape(*gresid.shape), shape(rows), shape(rows), shape(rows), shape(gdtp.shape[1] // 2), shape(width),
        shape(N), shape(1), shape(1), shape(4), shape(1), shape(1, 128), shape(1, 1), shape(1, 1),
    ]
    return pl.pallas_call(
        functools.partial(finish_kernel, 1.0 / (2 * block.shape[0] * block.shape[1])),
        out_shape=outs,
        in_specs=[in_any] * 9,
        out_specs=[in_any] * (len(outs) - 2) + [pl.BlockSpec(memory_space=vmem)] * 2,
        scratch_shapes=[
            vmem((2,) + block.shape, F32), vmem((3,) + ginx.shape, BF16), vmem(gdtp.shape, BF16), vmem(full.shape, BF16),
            vmem(ggain.shape, F32), vmem(squares.shape, F32), vmem((3, rows, wide), F32), vmem((gdtp.shape[1] // 2, wide), F32),
            vmem((width, wide), F32), vmem((32, wide), F32), dma((9,)), dma((len(outs) - 2,)),
        ],
        name="finish",
        compiler_params=pltpu.CompilerParams(vmem_limit_bytes=60 << 20),
    )(block, gresid, ginx, ginz, goutp, gdtp, full, ggain, squares)


def per_device_split(
    residual,
    norm_gain,
    in_proj_x,
    in_proj_z,
    x_proj,
    dt_proj,
    dt_bias,
    conv_weight,
    conv_bias,
    a_log,
    d_skip,
    out_proj,
    doc_ids,
    cotangent,
):
    parts = block_call(
        in_proj_x, in_proj_z, out_proj, residual, cotangent, norm_gain[None], doc_ids[None], dt_proj, x_proj, conv_weight,
        conv_bias[None], dt_bias[None], a_log, d_skip[None],
    )
    block, gresid, ggain, ginx, ginz, goutp, gdtp, full, squares = parts
    block, gresid, ginx, ginz, goutp, gdtp, g_xproj, g_alog, g_dtb, g_skip, g_convw, g_convb, ggain, rms, mrms = finish_call(
        block, gresid, ginx, ginz, goutp, gdtp, full, ggain, squares, x_proj.shape[0]
    )
    return (
        block,
        gresid,
        ggain[0],
        ginx,
        ginz,
        g_xproj,
        gdtp,
        g_dtb[0],
        g_convw,
        g_convb[0],
        g_alog,
        g_skip[0],
        goutp,
        rms[0],
        mrms[0],
    )


def norm_rows(values, gain_val):
    mean_square = jnp.mean(values * values, axis=1, keepdims=True)
    return values * lax.rsqrt(mean_square + eps_norm) * gain_val


def conv_local(x_in, doc_ids, conv_weight, conv_bias):
    kernel_len = conv_weight.shape[0]
    length = x_in.shape[0]
    padded = jnp.pad(x_in, ((kernel_len - 1, 0), (0, 0)))
    id_pad = jnp.concatenate([jnp.full((kernel_len - 1,), -1, jnp.int32), doc_ids])
    summed = conv_bias + jnp.zeros_like(x_in)
    for offset in range(kernel_len):
        same_doc = (id_pad[offset : offset + length] == doc_ids).astype(jnp.float32)
        summed = summed + conv_weight[offset] * padded[offset : offset + length] * same_doc[:, None]
    return summed


def per_device(
    residual,
    norm_gain,
    in_proj_x,
    in_proj_z,
    x_proj,
    dt_proj,
    dt_bias,
    conv_weight,
    conv_bias,
    a_log,
    d_skip,
    out_proj,
    doc_ids,
    cotangent,
):
    gathered = (
        lax.all_gather(norm_gain, "dp", axis=0, tiled=True),
        lax.all_gather(in_proj_x, "dp", axis=0, tiled=True),
        lax.all_gather(in_proj_z, "dp", axis=0, tiled=True),
        lax.all_gather(dt_proj, "dp", axis=0, tiled=True),
        lax.all_gather(out_proj, "dp", axis=0, tiled=True),
    )
    gain_all, inx_all, inz_all, step_all, out_all = gathered
    seq_len = doc_ids.shape[0]
    normed_f32, norm_back = jax.vjp(norm_rows, residual, gain_all.astype(jnp.float32))
    normed = lax.all_gather(normed_f32.astype(jnp.bfloat16), "tensor", axis=0, tiled=True)
    x_in = jnp.dot(normed, inx_all, preferred_element_type=jnp.float32)
    gate_in = jnp.dot(normed, inz_all, preferred_element_type=jnp.float32)

    def conv_act(x_val, weight_val, bias_val):
        return jax.nn.silu(conv_local(x_val, doc_ids, weight_val, bias_val))

    conv_out, conv_back = jax.vjp(conv_act, x_in, conv_weight, conv_bias)
    conv_low = conv_out.astype(jnp.bfloat16)
    dbl_part = lax.dot_general(
        conv_low, x_proj, (((1,), (1,)), ((), ())), preferred_element_type=jnp.float32
    )
    x_dbl, resid_square = lax.psum((dbl_part, jnp.sum(residual * residual)), "tensor")
    doc_starts = doc_ids != jnp.concatenate([jnp.full((1,), -1, jnp.int32), doc_ids[:-1]])
    carry_keep = 1.0 - doc_starts.astype(jnp.float32)

    cot_all = lax.all_gather(cotangent.astype(jnp.bfloat16), "tensor", axis=0, tiled=True)
    grad_gated = jnp.dot(cot_all, out_all, preferred_element_type=jnp.float32)
    gated_low, grad_gate_low, grad_conv, grad_dbl_part, grad_step_w, grad_bias, grad_alog, grad_skip = scan_call(
        x_dbl, conv_low, gate_in, grad_gated, step_all, dt_bias, a_log, d_skip, carry_keep
    )
    mixed = lax.psum_scatter(
        lax.dot_general(
            gated_low, out_all, (((1,), (1,)), ((), ())), preferred_element_type=jnp.float32
        ),
        "tensor",
        scatter_dimension=0,
        tiled=True,
    )
    block_out = residual + mixed
    mixed_square = lax.psum(jnp.sum(mixed * mixed), "tensor")
    rms_resid = jnp.sqrt(resid_square / (seq_len * D)).reshape(1)
    rms_mixed = jnp.sqrt(mixed_square / (seq_len * D)).reshape(1)
    grad_out_w = lax.dot_general(
        cot_all, gated_low, (((0,), (0,)), ((), ())), preferred_element_type=jnp.float32
    )
    grad_dbl = lax.psum(grad_dbl_part.T, "tensor")
    grad_dbl_low = grad_dbl.astype(jnp.bfloat16)
    grad_conv = grad_conv + jnp.dot(grad_dbl_low, x_proj, preferred_element_type=jnp.float32)
    grad_xproj = lax.dot_general(
        grad_dbl_low, conv_low, (((0,), (0,)), ((), ())), preferred_element_type=jnp.float32
    )
    grad_xin, grad_convw, grad_convb = conv_back(grad_conv)
    grad_xin_low = grad_xin.astype(jnp.bfloat16)
    grad_inx = lax.dot_general(
        normed, grad_xin_low, (((0,), (0,)), ((), ())), preferred_element_type=jnp.float32
    )
    grad_inz = lax.dot_general(
        normed, grad_gate_low, (((0,), (0,)), ((), ())), preferred_element_type=jnp.float32
    )
    first_term = lax.dot_general(
        grad_xin_low, inx_all, (((1,), (1,)), ((), ())), preferred_element_type=jnp.float32
    )
    second_term = lax.dot_general(
        grad_gate_low, inz_all, (((1,), (1,)), ((), ())), preferred_element_type=jnp.float32
    )
    grad_normed = lax.psum_scatter(
        first_term + second_term, "tensor", scatter_dimension=0, tiled=True
    )
    grad_rows_x, grad_gain_part = norm_back(grad_normed)
    grad_residual = cotangent + grad_rows_x
    grad_gain = lax.psum(grad_gain_part, "tensor")
    gain_shard, inx_shard, inz_shard, step_shard, out_shard = (
        lax.psum_scatter(grad_gain, "dp", scatter_dimension=0, tiled=True),
        lax.psum_scatter(grad_inx, "dp", scatter_dimension=0, tiled=True),
        lax.psum_scatter(grad_inz, "dp", scatter_dimension=0, tiled=True),
        lax.psum_scatter(grad_step_w, "dp", scatter_dimension=0, tiled=True),
        lax.psum_scatter(grad_out_w, "dp", scatter_dimension=0, tiled=True),
    )
    small_sums = lax.psum(
        (grad_xproj, grad_bias, grad_convw, grad_convb, grad_alog, grad_skip), "dp"
    )
    xproj_sum, bias_sum, convw_sum, convb_sum, alog_sum, skip_sum = small_sums
    return (
        block_out,
        grad_residual,
        gain_shard,
        inx_shard,
        inz_shard,
        xproj_sum,
        step_shard,
        bias_sum,
        convw_sum,
        convb_sum,
        alog_sum,
        skip_sum,
        out_shard,
        rms_resid,
        rms_mixed,
    )


def solution(mesh):
    placed = (
        P(("dp", "tensor"), None),
        P("dp"),
        P("dp", "tensor"),
        P("dp", "tensor"),
        P(None, "tensor"),
        P("dp", "tensor"),
        P("tensor"),
        P(None, "tensor"),
        P("tensor"),
        P(None, "tensor"),
        P("tensor"),
        P("dp", "tensor"),
        P("dp"),
        P(("dp", "tensor"), None),
    )
    return jax.shard_map(
        per_device_split if mesh.shape["dp"] == 4 * NZ else per_device,
        mesh=mesh,
        in_specs=placed,
        out_specs=(
            P(("dp", "tensor"), None),
            P(("dp", "tensor"), None),
            P("dp"),
            P("dp", "tensor"),
            P("dp", "tensor"),
            P(None, "tensor"),
            P("dp", "tensor"),
            P("tensor"),
            P(None, "tensor"),
            P("tensor"),
            P(None, "tensor"),
            P("tensor"),
            P("dp", "tensor"),
            P("dp"),
            P("dp"),
        ),
        check_vma=False,
    )
```

```python
import functools

import jax
import jax.numpy as jnp
from jax import lax
from jax.experimental import pallas as pl
from jax.experimental.pallas import tpu as pltpu
from jax.sharding import PartitionSpec as P

D = 2048
R = 128
N = 16

eps_norm = 1e-05


def sigmoid(v):
    return 1.0 / (1.0 + jnp.exp(-v))


def softplus(v):
    return jnp.maximum(v, 0.0) + jnp.log(1.0 + jnp.exp(-jnp.abs(v)))


def fold_rows(first, second, shift, lower):
    kept = jnp.where(lower, first, second)
    moved = jnp.where(lower, second, first)
    return kept + pltpu.roll(moved, shift, 0)


class RowSums:
    def __init__(self, masks):
        self.masks = masks
        self.held = {}
        self.result = None

    def add(self, token, value):
        level = 0
        while True:
            if level == 3:
                self.result = value
                return
            mate = (level, token ^ 1)
            if mate not in self.held:
                self.held[(level, token)] = value
                return
            other = self.held.pop(mate)
            first, second = (other, value) if token & 1 else (value, other)
            value = fold_rows(first, second, 1 << level, self.masks[level])
            token >>= 1
            level += 1


def split_dot(left, right_low, dims):
    high = left.astype(jnp.bfloat16)
    rest = (left - high.astype(jnp.float32)).astype(jnp.bfloat16)
    return lax.dot_general(high, right_low, dims, preferred_element_type=jnp.float32) + lax.dot_general(
        rest, right_low, dims, preferred_element_type=jnp.float32
    )


def scan_kernel(
    dbl_ref, conv_ref, gate_ref, gg_ref, dtp_ref, dtb_ref, alog_ref, skip_ref, keep_ref, in_ref, out_ref,
    gated_ref, ggate_ref, gconv_ref, gdbl_ref, gin_ref, gout_ref, gdtp_ref, gdtb_ref, galog_ref, gskip_ref,
    h_s, d_s, stepd_s, sc_s, gs_s, y_s, q_s, r_s, a_s,
):
    length, width = conv_ref.shape
    blocks = width // 128
    part = pl.program_id(0)
    sub = lax.broadcasted_iota(jnp.int32, (8, 128), 0)
    masks = [(sub & shift) == 0 for shift in (1, 2, 4)]
    lanes = [slice(b * 128, (b + 1) * 128) for b in range(blocks)]

    nn = (((1,), (0,)), ((), ()))
    step_raw = split_dot(dbl_ref[...], dtp_ref[...], nn) + dtb_ref[...]
    step = jnp.maximum(step_raw, 0.0) + jnp.log(1.0 + jnp.exp(-jnp.abs(step_raw)))
    stepd_s[...] = jnp.where(keep_ref[...] > 0.0, step, 1e30)
    sc_s[...] = step * conv_ref[...].astype(jnp.float32)
    gate = gate_ref[...]
    gs_s[...] = gg_ref[...] * gate * sigmoid(gate)
    a_s[...] = -jnp.exp(alog_ref[...])

    h_s[0] = jnp.zeros((N, width), jnp.float32)

    def forward(i, hs):
        base = pl.multiple_of(i * 8, 8)
        hs = list(hs)
        sums = [RowSums(masks) for _ in range(blocks)]
        stepd = [stepd_s[pl.ds(base, 8), lanes[b]] for b in range(blocks)]
        drive = [sc_s[pl.ds(base, 8), lanes[b]] for b in range(blocks)]
        for j in range(8):
            t = base + j
            in_t = in_ref[t]
            out_t = out_ref[t]
            for b in range(blocks):
                decay = jnp.exp(stepd[b][j : j + 1] * a_s[:, lanes[b]])
                hs[b] = decay * hs[b] + drive[b][j : j + 1] * in_t
                d_s[t, :, lanes[b]] = decay
                h_s[t + 1, :, lanes[b]] = hs[b]
                read = hs[b] * out_t
                sums[b].add(j, read[:8] + read[8:])
        for b in range(blocks):
            y_s[pl.ds(base, 8), lanes[b]] = sums[b].result
        return tuple(hs)

    zero = jnp.zeros((N, 128), jnp.float32)
    lax.fori_loop(0, length // 8, forward, (zero,) * blocks)

    conv = conv_ref[...].astype(jnp.float32)
    gate = gate_ref[...]
    sig = sigmoid(gate)
    scanned = y_s[...] + skip_ref[...] * conv
    gated_ref[...] = (scanned * gate * sig).astype(jnp.bfloat16)
    ggate_ref[...] = (gg_ref[...] * scanned * sig * (1.0 + gate * (1.0 - sig))).astype(jnp.bfloat16)

    @pl.when(part == 0)
    def _():
        gin_ref[...] = jnp.zeros_like(gin_ref)
        gout_ref[...] = jnp.zeros_like(gout_ref)
        gdbl_ref[...] = jnp.zeros_like(gdbl_ref)

    def backward(i, carried):
        base = pl.multiple_of(length - 8 - i * 8, 8)
        pulled, alog_sum = list(carried[0]), list(carried[1])
        q_sums = [RowSums(masks) for _ in range(blocks)]
        r_sums = [RowSums(masks) for _ in range(blocks)]
        stepd = [stepd_s[pl.ds(base, 8), lanes[b]] for b in range(blocks)]
        drive = [sc_s[pl.ds(base, 8), lanes[b]] for b in range(blocks)]
        gs = [gs_s[pl.ds(base, 8), lanes[b]] for b in range(blocks)]
        for j in reversed(range(8)):
            t = base + j
            in_t = in_ref[t]
            out_t = out_ref[t]
            gin_t = gin_ref[t]
            gout_t = gout_ref[t]
            for b in range(blocks):
                gs_t = gs[b][j : j + 1]
                adjoint = pulled[b] + out_t * gs_t
                gout_t = gout_t + gs_t * h_s[t + 1, :, lanes[b]]
                gin_t = gin_t + adjoint * drive[b][j : j + 1]
                q_t = adjoint * in_t
                q_sums[b].add(j, q_t[:8] + q_t[8:])
                pulled[b] = d_s[t, :, lanes[b]] * adjoint
                past = pulled[b] * h_s[t, :, lanes[b]]
                r_t = past * a_s[:, lanes[b]]
                r_sums[b].add(j, r_t[:8] + r_t[8:])
                alog_sum[b] = alog_sum[b] + past * stepd[b][j : j + 1]
            gin_ref[t] = gin_t
            gout_ref[t] = gout_t
        for b in range(blocks):
            q_s[pl.ds(base, 8), lanes[b]] = q_sums[b].result
            r_s[pl.ds(base, 8), lanes[b]] = r_sums[b].result
        return tuple(pulled), tuple(alog_sum)

    _, alog_sum = lax.fori_loop(0, length // 8, backward, ((zero,) * blocks, (zero,) * blocks))
    for b in range(blocks):
        galog_ref[:, lanes[b]] = alog_sum[b] * a_s[:, lanes[b]]

    conv = conv_ref[...].astype(jnp.float32)
    step_raw = split_dot(dbl_ref[...], dtp_ref[...], nn) + dtb_ref[...]
    step = jnp.maximum(step_raw, 0.0) + jnp.log(1.0 + jnp.exp(-jnp.abs(step_raw)))
    raw = (conv * q_s[...] + r_s[...]) * sigmoid(step_raw)
    gs = gs_s[...]
    gconv_ref[...] = step * q_s[...] + skip_ref[...] * gs
    gskip_ref[...] = jnp.sum(gs * conv, axis=0, keepdims=True)
    gdtb_ref[...] = jnp.sum(raw, axis=0, keepdims=True)
    raw_low = raw.astype(jnp.bfloat16)
    gdtp_ref[...] = lax.dot_general(
        dbl_ref[...].astype(jnp.bfloat16), raw_low, (((0,), (0,)), ((), ())), preferred_element_type=jnp.float32
    )
    gdbl_ref[...] += lax.dot_general(
        dtp_ref[...], raw_low, (((1,), (1,)), ((), ())), preferred_element_type=jnp.float32
    )


def scan_call(dbl, conv, gate, gg, dtp, dtb, alog, skip, keep):
    length, chans = conv.shape
    cb = min(65536 // length, chans)
    f32 = jnp.float32
    maps = jnp.broadcast_to(dbl[:, R:, None], (length, 2 * N, 128))
    tokens = lambda kind: (jax.ShapeDtypeStruct((length, chans), kind), pl.BlockSpec((length, cb), lambda i: (0, i)))
    whole = lambda *shape: (jax.ShapeDtypeStruct(shape, f32), pl.BlockSpec(shape, lambda i: (0,) * len(shape)))
    rows = lambda count: (jax.ShapeDtypeStruct((count, chans), f32), pl.BlockSpec((count, cb), lambda i: (0, i)))
    outs = [
        tokens(jnp.bfloat16), tokens(jnp.bfloat16), tokens(f32), whole(R, length), whole(length, N, 128), whole(length, N, 128),
        rows(R), rows(1), rows(N), rows(1),
    ]
    ins = [
        whole(length, R), tokens(f32), tokens(f32), tokens(f32), rows(R), rows(1), rows(N), rows(1),
        whole(length, 1),
    ]
    res = pl.pallas_call(
        scan_kernel,
        grid=(chans // cb,),
        in_specs=[spec for _, spec in ins] + [
            pl.BlockSpec((length, N, 128), lambda i: (0, 0, 0)), pl.BlockSpec((length, N, 128), lambda i: (0, 1, 0))],
        out_specs=[spec for _, spec in outs],
        out_shape=[shape for shape, _ in outs],
        scratch_shapes=[
            pltpu.VMEM((length + 1, N, cb), f32), pltpu.VMEM((length, N, cb), f32),
        ] + [pltpu.VMEM((length, cb), f32)] * 6 + [pltpu.VMEM((N, cb), f32)],
        name="selective_scan",
        compiler_params=pltpu.CompilerParams(vmem_limit_bytes=60 << 20),
    )(dbl[:, :R], conv, gate, gg, dtp, dtb[None], alog, skip[None], keep[:, None], maps, maps)
    gated, ggate, gconv, gdbl, gin, gout, gdtp, gdtb, galog, gskip = res
    gdbl_all = jnp.concatenate([gdbl, jnp.sum(gin, -1).T, jnp.sum(gout, -1).T], axis=0)
    return gated, ggate, gconv, gdbl_all, gdtp, gdtb[0], galog, gskip[0]


MESH = pl.DeviceIdType.MESH
NZ = 4
F32 = jnp.float32
BF16 = jnp.bfloat16
NN = (((1,), (0,)), ((), ()))
NT = (((1,), (1,)), ((), ()))
TN = (((0,), (0,)), ((), ()))


def dot(left, right, dims=NN):
    return lax.dot_general(left, right, dims, preferred_element_type=F32)


def place(z, x, c):
    return (z * 2 + x) * 2 + c


class Spot:
    def __init__(self):
        self.dp = lax.axis_index("dp")
        self.y = lax.axis_index("tensor")
        self.z, self.x, self.c = self.dp // 4, (self.dp // 2) % 2, self.dp % 2
        self.x_mate = (place(self.z, 1 - self.x, self.c), self.y)
        self.c_mate = (place(self.z, self.x, 1 - self.c), self.y)
        self.y_mate = (self.dp, 1 - self.y)

        far, near = jnp.where(self.z < 2, 3, 0), 1 + self.z % 2
        self.others = [far, 6 - self.z - far - near, near]

    def turn(self, k):
        return self.others[k - 1] if k else self.z

    def z_at(self, offset):
        return lax.rem(self.z + offset + NZ, NZ)

    def slot(self, origin, device):
        if device is self.c_mate:
            return 2 * NZ
        return origin // 4 + (NZ if device is self.x_mate else 0)

    def on_line(self, z, y=None):
        return (place(z, self.x, self.c), self.y if y is None else y)


def greet(devices):
    barrier = pltpu.get_barrier_semaphore()
    for device in devices:
        pl.semaphore_signal(barrier, inc=1, device_id=device, device_id_type=MESH)
    pl.semaphore_wait(barrier, len(devices))


class Copies:
    def __init__(self, send_sems, own_sems):
        self.send_sems, self.own_sems = send_sems, own_sems
        self.used, self.groups, self.begun, self.kept = 0, [], [], []

    def new_sem(self):
        self.used += 1
        return self.send_sems.at[self.used - 1]

    def group(self, whole):
        sem = self.new_sem()
        self.groups.append((sem, pltpu.make_async_copy(whole, whole, sem).wait))
        return sem

    def settle(self, *sems):
        for sem, wait in self.groups:
            if any(sem is one for one in sems):
                wait()
        self.groups = [(sem, wait) for sem, wait in self.groups if all(sem is not one for one in sems)]

    def send(self, src, dst, recv_sem, device, when=None, group=None):
        copy = pltpu.make_async_remote_copy(
            src_ref=src, dst_ref=dst, send_sem=self.new_sem() if group is None else group, recv_sem=recv_sem,
            device_id=device, device_id_type=MESH,
        )
        if group is None:
            self.begun.append((when, copy.wait_send))
        if when is None:
            copy.start()
        else:
            pl.when(when)(copy.start)

    def keep(self, src, dst):
        copy = pltpu.make_async_copy(src, dst, self.own_sems.at[len(self.kept)])
        copy.start()
        self.kept.append(copy)

    def wait_sent(self):
        self.settle(*[sem for sem, _ in self.groups])
        self.settle_alone(self.begun)
        for copy in self.kept:
            copy.wait()

    def settle_alone(self, begun):
        for when, wait in begun:
            if when is None:
                wait()
            else:
                pl.when(when)(wait)
        self.begun = [one for one in self.begun if all(one is not done for done in begun)]


def arrived(dst, recv_sem, when=None):
    copy = pltpu.make_async_copy(dst, dst, recv_sem)
    if when is None:
        copy.wait()
    else:
        pl.when(when)(copy.wait)


class Gather:
    def __init__(self, spot, copies, src, dst, recv_sems, own_sem):
        self.spot, self.copies, self.src, self.dst, self.recv_sems, self.own_sem = spot, copies, src, dst, recv_sems, own_sem
        self.width = dst.shape[-1]
        self.group = copies.group(dst.at[pl.ds(0, 4 * NZ - 1)])

    def columns(self, z):
        return self.src.at[:, pl.ds(pl.multiple_of(z * self.width, self.width), self.width)]

    def push(self, offsets=(1, 2, 3, 0)):
        spot, me = self.spot, self.spot.dp
        for offset in offsets:
            if offset == 0:
                self.push_own()
                continue
            z = spot.turn(offset)
            self.copies.send(self.columns(z), self.dst.at[me], self.recv_sems.at[spot.z], spot.on_line(z), group=self.group)

    def push_own(self):
        spot, me = self.spot, self.spot.dp
        self.own = pltpu.make_async_copy(self.columns(spot.z), self.dst.at[me], self.own_sem)
        self.own.start()
        self.pass_on(me, spot.x_mate, self.columns(spot.z))
        self.pass_on(me, spot.c_mate, self.columns(spot.z))

    def pass_on(self, origin, device, src=None):
        sem = self.recv_sems.at[self.spot.slot(origin, device)]
        src = self.dst.at[origin] if src is None else src
        self.copies.send(src, self.dst.at[origin], sem, device, group=self.group)

    def first(self):
        spot = self.spot
        for offset in range(1, NZ):
            z = spot.turn(offset)
            origin = place(z, spot.x, spot.c)
            arrived(self.dst.at[origin], self.recv_sems.at[z])
            self.pass_on(origin, spot.x_mate)
            self.pass_on(origin, spot.c_mate)

    def second(self):
        spot = self.spot
        for offset in range(NZ):
            z = spot.turn(offset)
            origin = place(z, 1 - spot.x, spot.c)
            arrived(self.dst.at[origin], self.recv_sems.at[NZ + z])
            self.pass_on(origin, spot.c_mate)

    def last(self):
        self.own.wait()
        arrived(self.dst.at[pl.ds(0, 2 * NZ)], self.recv_sems.at[2 * NZ])


class BlockGather(Gather):
    def columns(self, z):
        return self.src.at[z]


def fold_columns(values):
    half = values.shape[-1] // 2
    return jnp.concatenate([values[..., :half], values[..., half:]], axis=-2)


def unfold_columns(values):
    rows = values.shape[-2] // 2
    return jnp.concatenate([values[..., :rows, :], values[..., rows:, :]], axis=-1)


class LineSum:
    def __init__(self, spot, copies, part, landing, total, sems):
        self.spot, self.copies, self.part, self.landing, self.total, self.sems = spot, copies, part, landing, total, sems
        self.offsets = [(dz, dy) for dz in range(NZ) for dy in range(2) if dz + dy > 0]
        self.all_others = landing.at[pl.ds(0, len(self.offsets))]
        self.groups = [copies.group(self.all_others) for _ in range(2)]

    def there(self, dz, dy):
        return self.spot.z_at(dz), lax.rem(self.spot.y + dy, 2)

    def push(self):
        for k, (dz, dy) in enumerate(self.offsets):
            z, y = self.there(dz, dy)
            self.copies.send(self.part.at[z, y], self.landing.at[k], self.sems.at[0], self.spot.on_line(z, y), group=self.groups[0])

    def middle(self):
        own_z, own_y = self.spot.z, self.spot.y
        arrived(self.all_others, self.sems.at[0])
        summed = self.part[own_z, own_y].astype(F32)
        for k in range(len(self.offsets)):
            summed = summed + self.landing[k].astype(F32)
        self.total[own_z, own_y] = summed.astype(BF16)
        own = self.total.at[own_z, own_y]
        for dz, dy in self.offsets:
            self.copies.send(own, own, self.sems.at[1], self.spot.on_line(*self.there(dz, dy)), group=self.groups[1])

    def last(self):
        arrived(self.all_others, self.sems.at[1])


def column_masks(tile):
    return jnp.concatenate([tile] * 16, axis=0).T


class Share:
    def __init__(self, spot, copies, dst, recv_sems):
        self.spot, self.copies, self.dst, self.recv_sems = spot, copies, dst, recv_sems
        self.over_y, self.alone = copies.group(dst.at[pl.ds(0, NZ // 2)]), []

    def send(self, z, device, when=None):
        own = self.dst.at[z, self.spot.y]
        self.copies.send(own, own, self.recv_sems.at[z], device, when)
        self.alone.append(self.copies.begun[-1])

    def settle(self):
        self.copies.settle(self.over_y)
        self.copies.settle_alone(self.alone)

    def send_y(self, z, when=None):
        own = self.dst.at[z, self.spot.y]
        self.copies.send(own, own, self.recv_sems.at[NZ], self.spot.y_mate, when, self.over_y)

    def push(self, over_y=True):
        spot = self.spot
        self.send(spot.z, spot.on_line(spot.z_at(1)), spot.z < NZ - 1)
        self.send(spot.z, spot.on_line(spot.z_at(-1)), spot.z > 0)
        if over_y:
            self.send_y(spot.z)

    def first(self, far):
        spot = self.spot
        for way in (1, -1):
            origin = spot.z_at(-way * far)
            comes = spot.z >= far if way == 1 else spot.z < NZ - far
            goes = comes & (spot.z < NZ - 1 if way == 1 else spot.z > 0)
            arrived(self.dst.at[origin, spot.y], self.recv_sems.at[origin], comes)
            if far < NZ - 1:
                self.send(origin, spot.on_line(spot.z_at(way)), goes)
            self.send_y(origin, comes)

    def last(self):
        arrived(self.dst.at[pl.ds(0, NZ // 2)], self.recv_sems.at[NZ])


class Scan:
    def __init__(self, a_s, stepd_s, drive_s, gs_s, read_s, q_s, r_s, state_s, pulled_s, alog_s, spread_s, sum_s, gmap_s):
        self.a_s, self.stepd_s, self.drive_s, self.gs_s = a_s, stepd_s, drive_s, gs_s
        self.read_s, self.q_s, self.r_s, self.state_s = read_s, q_s, r_s, state_s
        self.pulled_s, self.alog_s, self.spread_s, self.sum_s, self.gmap_s = pulled_s, alog_s, spread_s, sum_s, gmap_s
        sub = lax.broadcasted_iota(jnp.int32, (8, 128), 0)
        self.masks = [(sub & shift) == 0 for shift in (1, 2, 4)]
        self.lane = lax.broadcasted_iota(jnp.int32, (N, 128), 1)
        self.blocks = [slice(b * 128, (b + 1) * 128) for b in range(a_s.shape[1] // 128)]

    def place(self, i):
        base = pl.multiple_of(i * 8, 8)
        tile = pl.ds(pl.multiple_of((base // 128) * 128, 128), 128)
        return base, tile, lax.rem(base, 128)

    def spread(self, maps, shifted_s):
        rows = maps.shape[0]
        for i in range(maps.shape[1] // 8):
            tile, first = maps[:, i // 16 * 128 : (i // 16 + 1) * 128], i % 16 * 8
            shifted_s[i * rows : (i + 1) * rows] = pltpu.roll(tile, (128 - first) % 128, 1).astype(BF16)
        row = lax.broadcasted_iota(jnp.int32, (128, 8 * 128), 0)
        column = lax.broadcasted_iota(jnp.int32, (128, 8 * 128), 1)
        chosen = jnp.where(row == column // 128, 1.0, 0.0).astype(BF16)
        self.spread_s[...] = dot(shifted_s[...], chosen).reshape(self.spread_s.shape)

    def maps_at(self, i, j):
        lanes = slice(j * 128, (j + 1) * 128)
        return self.spread_s[i, :N, lanes], self.spread_s[i, N:, lanes]

    def forward(self, start, stop):
        def chunk(i, none):
            base = pl.multiple_of(i * 8, 8)
            for lanes in self.blocks:
                state = self.state_s[i, :, lanes]
                a = self.a_s[:, lanes]
                stepd, drive = self.stepd_s[pl.ds(base, 8), lanes], self.drive_s[pl.ds(base, 8), lanes]
                sums = RowSums(self.masks)
                for j in range(8):
                    in_map, out_map = self.maps_at(i, j)
                    state = jnp.exp(stepd[j : j + 1] * a) * state + drive[j : j + 1] * in_map
                    read = state * out_map
                    sums.add(j, read[:8] + read[8:])
                self.state_s[i + 1, :, lanes] = state
                self.read_s[pl.ds(base, 8), lanes] = sums.result
            return none

        lax.fori_loop(start, stop, chunk, 0)

    def backward(self, start, stop):
        def chunk(step, none):
            i = start + stop - 1 - step
            base, tile, first = self.place(i)
            for b, lanes in enumerate(self.blocks):
                a = self.a_s[:, lanes]
                stepd, drive = self.stepd_s[pl.ds(base, 8), lanes], self.drive_s[pl.ds(base, 8), lanes]
                gs = self.gs_s[pl.ds(base, 8), lanes]
                states, decays = [self.state_s[i, :, lanes]], []
                for j in range(8):
                    decays.append(jnp.exp(stepd[j : j + 1] * a))
                    states.append(decays[j] * states[j] + drive[j : j + 1] * self.maps_at(i, j)[0])
                pulled, alog = self.pulled_s[:, lanes], self.alog_s[:, lanes]
                q_sums, r_sums = RowSums(self.masks), RowSums(self.masks)
                for j in reversed(range(8)):
                    in_map, out_map = self.maps_at(i, j)
                    adjoint = pulled + out_map * gs[j : j + 1]
                    g_in, g_out = adjoint * drive[j : j + 1], states[j + 1] * gs[j : j + 1]
                    if b > 0:
                        g_in, g_out = g_in + self.sum_s[0, j], g_out + self.sum_s[1, j]
                    self.sum_s[0, j], self.sum_s[1, j] = g_in, g_out
                    q_t = adjoint * in_map
                    q_sums.add(j, q_t[:8] + q_t[8:])
                    pulled = decays[j] * adjoint
                    past = pulled * states[j]
                    r_t = past * a
                    r_sums.add(j, r_t[:8] + r_t[8:])
                    alog = alog + past * stepd[j : j + 1]
                self.pulled_s[:, lanes], self.alog_s[:, lanes] = pulled, alog
                self.q_s[pl.ds(base, 8), lanes] = q_sums.result
                self.r_s[pl.ds(base, 8), lanes] = r_sums.result
            for k in range(2):
                row = self.gmap_s[k * N : (k + 1) * N, tile]
                for j in range(8):
                    row = jnp.where(self.lane == first + j, jnp.sum(self.sum_s[k, j], axis=1, keepdims=True), row)
                self.gmap_s[k * N : (k + 1) * N, tile] = row
            return none

        lax.fori_loop(start, stop, chunk, 0)


class TokenSum:
    def __init__(self, spot, copies, part, y_land, z_land, y_sems, z_sems):
        self.spot, self.copies, self.part, self.y_land, self.z_land = spot, copies, part, y_land, z_land
        self.y_sems, self.z_sems = y_sems, z_sems
        self.group = copies.group(y_land)

    def push(self):
        spot = self.spot
        for far in (3, 2, 1):
            for way in (1, -1):
                self.over_y(spot.z_at(way * far), self.within(way, far))
        self.over_y(spot.z, None)

    def within(self, way, far):
        return self.spot.z < NZ - far if way == 1 else self.spot.z >= far

    def over_y(self, z, when):
        self.copies.send(self.part.at[z, 1 - self.spot.y], self.y_land.at[z], self.y_sems.at[z], self.spot.y_mate, when, self.group)

    def add(self, z, landed):
        part, y = self.part, self.spot.y
        part[z, y] = (part[z, y].astype(F32) + landed[...].astype(F32)).astype(BF16)

    def stage(self, far):
        spot = self.spot
        for side, way in enumerate((1, -1)):
            z = spot.z_at(way * far)
            goes = self.within(way, far)
            grown = goes & self.within(-way, 1)
            land, sem = self.z_land.at[side, z], self.z_sems.at[side, z]

            @pl.when(goes)
            def _(z=z):
                arrived(self.y_land.at[z], self.y_sems.at[z])
                self.add(z, self.y_land.at[z])

            if far < NZ - 1:

                @pl.when(grown)
                def _(z=z, land=land, sem=sem):
                    arrived(land, sem)
                    self.add(z, land)

            self.copies.send(self.part.at[z, spot.y], land, sem, spot.on_line(spot.z_at(way)), goes)

    def last(self):
        spot = self.spot
        z = spot.z
        arrived(self.y_land.at[z], self.y_sems.at[z])
        self.add(z, self.y_land.at[z])
        for side, way in enumerate((1, -1)):

            @pl.when(self.within(-way, 1))
            def _(land=self.z_land.at[side, z], sem=self.z_sems.at[side, z]):
                arrived(land, sem)
                self.add(z, land)

        return self.part[z, spot.y].astype(F32)


class RowSum:
    def __init__(self, spot, copies, part, c_land, x_land, z_land, c_sems, x_sems, z_sem):
        self.spot, self.copies, self.part = spot, copies, part
        self.c_land, self.x_land, self.z_land = c_land, x_land, z_land
        self.c_sems, self.x_sems, self.z_sem = c_sems, x_sems, z_sem
        self.groups = [copies.group(whole) for whole in (c_land, x_land, z_land.at[pl.ds(0, NZ - 1)])]

    def push(self):
        spot = self.spot
        for offset in (1, 2, 3, 0):
            z = spot.turn(offset)
            for x in range(2):
                self.copies.send(
                    self.part.at[place(z, x, 1 - spot.c)], self.c_land.at[z, x], self.c_sems.at[z], spot.c_mate, group=self.groups[0]
                )

    def add(self, z, x, landed):
        part, owner = self.part, place(z, x, self.spot.c)
        part[owner] = (part[owner].astype(F32) + landed.astype(F32)).astype(part.dtype)

    def second(self):
        spot = self.spot
        for offset in (1, 2, 3, 0):
            z = spot.turn(offset)
            arrived(self.c_land.at[z], self.c_sems.at[z])
            for x in range(2):
                self.add(z, x, self.c_land[z, x])
            self.copies.send(
                self.part.at[place(z, 1 - spot.x, spot.c)], self.x_land.at[z], self.x_sems.at[z], spot.x_mate, group=self.groups[1]
            )

    def third(self, offsets=(1, 2, 3, 0)):
        spot = self.spot
        for offset in offsets:
            z = spot.turn(offset)
            arrived(self.x_land.at[z], self.x_sems.at[z])
            self.add(z, spot.x, self.x_land[z])
            own = self.part.at[place(z, spot.x, spot.c)]
            if offset:
                self.copies.send(own, self.z_land.at[spot.z], self.z_sem, spot.on_line(z), group=self.groups[2])
            else:
                self.copies.keep(own, self.z_land.at[z])

    def last(self):
        arrived(self.z_land.at[pl.ds(0, NZ - 1)], self.z_sem)


class ChannelSum:
    def __init__(self, spot, copies, part, c_land, x_land, own, full, c_sem, x_sem, full_sems):
        self.spot, self.copies, self.part, self.own, self.full, self.full_sems = spot, copies, part, own, full, full_sems
        self.c_land, self.x_land, self.c_sem, self.x_sem = c_land, x_land, c_sem, x_sem
        self.group = copies.group(full.at[pl.ds(0, 4 * NZ - 1)])

    def push(self):
        self.copies.send(self.part.at[1 - self.spot.c], self.c_land, self.c_sem, self.spot.c_mate)

    def second(self):
        spot = self.spot
        arrived(self.c_land, self.c_sem)
        self.part[spot.c] = self.part[spot.c] + self.c_land[...]
        self.copies.send(self.part.at[spot.c, 1 - spot.x], self.x_land, self.x_sem, spot.x_mate)

    def spread(self, origin, device, src=None):
        src = self.full.at[origin] if src is None else src
        sem = self.full_sems.at[self.spot.slot(origin, device)]
        self.copies.send(src, self.full.at[origin], sem, device, group=self.group)

    def third(self):
        spot = self.spot
        arrived(self.x_land, self.x_sem)
        self.own[...] = (self.part[spot.c, spot.x] + self.x_land[...]).astype(BF16)
        for device in [spot.on_line(spot.z_at(offset)) for offset in (1, 2, 3)] + [spot.x_mate, spot.c_mate]:
            self.spread(spot.dp, device, self.own)
        self.copies.keep(self.own, self.full.at[spot.dp])

    def fourth(self):
        spot = self.spot
        for offset in (1, 2, 3):
            z = spot.z_at(-offset)
            origin = place(z, spot.x, spot.c)
            arrived(self.full.at[origin], self.full_sems.at[z])
            self.spread(origin, spot.x_mate)
            self.spread(origin, spot.c_mate)

    def fifth(self):
        spot = self.spot
        for offset in range(NZ):
            z = spot.z_at(-offset)
            origin = place(z, 1 - spot.x, spot.c)
            arrived(self.full.at[origin], self.full_sems.at[NZ + z])
            self.spread(origin, spot.c_mate)

    def last(self):
        arrived(self.full.at[pl.ds(0, 2 * NZ)], self.full_sems.at[2 * NZ])


class Held:
    def __init__(self, names, refs):
        for name, ref in zip(names, refs, strict=True):
            setattr(self, name, ref)


def block_scratch(half, feats, rows, chans, step_rows, width):
    tokens, n_dp, length = 2 * half * NZ, 4 * NZ, 2 * half
    vmem, dma = pltpu.VMEM, pltpu.SemaphoreType.DMA
    owners, steps = (n_dp, rows, chans), (n_dp, 2 * step_rows, chans // 2)
    part = (NZ, 2, width // 2, length)
    small = (width + 32) // 4
    held = {
        "w": vmem((3, n_dp, rows, chans), BF16),
        "acts": vmem((2, NZ, 2, half, feats), BF16),
        "dtp_own": vmem((NZ,) + steps[1:], BF16),
        "dtp": vmem(steps, BF16),
        "info": vmem((n_dp, 8, 128), F32),
        "mask": vmem((NZ, length, 128), F32),
        "low": vmem((tokens, chans), BF16),
        "gated": vmem((tokens, chans), BF16),
        "ggate": vmem((tokens, chans), BF16),
    }
    for name in ("x_in", "pre", "gate", "gg", "raw", "stepd", "drive", "gs", "read"):
        held[name] = vmem((tokens, chans), F32)
    held |= {
        "a": vmem((N, chans), F32),
        "state": vmem((tokens // 8 + 1, N, chans), F32),
        "pulled": vmem((N, chans), F32),
        "alog": vmem((N, chans), F32),
        "spread": vmem((tokens // 8, 2 * N, 8 * 128), F32),
        "shifted": vmem((tokens // 8 * 2 * N, 128), BF16),
        "sum": vmem((2, 8, N, 128), F32),
        "gmap": vmem((2 * N, tokens), F32),
        "dbl": vmem((width, tokens), F32),
        "part": vmem((2,) + part, BF16),
        "landing": vmem((2, 2 * NZ) + part[2:], BF16),
        "total": vmem((2,) + part, BF16),
        "mixed": vmem((NZ, 2, half, feats), BF16),
        "outw": vmem(owners, BF16),
        "ginz": vmem(owners, BF16),
        "gdtp": vmem(steps, BF16),
        "chan": vmem((2, 2, small, chans), F32),
        "y_land": vmem((2, NZ, half, feats), BF16),
        "z_land": vmem((2, 2, NZ, half, feats), BF16),
        "wc_land": vmem((3, NZ, 2, rows, chans), BF16),
        "wx_land": vmem((3, NZ, rows, chans), BF16),
        "dc_land": vmem((NZ, 2) + steps[1:], BF16),
        "dx_land": vmem((NZ,) + steps[1:], BF16),
        "fc_land": vmem((2, small, chans), F32),
        "fx_land": vmem((small, chans), F32),
        "f_own": vmem((small, chans), BF16),
        "block": vmem((half, feats), F32),
        "gresid": vmem((half, feats), F32),
        "tile": vmem((4, 8, 128), F32),
        "gain_part": vmem((2, n_dp, 128), F32),
        "gain": vmem((n_dp, 8, 128), F32),
        "gain_total": vmem((8, 128), F32),
        "squares": vmem((2, 8, 128), F32),
        "gain_land": vmem((n_dp - 1, 8, 128), F32),
        "resid": vmem((half, feats), F32),
        "cot": vmem((half, feats), F32),
        "xproj": vmem((width, chans * NZ), BF16),
        "ids": vmem((1, length), jnp.int32),
        "convw": vmem((4, chans * NZ), F32),
        "convb": vmem((1, chans * NZ), F32),
        "dtb": vmem((1, chans * NZ), F32),
        "alog_in": vmem((N, chans * NZ), F32),
        "skip": vmem((1, chans * NZ), F32),
        "load_sems": dma((9,)),
        "send_sems": dma((56,)),
        "keep_sems": dma((9,)),
        "own_sems": dma((4,)),
        "w_sems": dma((4, 2 * NZ + 1)),
        "act_sems": dma((2, NZ + 1)),
        "info_sem": dma(()),
        "dbl_sems": dma((2, 2)),
        "y_sems": dma((2, NZ)),
        "z_sems": dma((2, 2, NZ)),
        "wc_sems": dma((4, NZ)),
        "wx_sems": dma((4, NZ)),
        "wz_sems": dma((4,)),
        "f_sems": dma((2,)),
        "full_sems": dma((2 * NZ + 1,)),
        "tile_sems": dma((2,)),
        "gain_sems": dma((2,)),
    }
    return held


def block_kernel(names, *refs):
    (
        inx_ref, inz_ref, outp_ref, resid_in, cot_in, xproj_in, ids_in, convw_in, convb_in, dtb_in, alog_in, skip_in, gain_ref, dtp_ref,
        block_ref, gresid_ref, ggain_ref, ginx_ref, ginz_ref, goutp_ref, gdtp_ref, full_ref, squares_ref,
    ) = refs[:23]
    s = Held(names, refs[23:])
    spot = Spot()
    resid_ref, cot_ref, xproj_ref, ids_ref = s.resid, s.cot, s.xproj, s.ids
    convw_ref, convb_ref, dtb_ref, alog_ref, skip_ref = s.convw, s.convb, s.dtb, s.alog_in, s.skip
    loads = [
        pltpu.make_async_copy(src, dst, s.load_sems.at[k])
        for k, (src, dst) in enumerate(
            (
                (ids_in, s.ids), (resid_in, s.resid), (cot_in, s.cot), (xproj_in, s.xproj), (convw_in, s.convw),
                (convb_in, s.convb), (dtb_in, s.dtb), (alog_in, s.alog_in), (skip_in, s.skip),
            )
        )
    ]
    for load in loads:
        load.start()
    plane = [lax.rem(spot.dp + offset, 4 * NZ) for offset in range(1, 4 * NZ)]
    greet([(dp, spot.y) for dp in plane] + [spot.on_line(spot.z_at(dz), 1 - spot.y) for dz in range(NZ)])
    copies = Copies(s.send_sems, s.keep_sems)
    tokens, chans = s.x_in.shape
    half, feats = resid_ref.shape
    length = 2 * half
    columns = pl.ds(pl.multiple_of(spot.z * chans, chans), chans)
    quarters = [
        (slice(k * feats // NZ, (k + 1) * feats // NZ), slice(k * NZ, (k + 1) * NZ)) for k in range(NZ)
    ]
    sequences = [slice(k * length, (k + 1) * length) for k in range(NZ)]

    step_rows = dtp_ref[...].astype(F32)
    for z in range(NZ):
        s.dtp_own[z] = fold_columns(step_rows[:, z * chans : (z + 1) * chans]).astype(BF16)
    inx, inz, outp = (
        Gather(spot, copies, src, s.w.at[k], s.w_sems.at[k], s.own_sems.at[k]) for k, src in enumerate((inx_ref, inz_ref, outp_ref))
    )
    dtp = BlockGather(spot, copies, s.dtp_own, s.dtp, s.w_sems.at[3], s.own_sems.at[3])
    normed, cot = (Share(spot, copies, s.acts.at[k], s.act_sems.at[k]) for k in range(2))

    loads[0].wait()
    ids = jnp.broadcast_to(ids_ref[...], (8, length))
    lane = lax.broadcasted_iota(jnp.int32, (8, length), 1)
    sub = lax.broadcasted_iota(jnp.int32, (8, length), 0)
    info = jnp.broadcast_to(gain_ref[...].astype(F32), (8, length))
    for back in range(1, 4):
        same = jnp.where((pltpu.roll(ids, back, 1) == ids) & (lane >= back), 1.0, 0.0)
        info = jnp.where(sub == back, same, info)
    s.info[spot.dp] = info
    other_info = s.info.at[pl.ds(0, 4 * NZ - 1)]
    info_group = copies.group(other_info)
    for dp in plane:
        copies.send(s.info.at[spot.dp], s.info.at[spot.dp], s.info_sem, (dp, spot.y), group=info_group)
    inx.push()

    loads[1].wait()
    resid = resid_ref[...]
    row_square = jnp.sum(resid * resid, axis=1, keepdims=True)
    scaled = resid * lax.rsqrt(row_square / feats + eps_norm)
    s.tile[0] = jnp.broadcast_to(jnp.sum(row_square, axis=0, keepdims=True), (8, 128))
    copies.send(s.tile.at[0], s.tile.at[1], s.tile_sems.at[0], spot.y_mate)
    arrived(other_info, s.info_sem)
    for k in range(4 * NZ):
        cols = slice(k * 128, (k + 1) * 128)
        s.acts[0, spot.z, spot.y, :, cols] = (scaled[:, cols] * s.info[k, 0:1, :]).astype(BF16)
    normed.push()
    dtp.push()
    for load in loads[2:]:
        load.wait()
    s.acts[1, spot.z, spot.y] = cot_ref[...].astype(BF16)
    for k in range(NZ):
        s.mask[k] = column_masks(s.info[place(k, spot.x, spot.c)])
    inx.first()
    normed.first(1)
    inx.second()
    normed.first(2)
    inz.push((3, 0))
    dtp.first()
    dtp.second()
    normed.first(3)
    inz.push((1, 2))
    cot.push(False)
    normed.last()
    cot.send_y(spot.z)
    inx.last()

    all_normed = s.acts[0].reshape(tokens, feats)
    s.x_in[...] = dot(all_normed, s.w[0].reshape(-1, chans))
    taps = convw_ref[:, columns]
    bias = convb_ref[:, columns]
    for k, rows in enumerate(sequences):
        one = s.x_in[rows]
        pre = bias + taps[3:4] * one
        for back in range(1, 4):
            pre = pre + taps[3 - back : 4 - back] * (pltpu.roll(one, back, 0) * s.mask[k, :, back : back + 1])
        s.pre[rows] = pre
        s.low[rows] = (pre * sigmoid(pre)).astype(BF16)
    x_proj = xproj_ref[:, columns]
    dbl = dot(x_proj, s.low[...], NT)
    blocks = [(k, y) for k in range(NZ) for y in range(2)]
    width = dbl.shape[0] // 2
    for k, y in blocks:
        s.part[0, k, y] = dbl[y * width : (y + 1) * width, sequences[k]].astype(BF16)
    x_dbl = LineSum(
        spot, copies, s.part.at[0], s.landing.at[0], s.total.at[0], s.dbl_sems.at[0]
    )
    x_dbl.push()
    cot.first(1)
    inz.first()
    x_dbl.middle()
    outp.push((1, 0))
    cot.first(2)
    x_dbl.last()
    outp.push((2, 3))

    dtp.last()
    for k, y in blocks:
        s.dbl[y * width : (y + 1) * width, sequences[k]] = s.total[0, k, y].astype(F32)
    step_w = unfold_columns(s.dtp[...].astype(F32)).reshape(R, chans).astype(BF16)
    s.raw[...] = dot(s.dbl[:R].astype(BF16), step_w, TN) + dtb_ref[:, columns]
    for k, rows in enumerate(sequences):
        step = softplus(s.raw[rows])
        s.stepd[rows] = jnp.where(s.mask[k, :, 1:2] > 0.0, step, 1e30)
        s.drive[rows] = step * s.low[rows].astype(F32)
    s.a[...] = -jnp.exp(alog_ref[:, columns])
    s.state[0] = jnp.zeros((N, chans), F32)
    scan = Scan(
        s.a, s.stepd, s.drive, s.gs, s.read, s.read, s.gate, s.state, s.pulled, s.alog, s.spread, s.sum, s.gmap
    )
    scan.spread(s.dbl[R : R + 2 * N], s.shifted)
    steps = tokens // 8
    eighth = steps // 8
    inz.second()
    scan.forward(0, 4 * eighth)
    cot.first(3)
    outp.first()
    scan.forward(4 * eighth, steps)
    inz.last()
    s.gate[...] = dot(s.acts[0].reshape(tokens, feats), s.w[1].reshape(-1, chans))
    skip = skip_ref[:, columns]
    for rows in sequences:
        gate = s.gate[rows]
        scanned = s.read[rows] + skip * s.low[rows].astype(F32)
        s.gated[rows] = (scanned * gate * sigmoid(gate)).astype(BF16)

    mixed_sum, normed_sum = (
        TokenSum(spot, copies, part, s.y_land.at[k], s.z_land.at[k], s.y_sems.at[k], s.z_sems.at[k])
        for k, part in enumerate((s.mixed, s.acts.at[1]))
    )
    outw_sum, ginz_sum, ginx_sum, gdtp_sum = (
        RowSum(spot, copies, part, c_land, x_land, out, s.wc_sems.at[k], s.wx_sems.at[k], s.wz_sems.at[k])
        for k, (part, c_land, x_land, out) in enumerate((
            (s.outw, s.wc_land.at[0], s.wx_land.at[0], goutp_ref),
            (s.ginz, s.wc_land.at[1], s.wx_land.at[1], ginz_ref),
            (s.w.at[2], s.wc_land.at[2], s.wx_land.at[2], ginx_ref),
            (s.gdtp, s.dc_land, s.dx_land, gdtp_ref),
        ))
    )
    cot.last()
    for cols, owners in quarters:
        given = s.acts[1, :, :, :, cols].reshape(tokens, -1)
        s.outw[owners] = dot(given, s.gated[...], TN).astype(BF16).reshape(-1, *s.outw.shape[1:])
    outw_sum.push()
    outp.second()
    outw_sum.second()
    outp.last()
    s.gg[...] = dot(s.acts[1].reshape(tokens, feats), s.w[2].reshape(-1, chans))
    for cols, owners in quarters:
        part = dot(s.gated[...], s.w[2, owners].reshape(-1, chans), NT)
        s.mixed[:, :, :, cols] = part.astype(BF16).reshape(*s.mixed.shape[:3], -1)
    mixed_sum.push()
    outw_sum.third((1,))
    for rows in sequences:
        gate, gg = s.gate[rows], s.gg[rows]
        sig = sigmoid(gate)
        scanned = s.read[rows] + skip * s.low[rows].astype(F32)
        s.gs[rows] = gg * gate * sig
        s.ggate[rows] = (gg * scanned * sig * (1.0 + gate * (1.0 - sig))).astype(BF16)
    for cols, owners in quarters:
        given = s.acts[0, :, :, :, cols].reshape(tokens, -1)
        s.ginz[owners] = dot(given, s.ggate[...], TN).astype(BF16).reshape(-1, *s.ginz.shape[1:])
    ginz_sum.push()

    s.pulled[...] = jnp.zeros_like(s.pulled)
    s.alog[...] = jnp.zeros_like(s.alog)
    scan.backward(7 * eighth, steps)
    outw_sum.third((2,))
    ginz_sum.second()
    scan.backward(6 * eighth, 7 * eighth)
    outw_sum.third((3, 0))
    mixed_sum.stage(3)
    scan.backward(4 * eighth, 6 * eighth)
    ginz_sum.third((1,))
    scan.backward(2 * eighth, 4 * eighth)
    ginz_sum.third((2,))
    scan.backward(0, 2 * eighth)
    grad_bias = jnp.zeros((1, chans), F32)
    grad_skip = jnp.zeros((1, chans), F32)
    raw_rows = []
    for rows in sequences:
        conv, raw, gs, q = s.low[rows].astype(F32), s.raw[rows], s.gs[rows], s.read[rows]
        grad_raw = (conv * q + s.gate[rows]) * sigmoid(raw)
        s.gg[rows] = softplus(raw) * q + skip * gs
        grad_bias = grad_bias + jnp.sum(grad_raw, axis=0, keepdims=True)
        grad_skip = grad_skip + jnp.sum(gs * conv, axis=0, keepdims=True)
        raw_rows.append(grad_raw.astype(BF16))
    raw_low = jnp.concatenate(raw_rows, axis=0)
    dbl = jnp.concatenate([dot(step_w, raw_low, NT), s.gmap[...]], axis=0)
    for k, y in blocks:
        s.part[1, k, y] = dbl[y * width : (y + 1) * width, sequences[k]].astype(BF16)
    grad_dbl_sum = LineSum(
        spot, copies, s.part.at[1], s.landing.at[1], s.total.at[1], s.dbl_sems.at[1]
    )
    grad_dbl_sum.push()
    grad_step = dot(s.dbl[:R].astype(BF16), raw_low).reshape(4 * NZ, -1, chans)
    s.gdtp[...] = fold_columns(grad_step).astype(BF16)
    gdtp_sum.push()
    grad_dbl_sum.middle()
    mixed_sum.stage(2)
    ginz_sum.third((3, 0))
    gdtp_sum.second()
    grad_dbl_sum.last()

    grad_dbl = jnp.concatenate(
        [jnp.concatenate([s.total[1, k, y] for k in range(NZ)], axis=1) for y in range(2)], axis=0
    )
    s.gg[...] += dot(grad_dbl, x_proj, TN)
    sums = [jnp.zeros((1, chans), F32) for _ in range(5)]
    low_rows = []
    for k, rows in enumerate(sequences):
        pre, x_one = s.pre[rows], s.x_in[rows]
        sig = sigmoid(pre)
        one = s.gg[rows] * sig * (1.0 + pre * (1.0 - sig))
        sums[3] = sums[3] + jnp.sum(one * x_one, axis=0, keepdims=True)
        sums[4] = sums[4] + jnp.sum(one, axis=0, keepdims=True)
        grad_x = taps[3:4] * one
        for back in range(1, 4):
            masked = one * s.mask[k, :, back : back + 1]
            sums[3 - back] = sums[3 - back] + jnp.sum(masked * pltpu.roll(x_one, back, 0), axis=0, keepdims=True)
            grad_x = grad_x + taps[3 - back : 4 - back] * pltpu.roll(masked, length - back, 0)
        low_rows.append(grad_x.astype(BF16))
    grad_xin = jnp.concatenate(low_rows, axis=0)
    s.chan[...] = jnp.concatenate(
        [dot(grad_dbl, s.low[...]), s.alog[...] * s.a[...], grad_bias, grad_skip, jnp.zeros((6, chans), F32)]
        + sums + [jnp.zeros((3, chans), F32)], axis=0
    ).reshape(s.chan.shape)
    small_sum = ChannelSum(
        spot, copies, s.chan, s.fc_land, s.fx_land, s.f_own, full_ref, s.f_sems.at[0], s.f_sems.at[1], s.full_sems
    )
    small_sum.push()
    copies.settle(outp.group)
    for cols, owners in quarters:
        given = s.acts[0, :, :, :, cols].reshape(tokens, -1)
        s.w[2, owners] = dot(given, grad_xin, TN).astype(BF16).reshape(-1, *s.outw.shape[1:])
    ginx_sum.push()
    small_sum.second()
    cot.settle()
    for cols, owners in quarters:
        part = dot(grad_xin, s.w[0, owners].reshape(-1, chans), NT) + dot(s.ggate[...], s.w[1, owners].reshape(-1, chans), NT)
        s.acts[1, :, :, :, cols] = part.astype(BF16).reshape(*s.mixed.shape[:3], -1)
        gain_part = jnp.sum(part * s.acts[0, :, :, :, cols].reshape(tokens, -1).astype(F32), axis=0, keepdims=True)
        for k in range(NZ):
            owner = owners.start + k
            s.gain_part[0, owner : owner + 1] = gain_part[:, k * 128 : (k + 1) * 128] / s.info[owner, 0:1]
    copies.send(s.gain_part.at[0], s.gain_part.at[1], s.gain_sems.at[0], spot.y_mate)
    normed_sum.push()
    mixed_sum.stage(1)
    ginx_sum.second()
    gdtp_sum.third()
    ginx_sum.third((1,))
    normed_sum.stage(3)
    small_sum.third()
    ginx_sum.third((2,))
    arrived(s.gain_part.at[1], s.gain_sems.at[0])
    for k in range(4 * NZ):
        s.gain[k] = jnp.broadcast_to(s.gain_part[0, k : k + 1] + s.gain_part[1, k : k + 1], (8, 128))
    gain_group = copies.group(s.gain_land)
    for offset, dp in enumerate(plane):
        copies.send(s.gain.at[dp], s.gain_land.at[offset], s.gain_sems.at[1], (dp, spot.y), group=gain_group)
    normed_sum.stage(2)
    ginx_sum.third((3, 0))
    normed_sum.stage(1)
    small_sum.fourth()

    mixed = mixed_sum.last()
    resid = resid_ref[...]
    s.block[...] = resid + mixed
    copies.keep(s.block, block_ref)
    s.tile[2] = jnp.broadcast_to(jnp.sum(jnp.sum(mixed * mixed, axis=1, keepdims=True), axis=0, keepdims=True), (8, 128))
    copies.send(s.tile.at[2], s.tile.at[3], s.tile_sems.at[1], spot.y_mate)
    small_sum.fifth()
    outw_sum.last()
    ginz_sum.last()
    gdtp_sum.last()
    arrived(s.tile.at[1], s.tile_sems.at[0])
    s.squares[0] = s.tile[0] + s.tile[1]
    arrived(s.tile.at[3], s.tile_sems.at[1])
    s.squares[1] = s.tile[2] + s.tile[3]
    copies.keep(s.squares, squares_ref)

    grad_rows = normed_sum.last()
    inv = lax.rsqrt(jnp.sum(resid * resid, axis=1, keepdims=True) / feats + eps_norm)
    scaled = resid * inv
    gain = jnp.concatenate([s.info[k, 0:1] for k in range(4 * NZ)], axis=1)
    grad_scaled = grad_rows * gain
    mean = jnp.sum(grad_scaled * scaled, axis=1, keepdims=True) / feats
    s.gresid[...] = cot_ref[...] + inv * (grad_scaled - scaled * mean)
    copies.keep(s.gresid, gresid_ref)
    arrived(s.gain_land, s.gain_sems.at[1])
    total = s.gain[spot.dp]
    for offset in range(4 * NZ - 1):
        total = total + s.gain_land[offset]
    s.gain_total[...] = total
    copies.keep(s.gain_total, ggain_ref)
    ginx_sum.last()
    small_sum.last()
    copies.wait_sent()
    assert copies.used == s.send_sems.shape[0], copies.used


def block_call(in_x, in_z, out_p, residual, cotangent, gain, ids, dt_p, x_proj, conv_w, conv_b, dt_b, a_log, d_skip):
    half, feats = residual.shape
    rows, wide = in_x.shape
    n_dp, chans = 4 * NZ, wide // NZ
    held = block_scratch(half, feats, rows, chans, dt_p.shape[0], x_proj.shape[0])
    shape = jax.ShapeDtypeStruct
    outs = [
        shape((half, feats), F32), shape((half, feats), F32), shape((8, 128), F32),
        shape((NZ, rows, chans), BF16), shape((NZ, rows, chans), BF16), shape((NZ, rows, chans), BF16),
        shape((NZ, 2 * dt_p.shape[0], chans // 2), BF16), shape((n_dp, (x_proj.shape[0] + 32) // 4, chans), BF16),
        shape((2, 8, 128), F32),
    ]
    in_any = pl.BlockSpec(memory_space=pl.ANY)
    in_vmem = pl.BlockSpec(memory_space=pltpu.VMEM)
    return pl.pallas_call(
        functools.partial(block_kernel, list(held)),
        out_shape=outs,
        in_specs=[in_any] * 12 + [in_vmem] * 2,
        out_specs=[in_any] * len(outs),
        scratch_shapes=list(held.values()),
        name="block",
        compiler_params=pltpu.CompilerParams(collective_id=1, has_side_effects=True, vmem_limit_bytes=62 << 20),
    )(in_x, in_z, out_p, residual, cotangent, x_proj, ids, conv_w, conv_b, dt_b, a_log, d_skip, gain, dt_p)


def finish_kernel(
    scale, block_in, gresid_in, ginx_in, ginz_in, goutp_in, gdtp_in, full_in, ggain_in, squares_in,
    block_ref, gresid_ref, ginx_ref, ginz_ref, goutp_ref, gdtp_ref, xproj_ref, alog_ref, dtb_ref, skip_ref, convw_ref, convb_ref,
    ggain_ref, rms_ref, mrms_ref,
    token_s, low_s, step_s, full_s, ggain_s, squares_s, wide_s, gdtp_s, xproj_s, rows_s, in_sems, out_sems,
):
    begun = []

    def out(src, dst):
        copy = pltpu.make_async_copy(src, dst, out_sems.at[len(begun)])
        copy.start()
        begun.append(copy)

    reads = [
        pltpu.make_async_copy(src, dst, in_sems.at[k])
        for k, (src, dst) in enumerate(
            (
                (ginx_in, low_s.at[0]), (ginz_in, low_s.at[1]), (goutp_in, low_s.at[2]), (full_in, full_s), (gdtp_in, step_s),
                (block_in, token_s.at[0]), (gresid_in, token_s.at[1]), (ggain_in, ggain_s), (squares_in, squares_s),
            )
        )
    ]
    for read in reads:
        read.start()
    chans = low_s.shape[3]
    columns = [slice(z * chans, (z + 1) * chans) for z in range(NZ)]
    for k, ref in enumerate((ginx_ref, ginz_ref, goutp_ref)):
        reads[k].wait()
        for z, cols in enumerate(columns):
            wide_s[k, :, cols] = low_s[k, z].astype(F32)
        out(wide_s.at[k], ref)
    reads[3].wait()
    rows, width = full_s.shape[1], xproj_s.shape[0]
    for z, cols in enumerate(columns):
        for k in range(4):
            found = full_s[place(z, k % 2, k // 2)].astype(F32)
            upto = min(rows, width - k * rows)
            xproj_s[k * rows : k * rows + upto, cols] = found[:upto]
        rows_s[:, cols] = found[upto:]
    out(xproj_s, xproj_ref)
    out(rows_s.at[pl.ds(0, N)], alog_ref)
    for at, ref in ((N, dtb_ref), (N + 1, skip_ref), (24, convw_ref), (28, convb_ref)):
        out(rows_s.at[pl.ds(at, ref.shape[0])], ref)
    reads[4].wait()
    for z, cols in enumerate(columns):
        gdtp_s[:, cols] = unfold_columns(step_s[z].astype(F32))
    out(gdtp_s, gdtp_ref)
    for k, ref in enumerate((block_ref, gresid_ref)):
        reads[5 + k].wait()
        out(token_s.at[k], ref)
    reads[7].wait()
    out(ggain_s.at[pl.ds(0, 1)], ggain_ref)
    reads[8].wait()
    for k, ref in enumerate((rms_ref, mrms_ref)):
        ref[...] = jnp.sqrt(squares_s[k, 0:1, 0:1] * scale)
    for copy in begun:
        copy.wait()


def finish_call(block, gresid, ginx, ginz, goutp, gdtp, full, ggain, squares, width):
    rows, chans = ginx.shape[1:]
    wide = chans * NZ
    shape = lambda count, columns=wide: jax.ShapeDtypeStruct((count, columns), F32)
    vmem, dma = pltpu.VMEM, pltpu.SemaphoreType.DMA
    in_any = pl.BlockSpec(memory_space=pl.ANY)
    outs = [
        shape(*block.shape), shape(*gresid.shape), shape(rows), shape(rows), shape(rows), shape(gdtp.shape[1] // 2), shape(width),
        shape(N), shape(1), shape(1), shape(4), shape(1), shape(1, 128), shape(1, 1), shape(1, 1),
    ]
    return pl.pallas_call(
        functools.partial(finish_kernel, 1.0 / (2 * block.shape[0] * block.shape[1])),
        out_shape=outs,
        in_specs=[in_any] * 9,
        out_specs=[in_any] * (len(outs) - 2) + [pl.BlockSpec(memory_space=vmem)] * 2,
        scratch_shapes=[
            vmem((2,) + block.shape, F32), vmem((3,) + ginx.shape, BF16), vmem(gdtp.shape, BF16), vmem(full.shape, BF16),
            vmem(ggain.shape, F32), vmem(squares.shape, F32), vmem((3, rows, wide), F32), vmem((gdtp.shape[1] // 2, wide), F32),
            vmem((width, wide), F32), vmem((32, wide), F32), dma((9,)), dma((len(outs) - 2,)),
        ],
        name="finish",
        compiler_params=pltpu.CompilerParams(vmem_limit_bytes=60 << 20),
    )(block, gresid, ginx, ginz, goutp, gdtp, full, ggain, squares)


def per_device_split(
    residual,
    norm_gain,
    in_proj_x,
    in_proj_z,
    x_proj,
    dt_proj,
    dt_bias,
    conv_weight,
    conv_bias,
    a_log,
    d_skip,
    out_proj,
    doc_ids,
    cotangent,
):
    parts = block_call(
        in_proj_x, in_proj_z, out_proj, residual, cotangent, norm_gain[None], doc_ids[None], dt_proj, x_proj, conv_weight,
        conv_bias[None], dt_bias[None], a_log, d_skip[None],
    )
    block, gresid, ggain, ginx, ginz, goutp, gdtp, full, squares = parts
    block, gresid, ginx, ginz, goutp, gdtp, g_xproj, g_alog, g_dtb, g_skip, g_convw, g_convb, ggain, rms, mrms = finish_call(
        block, gresid, ginx, ginz, goutp, gdtp, full, ggain, squares, x_proj.shape[0]
    )
    return (
        block,
        gresid,
        ggain[0],
        ginx,
        ginz,
        g_xproj,
        gdtp,
        g_dtb[0],
        g_convw,
        g_convb[0],
        g_alog,
        g_skip[0],
        goutp,
        rms[0],
        mrms[0],
    )


def norm_rows(values, gain_val):
    mean_square = jnp.mean(values * values, axis=1, keepdims=True)
    return values * lax.rsqrt(mean_square + eps_norm) * gain_val


def conv_local(x_in, doc_ids, conv_weight, conv_bias):
    kernel_len = conv_weight.shape[0]
    length = x_in.shape[0]
    padded = jnp.pad(x_in, ((kernel_len - 1, 0), (0, 0)))
    id_pad = jnp.concatenate([jnp.full((kernel_len - 1,), -1, jnp.int32), doc_ids])
    summed = conv_bias + jnp.zeros_like(x_in)
    for offset in range(kernel_len):
        same_doc = (id_pad[offset : offset + length] == doc_ids).astype(jnp.float32)
        summed = summed + conv_weight[offset] * padded[offset : offset + length] * same_doc[:, None]
    return summed


def per_device(
    residual,
    norm_gain,
    in_proj_x,
    in_proj_z,
    x_proj,
    dt_proj,
    dt_bias,
    conv_weight,
    conv_bias,
    a_log,
    d_skip,
    out_proj,
    doc_ids,
    cotangent,
):
    gathered = (
        lax.all_gather(norm_gain, "dp", axis=0, tiled=True),
        lax.all_gather(in_proj_x, "dp", axis=0, tiled=True),
        lax.all_gather(in_proj_z, "dp", axis=0, tiled=True),
        lax.all_gather(dt_proj, "dp", axis=0, tiled=True),
        lax.all_gather(out_proj, "dp", axis=0, tiled=True),
    )
    gain_all, inx_all, inz_all, step_all, out_all = gathered
    seq_len = doc_ids.shape[0]
    normed_f32, norm_back = jax.vjp(norm_rows, residual, gain_all.astype(jnp.float32))
    normed = lax.all_gather(normed_f32.astype(jnp.bfloat16), "tensor", axis=0, tiled=True)
    x_in = jnp.dot(normed, inx_all, preferred_element_type=jnp.float32)
    gate_in = jnp.dot(normed, inz_all, preferred_element_type=jnp.float32)

    def conv_act(x_val, weight_val, bias_val):
        return jax.nn.silu(conv_local(x_val, doc_ids, weight_val, bias_val))

    conv_out, conv_back = jax.vjp(conv_act, x_in, conv_weight, conv_bias)
    conv_low = conv_out.astype(jnp.bfloat16)
    dbl_part = lax.dot_general(
        conv_low, x_proj, (((1,), (1,)), ((), ())), preferred_element_type=jnp.float32
    )
    x_dbl, resid_square = lax.psum((dbl_part, jnp.sum(residual * residual)), "tensor")
    doc_starts = doc_ids != jnp.concatenate([jnp.full((1,), -1, jnp.int32), doc_ids[:-1]])
    carry_keep = 1.0 - doc_starts.astype(jnp.float32)

    cot_all = lax.all_gather(cotangent.astype(jnp.bfloat16), "tensor", axis=0, tiled=True)
    grad_gated = jnp.dot(cot_all, out_all, preferred_element_type=jnp.float32)
    gated_low, grad_gate_low, grad_conv, grad_dbl_part, grad_step_w, grad_bias, grad_alog, grad_skip = scan_call(
        x_dbl, conv_low, gate_in, grad_gated, step_all, dt_bias, a_log, d_skip, carry_keep
    )
    mixed = lax.psum_scatter(
        lax.dot_general(
            gated_low, out_all, (((1,), (1,)), ((), ())), preferred_element_type=jnp.float32
        ),
        "tensor",
        scatter_dimension=0,
        tiled=True,
    )
    block_out = residual + mixed
    mixed_square = lax.psum(jnp.sum(mixed * mixed), "tensor")
    rms_resid = jnp.sqrt(resid_square / (seq_len * D)).reshape(1)
    rms_mixed = jnp.sqrt(mixed_square / (seq_len * D)).reshape(1)
    grad_out_w = lax.dot_general(
        cot_all, gated_low, (((0,), (0,)), ((), ())), preferred_element_type=jnp.float32
    )
    grad_dbl = lax.psum(grad_dbl_part.T, "tensor")
    grad_dbl_low = grad_dbl.astype(jnp.bfloat16)
    grad_conv = grad_conv + jnp.dot(grad_dbl_low, x_proj, preferred_element_type=jnp.float32)
    grad_xproj = lax.dot_general(
        grad_dbl_low, conv_low, (((0,), (0,)), ((), ())), preferred_element_type=jnp.float32
    )
    grad_xin, grad_convw, grad_convb = conv_back(grad_conv)
    grad_xin_low = grad_xin.astype(jnp.bfloat16)
    grad_inx = lax.dot_general(
        normed, grad_xin_low, (((0,), (0,)), ((), ())), preferred_element_type=jnp.float32
    )
    grad_inz = lax.dot_general(
        normed, grad_gate_low, (((0,), (0,)), ((), ())), preferred_element_type=jnp.float32
    )
    first_term = lax.dot_general(
        grad_xin_low, inx_all, (((1,), (1,)), ((), ())), preferred_element_type=jnp.float32
    )
    second_term = lax.dot_general(
        grad_gate_low, inz_all, (((1,), (1,)), ((), ())), preferred_element_type=jnp.float32
    )
    grad_normed = lax.psum_scatter(
        first_term + second_term, "tensor", scatter_dimension=0, tiled=True
    )
    grad_rows_x, grad_gain_part = norm_back(grad_normed)
    grad_residual = cotangent + grad_rows_x
    grad_gain = lax.psum(grad_gain_part, "tensor")
    gain_shard, inx_shard, inz_shard, step_shard, out_shard = (
        lax.psum_scatter(grad_gain, "dp", scatter_dimension=0, tiled=True),
        lax.psum_scatter(grad_inx, "dp", scatter_dimension=0, tiled=True),
        lax.psum_scatter(grad_inz, "dp", scatter_dimension=0, tiled=True),
        lax.psum_scatter(grad_step_w, "dp", scatter_dimension=0, tiled=True),
        lax.psum_scatter(grad_out_w, "dp", scatter_dimension=0, tiled=True),
    )
    small_sums = lax.psum(
        (grad_xproj, grad_bias, grad_convw, grad_convb, grad_alog, grad_skip), "dp"
    )
    xproj_sum, bias_sum, convw_sum, convb_sum, alog_sum, skip_sum = small_sums
    return (
        block_out,
        grad_residual,
        gain_shard,
        inx_shard,
        inz_shard,
        xproj_sum,
        step_shard,
        bias_sum,
        convw_sum,
        convb_sum,
        alog_sum,
        skip_sum,
        out_shard,
        rms_resid,
        rms_mixed,
    )


def solution(mesh):
    placed = (
        P(("dp", "tensor"), None),
        P("dp"),
        P("dp", "tensor"),
        P("dp", "tensor"),
        P(None, "tensor"),
        P("dp", "tensor"),
        P("tensor"),
        P(None, "tensor"),
        P("tensor"),
        P(None, "tensor"),
        P("tensor"),
        P("dp", "tensor"),
        P("dp"),
        P(("dp", "tensor"), None),
    )
    return jax.shard_map(
        per_device_split if mesh.shape["dp"] == 4 * NZ else per_device,
        mesh=mesh,
        in_specs=placed,
        out_specs=(
            P(("dp", "tensor"), None),
            P(("dp", "tensor"), None),
            P("dp"),
            P("dp", "tensor"),
            P("dp", "tensor"),
            P(None, "tensor"),
            P("dp", "tensor"),
            P("tensor"),
            P(None, "tensor"),
            P("tensor"),
            P(None, "tensor"),
            P("tensor"),
            P("dp", "tensor"),
            P("dp"),
            P("dp"),
        ),
        check_vma=False,
    )
```
